128 devices in a mesh: wide: 32 (over x, z, core), narrow: 4 (over y).
Axes of the slice: x: 4, y: 4, z: 4, core: 2. Of those that a mesh axis runs over, the one named last changes fastest.
Arguments:
- tokens: bfloat16 [256, 588, 384], P(('wide', 'narrow')), may hold values from -6 to 6
- item_frames: int32 [256, 3], P(('wide', 'narrow')), may hold values from 0 to 3, as said below
- ln1_gain: bfloat16 [384], P(('wide', 'narrow')), may hold values from 0.25 to 1.75
- ln1_bias: bfloat16 [384], P(('wide', 'narrow')), may hold values from -2 to 2
- qkv_weight: bfloat16 [384, 1152], P(('wide', 'narrow')), may hold values from -0.3125 to 0.3125
- qv_bias: bfloat16 [768], P(('wide', 'narrow')), may hold values from -2 to 2
- out_weight: bfloat16 [384, 384], P(('wide', 'narrow')), may hold values from -1.25 to 1.25
- out_bias: bfloat16 [384], P(('wide', 'narrow')), may hold values from -2 to 2
- ln2_gain: bfloat16 [384], P(('wide', 'narrow')), may hold values from 0.25 to 1.75
- ln2_bias: bfloat16 [384], P(('wide', 'narrow')), may hold values from -2 to 2
- up_weight: bfloat16 [384, 1536], P(('wide', 'narrow')), may hold values from -0.3125 to 0.3125
- up_bias: bfloat16 [1536], P(('wide', 'narrow')), may hold values from -3 to 3
- down_weight: bfloat16 [1536, 384], P(('wide', 'narrow')), may hold values from -0.15625 to 0.15625
- down_bias: bfloat16 [384], P(('wide', 'narrow')), may hold values from -2 to 2
- cotangent: bfloat16 [256, 588, 384], P(('wide', 'narrow')), may hold values from -6 to 6
Outputs:
- output: bfloat16 [256, 588, 384], P(('wide', 'narrow'))
- input_grad: float32 [256, 588, 384], P(('wide', 'narrow'))
- grad_ln1_gain: float32 [384], P(('wide', 'narrow'))
- grad_ln1_bias: float32 [384], P(('wide', 'narrow'))
- grad_qkv_weight: float32 [384, 1152], P(('wide', 'narrow'))
- grad_qv_bias: float32 [768], P(('wide', 'narrow'))
- grad_out_weight: float32 [384, 384], P(('wide', 'narrow'))
- grad_out_bias: float32 [384], P(('wide', 'narrow'))
- grad_ln2_gain: float32 [384], P(('wide', 'narrow'))
- grad_ln2_bias: float32 [384], P(('wide', 'narrow'))
- grad_up_weight: float32 [384, 1536], P(('wide', 'narrow'))
- grad_up_bias: float32 [1536], P(('wide', 'narrow'))
- grad_down_weight: float32 [1536, 384], P(('wide', 'narrow'))
- grad_down_bias: float32 [384], P(('wide', 'narrow'))
The draws below stay inside these ranges and needn't reach their ends.
Inputs may be any that keep to these rules, and one draw needn't show every extreme that they name: `item_frames`: row s gives the frames of the items packed into slot s, in order; zeros stand only after the last item, a row sums to 3 or less, and the rest of the slot is padding. Every aligned block of 2 slots holds a slot with a single item of 3 frames.
All inputs are finite; a program needn't handle non-finite values.
Results may differ from the reference program's by a relative error of at most 0.015.
Values may be sent and summed in bfloat16 or wider, within the bound.
No kernel may reach another device: no remote copies, remote signals or barrier semaphores. Data moves between devices by JAX's collectives and lax.ppermute only.
A program may use at most 192 MiB of HBM per device.

```python
import jax
import jax.numpy as jnp
from jax import lax

D = 384
HEADS = 16
HEAD_DIM = 24
FF = 1536
FRAME = 196
SLOTS_DEV = 2
SLOT_TOK = 588
SLOTS = 256


def draw_item_frames(key, part):
    key = jax.random.fold_in(key, 11)
    key_pick, key_force = jax.random.split(key)
    layouts = jnp.array([[3, 0, 0], [2, 1, 0], [1, 2, 0], [1, 1, 1], [2, 0, 0], [1, 1, 0], [1, 0, 0]], dtype=jnp.int32)
    chosen = jax.random.randint(key_pick, (SLOTS,), 0, 7)
    forced = jax.random.randint(key_force, (SLOTS // SLOTS_DEV,), 0, SLOTS_DEV)
    slot_index = jnp.arange(SLOTS, dtype=jnp.int32)
    block_of = slot_index // SLOTS_DEV
    chosen = jnp.where(slot_index % SLOTS_DEV == forced[block_of], 0, chosen)
    return layouts[chosen]


def levels(key, shape, cuts, smallest, largest):
    def one(position, parts):
        heights = jax.random.uniform(jax.random.fold_in(jax.random.fold_in(key, 6), position), (parts,), jnp.float32, smallest / len(cuts), largest / len(cuts))
        return jnp.repeat(jnp.exp(heights), shape[position] // parts).reshape((-1,) + (1,) * (len(shape) - position - 1))

    level = one(*cuts[0])
    for cut in cuts[1:]:
        level = level * one(*cut)
    return level


def gaussian(stream_key, dims, scale, bound, pieces=(), kind=jnp.bfloat16):
    entries = jax.random.normal(stream_key, dims, jnp.float32) * scale
    if len(pieces) > 0:
        entries = levels(stream_key, dims, pieces, -0.22, 0.18) * entries
    return jnp.clip(entries, min=-bound, max=bound).astype(kind)


def setup_inputs(seed: int = 0) -> dict:
    arg_keys = jax.random.split(jax.random.key(seed), 16)
    return {
        "tokens": gaussian(arg_keys[0], (SLOTS, SLOT_TOK, D), 1.0, 6.0, ((0, 128),)),
        "item_frames": draw_item_frames(jax.random.fold_in(arg_keys[15], 71), 0),
        "ln1_gain": jnp.clip(1.0 + 0.15 * jax.random.normal(arg_keys[2], (D,), jnp.float32), 0.25, 1.75).astype(jnp.bfloat16),
        "ln1_bias": gaussian(arg_keys[3], (D,), 0.3, 2.0, ((0, 128),)),
        "qkv_weight": gaussian(arg_keys[4], (D, 3 * D), D ** -0.5, 0.3125, ((0, 128),)),
        "qv_bias": gaussian(arg_keys[5], (2 * D,), 0.3, 2.0, ((0, 128),)),
        "out_weight": gaussian(arg_keys[6], (D, D), (D // 16) ** -0.5, 1.25, ((0, 128),)),
        "out_bias": gaussian(arg_keys[7], (D,), 0.3, 2.0, ((0, 128),)),
        "ln2_gain": jnp.clip(1.0 + 0.15 * jax.random.normal(arg_keys[8], (D,), jnp.float32), 0.25, 1.75).astype(jnp.bfloat16),
        "ln2_bias": gaussian(arg_keys[9], (D,), 0.3, 2.0, ((0, 128),)),
        "up_weight": gaussian(arg_keys[10], (D, FF), D ** -0.5, 0.3125, ((0, 128),)),
        "up_bias": gaussian(arg_keys[11], (FF,), 0.5, 3.0, ((0, 128),)),
        "down_weight": gaussian(arg_keys[12], (FF, D), FF ** -0.5, 0.15625, ((0, 128),)),
        "down_bias": gaussian(arg_keys[13], (D,), 0.3, 2.0, ((0, 128),)),
        "cotangent": gaussian(arg_keys[14], (SLOTS, SLOT_TOK, D), 1.0, 6.0, ((0, 128),)),
    }


@jax.custom_vjp
def low(v):
    return lax.optimization_barrier(v.astype(jnp.bfloat16)).astype(jnp.float32)

@jax.custom_vjp
def low_back(v):
    return v

def low_keep(v):
    return (low(v), None)

def low_pass(kept, grad):
    return (grad,)

def back_keep(v):
    return (v, None)

def back_low(kept, grad):
    return (low(grad),)
low.defvjp(low_keep, low_pass)
low_back.defvjp(back_keep, back_low)
EPSILON = 1e-05
NEGATIVE = -1e+30

def matmul(left, right):
    return jnp.dot(left, right, precision=lax.Precision.HIGHEST)

def norm_rows(values, gain, offset):
    average = lax.optimization_barrier(jnp.mean(values, axis=-1, keepdims=True))
    centred = values - average
    variance = lax.optimization_barrier(jnp.mean(centred * centred, axis=-1, keepdims=True))
    return centred * lax.rsqrt(variance + EPSILON) * gain + offset

def slot_visible(counts):
    frame_of = jnp.arange(SLOT_TOK, dtype=jnp.int32) // FRAME
    first_end = counts[0]
    second_end = first_end + counts[1]
    third_end = second_end + counts[2]
    group_of = (frame_of >= first_end).astype(jnp.int32) + (frame_of >= second_end).astype(jnp.int32) + (frame_of >= third_end).astype(jnp.int32)
    return (group_of[:, None] == group_of[None, :]) & (frame_of[None, :] <= frame_of[:, None])

def layer(params, inputs, visible):
    gain_one, bias_one, qkv_w, qv_b, out_w, out_b, gain_two, bias_two, up_w, up_b, down_w, down_b = params
    first = low(norm_rows(inputs, gain_one, bias_one))
    projected = matmul(first, qkv_w)
    queries = low_back(low(projected[:, :D] + qv_b[:D]))
    keys = low_back(low(projected[:, D:2 * D]))
    values = low_back(low(projected[:, 2 * D:] + qv_b[D:]))
    query_heads = queries.reshape(SLOT_TOK, HEADS, HEAD_DIM)
    key_heads = keys.reshape(SLOT_TOK, HEADS, HEAD_DIM)
    value_heads = values.reshape(SLOT_TOK, HEADS, HEAD_DIM)
    score_scale = 1.0 / jnp.sqrt(jnp.float32(HEAD_DIM))
    scores = low_back(jnp.einsum('qhd,khd->hqk', query_heads, key_heads, precision=lax.Precision.HIGHEST) * score_scale)
    masked = jnp.where(visible[None], scores, NEGATIVE)
    row_peak = lax.optimization_barrier(jnp.max(masked, axis=-1, keepdims=True))
    weights = jnp.exp(masked - row_peak)
    probs = weights / lax.optimization_barrier(jnp.sum(weights, axis=-1, keepdims=True))
    mixed = jnp.einsum('hqk,khd->qhd', low(probs), value_heads, precision=lax.Precision.HIGHEST)
    mixed = low_back(low(mixed.reshape(SLOT_TOK, D)))
    attended = low_back(matmul(mixed, out_w) + out_b)
    resid = inputs + attended
    second = low(norm_rows(resid, gain_two, bias_two))
    up_pre = low_back(matmul(second, up_w) + up_b)
    activated = low(jax.nn.gelu(up_pre))
    branch = low_back(matmul(activated, down_w) + down_b)
    return resid + branch

def reference(tokens, item_frames, ln1_gain, ln1_bias, qkv_weight, qv_bias, out_weight, out_bias, ln2_gain, ln2_bias, up_weight, up_bias, down_weight, down_bias, cotangent):
    params = (ln1_gain.astype(jnp.float32), ln1_bias.astype(jnp.float32), qkv_weight.astype(jnp.float32), qv_bias.astype(jnp.float32), out_weight.astype(jnp.float32), out_bias.astype(jnp.float32), ln2_gain.astype(jnp.float32), ln2_bias.astype(jnp.float32), up_weight.astype(jnp.float32), up_bias.astype(jnp.float32), down_weight.astype(jnp.float32), down_bias.astype(jnp.float32))

    def one_slot(running, slot_data):
        slot_tokens, counts, slot_cotangent = slot_data
        visible = slot_visible(counts)
        result, pullback = jax.vjp(lambda weights_in, inputs: layer(weights_in, inputs, visible), params, slot_tokens.astype(jnp.float32))
        grad_params, grad_inputs = pullback(slot_cotangent.astype(jnp.float32))
        running = tuple((total + grad for total, grad in zip(running, grad_params)))
        return (running, (result.astype(jnp.bfloat16), grad_inputs))
    zero_sums = tuple((jnp.zeros_like(param) for param in params))
    totals, (output, input_grad) = lax.scan(one_slot, zero_sums, (tokens, item_frames, cotangent))
    return (output, input_grad, totals[0], totals[1], totals[2], totals[3], totals[4], totals[5], totals[6], totals[7], totals[8], totals[9], totals[10], totals[11])
```

```python
import math

import jax
import jax.numpy as jnp
from jax import lax
from jax.experimental import pallas as pl
from jax.experimental.pallas import tpu as pltpu
from jax.sharding import Mesh
from jax.sharding import PartitionSpec as P

HEADS = 16
HEAD = 24
FRAME = 196
WIDE = 640
EPSILON = 1e-05
NEGATIVE = -1e30
bf16 = jnp.bfloat16
f32 = jnp.float32
FORWARD_BLOCKS = ((0, 128, 208), (128, 384, 400), (384, 640, 592))
BACKWARD_BLOCKS = ((0, 128, 256), (128, 384, 512), (384, 592, 640))


def dot(left, right, over):
    return lax.dot_general(left, right, (((over[0],), (over[1],)), ((), ())), preferred_element_type=f32)


def norm_parts(values):
    centred = values - jnp.mean(values, axis=-1, keepdims=True)
    inverse = lax.rsqrt(jnp.mean(centred * centred, axis=-1, keepdims=True) + EPSILON)
    return centred * inverse, inverse


def three_parts(values):
    high = values.astype(bf16).astype(f32)
    rest = values - high
    middle = rest.astype(bf16).astype(f32)
    return high, middle, rest - middle


def rows_of(rows, width):
    index = lax.broadcasted_iota(jnp.int32, (8, width), 0)
    out = jnp.zeros((8, width), f32)
    for k, row in enumerate(rows):
        out = jnp.where(index == k, row, out)
    return out


def mask_rows(counts_ref, slot):
    lane = lax.broadcasted_iota(jnp.int32, (1, WIDE), 1)
    first_end = counts_ref[slot, 0]
    second_end = first_end + counts_ref[slot, 1]
    third_end = second_end + counts_ref[slot, 2]
    group = [
        (f >= first_end).astype(jnp.int32) + (f >= second_end).astype(jnp.int32) + (f >= third_end).astype(jnp.int32)
        for f in range(3)
    ]
    hidden = []
    for f in range(3):
        row = jnp.full((1, WIDE), NEGATIVE, f32)
        for k in range(f + 1):
            seen = jnp.where(group[f] == group[k], 0.0, NEGATIVE).astype(f32)
            row = jnp.where((lane >= FRAME * k) & (lane < FRAME * (k + 1)), seen, row)
        hidden.append(row)
    frame = [((lane >= FRAME * f) & (lane < FRAME * (f + 1))).astype(f32) for f in range(3)]
    return hidden, frame


def forward_attention(counts_ref, tokens_ref, weight_ref, bias_ref, gain_ref, offset_ref,
                      mixed_ref, query_ref, key_ref, value_ref, first_ref, projected_ref, mixed_scratch):
    slot = pl.program_id(0)
    span, width = tokens_ref.shape[1:]
    scale = math.log2(math.e) / math.sqrt(HEAD)
    normed, _ = norm_parts(tokens_ref[0].astype(f32))
    first_ref[...] = jnp.zeros_like(first_ref)
    first_ref[0:span, :] = (normed * gain_ref[...] + offset_ref[...]).astype(bf16)
    ones = jnp.where(lax.broadcasted_iota(jnp.int32, (WIDE, 16), 1) == 0, 1.0, 0.0).astype(bf16)
    bias_rows = jnp.broadcast_to(bias_ref[...], (16, 3 * width)).astype(bf16)
    projected_ref[...] = dot(weight_ref[...], first_ref[...], (0, 1)) + dot(bias_rows, ones, (0, 1))
    hidden, frame = mask_rows(counts_ref, slot)
    one = jnp.ones((1, WIDE), f32)
    query_more = rows_of(frame, WIDE)
    key_more = rows_of(hidden + [one, one, one], WIDE)
    value_more = rows_of([one, one, one], WIDE)

    def head_step(h, _):
        at = pl.multiple_of(h * HEAD, 8)
        to = pl.multiple_of(h * 32, 32)
        query = jnp.concatenate([projected_ref[pl.ds(at, HEAD), :] * scale, query_more], 0)
        key = jnp.concatenate([projected_ref[pl.ds(at + width, HEAD), :], key_more], 0).astype(bf16)
        value = jnp.concatenate([projected_ref[pl.ds(at + 2 * width, HEAD), :], value_more], 0).astype(bf16)
        query_low = query.astype(bf16)
        logs = []
        for low, high, keys in FORWARD_BLOCKS:
            scores = dot(key[:, :keys], query_low[:, low:high], (0, 0))
            peak = jnp.max(scores, axis=0, keepdims=True)
            weights = jnp.exp2(scores - peak).astype(bf16)
            got = dot(value[:, :keys], weights, (1, 0))
            total = got[HEAD : HEAD + 1]
            mixed_scratch[pl.ds(at, HEAD), low:high] = got[:HEAD] / total
            logs.append(peak + jnp.log2(total))
        log_total = jnp.concatenate(logs, 1)
        high_part, middle_part, low_part = three_parts(-log_total)
        zero = jnp.zeros((1, WIDE), f32)
        log_rows = rows_of([zero, zero, zero, high_part, middle_part, low_part], WIDE)
        query_ref[0, pl.ds(to, 32), :] = (query + jnp.concatenate([jnp.zeros((HEAD, WIDE), f32), log_rows], 0)).astype(bf16)
        key_ref[0, pl.ds(to, 32), :] = key
        value_ref[0, pl.ds(to, 32), :] = value
        return 0

    lax.fori_loop(0, HEADS, head_step, 0, unroll=2)
    mixed_ref[0] = mixed_scratch[...].astype(bf16)


def run_forward(counts, tokens, weight, bias, gain, offset):
    slots, span, width = tokens.shape
    whole = lambda shape: pl.BlockSpec(shape, lambda s: (0,) * len(shape))
    per_slot = lambda rows: pl.BlockSpec((1, rows, WIDE), lambda s: (s, 0, 0))
    return pl.pallas_call(
        forward_attention,
        grid=(slots,),
        in_specs=[
            pl.BlockSpec(memory_space=pltpu.SMEM),
            pl.BlockSpec((1, span, width), lambda s: (s, 0, 0)),
            whole((width, 3 * width)),
            whole((1, 3 * width)),
            whole((1, width)),
            whole((1, width)),
        ],
        out_specs=[per_slot(width), per_slot(512), per_slot(512), per_slot(512)],
        out_shape=[jax.ShapeDtypeStruct((slots, rows, WIDE), bf16) for rows in (width, 512, 512, 512)],
        scratch_shapes=[pltpu.VMEM((WIDE, width), bf16), pltpu.VMEM((3 * width, WIDE), f32), pltpu.VMEM((width, WIDE), f32)],
        compiler_params=pltpu.CompilerParams(vmem_limit_bytes=56 * 2**20),
        name="attention_forward",
    )(counts, tokens, weight, bias, gain, offset)


def feed_forward(tokens_ref, mixed_ref, cotangent_ref, out_w_ref, up_w_ref, down_w_ref, out_b_ref, gain_ref, offset_ref, up_b_ref, down_b_ref,
                 output_ref, grad_resid_ref, grad_mixed_ref, grad_out_ref, grad_up_ref, grad_down_ref, vector_ref, up_vector_ref):
    slot = pl.program_id(0)
    span, width = tokens_ref.shape[1:]
    hidden = up_w_ref.shape[1]
    chunk = 384

    @pl.when(slot == 0)
    def _():
        grad_out_ref[...] = jnp.zeros_like(grad_out_ref)
        grad_up_ref[...] = jnp.zeros_like(grad_up_ref)
        grad_down_ref[...] = jnp.zeros_like(grad_down_ref)
        vector_ref[...] = jnp.zeros_like(vector_ref)
        up_vector_ref[...] = jnp.zeros_like(up_vector_ref)

    mixed = mixed_ref[0]
    mixed = mixed[:, :span]
    resid = tokens_ref[0].astype(f32) + dot(mixed, out_w_ref[...], (0, 0)) + out_b_ref[...]
    normed, inverse = norm_parts(resid)
    second = (normed * gain_ref[...] + offset_ref[...]).astype(bf16)
    grad_branch = cotangent_ref[0]
    result = resid + down_b_ref[...]
    grad_second = jnp.zeros((span, width), f32)
    root = math.sqrt(2.0 / math.pi)
    for at in range(0, hidden, chunk):
        cols = slice(at, at + chunk)
        up = dot(second, up_w_ref[:, cols], (1, 0)) + up_b_ref[:, cols]
        square = up * up
        tanh = jnp.tanh(up * (root + (root * 0.044715) * square))
        half = 0.5 + 0.5 * tanh
        activated = (up * half).astype(bf16)
        slope = half + (up * (2.0 * half * (1.0 - half))) * (root + (3 * root * 0.044715) * square)
        result += dot(activated, down_w_ref[cols, :], (1, 0))
        grad_up = (dot(grad_branch, down_w_ref[cols, :], (1, 1)) * slope).astype(bf16)
        grad_down_ref[cols, :] += dot(activated, grad_branch, (0, 0))
        grad_up_ref[:, cols] += dot(second, grad_up, (0, 0))
        up_vector_ref[:, cols] += jnp.sum(grad_up.astype(f32), axis=0, keepdims=True)
        grad_second += dot(grad_up, up_w_ref[:, cols], (1, 1))
    output_ref[0] = result.astype(bf16)
    scaled = grad_second * gain_ref[...]
    mean_one = jnp.mean(scaled, axis=-1, keepdims=True)
    mean_two = jnp.mean(scaled * normed, axis=-1, keepdims=True)
    grad_full = grad_branch.astype(f32)
    grad_resid = grad_full + inverse * (scaled - mean_one - normed * mean_two)
    grad_resid_ref[0] = grad_resid
    attended = grad_resid.astype(bf16)
    grad_out_ref[...] += dot(mixed, attended, (1, 0))
    grad_mixed_ref[0] = jnp.zeros_like(grad_mixed_ref[0])
    grad_mixed_ref[0, :, :span] = dot(out_w_ref[...], attended, (1, 1)).astype(bf16)
    vector_ref[0:1] += jnp.sum(attended.astype(f32), axis=0, keepdims=True)
    vector_ref[1:2] += jnp.sum(grad_second * normed, axis=0, keepdims=True)
    vector_ref[2:3] += jnp.sum(grad_second, axis=0, keepdims=True)
    vector_ref[3:4] += jnp.sum(grad_full, axis=0, keepdims=True)


def run_feed_forward(tokens, mixed, cotangent, out_w, up_w, down_w, out_b, gain, offset, up_b, down_b):
    slots, span, width = tokens.shape
    hidden = up_w.shape[1]
    whole = lambda *shape: pl.BlockSpec(shape, lambda s: (0,) * len(shape))
    rows = pl.BlockSpec((1, span, width), lambda s: (s, 0, 0))
    turned = pl.BlockSpec((1, width, WIDE), lambda s: (s, 0, 0))
    return pl.pallas_call(
        feed_forward,
        grid=(slots,),
        in_specs=[rows, turned, rows, whole(width, width), whole(width, hidden), whole(hidden, width), whole(1, width),
                  whole(1, width), whole(1, width), whole(1, hidden), whole(1, width)],
        out_specs=[rows, rows, turned, whole(width, width), whole(width, hidden), whole(hidden, width), whole(8, width), whole(1, hidden)],
        out_shape=[
            jax.ShapeDtypeStruct((slots, span, width), bf16),
            jax.ShapeDtypeStruct((slots, span, width), f32),
            jax.ShapeDtypeStruct((slots, width, WIDE), bf16),
            jax.ShapeDtypeStruct((width, width), f32),
            jax.ShapeDtypeStruct((width, hidden), f32),
            jax.ShapeDtypeStruct((hidden, width), f32),
            jax.ShapeDtypeStruct((8, width), f32),
            jax.ShapeDtypeStruct((1, hidden), f32),
        ],
        compiler_params=pltpu.CompilerParams(vmem_limit_bytes=56 * 2**20),
        name="feed_forward",
    )(tokens, mixed, cotangent, out_w, up_w, down_w, out_b, gain, offset, up_b, down_b)


def backward_attention(tokens_ref, query_ref, key_ref, value_ref, mixed_ref, grad_mixed_ref, grad_resid_ref, weight_ref, gain_ref, offset_ref,
                       input_grad_ref, grad_weight_ref, grad_bias_ref, vector_ref, first_ref, turned_ref):
    slot = pl.program_id(0)
    span, width = tokens_ref.shape[1:]

    @pl.when(slot == 0)
    def _():
        grad_weight_ref[...] = jnp.zeros_like(grad_weight_ref)
        grad_bias_ref[...] = jnp.zeros_like(grad_bias_ref)
        vector_ref[...] = jnp.zeros_like(vector_ref)

    normed, inverse = norm_parts(tokens_ref[0].astype(f32))
    first_ref[...] = jnp.zeros_like(first_ref)
    first_ref[0:span, :] = (normed * gain_ref[...] + offset_ref[...]).astype(bf16)

    def head_step(pair, _):
        for part in range(2):
            h = pair * 2 + part
            to = pl.multiple_of(h * 32, 32)
            at = pl.multiple_of(h * HEAD, 8)
            query = query_ref[0, pl.ds(to, 32), :]
            key = key_ref[0, pl.ds(to, 32), :]
            value = value_ref[0, pl.ds(to, 32), :]
            both = pl.multiple_of(pair * 48, 16)
            grad = grad_mixed_ref[0, pl.ds(both, 48), :].astype(f32)[HEAD * part : HEAD * part + HEAD]
            mixed = mixed_ref[0, pl.ds(both, 48), :].astype(f32)[HEAD * part : HEAD * part + HEAD]
            shift = jnp.sum(grad * mixed, axis=0, keepdims=True)
            grad = jnp.concatenate([grad, rows_of(three_parts(-shift), WIDE)], 0).astype(bf16)
            grad_q = []
            grad_k = jnp.zeros((32, WIDE), f32)
            grad_v = jnp.zeros((32, WIDE), f32)
            for low, high, keys in BACKWARD_BLOCKS:
                probs = jnp.exp2(dot(query[:, low:high], key[:, :keys], (0, 0)))
                grad_scores = (probs * dot(grad[:, low:high], value[:, :keys], (0, 0))).astype(bf16)
                probs_low = probs.astype(bf16)
                more_v = dot(grad[:, low:high], probs_low, (1, 0))
                more_k = dot(query[:, low:high], grad_scores, (1, 0))
                grad_q.append(dot(key[:, :keys], grad_scores, (1, 1)))
                if keys < WIDE:
                    blank = jnp.zeros((32, WIDE - keys), f32)
                    more_v = jnp.concatenate([more_v, blank], 1)
                    more_k = jnp.concatenate([more_k, blank], 1)
                grad_v += more_v
                grad_k += more_k
            grad_q.append(jnp.zeros((32, WIDE - 592), f32))
            grad_q = jnp.concatenate(grad_q, 1)
            turned_ref[pl.ds(at, HEAD), :] = grad_q[:HEAD] * (1.0 / math.sqrt(HEAD))
            turned_ref[pl.ds(at + width, HEAD), :] = grad_k[:HEAD] * math.log(2.0)
            turned_ref[pl.ds(at + 2 * width, HEAD), :] = grad_v[:HEAD]
        return 0

    lax.fori_loop(0, HEADS // 2, head_step, 0)
    turned = turned_ref[...].astype(bf16)
    grad_bias_ref[...] += jnp.sum(turned.astype(f32), axis=1, keepdims=True)
    grad_weight_ref[...] += dot(first_ref[...], turned, (0, 1))
    grad_first = dot(turned, weight_ref[...], (0, 1))[:span]
    scaled = grad_first * gain_ref[...]
    mean_one = jnp.mean(scaled, axis=-1, keepdims=True)
    mean_two = jnp.mean(scaled * normed, axis=-1, keepdims=True)
    input_grad_ref[0] = grad_resid_ref[0] + inverse * (scaled - mean_one - normed * mean_two)
    vector_ref[0:1] += jnp.sum(grad_first * normed, axis=0, keepdims=True)
    vector_ref[1:2] += jnp.sum(grad_first, axis=0, keepdims=True)


def run_backward(tokens, query, key, value, mixed, grad_mixed, grad_resid, weight, gain, offset):
    slots, span, width = tokens.shape
    whole = lambda *shape: pl.BlockSpec(shape, lambda s: (0,) * len(shape))
    rows = pl.BlockSpec((1, span, width), lambda s: (s, 0, 0))
    turned = lambda n: pl.BlockSpec((1, n, WIDE), lambda s: (s, 0, 0))
    return pl.pallas_call(
        backward_attention,
        grid=(slots,),
        in_specs=[rows, turned(512), turned(512), turned(512), turned(width), turned(width), rows, whole(width, 3 * width), whole(1, width), whole(1, width)],
        out_specs=[rows, whole(width, 3 * width), whole(3 * width, 1), whole(8, width)],
        out_shape=[
            jax.ShapeDtypeStruct((slots, span, width), f32),
            jax.ShapeDtypeStruct((width, 3 * width), f32),
            jax.ShapeDtypeStruct((3 * width, 1), f32),
            jax.ShapeDtypeStruct((8, width), f32),
        ],
        scratch_shapes=[pltpu.VMEM((WIDE, width), bf16), pltpu.VMEM((3 * width, WIDE), f32)],
        compiler_params=pltpu.CompilerParams(vmem_limit_bytes=56 * 2**20),
        name="attention_backward",
    )(tokens, query, key, value, mixed, grad_mixed, grad_resid, weight, gain, offset)


ALL = ("wide_0", "wide_1", "wide_2", "narrow")
DEVICES = 128


def row(values):
    return values.astype(f32)[None]


def shards(tokens, item_frames, ln1_gain, ln1_bias, qkv_weight, qv_bias, out_weight, out_bias, ln2_gain, ln2_bias,
           up_weight, up_bias, down_weight, down_bias, cotangent):
    width = tokens.shape[2]
    own = width // DEVICES
    column = lambda v: v.reshape(-1, 1)
    early = jnp.concatenate([qkv_weight, column(ln1_gain), column(ln1_bias), qv_bias.reshape(own, 2)], 1)
    early = jnp.broadcast_to(early[None], (DEVICES, *early.shape))
    early = lax.all_to_all(early, ALL, 0, 0, tiled=True).reshape(width, -1)
    qkv = early[:, : 3 * width]
    gain_one, offset_one = early[:, 3 * width], early[:, 3 * width + 1]
    qv = early[:, 3 * width + 2 :].reshape(-1)
    wide = lax.all_gather(
        jnp.concatenate([out_weight, up_weight, column(out_bias), column(ln2_gain), column(ln2_bias), column(down_bias)], 1),
        ALL, axis=0, tiled=True)
    tall = lax.all_gather(jnp.concatenate([down_weight, column(up_bias)], 1), ALL, axis=0, tiled=True)
    bias = jnp.concatenate([qv[:width], jnp.zeros((width,), qv.dtype), qv[width:]])
    mixed, query, key, value = run_forward(item_frames, tokens, qkv, row(bias), row(gain_one), row(offset_one))
    hidden = up_weight.shape[1]
    out_w, up_w = wide[:, :width], wide[:, width : width + hidden]
    out_b, gain_two, offset_two, down_b = (row(wide[:, width + hidden + k]) for k in range(4))
    down_w, up_b = tall[:, :width], row(tall[:, width])
    output, grad_resid, grad_mixed, grad_out, grad_up, grad_down, vectors, up_vector = run_feed_forward(
        tokens, mixed, cotangent, out_w, up_w, down_w, out_b, gain_two, offset_two, up_b, down_b)

    def spread(parts, rows):
        both = jnp.concatenate(parts, 1).astype(bf16)
        both = both.reshape(DEVICES, rows, both.shape[1])
        return jnp.sum(lax.all_to_all(both, ALL, 0, 0, tiled=True).astype(f32), 0)

    wide_sum = spread([grad_out, grad_up, vectors[:4].T], own)
    tall_sum = spread([grad_down, up_vector.T], 4 * own)
    input_grad, grad_qkv, grad_bias, vectors_one = run_backward(
        tokens, query, key, value, mixed, grad_mixed, grad_resid, qkv, row(gain_one), row(offset_one))
    grad_bias = grad_bias[:, 0]
    grad_qv = jnp.concatenate([grad_bias[:width], grad_bias[2 * width :]]).reshape(width, 2)
    first_sum = spread([grad_qkv, vectors_one[:2].T, grad_qv], own)
    at = width + hidden
    return (
        output,
        input_grad,
        first_sum[:, 3 * width],
        first_sum[:, 3 * width + 1],
        first_sum[:, : 3 * width],
        first_sum[:, 3 * width + 2 :].reshape(-1),
        wide_sum[:, :width],
        wide_sum[:, at],
        wide_sum[:, at + 1],
        wide_sum[:, at + 2],
        wide_sum[:, width:at],
        tall_sum[:, width],
        tall_sum[:, :width],
        wide_sum[:, at + 3],
    )


def solution(mesh):
    split = Mesh(mesh.devices.reshape(4, 4, 2, mesh.shape["narrow"]), ALL)
    by_rank = lambda n: P(ALL, *([None] * (n - 1)))
    return jax.shard_map(
        shards,
        mesh=split,
        in_specs=tuple(by_rank(n) for n in (3, 2, 1, 1, 2, 1, 2, 1, 1, 1, 2, 1, 2, 1, 3)),
        out_specs=tuple(by_rank(n) for n in (3, 3, 1, 1, 2, 1, 2, 1, 1, 1, 2, 1, 2, 1)),
        check_vma=False,
    )
```

```python
import math

import jax
import jax.numpy as jnp
from jax import lax
from jax.experimental import pallas as pl
from jax.experimental.pallas import tpu as pltpu
from jax.sharding import Mesh
from jax.sharding import PartitionSpec as P

HEADS = 16
HEAD = 24
FRAME = 196
WIDTH = 384
HIDDEN = 1536
WIDE = 640
CHIPS = 64
EARLY_ROWS = 32
LATE_ROWS = 96
EPSILON = 1e-05
NEGATIVE = -1e30
bf16 = jnp.bfloat16
f32 = jnp.float32
FORWARD_BLOCKS = ((0, 128, 208), (128, 384, 400), (384, 640, 592))
BACKWARD_BLOCKS = ((0, 128, 256), (128, 384, 512), (384, 592, 640))
ALL = ("wide_0", "wide_1", "wide_2", "narrow")
CHIP_AXES = ("wide_0", "wide_1", "narrow")
CORE_AXIS = "wide_2"
VMEM_LIMIT = 56 * 2**20


def dot(left, right, over):
    return lax.dot_general(left, right, (((over[0],), (over[1],)), ((), ())), preferred_element_type=f32)


def norm_parts(values):
    centred = values - jnp.mean(values, axis=-1, keepdims=True)
    inverse = lax.rsqrt(jnp.mean(centred * centred, axis=-1, keepdims=True) + EPSILON)
    return centred * inverse, inverse


def two_parts(values):
    high = values.astype(bf16).astype(f32)
    return high, values - high


def three_parts(values):
    high, rest = two_parts(values)
    middle, low = two_parts(rest)
    return high, middle, low


def rows_of(rows, width, count=8):
    index = lax.broadcasted_iota(jnp.int32, (count, width), 0)
    out = jnp.zeros((count, width), f32)
    for k, row in enumerate(rows):
        out = jnp.where(index == k, row, out)
    return out


def arrival_order():
    place = lax.broadcasted_iota(jnp.int32, (WIDTH, WIDTH), 1)
    feature = lax.broadcasted_iota(jnp.int32, (WIDTH, WIDTH), 0)
    core = (place >= WIDTH // 2).astype(jnp.int32)
    rest = place - core * (WIDTH // 2)
    row = rest >> 6
    chip = rest & 63
    return (feature == 3 * (8 * (chip >> 2) + 4 * core + (chip & 3)) + row).astype(f32).astype(bf16)


def mask_rows(counts_ref, slot):
    lane = lax.broadcasted_iota(jnp.int32, (1, WIDE), 1)
    first_end = counts_ref[slot, 0]
    second_end = first_end + counts_ref[slot, 1]
    third_end = second_end + counts_ref[slot, 2]
    group = [
        (f >= first_end).astype(jnp.int32) + (f >= second_end).astype(jnp.int32) + (f >= third_end).astype(jnp.int32)
        for f in range(3)
    ]
    hidden = []
    for f in range(3):
        row = jnp.full((1, WIDE), NEGATIVE, f32)
        for k in range(f + 1):
            seen = jnp.where(group[f] == group[k], 0.0, NEGATIVE).astype(f32)
            row = jnp.where((lane >= FRAME * k) & (lane < FRAME * (k + 1)), seen, row)
        hidden.append(row)
    frame = [((lane >= FRAME * f) & (lane < FRAME * (f + 1))).astype(f32) for f in range(3)]
    return hidden, frame


def params(**more):
    return pltpu.CompilerParams(vmem_limit_bytes=VMEM_LIMIT, **more)


def whole(*shape):
    return pl.BlockSpec(shape, lambda *_: (0,) * len(shape))


def shape_of(shape, dtype):
    return jax.ShapeDtypeStruct(shape, dtype)


def pack_early(qkv_ref, gain_ref, offset_ref, qv_ref, out_ref, rows_ref):
    rows_ref[...] = jnp.zeros_like(rows_ref)
    weight = qkv_ref[...].astype(f32)
    gain = gain_ref[...].astype(f32).reshape(1, 3)
    offset = offset_ref[...].astype(f32).reshape(1, 3)
    qv = qv_ref[...].astype(f32).reshape(1, 6)
    for r in range(3):
        for j in range(9):
            rows_ref[10 * r + j : 10 * r + j + 1, :] = weight[r : r + 1, 128 * j : 128 * j + 128]
        rows_ref[10 * r + 9 : 10 * r + 10, 0:1] = gain[:, r : r + 1]
        rows_ref[10 * r + 9 : 10 * r + 10, 1:2] = offset[:, r : r + 1]
        rows_ref[10 * r + 9 : 10 * r + 10, 2:4] = qv[:, 2 * r : 2 * r + 2]
    out_ref[...] = jnp.broadcast_to(rows_ref[...].astype(bf16)[None], out_ref.shape)


def pack_late(out_w_ref, up_ref, down_ref, out_b_ref, gain_ref, offset_ref, down_b_ref, up_b_ref, out_ref, rows_ref):
    rows_ref[...] = jnp.zeros_like(rows_ref)
    out_w = out_w_ref[...].astype(f32)
    up = up_ref[...].astype(f32)
    down = down_ref[...].astype(f32)
    vectors = [ref[...].astype(f32).reshape(1, 3) for ref in (out_b_ref, gain_ref, offset_ref, down_b_ref)]
    for r in range(3):
        for j in range(3):
            rows_ref[3 * r + j : 3 * r + j + 1, :] = out_w[r : r + 1, 128 * j : 128 * j + 128]
        for j in range(12):
            rows_ref[9 + 12 * r + j : 10 + 12 * r + j, :] = up[r : r + 1, 128 * j : 128 * j + 128]
        for k, vector in enumerate(vectors):
            rows_ref[81 + r : 82 + r, k : k + 1] = vector[:, r : r + 1]
    for r in range(12):
        for j in range(3):
            rows_ref[45 + 3 * r + j : 46 + 3 * r + j, :] = down[r : r + 1, 128 * j : 128 * j + 128]
    rows_ref[84:85, 0:12] = up_b_ref[...].astype(f32).reshape(1, 12)
    out_ref[...] = jnp.broadcast_to(rows_ref[...].astype(bf16)[None], out_ref.shape)


def run_pack_early(*args):
    return pl.pallas_call(
        pack_early,
        out_shape=shape_of((CHIPS, EARLY_ROWS, 128), bf16),
        scratch_shapes=[pltpu.VMEM((EARLY_ROWS, 128), f32)],
        compiler_params=params(),
        name="pack_early",
    )(*args)


def run_pack_late(*args):
    return pl.pallas_call(
        pack_late,
        out_shape=shape_of((CHIPS, LATE_ROWS, 128), bf16),
        scratch_shapes=[pltpu.VMEM((LATE_ROWS, 128), f32)],
        compiler_params=params(),
        name="pack_late",
    )(*args)


def total(arrived_ref):
    return jnp.sum(arrived_ref[...].astype(f32), axis=0)


def spread_lanes(rows, lane, width):
    index = lax.broadcasted_iota(jnp.int32, (1, width), 1)
    out = jnp.zeros((1, width), f32)
    for k, row in enumerate(rows):
        out = jnp.where(index == k, row[:, lane : lane + 1], out)
    return out.reshape(width)


def unpack_first(arrived_ref, qkv_ref, gain_ref, offset_ref, qv_ref):
    sums = total(arrived_ref)
    more = []
    for r in range(3):
        for j in range(9):
            qkv_ref[r : r + 1, 128 * j : 128 * j + 128] = sums[10 * r + j : 10 * r + j + 1, :]
        row = sums[10 * r + 9 : 10 * r + 10, :]
        more.append(row[:, 0:4] + row[:, 4:8])
    gain_ref[...] = spread_lanes(more, 0, 3)
    offset_ref[...] = spread_lanes(more, 1, 3)
    index = lax.broadcasted_iota(jnp.int32, (1, 6), 1)
    out = jnp.zeros((1, 6), f32)
    for k in range(6):
        out = jnp.where(index == k, more[k // 2][:, 2 + k % 2 : 3 + k % 2], out)
    qv_ref[...] = out.reshape(6)


def run_unpack_first(arrived):
    return pl.pallas_call(
        unpack_first,
        out_shape=[shape_of((3, 3 * WIDTH), f32), shape_of((3,), f32), shape_of((3,), f32), shape_of((6,), f32)],
        compiler_params=params(),
        name="unpack_first",
    )(arrived)


def unpack_rest(arrived_ref, out_ref, up_ref, down_ref, out_b_ref, gain_ref, offset_ref, down_b_ref, up_b_ref):
    sums = total(arrived_ref)
    more = []
    for r in range(3):
        for j in range(3):
            out_ref[r : r + 1, 128 * j : 128 * j + 128] = sums[3 * r + j : 3 * r + j + 1, :]
        for j in range(12):
            up_ref[r : r + 1, 128 * j : 128 * j + 128] = sums[9 + 12 * r + j : 10 + 12 * r + j, :]
        row = sums[81 + r : 82 + r, :]
        more.append(row[:, 0:4] + row[:, 4:8])
    for r in range(12):
        for j in range(3):
            down_ref[r : r + 1, 128 * j : 128 * j + 128] = sums[45 + 3 * r + j : 46 + 3 * r + j, :]
    for k, ref in enumerate((out_b_ref, gain_ref, offset_ref, down_b_ref)):
        ref[...] = spread_lanes(more, k, 3)
    up_b_ref[...] = (sums[84:85, 0:12] + sums[84:85, 12:24]).reshape(12)


def run_unpack_rest(arrived):
    return pl.pallas_call(
        unpack_rest,
        out_shape=[shape_of((3, WIDTH), f32), shape_of((3, HIDDEN), f32), shape_of((12, WIDTH), f32)]
        + [shape_of((3,), f32)] * 4
        + [shape_of((12,), f32)],
        compiler_params=params(),
        name="unpack_rest",
    )(arrived)


def attention_forward(core_ref, counts_ref, tokens_ref, own_ref, other_ref,
                      mixed_ref, query_ref, key_ref, value_ref, weight_ref, vector_ref,
                      first_ref, projected_ref, mixed_scratch, arrived_ref, bias_ref):
    slot = pl.program_id(0)
    span = tokens_ref.shape[1]
    scale = math.log2(math.e) / math.sqrt(HEAD)

    @pl.when(slot == 0)
    def _():
        core = core_ref[0]
        for side, ref in ((core, own_ref), (1 - core, other_ref)):
            blocks = jnp.swapaxes(ref[...], 0, 1)
            for r in range(3):
                at = pl.multiple_of(side * 192 + 64 * r, 64)
                for j in range(10):
                    arrived_ref[pl.ds(at, 64), 128 * j : 128 * j + 128] = blocks[10 * r + j]
        order = arrival_order()
        ordered = dot(order, arrived_ref[...], (1, 0))
        weight_ref[...] = ordered[:, : 3 * WIDTH].astype(bf16)
        vector_ref[...] = dot(arrived_ref[:, 3 * WIDTH :], order, (0, 1))[0:8]
        for s in range(2):
            column = ordered[:, 3 * WIDTH + 2 + s : 3 * WIDTH + 3 + s]
            bias_ref[pl.ds(s, WIDTH, stride=2), :] = jnp.broadcast_to(column, (WIDTH, 128))

    normed, _ = norm_parts(tokens_ref[0].astype(f32))
    first_ref[576:WIDE, :] = jnp.zeros((WIDE - 576, WIDTH), bf16)
    first_ref[0:span, :] = (normed * vector_ref[0:1] + vector_ref[1:2]).astype(bf16)
    projected_ref[...] = dot(weight_ref[...], first_ref[...], (0, 1))
    hidden, frame = mask_rows(counts_ref, slot)
    one = jnp.ones((1, WIDE), f32)
    query_more = rows_of(frame, WIDE)
    key_more = rows_of(hidden + [one, one, one], WIDE)
    value_more = rows_of([one, one, one], WIDE)

    def head_step(h, _):
        at = pl.multiple_of(h * HEAD, 8)
        to = pl.multiple_of(h * 32, 32)
        wide = lambda start: jnp.concatenate([bias_ref[pl.ds(start, HEAD), :]] * (WIDE // 128), 1)
        query = (projected_ref[pl.ds(at, HEAD), :] + wide(at)) * scale
        value = projected_ref[pl.ds(at + 2 * WIDTH, HEAD), :] + wide(at + WIDTH)
        query = jnp.concatenate([query, query_more], 0)
        key = jnp.concatenate([projected_ref[pl.ds(at + WIDTH, HEAD), :], key_more], 0).astype(bf16)
        value = jnp.concatenate([value, value_more], 0).astype(bf16)
        query_low = query.astype(bf16)
        logs = []
        for low, high, keys in FORWARD_BLOCKS:
            scores = dot(key[:, :keys], query_low[:, low:high], (0, 0))
            peak = jnp.max(scores, axis=0, keepdims=True)
            weights = jnp.exp2(scores - peak).astype(bf16)
            got = dot(value[:, :keys], weights, (1, 0))
            row_total = got[HEAD : HEAD + 1]
            mixed_scratch[pl.ds(at, HEAD), low:high] = got[:HEAD] / row_total
            logs.append(peak + jnp.log2(row_total))
        parts = three_parts(-jnp.concatenate(logs, 1))
        zero = jnp.zeros((1, WIDE), f32)
        log_rows = rows_of([zero, zero, zero, *parts], WIDE)
        query_ref[0, pl.ds(to, 32), :] = (query + jnp.concatenate([jnp.zeros((HEAD, WIDE), f32), log_rows], 0)).astype(bf16)
        key_ref[0, pl.ds(to, 32), :] = key
        value_ref[0, pl.ds(to, 32), :] = value
        return 0

    lax.fori_loop(0, HEADS, head_step, 0, unroll=2)
    mixed_ref[0] = mixed_scratch[...].astype(bf16)


def run_forward(core, counts, tokens, own, other):
    slots, span, _ = tokens.shape
    per_slot = lambda rows: pl.BlockSpec((1, rows, WIDE), lambda s: (s, 0, 0))
    scalars = pl.BlockSpec(memory_space=pltpu.SMEM)
    return pl.pallas_call(
        attention_forward,
        grid=(slots,),
        in_specs=[
            scalars,
            scalars,
            pl.BlockSpec((1, span, WIDTH), lambda s: (s, 0, 0)),
            whole(CHIPS, EARLY_ROWS, 128),
            whole(CHIPS, EARLY_ROWS, 128),
        ],
        out_specs=[per_slot(WIDTH), per_slot(512), per_slot(512), per_slot(512), whole(WIDTH, 3 * WIDTH), whole(8, WIDTH)],
        out_shape=[shape_of((slots, rows, WIDE), bf16) for rows in (WIDTH, 512, 512, 512)]
        + [shape_of((WIDTH, 3 * WIDTH), bf16), shape_of((8, WIDTH), f32)],
        scratch_shapes=[
            pltpu.VMEM((WIDE, WIDTH), bf16),
            pltpu.VMEM((3 * WIDTH, WIDE), f32),
            pltpu.VMEM((WIDTH, WIDE), f32),
            pltpu.VMEM((WIDTH, 3 * WIDTH + 128), bf16),
            pltpu.VMEM((2 * WIDTH, 128), f32),
        ],
        compiler_params=params(),
        name="attention_forward",
    )(core, counts, tokens, own, other)


def feed_forward(core_ref, tokens_ref, mixed_ref, cotangent_ref, own_ref, other_ref,
                 output_ref, grad_resid_ref, grad_mixed_ref, mine_ref, theirs_ref,
                 arrived_ref, out_w_ref, up_w_ref, down_w_ref, row_ref, up_b_ref,
                 grad_out_ref, grad_up_ref, grad_down_ref, vector_ref, up_vector_ref, packed_ref):
    slot = pl.program_id(0)
    span = tokens_ref.shape[1]
    chunk = 384

    @pl.when(slot == 0)
    def _():
        core = core_ref[0]
        for side, ref in ((core, own_ref), (1 - core, other_ref)):
            blocks = jnp.swapaxes(ref[...], 0, 1)
            for r in range(3):
                at = pl.multiple_of(side * 192 + 64 * r, 64)
                for j in range(15):
                    arrived_ref[pl.ds(at, 64), 128 * j : 128 * j + 128] = blocks[3 * r + j] if j < 3 else blocks[6 + 12 * r + j]
                arrived_ref[pl.ds(at, 64), 1920:2048] = blocks[81 + r]
            for r in range(12):
                at = pl.multiple_of(side * 768 + 64 * r, 64)
                for j in range(3):
                    down_w_ref[pl.ds(at, 64), 128 * j : 128 * j + 128] = blocks[45 + 3 * r + j]
            turned = blocks[84].astype(f32).T
            up_b = jnp.concatenate([turned[r : r + 1] for r in range(12)], 1)
            up_b_ref[:, pl.ds(pl.multiple_of(side * 768, 128), 768)] = up_b
        order = arrival_order()
        ordered = dot(order, arrived_ref[:, :1920], (1, 0)).astype(bf16)
        out_w_ref[...] = ordered[:, :WIDTH]
        up_w_ref[...] = ordered[:, WIDTH:]
        row_ref[...] = dot(arrived_ref[:, 1920:], order, (0, 1))[0:8]
        grad_out_ref[...] = jnp.zeros_like(grad_out_ref)
        grad_up_ref[...] = jnp.zeros_like(grad_up_ref)
        grad_down_ref[...] = jnp.zeros_like(grad_down_ref)
        vector_ref[...] = jnp.zeros_like(vector_ref)
        up_vector_ref[...] = jnp.zeros_like(up_vector_ref)

    out_b, gain, offset, down_b = (row_ref[k : k + 1] for k in range(4))
    mixed = mixed_ref[0]
    mixed = mixed[:, :span]
    resid = tokens_ref[0].astype(f32) + dot(mixed, out_w_ref[...], (0, 0)) + out_b
    normed, inverse = norm_parts(resid)
    second = (normed * gain + offset).astype(bf16)
    grad_branch = cotangent_ref[0]
    result = resid + down_b
    grad_second = jnp.zeros((span, WIDTH), f32)
    root = math.sqrt(2.0 / math.pi)
    for at in range(0, HIDDEN, chunk):
        cols = slice(at, at + chunk)
        up = dot(second, up_w_ref[:, cols], (1, 0)) + up_b_ref[:, cols]
        square = up * up
        tanh = jnp.tanh(up * (root + (root * 0.044715) * square))
        half = 0.5 + 0.5 * tanh
        activated = (up * half).astype(bf16)
        slope = half + (up * (2.0 * half * (1.0 - half))) * (root + (3 * root * 0.044715) * square)
        result += dot(activated, down_w_ref[cols, :], (1, 0))
        grad_up = (dot(grad_branch, down_w_ref[cols, :], (1, 1)) * slope).astype(bf16)
        grad_down_ref[cols, :] += dot(activated, grad_branch, (0, 0))
        grad_up_ref[:, cols] += dot(second, grad_up, (0, 0))
        up_vector_ref[:, cols] += jnp.sum(grad_up.astype(f32), axis=0, keepdims=True)
        grad_second += dot(grad_up, up_w_ref[:, cols], (1, 1))
    output_ref[0] = result.astype(bf16)
    scaled = grad_second * gain
    mean_one = jnp.mean(scaled, axis=-1, keepdims=True)
    mean_two = jnp.mean(scaled * normed, axis=-1, keepdims=True)
    grad_full = grad_branch.astype(f32)
    grad_resid = grad_full + inverse * (scaled - mean_one - normed * mean_two)
    grad_resid_ref[0] = grad_resid
    attended = grad_resid.astype(bf16)
    grad_out_ref[...] += dot(mixed, attended, (1, 0))
    grad_mixed_ref[0] = jnp.zeros_like(grad_mixed_ref[0])
    grad_mixed_ref[0, :, :span] = dot(out_w_ref[...], attended, (1, 1)).astype(bf16)
    vector_ref[0:1] += jnp.sum(attended.astype(f32), axis=0, keepdims=True)
    vector_ref[1:2] += jnp.sum(grad_second * normed, axis=0, keepdims=True)
    vector_ref[2:3] += jnp.sum(grad_second, axis=0, keepdims=True)
    vector_ref[3:4] += jnp.sum(grad_full, axis=0, keepdims=True)

    @pl.when(slot == pl.num_programs(0) - 1)
    def _():
        core = core_ref[0]
        order = arrival_order()
        packed_ref[:, :WIDTH] = dot(order, grad_out_ref[...].astype(bf16), (0, 0)).astype(bf16)
        packed_ref[:, WIDTH:1920] = dot(order, grad_up_ref[...].astype(bf16), (0, 0)).astype(bf16)
        high, low = two_parts(vector_ref[0:4])
        rows = jnp.concatenate([high, low, jnp.zeros((120, WIDTH), f32)], 0).astype(bf16)
        packed_ref[:, 1920:] = dot(order, rows, (0, 1)).astype(bf16)
        blank = jnp.zeros((CHIPS, 128), bf16)
        for side, ref in ((core, mine_ref), (1 - core, theirs_ref)):
            blocks = [blank] * LATE_ROWS
            for r in range(3):
                at = pl.multiple_of(side * 192 + 64 * r, 64)
                for j in range(15):
                    blocks[3 * r + j if j < 3 else 6 + 12 * r + j] = packed_ref[pl.ds(at, 64), 128 * j : 128 * j + 128]
                blocks[81 + r] = packed_ref[pl.ds(at, 64), 1920:2048]
            for r in range(12):
                at = pl.multiple_of(side * 768 + 64 * r, 64)
                for j in range(3):
                    blocks[45 + 3 * r + j] = grad_down_ref[pl.ds(at, 64), 128 * j : 128 * j + 128].astype(bf16)
            line = up_vector_ref[:, pl.ds(pl.multiple_of(side * 768, 128), 768)]
            high, low = two_parts(line)
            rows = [part[:, 64 * r : 64 * r + 64] for part in (high, low) for r in range(12)]
            blocks[84] = rows_of(rows, 64, 128).T.astype(bf16)
            ref[...] = jnp.swapaxes(jnp.stack(blocks), 0, 1)


def run_feed_forward(core, tokens, mixed, cotangent, own, other):
    slots, span, _ = tokens.shape
    rows = pl.BlockSpec((1, span, WIDTH), lambda s: (s, 0, 0))
    turned = pl.BlockSpec((1, WIDTH, WIDE), lambda s: (s, 0, 0))
    message = whole(CHIPS, LATE_ROWS, 128)
    return pl.pallas_call(
        feed_forward,
        grid=(slots,),
        in_specs=[pl.BlockSpec(memory_space=pltpu.SMEM), rows, turned, rows, message, message],
        out_specs=[rows, rows, turned, message, message],
        out_shape=[
            shape_of((slots, span, WIDTH), bf16),
            shape_of((slots, span, WIDTH), f32),
            shape_of((slots, WIDTH, WIDE), bf16),
            shape_of((CHIPS, LATE_ROWS, 128), bf16),
            shape_of((CHIPS, LATE_ROWS, 128), bf16),
        ],
        scratch_shapes=[
            pltpu.VMEM((WIDTH, 2048), bf16),
            pltpu.VMEM((WIDTH, WIDTH), bf16),
            pltpu.VMEM((WIDTH, HIDDEN), bf16),
            pltpu.VMEM((HIDDEN, WIDTH), bf16),
            pltpu.VMEM((8, WIDTH), f32),
            pltpu.VMEM((1, HIDDEN), f32),
            pltpu.VMEM((WIDTH, WIDTH), f32),
            pltpu.VMEM((WIDTH, HIDDEN), f32),
            pltpu.VMEM((HIDDEN, WIDTH), f32),
            pltpu.VMEM((8, WIDTH), f32),
            pltpu.VMEM((1, HIDDEN), f32),
            pltpu.VMEM((WIDTH, 2048), bf16),
        ],
        compiler_params=params(),
        name="feed_forward",
    )(core, tokens, mixed, cotangent, own, other)


def attention_backward(core_ref, tokens_ref, query_ref, key_ref, value_ref, mixed_ref, grad_mixed_ref, grad_resid_ref, weight_ref, row_ref,
                       input_grad_ref, mine_ref, theirs_ref,
                       first_ref, turned_ref, grad_weight_ref, grad_bias_ref, vector_ref, packed_ref):
    slot = pl.program_id(0)
    span = tokens_ref.shape[1]

    @pl.when(slot == 0)
    def _():
        grad_weight_ref[...] = jnp.zeros_like(grad_weight_ref)
        grad_bias_ref[...] = jnp.zeros_like(grad_bias_ref)
        vector_ref[...] = jnp.zeros_like(vector_ref)

    gain, offset = row_ref[0:1], row_ref[1:2]
    normed, inverse = norm_parts(tokens_ref[0].astype(f32))
    first_ref[576:WIDE, :] = jnp.zeros((WIDE - 576, WIDTH), bf16)
    first_ref[0:span, :] = (normed * gain + offset).astype(bf16)

    def head_step(pair, _):
        for part in range(2):
            h = pair * 2 + part
            to = pl.multiple_of(h * 32, 32)
            at = pl.multiple_of(h * HEAD, 8)
            query = query_ref[0, pl.ds(to, 32), :]
            key = key_ref[0, pl.ds(to, 32), :]
            value = value_ref[0, pl.ds(to, 32), :]
            both = pl.multiple_of(pair * 48, 16)
            grad = grad_mixed_ref[0, pl.ds(both, 48), :].astype(f32)[HEAD * part : HEAD * part + HEAD]
            mixed = mixed_ref[0, pl.ds(both, 48), :].astype(f32)[HEAD * part : HEAD * part + HEAD]
            shift = jnp.sum(grad * mixed, axis=0, keepdims=True)
            grad = jnp.concatenate([grad, rows_of(three_parts(-shift), WIDE)], 0).astype(bf16)
            grad_q = []
            grad_k = jnp.zeros((32, WIDE), f32)
            grad_v = jnp.zeros((32, WIDE), f32)
            for low, high, keys in BACKWARD_BLOCKS:
                probs = jnp.exp2(dot(query[:, low:high], key[:, :keys], (0, 0)))
                grad_scores = (probs * dot(grad[:, low:high], value[:, :keys], (0, 0))).astype(bf16)
                probs_low = probs.astype(bf16)
                more_v = dot(grad[:, low:high], probs_low, (1, 0))
                more_k = dot(query[:, low:high], grad_scores, (1, 0))
                grad_q.append(dot(key[:, :keys], grad_scores, (1, 1)))
                if keys < WIDE:
                    blank = jnp.zeros((32, WIDE - keys), f32)
                    more_v = jnp.concatenate([more_v, blank], 1)
                    more_k = jnp.concatenate([more_k, blank], 1)
                grad_v += more_v
                grad_k += more_k
            grad_q.append(jnp.zeros((32, WIDE - 592), f32))
            grad_q = jnp.concatenate(grad_q, 1)
            turned_ref[pl.ds(at, HEAD), :] = grad_q[:HEAD] * (1.0 / math.sqrt(HEAD))
            turned_ref[pl.ds(at + WIDTH, HEAD), :] = grad_k[:HEAD] * math.log(2.0)
            turned_ref[pl.ds(at + 2 * WIDTH, HEAD), :] = grad_v[:HEAD]
        return 0

    lax.fori_loop(0, HEADS // 2, head_step, 0)
    turned = turned_ref[...].astype(bf16)
    sums = jnp.sum(turned.astype(f32), axis=1, keepdims=True)
    grad_bias_ref[0:WIDTH] += jnp.broadcast_to(sums[:WIDTH], (WIDTH, 128))
    grad_bias_ref[WIDTH:] += jnp.broadcast_to(sums[2 * WIDTH :], (WIDTH, 128))
    grad_weight_ref[...] += dot(first_ref[...], turned, (0, 1))
    grad_first = dot(turned, weight_ref[...], (0, 1))[:span]
    scaled = grad_first * gain
    mean_one = jnp.mean(scaled, axis=-1, keepdims=True)
    mean_two = jnp.mean(scaled * normed, axis=-1, keepdims=True)
    input_grad_ref[0] = grad_resid_ref[0] + inverse * (scaled - mean_one - normed * mean_two)
    vector_ref[0:1] += jnp.sum(grad_first * normed, axis=0, keepdims=True)
    vector_ref[1:2] += jnp.sum(grad_first, axis=0, keepdims=True)

    @pl.when(slot == pl.num_programs(0) - 1)
    def _():
        core = core_ref[0]
        order = arrival_order()
        packed_ref[:, : 3 * WIDTH] = dot(order, grad_weight_ref[...].astype(bf16), (0, 0)).astype(bf16)
        blank = jnp.zeros((2, WIDTH), f32)
        high, low = two_parts(vector_ref[0:2])
        rows = jnp.concatenate([high, blank, low, jnp.zeros((122, WIDTH), f32)], 0).astype(bf16)
        more = dot(order, rows, (0, 1))
        lane = lax.broadcasted_iota(jnp.int32, (WIDTH, 128), 1)
        columns = jnp.zeros((WIDTH, 128), f32)
        for s in range(2):
            high, low = two_parts(grad_bias_ref[pl.ds(s, WIDTH, stride=2), :])
            columns = jnp.where(lane == 2 + s, high, jnp.where(lane == 6 + s, low, columns))
        more += dot(order, columns.astype(bf16), (0, 0))
        packed_ref[:, 3 * WIDTH :] = more.astype(bf16)
        blank = jnp.zeros((CHIPS, 128), bf16)
        for side, ref in ((core, mine_ref), (1 - core, theirs_ref)):
            blocks = []
            for r in range(3):
                at = pl.multiple_of(side * 192 + 64 * r, 64)
                for j in range(10):
                    blocks.append(packed_ref[pl.ds(at, 64), 128 * j : 128 * j + 128])
            ref[...] = jnp.swapaxes(jnp.stack(blocks + [blank, blank]), 0, 1)


def run_backward(core, tokens, query, key, value, mixed, grad_mixed, grad_resid, weight, row):
    slots, span, _ = tokens.shape
    rows = pl.BlockSpec((1, span, WIDTH), lambda s: (s, 0, 0))
    turned = lambda n: pl.BlockSpec((1, n, WIDE), lambda s: (s, 0, 0))
    message = whole(CHIPS, EARLY_ROWS, 128)
    return pl.pallas_call(
        attention_backward,
        grid=(slots,),
        in_specs=[pl.BlockSpec(memory_space=pltpu.SMEM), rows, turned(512), turned(512), turned(512), turned(WIDTH), turned(WIDTH), rows,
                  whole(WIDTH, 3 * WIDTH), whole(8, WIDTH)],
        out_specs=[rows, message, message],
        out_shape=[
            shape_of((slots, span, WIDTH), f32),
            shape_of((CHIPS, EARLY_ROWS, 128), bf16),
            shape_of((CHIPS, EARLY_ROWS, 128), bf16),
        ],
        scratch_shapes=[
            pltpu.VMEM((WIDE, WIDTH), bf16),
            pltpu.VMEM((3 * WIDTH, WIDE), f32),
            pltpu.VMEM((WIDTH, 3 * WIDTH), f32),
            pltpu.VMEM((2 * WIDTH, 128), f32),
            pltpu.VMEM((8, WIDTH), f32),
            pltpu.VMEM((WIDTH, 3 * WIDTH + 128), bf16),
        ],
        compiler_params=params(),
        name="attention_backward",
    )(core, tokens, query, key, value, mixed, grad_mixed, grad_resid, weight, row)


def to_chips(message):
    return lax.all_to_all(message, CHIP_AXES, 0, 0, tiled=True)


def across(message):
    return lax.ppermute(message, CORE_AXIS, [(0, 1), (1, 0)])


def shards(tokens, item_frames, ln1_gain, ln1_bias, qkv_weight, qv_bias, out_weight, out_bias, ln2_gain, ln2_bias,
           up_weight, up_bias, down_weight, down_bias, cotangent):
    core = lax.axis_index(CORE_AXIS).astype(jnp.int32).reshape(1)
    early = to_chips(run_pack_early(qkv_weight, ln1_gain, ln1_bias, qv_bias))
    up_sent = up_weight.reshape(3, 16, 2, 4, 12).transpose(0, 2, 4, 1, 3).reshape(3, HIDDEN)
    late = to_chips(run_pack_late(out_weight, up_sent, down_weight, out_bias, ln2_gain, ln2_bias, down_bias, up_bias))
    mixed, query, key, value, weight, row = run_forward(core, item_frames, tokens, early, across(early))
    output, grad_resid, grad_mixed, mine, theirs = run_feed_forward(core, tokens, mixed, cotangent, late, across(late))
    rest = (mine.astype(f32) + across(theirs).astype(f32)).astype(bf16)
    rest = to_chips(rest)
    input_grad, mine, theirs = run_backward(core, tokens, query, key, value, mixed, grad_mixed, grad_resid, weight, row)
    own = (mine.astype(f32) + across(theirs).astype(f32)).astype(bf16)
    own = to_chips(own)
    grad_out, grad_up, grad_down, grad_out_b, grad_gain_two, grad_offset_two, grad_down_b, grad_up_b = run_unpack_rest(rest)
    grad_up = grad_up.reshape(3, 2, 12, 16, 4).transpose(0, 3, 1, 4, 2).reshape(3, HIDDEN)
    grad_qkv, grad_gain, grad_offset, grad_qv = run_unpack_first(own)
    return (output, input_grad, grad_gain, grad_offset, grad_qkv, grad_qv, grad_out, grad_out_b, grad_gain_two, grad_offset_two,
            grad_up, grad_up_b, grad_down, grad_down_b)


def solution(mesh):
    split = Mesh(mesh.devices.reshape(4, 4, 2, mesh.shape["narrow"]), ALL)
    by_rank = lambda n: P(ALL, *([None] * (n - 1)))
    return jax.shard_map(
        shards,
        mesh=split,
        in_specs=tuple(by_rank(n) for n in (3, 2, 1, 1, 2, 1, 2, 1, 1, 1, 2, 1, 2, 1, 3)),
        out_specs=tuple(by_rank(n) for n in (3, 3, 1, 1, 2, 1, 2, 1, 1, 1, 2, 1, 2, 1)),
        check_vma=False,
    )
```

```python
import math

import jax
import jax.numpy as jnp
from jax import lax
from jax.experimental import pallas as pl
from jax.experimental.pallas import tpu as pltpu
from jax.sharding import Mesh
from jax.sharding import PartitionSpec as P

HEADS = 16
HEAD = 24
FRAME = 196
WIDTH = 384
HIDDEN = 1536
WIDE = 640
CHIPS = 64
EARLY_ROWS = 32
LATE_ROWS = 96
EPSILON = 1e-05
NEGATIVE = -1e30
bf16 = jnp.bfloat16
f32 = jnp.float32
FORWARD_BLOCKS = ((0, 128, 208), (128, 384, 400), (384, 640, 592))
FORWARD_BATCH = 16
BACKWARD_BATCH = 8
BACKWARD_BLOCKS = ((0, 128, 256), (128, 384, 512), (384, 592, 640))
ALL = ("wide_0", "wide_1", "wide_2", "narrow")
CHIP_AXES = ("wide_0", "wide_1", "narrow")
CORE_AXIS = "wide_2"
VMEM_LIMIT = 56 * 2**20


def dot(left, right, over):
    return lax.dot_general(left, right, (((over[0],), (over[1],)), ((), ())), preferred_element_type=f32)


def norm_parts(values):
    centred = values - jnp.mean(values, axis=-1, keepdims=True)
    inverse = lax.rsqrt(jnp.mean(centred * centred, axis=-1, keepdims=True) + EPSILON)
    return centred * inverse, inverse


def two_parts(values):
    high = values.astype(bf16).astype(f32)
    return high, values - high


def three_parts(values):
    high, rest = two_parts(values)
    middle, low = two_parts(rest)
    return high, middle, low


def rows_of(rows, width, count=8):
    index = lax.broadcasted_iota(jnp.int32, (count, width), 0)
    out = jnp.zeros((count, width), f32)
    for k, row in enumerate(rows):
        out = jnp.where(index == k, row, out)
    return out


def arrival_order():
    place = lax.broadcasted_iota(jnp.int32, (WIDTH, WIDTH), 1)
    feature = lax.broadcasted_iota(jnp.int32, (WIDTH, WIDTH), 0)
    core = (place >= WIDTH // 2).astype(jnp.int32)
    rest = place - core * (WIDTH // 2)
    row = rest >> 6
    chip = rest & 63
    return (feature == 3 * (8 * (chip >> 2) + 4 * core + (chip & 3)) + row).astype(f32).astype(bf16)


def mask_rows(counts_ref, slot):
    lane = lax.broadcasted_iota(jnp.int32, (1, WIDE), 1)
    first_end = counts_ref[slot, 0]
    second_end = first_end + counts_ref[slot, 1]
    third_end = second_end + counts_ref[slot, 2]
    group = [
        (f >= first_end).astype(jnp.int32) + (f >= second_end).astype(jnp.int32) + (f >= third_end).astype(jnp.int32)
        for f in range(3)
    ]
    hidden = []
    for f in range(3):
        row = jnp.full((1, WIDE), NEGATIVE, f32)
        for k in range(f + 1):
            seen = jnp.where(group[f] == group[k], 0.0, NEGATIVE).astype(f32)
            row = jnp.where((lane >= FRAME * k) & (lane < FRAME * (k + 1)), seen, row)
        hidden.append(row)
    frame = [((lane >= FRAME * f) & (lane < FRAME * (f + 1))).astype(f32) for f in range(3)]
    return hidden, frame


def params(**more):
    return pltpu.CompilerParams(vmem_limit_bytes=VMEM_LIMIT, **more)


def cost(microseconds):
    return pl.CostEstimate(flops=int(microseconds * 1.1e9), bytes_accessed=2**20, transcendentals=0)


def whole(*shape):
    return pl.BlockSpec(shape, lambda *_: (0,) * len(shape))


def shape_of(shape, dtype):
    return jax.ShapeDtypeStruct(shape, dtype)


def pack_early(qkv_ref, gain_ref, offset_ref, qv_ref, out_ref, rows_ref):
    rows_ref[...] = jnp.zeros_like(rows_ref)
    weight = qkv_ref[...].astype(f32)
    gain = gain_ref[...].astype(f32).reshape(1, 3)
    offset = offset_ref[...].astype(f32).reshape(1, 3)
    qv = qv_ref[...].astype(f32).reshape(1, 6)
    for r in range(3):
        for j in range(9):
            rows_ref[10 * r + j : 10 * r + j + 1, :] = weight[r : r + 1, 128 * j : 128 * j + 128]
        rows_ref[10 * r + 9 : 10 * r + 10, 0:1] = gain[:, r : r + 1]
        rows_ref[10 * r + 9 : 10 * r + 10, 1:2] = offset[:, r : r + 1]
        rows_ref[10 * r + 9 : 10 * r + 10, 2:4] = qv[:, 2 * r : 2 * r + 2]
    out_ref[...] = jnp.broadcast_to(rows_ref[...].astype(bf16)[None], out_ref.shape)


def pack_late(out_w_ref, up_ref, down_ref, out_b_ref, gain_ref, offset_ref, down_b_ref, up_b_ref, out_ref, rows_ref):
    rows_ref[...] = jnp.zeros_like(rows_ref)
    out_w = out_w_ref[...].astype(f32)
    up = up_ref[...].astype(f32)
    down = down_ref[...].astype(f32)
    vectors = [ref[...].astype(f32).reshape(1, 3) for ref in (out_b_ref, gain_ref, offset_ref, down_b_ref)]
    for r in range(3):
        for j in range(3):
            rows_ref[3 * r + j : 3 * r + j + 1, :] = out_w[r : r + 1, 128 * j : 128 * j + 128]
        for j in range(12):
            rows_ref[9 + 12 * r + j : 10 + 12 * r + j, :] = up[r : r + 1, 128 * j : 128 * j + 128]
        for k, vector in enumerate(vectors):
            rows_ref[81 + r : 82 + r, k : k + 1] = vector[:, r : r + 1]
    for r in range(12):
        for j in range(3):
            rows_ref[45 + 3 * r + j : 46 + 3 * r + j, :] = down[r : r + 1, 128 * j : 128 * j + 128]
    rows_ref[84:85, 0:12] = up_b_ref[...].astype(f32).reshape(1, 12)
    out_ref[...] = jnp.broadcast_to(rows_ref[...].astype(bf16)[None], out_ref.shape)


def run_pack_early(*args):
    return pl.pallas_call(
        pack_early,
        out_shape=shape_of((CHIPS, EARLY_ROWS, 128), bf16),
        scratch_shapes=[pltpu.VMEM((EARLY_ROWS, 128), f32)],
        compiler_params=params(),
        cost_estimate=cost(2),
        name="pack_early",
    )(*args)


def run_pack_late(*args):
    return pl.pallas_call(
        pack_late,
        out_shape=shape_of((CHIPS, LATE_ROWS, 128), bf16),
        scratch_shapes=[pltpu.VMEM((LATE_ROWS, 128), f32)],
        compiler_params=params(),
        cost_estimate=cost(2),
        name="pack_late",
    )(*args)


def total(arrived_ref):
    return jnp.sum(arrived_ref[...].astype(f32), axis=0)


def spread_lanes(rows, lane, width):
    index = lax.broadcasted_iota(jnp.int32, (1, width), 1)
    out = jnp.zeros((1, width), f32)
    for k, row in enumerate(rows):
        out = jnp.where(index == k, row[:, lane : lane + 1], out)
    return out.reshape(width)


def unpack_first(arrived_ref, qkv_ref, gain_ref, offset_ref, qv_ref):
    sums = total(arrived_ref)
    more = []
    for r in range(3):
        for j in range(9):
            qkv_ref[r : r + 1, 128 * j : 128 * j + 128] = sums[10 * r + j : 10 * r + j + 1, :]
        row = sums[10 * r + 9 : 10 * r + 10, :]
        more.append(row[:, 0:4] + row[:, 4:8])
    gain_ref[...] = spread_lanes(more, 0, 3)
    offset_ref[...] = spread_lanes(more, 1, 3)
    index = lax.broadcasted_iota(jnp.int32, (1, 6), 1)
    out = jnp.zeros((1, 6), f32)
    for k in range(6):
        out = jnp.where(index == k, more[k // 2][:, 2 + k % 2 : 3 + k % 2], out)
    qv_ref[...] = out.reshape(6)


def run_unpack_first(arrived):
    return pl.pallas_call(
        unpack_first,
        out_shape=[shape_of((3, 3 * WIDTH), f32), shape_of((3,), f32), shape_of((3,), f32), shape_of((6,), f32)],
        compiler_params=params(),
        cost_estimate=cost(2),
        name="unpack_first",
    )(arrived)


def unpack_rest(arrived_ref, out_ref, up_ref, down_ref, out_b_ref, gain_ref, offset_ref, down_b_ref, up_b_ref):
    sums = total(arrived_ref)
    more = []
    for r in range(3):
        for j in range(3):
            out_ref[r : r + 1, 128 * j : 128 * j + 128] = sums[3 * r + j : 3 * r + j + 1, :]
        for j in range(12):
            up_ref[r : r + 1, 128 * j : 128 * j + 128] = sums[9 + 12 * r + j : 10 + 12 * r + j, :]
        row = sums[81 + r : 82 + r, :]
        more.append(row[:, 0:4] + row[:, 4:8])
    for r in range(12):
        for j in range(3):
            down_ref[r : r + 1, 128 * j : 128 * j + 128] = sums[45 + 3 * r + j : 46 + 3 * r + j, :]
    for k, ref in enumerate((out_b_ref, gain_ref, offset_ref, down_b_ref)):
        ref[...] = spread_lanes(more, k, 3)
    up_b_ref[...] = (sums[84:85, 0:12] + sums[84:85, 12:24]).reshape(12)


def run_unpack_rest(arrived):
    return pl.pallas_call(
        unpack_rest,
        out_shape=[shape_of((3, WIDTH), f32), shape_of((3, HIDDEN), f32), shape_of((12, WIDTH), f32)]
        + [shape_of((3,), f32)] * 4
        + [shape_of((12,), f32)],
        compiler_params=params(),
        cost_estimate=cost(2),
        name="unpack_rest",
    )(arrived)


def attention_forward(core_ref, counts_ref, tokens_ref, own_ref, other_ref,
                      mixed_ref, query_ref, key_ref, value_ref, weight_ref, vector_ref,
                      first_ref, projected_ref, mixed_scratch, arrived_ref, bias_ref):
    slot = pl.program_id(0)
    span = tokens_ref.shape[1]
    scale = math.log2(math.e) / math.sqrt(HEAD)

    @pl.when(slot == 0)
    def _():
        core = core_ref[0]
        for side, ref in ((core, own_ref), (1 - core, other_ref)):
            blocks = jnp.swapaxes(ref[...], 0, 1)
            for r in range(3):
                at = pl.multiple_of(side * 192 + 64 * r, 64)
                for j in range(10):
                    arrived_ref[pl.ds(at, 64), 128 * j : 128 * j + 128] = blocks[10 * r + j]
        order = arrival_order()
        ordered = dot(order, arrived_ref[...], (1, 0))
        weight_ref[...] = ordered[:, : 3 * WIDTH].astype(bf16)
        vector_ref[...] = dot(arrived_ref[:, 3 * WIDTH :], order, (0, 1))[0:8]
        for s in range(2):
            column = ordered[:, 3 * WIDTH + 2 + s : 3 * WIDTH + 3 + s]
            bias_ref[pl.ds(s, WIDTH, stride=2), :] = jnp.broadcast_to(column, (WIDTH, 128))

    normed, _ = norm_parts(tokens_ref[0].astype(f32))
    first_ref[576:WIDE, :] = jnp.zeros((WIDE - 576, WIDTH), bf16)
    first_ref[0:span, :] = (normed * vector_ref[0:1] + vector_ref[1:2]).astype(bf16)
    projected_ref[...] = dot(weight_ref[...], first_ref[...], (0, 1))
    hidden, frame = mask_rows(counts_ref, slot)
    one = jnp.ones((1, WIDE), f32)
    query_more = rows_of(frame, WIDE)
    key_more = rows_of(hidden + [one, one, one], WIDE)
    value_more = rows_of([one, one, one], WIDE)

    def heads_step(step, _):
        heads = [step * FORWARD_BATCH + k for k in range(FORWARD_BATCH)]
        queries, keys, values = [], [], []
        for h in heads:
            at = pl.multiple_of(h * HEAD, 8)
            to = pl.multiple_of(h * 32, 32)
            wide = lambda start: jnp.concatenate([bias_ref[pl.ds(start, HEAD), :]] * (WIDE // 128), 1)
            query = (projected_ref[pl.ds(at, HEAD), :] + wide(at)) * scale
            value = projected_ref[pl.ds(at + 2 * WIDTH, HEAD), :] + wide(at + WIDTH)
            queries.append(jnp.concatenate([query, query_more], 0))
            keys.append(jnp.concatenate([projected_ref[pl.ds(at + WIDTH, HEAD), :], key_more], 0).astype(bf16))
            values.append(jnp.concatenate([value, value_more], 0).astype(bf16))
            key_ref[0, pl.ds(to, 32), :] = keys[-1]
            value_ref[0, pl.ds(to, 32), :] = values[-1]
        lows = [query.astype(bf16) for query in queries]
        scores = [[dot(key[:, :count], low[:, a:b], (0, 0)) for a, b, count in FORWARD_BLOCKS] for low, key in zip(lows, keys)]
        peaks = [[jnp.max(part, axis=0, keepdims=True) for part in parts] for parts in scores]
        weights = [[jnp.exp2(part - top).astype(bf16) for part, top in zip(*pair)] for pair in zip(scores, peaks)]
        got = [
            [dot(value[:, :count], part, (1, 0)) for part, (_, _, count) in zip(parts, FORWARD_BLOCKS)]
            for value, parts in zip(values, weights)
        ]
        for h, query, tops, parts in zip(heads, queries, peaks, got):
            at = pl.multiple_of(h * HEAD, 8)
            to = pl.multiple_of(h * 32, 32)
            both = jnp.concatenate(parts, 1)
            row_total = both[HEAD : HEAD + 1]
            mixed_scratch[pl.ds(at, HEAD), :] = both[:HEAD] * (1.0 / row_total)
            logs = jnp.concatenate(tops, 1) + jnp.log2(row_total)
            zero = jnp.zeros((1, WIDE), f32)
            log_rows = rows_of([zero, zero, zero, *three_parts(-logs)], WIDE)
            query_ref[0, pl.ds(to, 32), :] = (query + jnp.concatenate([jnp.zeros((HEAD, WIDE), f32), log_rows], 0)).astype(bf16)
        return 0

    lax.fori_loop(0, HEADS // FORWARD_BATCH, heads_step, 0)
    mixed_ref[0] = mixed_scratch[...].astype(bf16)


def run_forward(core, counts, tokens, own, other):
    slots, span, _ = tokens.shape
    per_slot = lambda rows: pl.BlockSpec((1, rows, WIDE), lambda s: (s, 0, 0))
    scalars = pl.BlockSpec(memory_space=pltpu.SMEM)
    return pl.pallas_call(
        attention_forward,
        grid=(slots,),
        in_specs=[
            scalars,
            scalars,
            pl.BlockSpec((1, span, WIDTH), lambda s: (s, 0, 0)),
            whole(CHIPS, EARLY_ROWS, 128),
            whole(CHIPS, EARLY_ROWS, 128),
        ],
        out_specs=[per_slot(WIDTH), per_slot(512), per_slot(512), per_slot(512), whole(WIDTH, 3 * WIDTH), whole(8, WIDTH)],
        out_shape=[shape_of((slots, rows, WIDE), bf16) for rows in (WIDTH, 512, 512, 512)]
        + [shape_of((WIDTH, 3 * WIDTH), bf16), shape_of((8, WIDTH), f32)],
        scratch_shapes=[
            pltpu.VMEM((WIDE, WIDTH), bf16),
            pltpu.VMEM((3 * WIDTH, WIDE), f32),
            pltpu.VMEM((WIDTH, WIDE), f32),
            pltpu.VMEM((WIDTH, 3 * WIDTH + 128), bf16),
            pltpu.VMEM((2 * WIDTH, 128), f32),
        ],
        compiler_params=params(),
        cost_estimate=cost(40),
        name="attention_forward",
    )(core, counts, tokens, own, other)


def feed_forward(core_ref, tokens_ref, mixed_ref, cotangent_ref, own_ref, other_ref,
                 output_ref, grad_resid_ref, grad_mixed_ref, mine_ref, theirs_ref,
                 arrived_ref, out_w_ref, up_w_ref, down_w_ref, row_ref, up_b_ref,
                 grad_out_ref, grad_up_ref, grad_down_ref, vector_ref, up_vector_ref, packed_ref):
    slot = pl.program_id(0)
    span = tokens_ref.shape[1]
    chunk = 768

    @pl.when(slot == 0)
    def _():
        core = core_ref[0]
        for side, ref in ((core, own_ref), (1 - core, other_ref)):
            blocks = jnp.swapaxes(ref[...], 0, 1)
            for r in range(3):
                at = pl.multiple_of(side * 192 + 64 * r, 64)
                for j in range(15):
                    arrived_ref[pl.ds(at, 64), 128 * j : 128 * j + 128] = blocks[3 * r + j] if j < 3 else blocks[6 + 12 * r + j]
                arrived_ref[pl.ds(at, 64), 1920:2048] = blocks[81 + r]
            for r in range(12):
                at = pl.multiple_of(side * 768 + 64 * r, 64)
                for j in range(3):
                    down_w_ref[pl.ds(at, 64), 128 * j : 128 * j + 128] = blocks[45 + 3 * r + j]
            turned = blocks[84].astype(f32).T
            up_b = jnp.concatenate([turned[r : r + 1] for r in range(12)], 1)
            up_b_ref[:, pl.ds(pl.multiple_of(side * 768, 128), 768)] = up_b
        order = arrival_order()
        ordered = dot(order, arrived_ref[:, :1920], (1, 0)).astype(bf16)
        out_w_ref[...] = ordered[:, :WIDTH]
        up_w_ref[...] = ordered[:, WIDTH:]
        row_ref[...] = dot(arrived_ref[:, 1920:], order, (0, 1))[0:8]
        grad_out_ref[...] = jnp.zeros_like(grad_out_ref)
        grad_up_ref[...] = jnp.zeros_like(grad_up_ref)
        grad_down_ref[...] = jnp.zeros_like(grad_down_ref)
        vector_ref[...] = jnp.zeros_like(vector_ref)
        up_vector_ref[...] = jnp.zeros_like(up_vector_ref)

    out_b, gain, offset, down_b = (row_ref[k : k + 1] for k in range(4))
    mixed = mixed_ref[0]
    mixed = mixed[:, :span]
    resid = tokens_ref[0].astype(f32) + dot(mixed, out_w_ref[...], (0, 0)) + out_b
    normed, inverse = norm_parts(resid)
    second = (normed * gain + offset).astype(bf16)
    grad_branch = cotangent_ref[0]
    result = resid + down_b
    grad_second = jnp.zeros((span, WIDTH), f32)
    root = math.sqrt(2.0 / math.pi)
    for at in range(0, HIDDEN, chunk):
        cols = slice(at, at + chunk)
        up = dot(second, up_w_ref[:, cols], (1, 0)) + up_b_ref[:, cols]
        square = up * up
        tanh = jnp.tanh(up * (root + (root * 0.044715) * square))
        half = 0.5 + 0.5 * tanh
        activated = (up * half).astype(bf16)
        slope = half + (up * (2.0 * half * (1.0 - half))) * (root + (3 * root * 0.044715) * square)
        result += dot(activated, down_w_ref[cols, :], (1, 0))
        grad_up = (dot(grad_branch, down_w_ref[cols, :], (1, 1)) * slope).astype(bf16)
        grad_down_ref[cols, :] += dot(activated, grad_branch, (0, 0))
        grad_up_ref[:, cols] += dot(second, grad_up, (0, 0))
        up_vector_ref[:, cols] += jnp.sum(grad_up.astype(f32), axis=0, keepdims=True)
        grad_second += dot(grad_up, up_w_ref[:, cols], (1, 1))
    output_ref[0] = result.astype(bf16)
    scaled = grad_second * gain
    mean_one = jnp.mean(scaled, axis=-1, keepdims=True)
    mean_two = jnp.mean(scaled * normed, axis=-1, keepdims=True)
    grad_full = grad_branch.astype(f32)
    grad_resid = grad_full + inverse * (scaled - mean_one - normed * mean_two)
    grad_resid_ref[0] = grad_resid
    attended = grad_resid.astype(bf16)
    grad_out_ref[...] += dot(mixed, attended, (1, 0))
    grad_mixed_ref[0] = jnp.zeros_like(grad_mixed_ref[0])
    grad_mixed_ref[0, :, :span] = dot(out_w_ref[...], attended, (1, 1)).astype(bf16)
    vector_ref[0:1] += jnp.sum(attended.astype(f32), axis=0, keepdims=True)
    vector_ref[1:2] += jnp.sum(grad_second * normed, axis=0, keepdims=True)
    vector_ref[2:3] += jnp.sum(grad_second, axis=0, keepdims=True)
    vector_ref[3:4] += jnp.sum(grad_full, axis=0, keepdims=True)

    @pl.when(slot == pl.num_programs(0) - 1)
    def _():
        core = core_ref[0]
        order = arrival_order()
        packed_ref[:, :WIDTH] = dot(order, grad_out_ref[...].astype(bf16), (0, 0)).astype(bf16)
        packed_ref[:, WIDTH:1920] = dot(order, grad_up_ref[...].astype(bf16), (0, 0)).astype(bf16)
        high, low = two_parts(vector_ref[0:4])
        rows = jnp.concatenate([high, low, jnp.zeros((120, WIDTH), f32)], 0).astype(bf16)
        packed_ref[:, 1920:] = dot(order, rows, (0, 1)).astype(bf16)
        blank = jnp.zeros((CHIPS, 128), bf16)
        for side, ref in ((core, mine_ref), (1 - core, theirs_ref)):
            blocks = [blank] * LATE_ROWS
            for r in range(3):
                at = pl.multiple_of(side * 192 + 64 * r, 64)
                for j in range(15):
                    blocks[3 * r + j if j < 3 else 6 + 12 * r + j] = packed_ref[pl.ds(at, 64), 128 * j : 128 * j + 128]
                blocks[81 + r] = packed_ref[pl.ds(at, 64), 1920:2048]
            for r in range(12):
                at = pl.multiple_of(side * 768 + 64 * r, 64)
                for j in range(3):
                    blocks[45 + 3 * r + j] = grad_down_ref[pl.ds(at, 64), 128 * j : 128 * j + 128].astype(bf16)
            line = up_vector_ref[:, pl.ds(pl.multiple_of(side * 768, 128), 768)]
            high, low = two_parts(line)
            rows = [part[:, 64 * r : 64 * r + 64] for part in (high, low) for r in range(12)]
            blocks[84] = rows_of(rows, 64, 128).T.astype(bf16)
            ref[...] = jnp.swapaxes(jnp.stack(blocks), 0, 1)


def run_feed_forward(core, tokens, mixed, cotangent, own, other):
    slots, span, _ = tokens.shape
    rows = pl.BlockSpec((1, span, WIDTH), lambda s: (s, 0, 0))
    turned = pl.BlockSpec((1, WIDTH, WIDE), lambda s: (s, 0, 0))
    message = whole(CHIPS, LATE_ROWS, 128)
    return pl.pallas_call(
        feed_forward,
        grid=(slots,),
        in_specs=[pl.BlockSpec(memory_space=pltpu.SMEM), rows, turned, rows, message, message],
        out_specs=[rows, rows, turned, message, message],
        out_shape=[
            shape_of((slots, span, WIDTH), bf16),
            shape_of((slots, span, WIDTH), f32),
            shape_of((slots, WIDTH, WIDE), bf16),
            shape_of((CHIPS, LATE_ROWS, 128), bf16),
            shape_of((CHIPS, LATE_ROWS, 128), bf16),
        ],
        scratch_shapes=[
            pltpu.VMEM((WIDTH, 2048), bf16),
            pltpu.VMEM((WIDTH, WIDTH), bf16),
            pltpu.VMEM((WIDTH, HIDDEN), bf16),
            pltpu.VMEM((HIDDEN, WIDTH), bf16),
            pltpu.VMEM((8, WIDTH), f32),
            pltpu.VMEM((1, HIDDEN), f32),
            pltpu.VMEM((WIDTH, WIDTH), f32),
            pltpu.VMEM((WIDTH, HIDDEN), f32),
            pltpu.VMEM((HIDDEN, WIDTH), f32),
            pltpu.VMEM((8, WIDTH), f32),
            pltpu.VMEM((1, HIDDEN), f32),
            pltpu.VMEM((WIDTH, 2048), bf16),
        ],
        compiler_params=params(),
        cost_estimate=cost(30),
        name="feed_forward",
    )(core, tokens, mixed, cotangent, own, other)


def attention_backward(core_ref, tokens_ref, query_ref, key_ref, value_ref, mixed_ref, grad_mixed_ref, grad_resid_ref, weight_ref, row_ref,
                       input_grad_ref, mine_ref, theirs_ref,
                       first_ref, turned_ref, grad_weight_ref, grad_bias_ref, vector_ref, packed_ref):
    slot = pl.program_id(0)
    span = tokens_ref.shape[1]

    @pl.when(slot == 0)
    def _():
        grad_weight_ref[...] = jnp.zeros_like(grad_weight_ref)
        grad_bias_ref[...] = jnp.zeros_like(grad_bias_ref)
        vector_ref[...] = jnp.zeros_like(vector_ref)

    gain, offset = row_ref[0:1], row_ref[1:2]
    normed, inverse = norm_parts(tokens_ref[0].astype(f32))
    first_ref[576:WIDE, :] = jnp.zeros((WIDE - 576, WIDTH), bf16)
    first_ref[0:span, :] = (normed * gain + offset).astype(bf16)

    def heads_step(step, _):
        heads = [step * BACKWARD_BATCH + k for k in range(BACKWARD_BATCH)]
        queries, keys, values, grads = [], [], [], []
        for k, h in enumerate(heads):
            to = pl.multiple_of(h * 32, 32)
            queries.append(query_ref[0, pl.ds(to, 32), :])
            keys.append(key_ref[0, pl.ds(to, 32), :])
            values.append(value_ref[0, pl.ds(to, 32), :])
            both = pl.multiple_of(step * (BACKWARD_BATCH * HEAD) + (k // 2) * 48, 16)
            part = slice(HEAD * (k % 2), HEAD * (k % 2) + HEAD)
            grad = grad_mixed_ref[0, pl.ds(both, 48), :].astype(f32)[part]
            mixed = mixed_ref[0, pl.ds(both, 48), :].astype(f32)[part]
            shift = jnp.sum(grad * mixed, axis=0, keepdims=True)
            grads.append(jnp.concatenate([grad, rows_of(three_parts(-shift), WIDE)], 0).astype(bf16))
        scores = [[dot(query[:, a:b], key[:, :count], (0, 0)) for a, b, count in BACKWARD_BLOCKS] for query, key in zip(queries, keys)]
        slopes = [[dot(grad[:, a:b], value[:, :count], (0, 0)) for a, b, count in BACKWARD_BLOCKS] for grad, value in zip(grads, values)]
        probs = [[jnp.exp2(part) for part in parts] for parts in scores]
        grad_scores = [[(part * slope).astype(bf16) for part, slope in zip(*pair)] for pair in zip(probs, slopes)]
        probs = [[part.astype(bf16) for part in parts] for parts in probs]
        over = lambda left, parts: [dot(left[:, a:b], part, (1, 0)) for part, (a, b, _) in zip(parts, BACKWARD_BLOCKS)]
        grad_v = [over(grad, parts) for grad, parts in zip(grads, probs)]
        grad_k = [over(query, parts) for query, parts in zip(queries, grad_scores)]
        grad_q = [
            [dot(key[:, :count], part, (1, 1)) for part, (_, _, count) in zip(parts, BACKWARD_BLOCKS)]
            for key, parts in zip(keys, grad_scores)
        ]
        fill = lambda part: part if part.shape[1] == WIDE else jnp.concatenate([part, jnp.zeros((32, WIDE - part.shape[1]), f32)], 1)
        for k, h in enumerate(heads):
            at = pl.multiple_of(h * HEAD, 8)
            turned_ref[pl.ds(at, HEAD), :] = fill(jnp.concatenate(grad_q[k], 1))[:HEAD] * (1.0 / math.sqrt(HEAD))
            turned_ref[pl.ds(at + WIDTH, HEAD), :] = sum(fill(part) for part in grad_k[k])[:HEAD] * math.log(2.0)
            turned_ref[pl.ds(at + 2 * WIDTH, HEAD), :] = sum(fill(part) for part in grad_v[k])[:HEAD]
        return 0

    lax.fori_loop(0, HEADS // BACKWARD_BATCH, heads_step, 0)
    turned = turned_ref[...].astype(bf16)
    sums = jnp.sum(turned.astype(f32), axis=1, keepdims=True)
    grad_bias_ref[0:WIDTH] += jnp.broadcast_to(sums[:WIDTH], (WIDTH, 128))
    grad_bias_ref[WIDTH:] += jnp.broadcast_to(sums[2 * WIDTH :], (WIDTH, 128))
    grad_weight_ref[...] += dot(first_ref[...], turned, (0, 1))
    grad_first = dot(turned, weight_ref[...], (0, 1))[:span]
    scaled = grad_first * gain
    mean_one = jnp.mean(scaled, axis=-1, keepdims=True)
    mean_two = jnp.mean(scaled * normed, axis=-1, keepdims=True)
    input_grad_ref[0] = grad_resid_ref[0] + inverse * (scaled - mean_one - normed * mean_two)
    vector_ref[0:1] += jnp.sum(grad_first * normed, axis=0, keepdims=True)
    vector_ref[1:2] += jnp.sum(grad_first, axis=0, keepdims=True)

    @pl.when(slot == pl.num_programs(0) - 1)
    def _():
        core = core_ref[0]
        order = arrival_order()
        packed_ref[:, : 3 * WIDTH] = dot(order, grad_weight_ref[...].astype(bf16), (0, 0)).astype(bf16)
        blank = jnp.zeros((2, WIDTH), f32)
        high, low = two_parts(vector_ref[0:2])
        rows = jnp.concatenate([high, blank, low, jnp.zeros((122, WIDTH), f32)], 0).astype(bf16)
        more = dot(order, rows, (0, 1))
        lane = lax.broadcasted_iota(jnp.int32, (WIDTH, 128), 1)
        columns = jnp.zeros((WIDTH, 128), f32)
        for s in range(2):
            high, low = two_parts(grad_bias_ref[pl.ds(s, WIDTH, stride=2), :])
            columns = jnp.where(lane == 2 + s, high, jnp.where(lane == 6 + s, low, columns))
        more += dot(order, columns.astype(bf16), (0, 0))
        packed_ref[:, 3 * WIDTH :] = more.astype(bf16)
        blank = jnp.zeros((CHIPS, 128), bf16)
        for side, ref in ((core, mine_ref), (1 - core, theirs_ref)):
            blocks = []
            for r in range(3):
                at = pl.multiple_of(side * 192 + 64 * r, 64)
                for j in range(10):
                    blocks.append(packed_ref[pl.ds(at, 64), 128 * j : 128 * j + 128])
            ref[...] = jnp.swapaxes(jnp.stack(blocks + [blank, blank]), 0, 1)


def run_backward(core, tokens, query, key, value, mixed, grad_mixed, grad_resid, weight, row):
    slots, span, _ = tokens.shape
    rows = pl.BlockSpec((1, span, WIDTH), lambda s: (s, 0, 0))
    turned = lambda n: pl.BlockSpec((1, n, WIDE), lambda s: (s, 0, 0))
    message = whole(CHIPS, EARLY_ROWS, 128)
    return pl.pallas_call(
        attention_backward,
        grid=(slots,),
        in_specs=[pl.BlockSpec(memory_space=pltpu.SMEM), rows, turned(512), turned(512), turned(512), turned(WIDTH), turned(WIDTH), rows,
                  whole(WIDTH, 3 * WIDTH), whole(8, WIDTH)],
        out_specs=[rows, message, message],
        out_shape=[
            shape_of((slots, span, WIDTH), f32),
            shape_of((CHIPS, EARLY_ROWS, 128), bf16),
            shape_of((CHIPS, EARLY_ROWS, 128), bf16),
        ],
        scratch_shapes=[
            pltpu.VMEM((WIDE, WIDTH), bf16),
            pltpu.VMEM((3 * WIDTH, WIDE), f32),
            pltpu.VMEM((WIDTH, 3 * WIDTH), f32),
            pltpu.VMEM((2 * WIDTH, 128), f32),
            pltpu.VMEM((8, WIDTH), f32),
            pltpu.VMEM((WIDTH, 3 * WIDTH + 128), bf16),
        ],
        compiler_params=params(),
        cost_estimate=cost(45),
        name="attention_backward",
    )(core, tokens, query, key, value, mixed, grad_mixed, grad_resid, weight, row)


def to_chips(message):
    return lax.all_to_all(message, CHIP_AXES, 0, 0, tiled=True)


def across(message):
    return lax.ppermute(message, CORE_AXIS, [(0, 1), (1, 0)])


def shards(tokens, item_frames, ln1_gain, ln1_bias, qkv_weight, qv_bias, out_weight, out_bias, ln2_gain, ln2_bias,
           up_weight, up_bias, down_weight, down_bias, cotangent):
    core = lax.axis_index(CORE_AXIS).astype(jnp.int32).reshape(1)
    early = run_pack_early(qkv_weight, ln1_gain, ln1_bias, qv_bias)
    early, up_weight = lax.optimization_barrier((early, up_weight))
    early = to_chips(early)
    up_sent = up_weight.reshape(3, 16, 2, 4, 12).transpose(0, 2, 4, 1, 3).reshape(3, HIDDEN)
    late = to_chips(run_pack_late(out_weight, up_sent, down_weight, out_bias, ln2_gain, ln2_bias, down_bias, up_bias))
    mixed, query, key, value, weight, row = run_forward(core, item_frames, tokens, early, across(early))
    late, mixed = lax.optimization_barrier((late, mixed))
    output, grad_resid, grad_mixed, mine, theirs = run_feed_forward(core, tokens, mixed, cotangent, late, across(late))
    rest = (mine.astype(f32) + across(theirs).astype(f32)).astype(bf16)
    rest, grad_mixed = lax.optimization_barrier((rest, grad_mixed))
    rest = to_chips(rest)
    input_grad, mine, theirs = run_backward(core, tokens, query, key, value, mixed, grad_mixed, grad_resid, weight, row)
    own = (mine.astype(f32) + across(theirs).astype(f32)).astype(bf16)
    own, rest = lax.optimization_barrier((own, rest))
    own = to_chips(own)
    grad_out, grad_up, grad_down, grad_out_b, grad_gain_two, grad_offset_two, grad_down_b, grad_up_b = run_unpack_rest(rest)
    grad_up = grad_up.reshape(3, 2, 12, 16, 4).transpose(0, 3, 1, 4, 2).reshape(3, HIDDEN)
    grad_qkv, grad_gain, grad_offset, grad_qv = run_unpack_first(own)
    return (output, input_grad, grad_gain, grad_offset, grad_qkv, grad_qv, grad_out, grad_out_b, grad_gain_two, grad_offset_two,
            grad_up, grad_up_b, grad_down, grad_down_b)


def solution(mesh):
    split = Mesh(mesh.devices.reshape(4, 4, 2, mesh.shape["narrow"]), ALL)
    by_rank = lambda n: P(ALL, *([None] * (n - 1)))
    return jax.shard_map(
        shards,
        mesh=split,
        in_specs=tuple(by_rank(n) for n in (3, 2, 1, 1, 2, 1, 2, 1, 1, 1, 2, 1, 2, 1, 3)),
        out_specs=tuple(by_rank(n) for n in (3, 3, 1, 1, 2, 1, 2, 1, 1, 1, 2, 1, 2, 1)),
        check_vma=False,
    )
```

```python
import math

import jax
import jax.numpy as jnp
from jax import lax
from jax.experimental import pallas as pl
from jax.experimental.pallas import tpu as pltpu
from jax.sharding import Mesh
from jax.sharding import PartitionSpec as P

HEADS = 16
HEAD = 24
FRAME = 196
WIDTH = 384
HIDDEN = 1536
WIDE = 640
SPAN = 588
ROWS = 592
CHIPS = 64
FIRST_ROWS = 32
REST_ROWS = 88
EPSILON = 1e-05
NEGATIVE = -1e30
bf16 = jnp.bfloat16
f32 = jnp.float32
FORWARD_BLOCKS = ((0, 128, 208), (128, 384, 400), (384, 640, 592))
FORWARD_BATCH = 16
BACKWARD_BATCH = 8
BACKWARD_BLOCKS = ((0, 128, 256), (128, 384, 512), (384, 592, 640))
ALL = ("wide_0", "wide_1", "wide_2", "narrow")
CHIP_AXES = ("wide_0", "wide_1", "narrow")
CORE_AXIS = "wide_2"


def dot(left, right, over):
    return lax.dot_general(left, right, (((over[0],), (over[1],)), ((), ())), preferred_element_type=f32)


def norm_parts(values):
    centred = values - jnp.mean(values, axis=-1, keepdims=True)
    inverse = lax.rsqrt(jnp.mean(centred * centred, axis=-1, keepdims=True) + EPSILON)
    return centred * inverse, inverse


def two_parts(values):
    high = values.astype(bf16).astype(f32)
    return high, values - high


def three_parts(values):
    high, rest = two_parts(values)
    middle, low = two_parts(rest)
    return high, middle, low


def rows_of(rows, width, count=8):
    index = lax.broadcasted_iota(jnp.int32, (count, width), 0)
    out = jnp.zeros((count, width), f32)
    for k, row in enumerate(rows):
        out = jnp.where(index == k, row, out)
    return out


def arrival_order():
    place = lax.broadcasted_iota(jnp.int32, (WIDTH, WIDTH), 1)
    feature = lax.broadcasted_iota(jnp.int32, (WIDTH, WIDTH), 0)
    core = (place >= WIDTH // 2).astype(jnp.int32)
    rest = place - core * (WIDTH // 2)
    row = rest >> 6
    chip = rest & 63
    return (feature == 3 * (8 * (chip >> 2) + 4 * core + (chip & 3)) + row).astype(f32).astype(bf16)


def mask_rows(counts_ref, slot):
    lane = lax.broadcasted_iota(jnp.int32, (1, WIDE), 1)
    first_end = counts_ref[slot, 0]
    second_end = first_end + counts_ref[slot, 1]
    third_end = second_end + counts_ref[slot, 2]
    group = [
        (f >= first_end).astype(jnp.int32) + (f >= second_end).astype(jnp.int32) + (f >= third_end).astype(jnp.int32)
        for f in range(3)
    ]
    hidden = []
    for f in range(3):
        row = jnp.full((1, WIDE), NEGATIVE, f32)
        for k in range(f + 1):
            seen = jnp.where(group[f] == group[k], 0.0, NEGATIVE).astype(f32)
            row = jnp.where((lane >= FRAME * k) & (lane < FRAME * (k + 1)), seen, row)
        hidden.append(row)
    frame = [((lane >= FRAME * f) & (lane < FRAME * (f + 1))).astype(f32) for f in range(3)]
    return hidden, frame


def params(mebibytes):
    return pltpu.CompilerParams(vmem_limit_bytes=mebibytes * 2**20)


def cost(microseconds):
    return pl.CostEstimate(flops=int(microseconds * 1.1e9), bytes_accessed=2**20, transcendentals=0)


def shape_of(shape, dtype):
    return jax.ShapeDtypeStruct(shape, dtype)


def held(*arrays):
    return [pltpu.with_memory_space_constraint(a, pltpu.VMEM) for a in arrays]


def far(*arrays):
    return [pltpu.with_memory_space_constraint(a, pltpu.HBM) for a in arrays]


class Copies:
    def __init__(self, semaphores):
        self.semaphores, self.count, self.open = semaphores, 0, []

    def start(self, source, target):
        copy = pltpu.make_async_copy(source, target, self.semaphores.at[self.count])
        self.count += 1
        copy.start()
        self.open.append(copy)
        return copy

    def wait(self, *copies):
        for copy in copies:
            if copy in self.open:
                self.open.remove(copy)
                copy.wait()

    def wait_all(self):
        self.wait(*list(self.open))


def pack_first(qkv_ref, gain_ref, offset_ref, qv_ref, out_ref, rows_ref):
    rows_ref[...] = jnp.zeros_like(rows_ref)
    weight = qkv_ref[...].astype(f32)
    line = lambda ref, count: ref[...].astype(f32).reshape(1, count)
    gain, offset, qv = line(gain_ref, 3), line(offset_ref, 3), line(qv_ref, 6)
    for r in range(3):
        for j in range(9):
            rows_ref[10 * r + j : 10 * r + j + 1, :] = weight[r : r + 1, 128 * j : 128 * j + 128]
        rows_ref[10 * r + 9 : 10 * r + 10, 0:1] = gain[:, r : r + 1]
        rows_ref[10 * r + 9 : 10 * r + 10, 1:2] = offset[:, r : r + 1]
        rows_ref[10 * r + 9 : 10 * r + 10, 2:4] = qv[:, 2 * r : 2 * r + 2]
    out_ref[...] = jnp.broadcast_to(rows_ref[...].astype(bf16)[None], out_ref.shape)


def pack_second(out_w_ref, up_ref, down_ref, out_b_ref, gain_ref, offset_ref, down_b_ref, up_b_ref, tokens_ref, cotangent_ref,
                out_ref, tokens_out_ref, cotangent_out_ref, rows_ref):
    rows_ref[...] = jnp.zeros_like(rows_ref)
    out_w = out_w_ref[...].astype(f32)
    up = up_ref[...].astype(f32)
    down = down_ref[...].astype(f32)
    line = lambda ref, count: ref[...].astype(f32).reshape(1, count)
    vectors = [line(ref, 3) for ref in (out_b_ref, gain_ref, offset_ref, down_b_ref)]
    for r in range(3):
        for j in range(3):
            rows_ref[3 * r + j : 3 * r + j + 1, :] = out_w[r : r + 1, 128 * j : 128 * j + 128]
        for j in range(12):
            rows_ref[9 + 12 * r + j : 10 + 12 * r + j, :] = up[r : r + 1, 128 * j : 128 * j + 128]
        for k, vector in enumerate(vectors):
            rows_ref[81 + r : 82 + r, k : k + 1] = vector[:, r : r + 1]
    for r in range(12):
        for j in range(3):
            rows_ref[45 + 3 * r + j : 46 + 3 * r + j, :] = down[r : r + 1, 128 * j : 128 * j + 128]
    rows_ref[81:82, 4:16] = line(up_b_ref, 12)
    out_ref[...] = jnp.broadcast_to(rows_ref[...].astype(bf16)[None], out_ref.shape)
    tokens_out_ref[...] = jnp.swapaxes(tokens_ref[...], 0, 1)
    cotangent_out_ref[...] = jnp.swapaxes(cotangent_ref[...], 0, 1)


def swap_leading(values_ref, out_ref):
    out_ref[...] = jnp.swapaxes(values_ref[...], 0, 1)


def run_swap(values):
    rows, columns, width = values.shape
    return pl.pallas_call(
        swap_leading,
        out_shape=shape_of((columns, rows, width), values.dtype),
        compiler_params=params(12),
        cost_estimate=cost(2),
        name="swap_leading",
    )(values)


def run_pack_first(*args):
    return pl.pallas_call(
        pack_first,
        out_shape=shape_of((CHIPS, FIRST_ROWS, 128), bf16),
        scratch_shapes=[pltpu.VMEM((FIRST_ROWS, 128), f32)],
        compiler_params=params(8),
        cost_estimate=cost(2),
        name="pack_first",
    )(*args)


def run_pack_second(*args):
    span, slots, width = args[-1].shape
    kept = shape_of((slots, span, width), bf16)
    return pl.pallas_call(
        pack_second,
        out_shape=[shape_of((CHIPS, REST_ROWS, 128), bf16), kept, kept],
        scratch_shapes=[pltpu.VMEM((REST_ROWS, 128), f32)],
        compiler_params=params(16),
        cost_estimate=cost(4),
        name="pack_second",
    )(*args)


def total(arrived_ref):
    return jnp.sum(arrived_ref[...].astype(f32), axis=0)


def spread_lanes(rows, lane, width):
    index = lax.broadcasted_iota(jnp.int32, (1, width), 1)
    out = jnp.zeros((1, width), f32)
    for k, row in enumerate(rows):
        out = jnp.where(index == k, row[:, lane : lane + 1], out)
    return out.reshape(width)


def unpack_first(arrived_ref, qkv_ref, gain_ref, offset_ref, qv_ref):
    sums = total(arrived_ref)
    more = []
    for r in range(3):
        for j in range(9):
            qkv_ref[r : r + 1, 128 * j : 128 * j + 128] = sums[10 * r + j : 10 * r + j + 1, :]
        row = sums[10 * r + 9 : 10 * r + 10, :]
        more.append(row[:, 0:4] + row[:, 4:8])
    gain_ref[...] = spread_lanes(more, 0, 3)
    offset_ref[...] = spread_lanes(more, 1, 3)
    index = lax.broadcasted_iota(jnp.int32, (1, 6), 1)
    out = jnp.zeros((1, 6), f32)
    for k in range(6):
        out = jnp.where(index == k, more[k // 2][:, 2 + k % 2 : 3 + k % 2], out)
    qv_ref[...] = out.reshape(6)


def run_unpack_first(arrived):
    return pl.pallas_call(
        unpack_first,
        out_shape=[shape_of((3, 3 * WIDTH), f32), shape_of((3,), f32), shape_of((3,), f32), shape_of((6,), f32)],
        compiler_params=params(8),
        cost_estimate=cost(2),
        name="unpack_first",
    )(arrived)


def unpack_rest(arrived_ref, out_ref, up_ref, down_ref, out_b_ref, gain_ref, offset_ref, down_b_ref, up_b_ref):
    sums = total(arrived_ref)
    more = []
    for r in range(3):
        for j in range(3):
            out_ref[r : r + 1, 128 * j : 128 * j + 128] = sums[3 * r + j : 3 * r + j + 1, :]
        for j in range(12):
            up_ref[r : r + 1, 128 * j : 128 * j + 128] = sums[9 + 12 * r + j : 10 + 12 * r + j, :]
        row = sums[81 + r : 82 + r, :]
        more.append(row[:, 0:4] + row[:, 4:8])
    for r in range(12):
        for j in range(3):
            down_ref[r : r + 1, 128 * j : 128 * j + 128] = sums[45 + 3 * r + j : 46 + 3 * r + j, :]
    for k, ref in enumerate((out_b_ref, gain_ref, offset_ref, down_b_ref)):
        ref[...] = spread_lanes(more, k, 3)
    up_b_ref[...] = (sums[84:85, 0:12] + sums[84:85, 12:24]).reshape(12)


def run_unpack_rest(arrived):
    return pl.pallas_call(
        unpack_rest,
        out_shape=[shape_of((3, WIDTH), f32), shape_of((3, HIDDEN), f32), shape_of((12, WIDTH), f32)]
        + [shape_of((3,), f32)] * 4
        + [shape_of((12,), f32)],
        compiler_params=params(12),
        cost_estimate=cost(2),
        name="unpack_rest",
    )(arrived)


def heads_forward(slot, base, projected_ref, bias_ref, mixed_scratch, query_ref, key_ref, value_ref, query_more, key_more, value_more):
    scale = math.log2(math.e) / math.sqrt(HEAD)
    lanes = slice(slot * WIDE, slot * WIDE + WIDE)
    heads = range(base, base + FORWARD_BATCH)
    wide = lambda start: jnp.concatenate([bias_ref[start : start + HEAD, :]] * (WIDE // 128), 1)
    queries, keys, values = [], [], []
    for h in heads:
        at = h * HEAD
        query = (projected_ref[at : at + HEAD, lanes] + wide(at)) * scale
        key = projected_ref[at + WIDTH : at + WIDTH + HEAD, lanes]
        value = projected_ref[at + 2 * WIDTH : at + 2 * WIDTH + HEAD, lanes] + wide(at + WIDTH)
        queries.append(jnp.concatenate([query, query_more], 0))
        keys.append(jnp.concatenate([key, key_more], 0).astype(bf16))
        values.append(jnp.concatenate([value, value_more], 0).astype(bf16))
        key_ref[slot, 32 * h : 32 * h + 32, :] = keys[-1]
        value_ref[slot, 32 * h : 32 * h + 32, :] = values[-1]
    lows = [query.astype(bf16) for query in queries]
    scores = [[dot(key[:, :count], low[:, a:b], (0, 0)) for a, b, count in FORWARD_BLOCKS] for low, key in zip(lows, keys)]
    peaks = [[jnp.max(part, axis=0, keepdims=True) for part in parts] for parts in scores]
    weights = [[jnp.exp2(part - top).astype(bf16) for part, top in zip(*pair)] for pair in zip(scores, peaks)]
    got = [
        [dot(value[:, :count], part, (1, 0)) for part, (_, _, count) in zip(parts, FORWARD_BLOCKS)]
        for value, parts in zip(values, weights)
    ]
    zero = jnp.zeros((1, WIDE), f32)
    for h, query, tops, parts in zip(heads, queries, peaks, got):
        both = jnp.concatenate(parts, 1)
        row_total = both[HEAD : HEAD + 1]
        mixed_scratch[h * HEAD : h * HEAD + HEAD, :] = both[:HEAD] * (1.0 / row_total)
        logs = jnp.concatenate(tops, 1) + jnp.log2(row_total)
        log_rows = rows_of([zero, zero, zero, *three_parts(-logs)], WIDE)
        query_ref[slot, 32 * h : 32 * h + 32, :] = (query + jnp.concatenate([jnp.zeros((HEAD, WIDE), f32), log_rows], 0)).astype(bf16)


def attention_forward(core_ref, counts_ref, tokens_far, own_ref, other_ref,
                      mixed_far, query_far, key_far, value_far, weight_far, vector_ref,
                      first_ref, projected_ref, mixed_scratch, arrived_ref, bias_ref,
                      tokens_ref, mixed_ref, query_ref, key_ref, value_ref, weight_ref, semaphores):
    slots = tokens_ref.shape[0]
    copies = Copies(semaphores)
    copies.start(tokens_far, tokens_ref)
    core = core_ref[0]
    for side, ref in ((core, own_ref), (1 - core, other_ref)):
        blocks = jnp.swapaxes(ref[...], 0, 1)
        for r in range(3):
            at = pl.multiple_of(side * 192 + 64 * r, 64)
            for j in range(10):
                arrived_ref[pl.ds(at, 64), 128 * j : 128 * j + 128] = blocks[10 * r + j]
    order = arrival_order()
    ordered = dot(order, arrived_ref[...], (1, 0))
    weight_ref[...] = ordered[:, : 3 * WIDTH].astype(bf16)
    vector_ref[...] = dot(arrived_ref[:, 3 * WIDTH :], order, (0, 1))[0:8]
    for s in range(2):
        column = ordered[:, 3 * WIDTH + 2 + s : 3 * WIDTH + 3 + s]
        bias_ref[pl.ds(s, WIDTH, stride=2), :] = jnp.broadcast_to(column, (WIDTH, 128))
    first_ref[...] = jnp.zeros_like(first_ref)
    copies.wait_all()
    copies.start(weight_ref, weight_far)
    for slot in range(slots):
        normed, _ = norm_parts(tokens_ref[slot].astype(f32))
        first_ref[slot * WIDE : slot * WIDE + SPAN, :] = (normed * vector_ref[0:1] + vector_ref[1:2]).astype(bf16)
    projected_ref[...] = dot(weight_ref[...], first_ref[...], (0, 1))
    one = jnp.ones((1, WIDE), f32)
    for slot in range(slots):
        hidden, frame = mask_rows(counts_ref, slot)
        more = (rows_of(frame, WIDE), rows_of(hidden + [one, one, one], WIDE), rows_of([one, one, one], WIDE))
        for base in range(0, HEADS, FORWARD_BATCH):
            heads_forward(slot, base, projected_ref, bias_ref, mixed_scratch, query_ref, key_ref, value_ref, *more)
        mixed_ref[slot] = mixed_scratch[...].astype(bf16)
        for near, away in ((key_ref, key_far), (value_ref, value_far), (query_ref, query_far), (mixed_ref, mixed_far)):
            copies.start(near.at[slot], away.at[slot])
    copies.wait_all()


def run_forward(core, counts, tokens, own, other):
    slots = tokens.shape[0]
    scalars = pl.BlockSpec(memory_space=pltpu.SMEM)
    arrays = pl.BlockSpec(memory_space=pltpu.VMEM)
    away = pl.BlockSpec(memory_space=pl.ANY)
    return pl.pallas_call(
        attention_forward,
        in_specs=[scalars, scalars, away, arrays, arrays],
        out_specs=[away] * 5 + [arrays],
        out_shape=[pltpu.HBM((slots, rows, WIDE), bf16) for rows in (WIDTH, 512, 512, 512)]
        + [pltpu.HBM((WIDTH, 3 * WIDTH), bf16), shape_of((8, WIDTH), f32)],
        scratch_shapes=[
            pltpu.VMEM((slots * WIDE, WIDTH), bf16),
            pltpu.VMEM((3 * WIDTH, slots * WIDE), f32),
            pltpu.VMEM((WIDTH, WIDE), f32),
            pltpu.VMEM((WIDTH, 3 * WIDTH + 128), bf16),
            pltpu.VMEM((2 * WIDTH, 128), f32),
            pltpu.VMEM((slots, SPAN, WIDTH), bf16),
        ]
        + [pltpu.VMEM((slots, rows, WIDE), bf16) for rows in (WIDTH, 512, 512, 512)]
        + [pltpu.VMEM((WIDTH, 3 * WIDTH), bf16), pltpu.SemaphoreType.DMA((10,))],
        compiler_params=params(36),
        cost_estimate=cost(13),
        name="attention_forward",
    )(core, counts, *far(tokens), *held(own, other))


def feed_forward(core_ref, tokens_far, mixed_far, cotangent_far, own_ref, other_ref,
                 output_ref, grad_resid_far, grad_mixed_far, mine_ref, theirs_ref,
                 arrived_ref, out_w_ref, up_w_ref, down_w_ref, up_b_ref, grad_branch_ref, resid_ref, packed_ref, grad_down_ref,
                 tokens_ref, mixed_ref, cotangent_ref, grad_resid_ref, grad_mixed_ref, semaphores):
    slots = tokens_ref.shape[0]
    copies = Copies(semaphores)
    for away, near in ((mixed_far, mixed_ref), (tokens_far, tokens_ref), (cotangent_far, cotangent_ref)):
        copies.start(away, near)
    chunk = HIDDEN // 2
    core = core_ref[0]
    for side, ref in ((core, own_ref), (1 - core, other_ref)):
        blocks = jnp.swapaxes(ref[...], 0, 1)
        for r in range(3):
            at = pl.multiple_of(side * 192 + 64 * r, 64)
            for j in range(15):
                arrived_ref[pl.ds(at, 64), 128 * j : 128 * j + 128] = blocks[3 * r + j] if j < 3 else blocks[6 + 12 * r + j]
            arrived_ref[pl.ds(at, 64), 1920:2048] = blocks[81 + r]
        for r in range(12):
            at = pl.multiple_of(side * 768 + 64 * r, 64)
            for j in range(3):
                down_w_ref[pl.ds(at, 64), 128 * j : 128 * j + 128] = blocks[45 + 3 * r + j]
        turned = blocks[81].astype(f32).T
        up_b = jnp.concatenate([turned[4 + r : 5 + r] for r in range(12)], 1)
        up_b_ref[:, pl.ds(pl.multiple_of(side * 768, 128), 768)] = up_b
    order = arrival_order()
    ordered = dot(order, arrived_ref[:, :1920], (1, 0)).astype(bf16)
    out_w_ref[...] = ordered[:, :WIDTH]
    up_w_ref[...] = ordered[:, WIDTH:]
    rows = dot(arrived_ref[:, 1920:], order, (0, 1))[0:8]
    out_b, gain, offset, down_b = (rows[k : k + 1] for k in range(4))

    grad_branch_ref[...] = jnp.zeros_like(grad_branch_ref)
    resid_ref[...] = jnp.zeros_like(resid_ref)
    copies.wait_all()
    for slot in range(slots):
        at = slice(slot * ROWS, slot * ROWS + SPAN)
        grad_branch_ref[at, :] = cotangent_ref[slot]
        resid_ref[at, :] = tokens_ref[slot].astype(f32) + dot(mixed_ref[slot, :, :ROWS], out_w_ref[...], (0, 0))[:SPAN] + out_b
    resid = resid_ref[...]
    normed, inverse = norm_parts(resid)
    second = (normed * gain + offset).astype(bf16)
    grad_branch = grad_branch_ref[...]
    result = resid + down_b
    grad_second = jnp.zeros_like(resid)
    grad_ups, up_lines = [], []
    root = math.sqrt(2.0 / math.pi)
    for at in range(0, HIDDEN, chunk):
        cols = slice(at, at + chunk)
        up = dot(second, up_w_ref[:, cols], (1, 0)) + up_b_ref[:, cols]
        grad_activated = dot(grad_branch, down_w_ref[cols, :], (1, 1))
        square = up * up
        tanh = jnp.tanh(up * (root + (root * 0.044715) * square))
        half = 0.5 + 0.5 * tanh
        activated = (up * half).astype(bf16)
        slope = half + (up * (2.0 * half * (1.0 - half))) * (root + (3 * root * 0.044715) * square)
        grad_up = (grad_activated * slope).astype(bf16)
        result += dot(activated, down_w_ref[cols, :], (1, 0))
        grad_down_ref[cols, :] = dot(activated, grad_branch, (0, 0)).astype(bf16)
        grad_ups.append(dot(second, grad_up, (0, 0)).astype(bf16))
        up_lines.append(jnp.sum(grad_up.astype(f32), axis=0, keepdims=True))
        grad_second += dot(grad_up, up_w_ref[:, cols], (1, 1))
    scaled = grad_second * gain
    mean_one = jnp.mean(scaled, axis=-1, keepdims=True)
    mean_two = jnp.mean(scaled * normed, axis=-1, keepdims=True)
    grad_full = grad_branch.astype(f32)
    grad_resid = grad_full + inverse * (scaled - mean_one - normed * mean_two)
    grad_resid_ref[...] = grad_resid
    copies.start(grad_resid_ref, grad_resid_far)
    attended = grad_resid.astype(bf16)
    grad_out = jnp.zeros((WIDTH, WIDTH), f32)
    for slot in range(slots):
        part = attended[slot * ROWS : slot * ROWS + ROWS]
        output_ref[slot] = result[slot * ROWS : slot * ROWS + SPAN].astype(bf16)
        grad_out += dot(mixed_ref[slot, :, :ROWS], part, (1, 0))
        grad_mixed_ref[slot, :, 512:WIDE] = jnp.zeros((WIDTH, WIDE - 512), bf16)
        grad_mixed_ref[slot, :, :ROWS] = dot(out_w_ref[...], part, (1, 1)).astype(bf16)
    copies.start(grad_mixed_ref, grad_mixed_far)
    sums = [attended.astype(f32), grad_second * normed, grad_second, grad_full]
    vectors = jnp.concatenate([jnp.sum(values, axis=0, keepdims=True) for values in sums], 0)

    gathered = jnp.concatenate([grad_out.astype(bf16)] + grad_ups, 1)
    packed_ref[:, :1920] = dot(order, gathered, (0, 0)).astype(bf16)
    high, low = two_parts(vectors)
    rows = jnp.concatenate([high, low, jnp.zeros((120, WIDTH), f32)], 0).astype(bf16)
    packed_ref[:, 1920:] = dot(order, rows, (0, 1)).astype(bf16)
    up_b_ref[...] = jnp.concatenate(up_lines, 1)
    blank = jnp.zeros((CHIPS, 128), bf16)
    for side, ref in ((core, mine_ref), (1 - core, theirs_ref)):
        blocks = [blank] * REST_ROWS
        for r in range(3):
            at = pl.multiple_of(side * 192 + 64 * r, 64)
            for j in range(15):
                blocks[3 * r + j if j < 3 else 6 + 12 * r + j] = packed_ref[pl.ds(at, 64), 128 * j : 128 * j + 128]
            blocks[81 + r] = packed_ref[pl.ds(at, 64), 1920:2048]
        for r in range(12):
            at = pl.multiple_of(side * 768 + 64 * r, 64)
            for j in range(3):
                blocks[45 + 3 * r + j] = grad_down_ref[pl.ds(at, 64), 128 * j : 128 * j + 128]
        high, low = two_parts(up_b_ref[:, pl.ds(pl.multiple_of(side * 768, 128), 768)])
        rows = [part[:, 64 * r : 64 * r + 64] for part in (high, low) for r in range(12)]
        blocks[84] = rows_of(rows, 64, 128).T.astype(bf16)
        ref[...] = jnp.swapaxes(jnp.stack(blocks), 0, 1)
    copies.wait_all()


def run_feed_forward(core, tokens, mixed, cotangent, own, other):
    slots = tokens.shape[0]
    arrays = pl.BlockSpec(memory_space=pltpu.VMEM)
    away = pl.BlockSpec(memory_space=pl.ANY)
    return pl.pallas_call(
        feed_forward,
        in_specs=[pl.BlockSpec(memory_space=pltpu.SMEM), away, away, away, arrays, arrays],
        out_specs=[arrays, away, away, arrays, arrays],
        out_shape=[
            pltpu.VMEM((slots, SPAN, WIDTH), bf16),
            pltpu.HBM((slots * ROWS, WIDTH), f32),
            pltpu.HBM((slots, WIDTH, WIDE), bf16),
            pltpu.VMEM((CHIPS, REST_ROWS, 128), bf16),
            pltpu.VMEM((CHIPS, REST_ROWS, 128), bf16),
        ],
        scratch_shapes=[
            pltpu.VMEM((WIDTH, 2048), bf16),
            pltpu.VMEM((WIDTH, WIDTH), bf16),
            pltpu.VMEM((WIDTH, HIDDEN), bf16),
            pltpu.VMEM((HIDDEN, WIDTH), bf16),
            pltpu.VMEM((1, HIDDEN), f32),
            pltpu.VMEM((slots * ROWS, WIDTH), bf16),
            pltpu.VMEM((slots * ROWS, WIDTH), f32),
            pltpu.VMEM((WIDTH, 2048), bf16),
            pltpu.VMEM((HIDDEN, WIDTH), bf16),
            pltpu.VMEM((slots, SPAN, WIDTH), bf16),
            pltpu.VMEM((slots, WIDTH, WIDE), bf16),
            pltpu.VMEM((slots, SPAN, WIDTH), bf16),
            pltpu.VMEM((slots * ROWS, WIDTH), f32),
            pltpu.VMEM((slots, WIDTH, WIDE), bf16),
            pltpu.SemaphoreType.DMA((5,)),
        ],
        compiler_params=params(44),
        cost_estimate=cost(20),
        name="feed_forward",
    )(core, *far(tokens, mixed, cotangent), *held(own, other))


def heads_backward(slot, base, query_ref, key_ref, value_ref, mixed_ref, grad_mixed_ref, turned_ref):
    heads = range(base, base + BACKWARD_BATCH)
    queries = [query_ref[slot, 32 * h : 32 * h + 32, :] for h in heads]
    keys = [key_ref[slot, 32 * h : 32 * h + 32, :] for h in heads]
    values = [value_ref[slot, 32 * h : 32 * h + 32, :] for h in heads]
    grads = []
    for h in heads:
        both = slice(48 * (h // 2), 48 * (h // 2) + 48)
        part = slice(HEAD * (h % 2), HEAD * (h % 2) + HEAD)
        grad = grad_mixed_ref[slot, both, :].astype(f32)[part]
        mixed = mixed_ref[slot, both, :].astype(f32)[part]
        shift = jnp.sum(grad * mixed, axis=0, keepdims=True)
        grads.append(jnp.concatenate([grad, rows_of(three_parts(-shift), WIDE)], 0).astype(bf16))
    scores = [[dot(query[:, a:b], key[:, :count], (0, 0)) for a, b, count in BACKWARD_BLOCKS] for query, key in zip(queries, keys)]
    slopes = [[dot(grad[:, a:b], value[:, :count], (0, 0)) for a, b, count in BACKWARD_BLOCKS] for grad, value in zip(grads, values)]
    probs = [[jnp.exp2(part) for part in parts] for parts in scores]
    grad_scores = [[(part * slope).astype(bf16) for part, slope in zip(*pair)] for pair in zip(probs, slopes)]
    probs = [[part.astype(bf16) for part in parts] for parts in probs]
    over = lambda left, parts: [dot(left[:, a:b], part, (1, 0)) for part, (a, b, _) in zip(parts, BACKWARD_BLOCKS)]
    grad_v = [over(grad, parts) for grad, parts in zip(grads, probs)]
    grad_k = [over(query, parts) for query, parts in zip(queries, grad_scores)]
    grad_q = [
        [dot(key[:, :count], part, (1, 1)) for part, (_, _, count) in zip(parts, BACKWARD_BLOCKS)]
        for key, parts in zip(keys, grad_scores)
    ]
    fill = lambda part: part if part.shape[1] == WIDE else jnp.concatenate([part, jnp.zeros((32, WIDE - part.shape[1]), f32)], 1)
    lanes = slice(slot * WIDE, slot * WIDE + WIDE)
    for k, h in enumerate(heads):
        at = h * HEAD
        turned_ref[at : at + HEAD, lanes] = fill(jnp.concatenate(grad_q[k], 1))[:HEAD] * (1.0 / math.sqrt(HEAD))
        turned_ref[at + WIDTH : at + WIDTH + HEAD, lanes] = sum(fill(part) for part in grad_k[k])[:HEAD] * math.log(2.0)
        turned_ref[at + 2 * WIDTH : at + 2 * WIDTH + HEAD, lanes] = sum(fill(part) for part in grad_v[k])[:HEAD]


def attention_backward(core_ref, tokens_far, query_far, key_far, value_far, mixed_far, grad_mixed_far, grad_resid_far, weight_far, row_ref,
                       input_grad_ref, mine_ref, theirs_ref,
                       first_ref, turned_ref, bias_ref, packed_ref,
                       tokens_ref, query_ref, key_ref, value_ref, mixed_ref, grad_mixed_ref, grad_resid_ref, weight_ref, semaphores):
    slots = tokens_ref.shape[0]
    copies = Copies(semaphores)
    slot_pairs = [(query_far, query_ref), (key_far, key_ref), (value_far, value_ref), (grad_mixed_far, grad_mixed_ref), (mixed_far, mixed_ref)]
    by_slot = [[copies.start(away.at[0], near.at[0]) for away, near in slot_pairs]]
    tokens_copy = copies.start(tokens_far, tokens_ref)
    weight_copy = copies.start(weight_far, weight_ref)
    resid_copy = copies.start(grad_resid_far, grad_resid_ref)
    for slot in range(1, slots):
        by_slot.append([copies.start(away.at[slot], near.at[slot]) for away, near in slot_pairs])
    core = core_ref[0]
    gain, offset = row_ref[0:1], row_ref[1:2]
    first_ref[...] = jnp.zeros_like(first_ref)
    sums = jnp.zeros((3 * WIDTH, 1), f32)
    vectors = jnp.zeros((2, WIDTH), f32)
    for slot in range(slots):
        copies.wait(*by_slot[slot])
        for base in range(0, HEADS, BACKWARD_BATCH):
            heads_backward(slot, base, query_ref, key_ref, value_ref, mixed_ref, grad_mixed_ref, turned_ref)
        copies.wait(tokens_copy, weight_copy, resid_copy)
        normed, inverse = norm_parts(tokens_ref[slot].astype(f32))
        first_ref[slot * WIDE : slot * WIDE + SPAN, :] = (normed * gain + offset).astype(bf16)
        turned = turned_ref[:, slot * WIDE : slot * WIDE + WIDE]
        sums += jnp.sum(turned, axis=1, keepdims=True)
        grad_first = dot(turned.astype(bf16), weight_ref[...], (0, 1))[:SPAN]
        scaled = grad_first * gain
        mean_one = jnp.mean(scaled, axis=-1, keepdims=True)
        mean_two = jnp.mean(scaled * normed, axis=-1, keepdims=True)
        resid = grad_resid_ref[slot * ROWS : slot * ROWS + SPAN, :]
        input_grad_ref[slot] = resid + inverse * (scaled - mean_one - normed * mean_two)
        more = [jnp.sum(grad_first * normed, axis=0, keepdims=True), jnp.sum(grad_first, axis=0, keepdims=True)]
        vectors += jnp.concatenate(more, 0)
    order = arrival_order()
    grad_weight = dot(first_ref[...], turned_ref[...].astype(bf16), (0, 1)).astype(bf16)
    packed_ref[:, : 3 * WIDTH] = dot(order, grad_weight, (0, 0)).astype(bf16)
    blank = jnp.zeros((2, WIDTH), f32)
    high, low = two_parts(vectors)
    rows = jnp.concatenate([high, blank, low, jnp.zeros((122, WIDTH), f32)], 0).astype(bf16)
    more = dot(order, rows, (0, 1))
    bias_ref[0:WIDTH] = jnp.broadcast_to(sums[:WIDTH], (WIDTH, 128))
    bias_ref[WIDTH:] = jnp.broadcast_to(sums[2 * WIDTH :], (WIDTH, 128))
    lane = lax.broadcasted_iota(jnp.int32, (WIDTH, 128), 1)
    columns = jnp.zeros((WIDTH, 128), f32)
    for s in range(2):
        high, low = two_parts(bias_ref[pl.ds(s, WIDTH, stride=2), :])
        columns = jnp.where(lane == 2 + s, high, jnp.where(lane == 6 + s, low, columns))
    more += dot(order, columns.astype(bf16), (0, 0))
    packed_ref[:, 3 * WIDTH :] = more.astype(bf16)
    blank = jnp.zeros((CHIPS, 128), bf16)
    for side, ref in ((core, mine_ref), (1 - core, theirs_ref)):
        blocks = []
        for r in range(3):
            at = pl.multiple_of(side * 192 + 64 * r, 64)
            for j in range(10):
                blocks.append(packed_ref[pl.ds(at, 64), 128 * j : 128 * j + 128])
        ref[...] = jnp.swapaxes(jnp.stack(blocks + [blank, blank]), 0, 1)


def run_backward(core, tokens, query, key, value, mixed, grad_mixed, grad_resid, weight, row):
    slots = tokens.shape[0]
    arrays = pl.BlockSpec(memory_space=pltpu.VMEM)
    away = pl.BlockSpec(memory_space=pl.ANY)
    message = pltpu.VMEM((CHIPS, FIRST_ROWS, 128), bf16)
    return pl.pallas_call(
        attention_backward,
        in_specs=[pl.BlockSpec(memory_space=pltpu.SMEM)] + [away] * 8 + [arrays],
        out_shape=[pltpu.VMEM((slots, SPAN, WIDTH), f32), message, message],
        scratch_shapes=[
            pltpu.VMEM((slots * WIDE, WIDTH), bf16),
            pltpu.VMEM((3 * WIDTH, slots * WIDE), f32),
            pltpu.VMEM((2 * WIDTH, 128), f32),
            pltpu.VMEM((WIDTH, 3 * WIDTH + 128), bf16),
            pltpu.VMEM((slots, SPAN, WIDTH), bf16),
        ]
        + [pltpu.VMEM((slots, rows, WIDE), bf16) for rows in (512, 512, 512, WIDTH, WIDTH)]
        + [pltpu.VMEM((slots * ROWS, WIDTH), f32), pltpu.VMEM((WIDTH, 3 * WIDTH), bf16), pltpu.SemaphoreType.DMA((13,))],
        compiler_params=params(36),
        cost_estimate=cost(30),
        name="attention_backward",
    )(core, *far(tokens, query, key, value, mixed, grad_mixed, grad_resid, weight), row)


def to_chips(message):
    return lax.all_to_all(message, CHIP_AXES, 0, 0, tiled=True)


def across(message):
    return lax.ppermute(message, CORE_AXIS, [(0, 1), (1, 0)])


def add_halves(mine, theirs):
    return (mine.astype(f32) + theirs.astype(f32)).astype(bf16)


def shards(tokens, item_frames, ln1_gain, ln1_bias, qkv_weight, qv_bias, out_weight, out_bias, ln2_gain, ln2_bias,
           up_weight, up_bias, down_weight, down_bias, cotangent):
    together = lax.optimization_barrier
    core = lax.axis_index(CORE_AXIS).astype(jnp.int32).reshape(1)
    first = run_pack_first(qkv_weight, ln1_gain, ln1_bias, qv_bias)
    first, up_weight = together((first, up_weight))
    first = to_chips(first)
    up_sent = up_weight.reshape(3, 16, 2, 4, 12).transpose(0, 2, 4, 1, 3).reshape(3, HIDDEN)
    second, tokens, cotangent = run_pack_second(
        out_weight, up_sent, down_weight, out_bias, ln2_gain, ln2_bias, down_bias, up_bias, tokens.transpose(1, 0, 2), cotangent.transpose(1, 0, 2))
    first, second = together((first, second))
    first_other = across(first)
    second = to_chips(second)
    mixed, query, key, value, weight, row = run_forward(core, item_frames, tokens, first, first_other)
    second, mixed = together((second, mixed))
    output, grad_resid, grad_mixed, mine, theirs = run_feed_forward(core, tokens, mixed, cotangent, second, across(second))
    theirs = across(theirs)
    output = run_swap(output)
    output, mine = together((output, mine))
    output = output.transpose(1, 0, 2)
    rest = add_halves(mine, theirs)
    rest, grad_mixed = together((rest, grad_mixed))
    rest = to_chips(rest)
    input_grad, mine, theirs = run_backward(core, tokens, query, key, value, mixed, grad_mixed, grad_resid, weight, row)
    theirs = across(theirs)
    mine, rest = together((mine, rest))
    grad_out, grad_up, *others = run_unpack_rest(rest)
    grad_out, mine = together((grad_out, mine))
    own = to_chips(add_halves(mine, theirs))
    grad_up = grad_up.reshape(3, 2, 12, 16, 4).transpose(0, 3, 1, 4, 2).reshape(3, HIDDEN)
    grad_down, grad_out_b, grad_gain_two, grad_offset_two, grad_down_b, grad_up_b = others
    grad_qkv, grad_gain, grad_offset, grad_qv = run_unpack_first(own)
    return (output, input_grad, grad_gain, grad_offset, grad_qkv, grad_qv, grad_out, grad_out_b, grad_gain_two, grad_offset_two,
            grad_up, grad_up_b, grad_down, grad_down_b)


def solution(mesh):
    split = Mesh(mesh.devices.reshape(4, 4, 2, mesh.shape["narrow"]), ALL)
    by_rank = lambda n: P(ALL, *([None] * (n - 1)))
    return jax.shard_map(
        shards,
        mesh=split,
        in_specs=tuple(by_rank(n) for n in (3, 2, 1, 1, 2, 1, 2, 1, 1, 1, 2, 1, 2, 1, 3)),
        out_specs=tuple(by_rank(n) for n in (3, 3, 1, 1, 2, 1, 2, 1, 1, 1, 2, 1, 2, 1)),
        check_vma=False,
    )
```

```python
import math

import jax
import jax.numpy as jnp
from jax import lax
from jax.experimental import pallas as pl
from jax.experimental.pallas import tpu as pltpu
from jax.sharding import Mesh
from jax.sharding import PartitionSpec as P

HEADS = 16
HEAD = 24
FRAME = 196
WIDTH = 384
HIDDEN = 1536
WIDE = 640
SPAN = 588
ROWS = 592
CHIPS = 64
FIRST_ROWS = 32
REST_ROWS = 88
EPSILON = 1e-05
NEGATIVE = -1e30
bf16 = jnp.bfloat16
f32 = jnp.float32
FORWARD_BLOCKS = ((0, 128, 208), (128, 384, 400), (384, 640, 592))
FORWARD_BATCH = 8
LOAD_BATCH = 8
KEPT_SLOTS = 2
BACKWARD_BATCH = 8
BACKWARD_BLOCKS = ((0, 0, 256), (128, 256, 512), (384, 512, 640))
ALL = ("wide_0", "wide_1", "wide_2", "narrow")
CHIP_AXES = ("wide_0", "wide_1", "narrow")
COLUMN_AXES = ("wide_0", "wide_1")
LINE_AXIS = "narrow"
LINE = 4
CORE_AXIS = "wide_2"


def dot(left, right, over):
    return lax.dot_general(left, right, (((over[0],), (over[1],)), ((), ())), preferred_element_type=f32)


def norm_parts(values):
    centred = values - jnp.mean(values, axis=-1, keepdims=True)
    inverse = lax.rsqrt(jnp.mean(centred * centred, axis=-1, keepdims=True) + EPSILON)
    return centred * inverse, inverse


def two_parts(values):
    high = values.astype(bf16).astype(f32)
    return high, values - high


def three_parts(values):
    high, rest = two_parts(values)
    middle, low = two_parts(rest)
    return high, middle, low


def rows_of(rows, width, count=8):
    index = lax.broadcasted_iota(jnp.int32, (count, width), 0)
    out = jnp.zeros((count, width), f32)
    for k, row in enumerate(rows):
        out = jnp.where(index == k, row, out)
    return out


def arrival_order():
    place = lax.broadcasted_iota(jnp.int32, (WIDTH, WIDTH), 1)
    feature = lax.broadcasted_iota(jnp.int32, (WIDTH, WIDTH), 0)
    core = (place >= WIDTH // 2).astype(jnp.int32)
    rest = place - core * (WIDTH // 2)
    row = rest >> 6
    chip = rest & 63
    return (feature == 3 * (8 * (chip >> 2) + 4 * core + (chip & 3)) + row).astype(f32).astype(bf16)


def mask_rows(counts_ref, slot):
    lane = lax.broadcasted_iota(jnp.int32, (1, WIDE), 1)
    first_end = counts_ref[slot, 0]
    second_end = first_end + counts_ref[slot, 1]
    third_end = second_end + counts_ref[slot, 2]
    group = [
        (f >= first_end).astype(jnp.int32) + (f >= second_end).astype(jnp.int32) + (f >= third_end).astype(jnp.int32)
        for f in range(3)
    ]
    hidden = []
    for f in range(3):
        row = jnp.full((1, WIDE), NEGATIVE, f32)
        for k in range(f + 1):
            seen = jnp.where(group[f] == group[k], 0.0, NEGATIVE).astype(f32)
            row = jnp.where((lane >= FRAME * k) & (lane < FRAME * (k + 1)), seen, row)
        hidden.append(row)
    frame = [((lane >= FRAME * f) & (lane < FRAME * (f + 1))).astype(f32) for f in range(3)]
    return hidden, frame


def params(mebibytes):
    return pltpu.CompilerParams(vmem_limit_bytes=mebibytes * 2**20)


def cost(microseconds):
    return pl.CostEstimate(flops=int(microseconds * 1.1e9), bytes_accessed=2**20, transcendentals=0)


def shape_of(shape, dtype):
    return jax.ShapeDtypeStruct(shape, dtype)


def held(*arrays):
    return [pltpu.with_memory_space_constraint(a, pltpu.VMEM) for a in arrays]


def far(*arrays):
    return [pltpu.with_memory_space_constraint(a, pltpu.HBM) for a in arrays]


class Copies:
    def __init__(self, semaphores):
        self.semaphores, self.count, self.open = semaphores, 0, []

    def start(self, source, target):
        copy = pltpu.make_async_copy(source, target, self.semaphores.at[self.count])
        self.count += 1
        copy.start()
        self.open.append(copy)
        return copy

    def wait(self, *copies):
        for copy in copies:
            if any(copy is other for other in self.open):
                self.open = [other for other in self.open if other is not copy]
                copy.wait()

    def wait_all(self):
        self.wait(*self.open)


def pack_first(qkv_ref, gain_ref, offset_ref, qv_ref, out_ref, rows_ref):
    rows_ref[...] = jnp.zeros_like(rows_ref)
    weight = qkv_ref[...].astype(f32)
    line = lambda ref, count: ref[...].astype(f32).reshape(1, count)
    gain, offset, qv = line(gain_ref, 3), line(offset_ref, 3), line(qv_ref, 6)
    for r in range(3):
        for j in range(9):
            rows_ref[10 * r + j : 10 * r + j + 1, :] = weight[r : r + 1, 128 * j : 128 * j + 128]
        rows_ref[10 * r + 9 : 10 * r + 10, 0:1] = gain[:, r : r + 1]
        rows_ref[10 * r + 9 : 10 * r + 10, 1:2] = offset[:, r : r + 1]
        rows_ref[10 * r + 9 : 10 * r + 10, 2:4] = qv[:, 2 * r : 2 * r + 2]
    out_ref[...] = jnp.broadcast_to(rows_ref[...].astype(bf16)[None], out_ref.shape)


def pack_second(out_w_ref, up_ref, down_ref, out_b_ref, gain_ref, offset_ref, down_b_ref, up_b_ref, out_ref, rows_ref):
    rows_ref[...] = jnp.zeros_like(rows_ref)
    out_w = out_w_ref[...].astype(f32)
    up = up_ref[...].astype(f32)
    down = down_ref[...].astype(f32)
    line = lambda ref, count: ref[...].astype(f32).reshape(1, count)
    vectors = [line(ref, 3) for ref in (out_b_ref, gain_ref, offset_ref, down_b_ref)]
    for r in range(3):
        for j in range(3):
            rows_ref[3 * r + j : 3 * r + j + 1, :] = out_w[r : r + 1, 128 * j : 128 * j + 128]
        for j in range(12):
            rows_ref[9 + 12 * r + j : 10 + 12 * r + j, :] = up[r : r + 1, 128 * j : 128 * j + 128]
        for k, vector in enumerate(vectors):
            rows_ref[81 + r : 82 + r, k : k + 1] = vector[:, r : r + 1]
    for r in range(12):
        for j in range(3):
            rows_ref[45 + 3 * r + j : 46 + 3 * r + j, :] = down[r : r + 1, 128 * j : 128 * j + 128]
    rows_ref[81:82, 4:16] = line(up_b_ref, 12)
    out_ref[...] = jnp.broadcast_to(rows_ref[...].astype(bf16)[None], out_ref.shape)


def merge_slots(raw_ref, merged_ref):
    both = jnp.swapaxes(raw_ref[...], 0, 1)
    for slot in range(both.shape[0]):
        at = slot * ROWS
        merged_ref[at + ROWS - 16 : at + ROWS, :] = jnp.zeros((16, WIDTH), bf16)
        merged_ref[at : at + SPAN, :] = both[slot]


def run_pack_first(*args):
    return pl.pallas_call(
        pack_first,
        out_shape=pltpu.HBM((CHIPS, FIRST_ROWS, 128), bf16),
        scratch_shapes=[pltpu.VMEM((FIRST_ROWS, 128), f32)],
        compiler_params=params(8),
        cost_estimate=cost(2),
        name="pack_first",
    )(*far(*args))


def run_pack_second(*args):
    return pl.pallas_call(
        pack_second,
        out_shape=pltpu.HBM((CHIPS, REST_ROWS, 128), bf16),
        scratch_shapes=[pltpu.VMEM((REST_ROWS, 128), f32)],
        compiler_params=params(8),
        cost_estimate=cost(2),
        name="pack_second",
    )(*far(*args))


def total(arrived_ref):
    return jnp.sum(arrived_ref[...].astype(f32), axis=0)


def spread_lanes(rows, lane, width):
    index = lax.broadcasted_iota(jnp.int32, (1, width), 1)
    out = jnp.zeros((1, width), f32)
    for k, row in enumerate(rows):
        out = jnp.where(index == k, row[:, lane : lane + 1], out)
    return out.reshape(width)


def unpack_first(arrived_ref, qkv_ref, gain_ref, offset_ref, qv_ref):
    sums = total(arrived_ref)
    more = []
    for r in range(3):
        for j in range(9):
            qkv_ref[r : r + 1, 128 * j : 128 * j + 128] = sums[10 * r + j : 10 * r + j + 1, :]
        row = sums[10 * r + 9 : 10 * r + 10, :]
        more.append(row[:, 0:4] + row[:, 4:8])
    gain_ref[...] = spread_lanes(more, 0, 3)
    offset_ref[...] = spread_lanes(more, 1, 3)
    index = lax.broadcasted_iota(jnp.int32, (1, 6), 1)
    out = jnp.zeros((1, 6), f32)
    for k in range(6):
        out = jnp.where(index == k, more[k // 2][:, 2 + k % 2 : 3 + k % 2], out)
    qv_ref[...] = out.reshape(6)


def run_unpack_first(arrived):
    return pl.pallas_call(
        unpack_first,
        out_shape=[shape_of((3, 3 * WIDTH), f32), shape_of((3,), f32), shape_of((3,), f32), shape_of((6,), f32)],
        compiler_params=params(8),
        cost_estimate=cost(2),
        name="unpack_first",
    )(arrived)


def sum_column(line_ref, arrived_ref, keep_ref, one_ref, two_ref, three_ref, sums_ref):
    sums_ref[...] = total(arrived_ref)
    block = lambda shift: sums_ref[pl.ds(pl.multiple_of(lax.rem(line_ref[0] + shift, LINE) * REST_ROWS, 8), REST_ROWS), :]
    keep_ref[...] = block(0)
    for shift, ref in enumerate((one_ref, two_ref, three_ref)):
        ref[...] = block(shift + 1).astype(bf16)


def run_sum_column(line, arrived):
    arrays = pl.BlockSpec(memory_space=pltpu.VMEM)
    part = shape_of((REST_ROWS, 128), bf16)
    return pl.pallas_call(
        sum_column,
        in_specs=[pl.BlockSpec(memory_space=pltpu.SMEM), arrays],
        out_shape=[shape_of((REST_ROWS, 128), f32), part, part, part],
        scratch_shapes=[pltpu.VMEM((LINE * REST_ROWS, 128), f32)],
        compiler_params=params(12),
        cost_estimate=cost(2),
        name="sum_column",
    )(line, arrived)


def unpack_rest(keep_ref, one_ref, two_ref, three_ref, out_ref, up_ref, down_ref, out_b_ref, gain_ref, offset_ref, down_b_ref, up_b_ref):
    sums = keep_ref[...] + sum(ref[...].astype(f32) for ref in (one_ref, two_ref, three_ref))
    more = []
    for r in range(3):
        for j in range(3):
            out_ref[r : r + 1, 128 * j : 128 * j + 128] = sums[3 * r + j : 3 * r + j + 1, :]
        for j in range(12):
            up_ref[r : r + 1, 128 * j : 128 * j + 128] = sums[9 + 12 * r + j : 10 + 12 * r + j, :]
        row = sums[81 + r : 82 + r, :]
        more.append(row[:, 0:4] + row[:, 4:8])
    for r in range(12):
        for j in range(3):
            down_ref[r : r + 1, 128 * j : 128 * j + 128] = sums[45 + 3 * r + j : 46 + 3 * r + j, :]
    for k, ref in enumerate((out_b_ref, gain_ref, offset_ref, down_b_ref)):
        ref[...] = spread_lanes(more, k, 3)
    up_b_ref[...] = (sums[84:85, 0:12] + sums[84:85, 12:24]).reshape(12)


def run_unpack_rest(*parts):
    return pl.pallas_call(
        unpack_rest,
        out_shape=[shape_of((3, WIDTH), f32), shape_of((3, HIDDEN), f32), shape_of((12, WIDTH), f32)]
        + [shape_of((3,), f32)] * 4
        + [shape_of((12,), f32)],
        compiler_params=params(12),
        cost_estimate=cost(2),
        name="unpack_rest",
    )(*parts)


def add_halves(mine_ref, theirs_ref, out_ref):
    out_ref[...] = (mine_ref[...].astype(f32) + theirs_ref[...].astype(f32)).astype(bf16)


def run_add_halves(mine, theirs):
    arrays = pl.BlockSpec(memory_space=pltpu.VMEM)
    return pl.pallas_call(
        add_halves,
        in_specs=[arrays, arrays],
        out_shape=pltpu.HBM(mine.shape, bf16),
        compiler_params=params(12),
        cost_estimate=cost(1),
        name="add_halves",
    )(*held(mine, theirs))


def forward_scores(unit, projected_ref, bias_ref, key_ref, value_ref, more):
    slot, base = unit
    scale = math.log2(math.e) / math.sqrt(HEAD)
    lanes = slice(slot * WIDE, slot * WIDE + WIDE)
    query_more, key_more, value_more = more[slot]
    wide = lambda start: jnp.concatenate([bias_ref[start : start + HEAD, :]] * (WIDE // 128), 1)
    queries, scores = [], []
    for h in range(base, base + FORWARD_BATCH):
        at = h * HEAD
        query = (projected_ref[at : at + HEAD, lanes] + wide(at)) * scale
        key = projected_ref[at + WIDTH : at + WIDTH + HEAD, lanes]
        value = projected_ref[at + 2 * WIDTH : at + 2 * WIDTH + HEAD, lanes] + wide(at + WIDTH)
        query = jnp.concatenate([query, query_more], 0)
        key = jnp.concatenate([key, key_more], 0).astype(bf16)
        key_ref[slot, 32 * h : 32 * h + 32, :] = key
        value_ref[slot, 32 * h : 32 * h + 32, :] = jnp.concatenate([value, value_more], 0).astype(bf16)
        low = query.astype(bf16)
        queries.append(query)
        scores.append([dot(key[:, :count], low[:, a:b], (0, 0)) for a, b, count in FORWARD_BLOCKS])
    return queries, scores


def forward_mixed(unit, queries, scores, mixed_scratch, query_ref, value_ref):
    slot, base = unit
    heads = range(base, base + FORWARD_BATCH)
    peaks = [[jnp.max(part, axis=0, keepdims=True) for part in parts] for parts in scores]
    weights = [[jnp.exp2(part - top).astype(bf16) for part, top in zip(*pair)] for pair in zip(scores, peaks)]
    values = [value_ref[slot, 32 * h : 32 * h + 32, :] for h in heads]
    got = [
        [dot(value[:, :count], part, (1, 0)) for part, (_, _, count) in zip(parts, FORWARD_BLOCKS)]
        for value, parts in zip(values, weights)
    ]
    zero = jnp.zeros((1, WIDE), f32)
    for h, query, tops, parts in zip(heads, queries, peaks, got):
        both = jnp.concatenate(parts, 1)
        row_total = both[HEAD : HEAD + 1]
        mixed_scratch[h * HEAD : h * HEAD + HEAD, :] = both[:HEAD] * (1.0 / row_total)
        logs = jnp.concatenate(tops, 1) + jnp.log2(row_total)
        log_rows = rows_of([zero, zero, zero, *three_parts(-logs)], WIDE)
        query_ref[slot, 32 * h : 32 * h + 32, :] = (query + jnp.concatenate([jnp.zeros((HEAD, WIDE), f32), log_rows], 0)).astype(bf16)


def forward_probs(unit, query_ref, key_ref, refs):
    slot, base = unit
    for h in range(base, base + FORWARD_BATCH):
        query, key = query_ref[slot, 32 * h : 32 * h + 32, :], key_ref[slot, 32 * h : 32 * h + 32, :]
        for ref, (start, a, b) in zip(refs, BACKWARD_BLOCKS):
            ref[h] = jnp.exp2(dot(query[:, start:ROWS], key[:, a:b], (0, 0))).astype(bf16)


def attention_forward(core_ref, counts_ref, tokens_far, own_ref, other_ref,
                      mixed_far, query_far, key_far, value_far, weight_far, first_far, merged_far, low_far, middle_far, high_far, column_ref,
                      first_ref, projected_ref, mixed_scratch, arrived_ref, bias_ref,
                      raw_ref, tokens_ref, mixed_ref, query_ref, key_ref, value_ref, weight_ref, low_ref, middle_ref, high_ref, semaphores):
    slots = mixed_ref.shape[0]
    copies = Copies(semaphores)
    copies.start(tokens_far, raw_ref)
    core = core_ref[0]
    for side, ref in ((core, own_ref), (1 - core, other_ref)):
        blocks = jnp.swapaxes(ref[...], 0, 1)
        for r in range(3):
            at = pl.multiple_of(side * 192 + 64 * r, 64)
            for j in range(10):
                arrived_ref[pl.ds(at, 64), 128 * j : 128 * j + 128] = blocks[10 * r + j]
    order = arrival_order()
    ordered = dot(order, arrived_ref[...], (1, 0))
    weight_ref[...] = ordered[:, : 3 * WIDTH].astype(bf16)
    column_ref[...] = ordered[:, 3 * WIDTH :]
    rows = dot(arrived_ref[:, 3 * WIDTH :], order, (0, 1))
    gain, offset = rows[0:1], rows[1:2]
    for s in range(2):
        column = ordered[:, 3 * WIDTH + 2 + s : 3 * WIDTH + 3 + s]
        bias_ref[pl.ds(s, WIDTH, stride=2), :] = jnp.broadcast_to(column, (WIDTH, 128))
    first_ref[...] = jnp.zeros_like(first_ref)
    copies.wait_all()
    merge_slots(raw_ref, tokens_ref)
    copies.start(tokens_ref, merged_far)
    copies.start(weight_ref, weight_far)
    for slot in range(slots):
        normed, _ = norm_parts(tokens_ref[slot * ROWS : slot * ROWS + ROWS, :].astype(f32))
        first_ref[slot * WIDE : slot * WIDE + ROWS, :] = (normed * gain + offset).astype(bf16)
    copies.start(first_ref, first_far)
    projected_ref[...] = dot(weight_ref[...], first_ref[...], (0, 1))
    one = jnp.ones((1, WIDE), f32)
    more = []
    for slot in range(slots):
        hidden, frame = mask_rows(counts_ref, slot)
        more.append((rows_of(frame, WIDE), rows_of(hidden + [one, one, one], WIDE), rows_of([one, one, one], WIDE)))
    units = [(slot, base) for slot in range(slots) for base in range(0, HEADS, FORWARD_BATCH)]
    refs = (low_ref, middle_ref, high_ref)
    kept = {}

    def probs(unit):
        slot, base = unit
        if slot >= KEPT_SLOTS:
            return
        copies.wait(*kept.get((slot - 1, base // LOAD_BATCH), ()))
        forward_probs(unit, query_ref, key_ref, refs)
        if (base + FORWARD_BATCH) % LOAD_BATCH == 0:
            part = pl.ds(base // LOAD_BATCH * LOAD_BATCH, LOAD_BATCH)
            pairs = zip(refs, (low_far, middle_far, high_far))
            kept[slot, base // LOAD_BATCH] = [copies.start(near.at[part], away.at[slot, part]) for near, away in pairs]

    ready = forward_scores(units[0], projected_ref, bias_ref, key_ref, value_ref, more)
    for k, unit in enumerate(units):
        slot = unit[0]
        now, ready = ready, None
        if k + 1 < len(units):
            ready = forward_scores(units[k + 1], projected_ref, bias_ref, key_ref, value_ref, more)
        forward_mixed(unit, *now, mixed_scratch, query_ref, value_ref)
        if unit[1] + FORWARD_BATCH == HEADS:
            mixed_ref[slot] = mixed_scratch[...].astype(bf16)
            for near, away in ((key_ref, key_far), (value_ref, value_far), (query_ref, query_far), (mixed_ref, mixed_far)):
                copies.start(near.at[slot], away.at[slot])
        if k >= 1:
            probs(units[k - 1])
    probs(units[-1])
    copies.wait_all()


def probs_shapes():
    return [(ROWS - start, b - a) for start, a, b in BACKWARD_BLOCKS]


def run_forward(core, counts, tokens, own, other):
    slots = tokens.shape[1]
    scalars = pl.BlockSpec(memory_space=pltpu.SMEM)
    arrays = pl.BlockSpec(memory_space=pltpu.VMEM)
    away = pl.BlockSpec(memory_space=pl.ANY)
    return pl.pallas_call(
        attention_forward,
        in_specs=[scalars, scalars, away, arrays, arrays],
        out_specs=[away] * 10 + [arrays],
        out_shape=[pltpu.HBM((slots, rows, WIDE), bf16) for rows in (WIDTH, 512, 512, 512)]
        + [pltpu.HBM((WIDTH, 3 * WIDTH), bf16), pltpu.HBM((slots * WIDE, WIDTH), bf16), pltpu.HBM((slots * ROWS, WIDTH), bf16)]
        + [pltpu.HBM((KEPT_SLOTS, HEADS, *shape), bf16) for shape in probs_shapes()]
        + [pltpu.HBM((WIDTH, 128), f32)],
        scratch_shapes=[
            pltpu.VMEM((slots * WIDE, WIDTH), bf16),
            pltpu.VMEM((3 * WIDTH, slots * WIDE), f32),
            pltpu.VMEM((WIDTH, WIDE), f32),
            pltpu.VMEM((WIDTH, 3 * WIDTH + 128), bf16),
            pltpu.VMEM((2 * WIDTH, 128), f32),
            pltpu.VMEM((SPAN, slots, WIDTH), bf16),
            pltpu.VMEM((slots * ROWS, WIDTH), bf16),
        ]
        + [pltpu.VMEM((slots, rows, WIDE), bf16) for rows in (WIDTH, 512, 512, 512)]
        + [pltpu.VMEM((WIDTH, 3 * WIDTH), bf16)]
        + [pltpu.VMEM((HEADS, *shape), bf16) for shape in probs_shapes()]
        + [pltpu.SemaphoreType.DMA((40,))],
        compiler_params=params(48),
        cost_estimate=cost(20),
        name="attention_forward",
    )(core, counts, *far(tokens), *held(own, other))


def feed_forward(core_ref, tokens_far, mixed_far, cotangent_far, own_ref, other_ref,
                 activated_ref, resid_ref, down_w_ref, row_ref, grad_resid_far, grad_mixed_far, mine_ref, theirs_ref,
                 arrived_ref, out_w_ref, up_w_ref, up_b_ref, packed_ref, grad_down_ref,
                 tokens_ref, mixed_ref, raw_ref, cotangent_ref, grad_resid_ref, grad_mixed_ref, second_ref, grad_up_ref, semaphores):
    slots = mixed_ref.shape[0]
    copies = Copies(semaphores)
    for away, near in ((mixed_far, mixed_ref), (tokens_far, tokens_ref), (cotangent_far, raw_ref)):
        copies.start(away, near)
    chunk = HIDDEN // 2
    core = core_ref[0]
    for side, ref in ((core, own_ref), (1 - core, other_ref)):
        blocks = jnp.swapaxes(ref[...], 0, 1)
        for r in range(3):
            at = pl.multiple_of(side * 192 + 64 * r, 64)
            for j in range(15):
                arrived_ref[pl.ds(at, 64), 128 * j : 128 * j + 128] = blocks[3 * r + j] if j < 3 else blocks[6 + 12 * r + j]
            arrived_ref[pl.ds(at, 64), 1920:2048] = blocks[81 + r]
        for r in range(12):
            at = pl.multiple_of(side * 768 + 64 * r, 64)
            for j in range(3):
                down_w_ref[pl.ds(at, 64), 128 * j : 128 * j + 128] = blocks[45 + 3 * r + j]
        turned = blocks[81].astype(f32).T
        up_b = jnp.concatenate([turned[4 + r : 5 + r] for r in range(12)], 1)
        up_b_ref[:, pl.ds(pl.multiple_of(side * 768, 128), 768)] = up_b
    order = arrival_order()
    ordered = dot(order, arrived_ref[:, :1920], (1, 0)).astype(bf16)
    out_w_ref[...] = ordered[:, :WIDTH]
    up_w_ref[...] = ordered[:, WIDTH:]
    row_ref[...] = dot(arrived_ref[:, 1920:], order, (0, 1))[0:8]
    copies.wait_all()
    merge_slots(raw_ref, cotangent_ref)
    grad_branch = cotangent_ref[...]
    out_b, gain, offset = (row_ref[k : k + 1] for k in range(3))
    for slot in range(slots):
        at = slice(slot * ROWS, slot * ROWS + ROWS)
        resid_ref[at, :] = tokens_ref[at, :].astype(f32) + dot(mixed_ref[slot, :, :ROWS], out_w_ref[...], (0, 0)) + out_b
    resid = resid_ref[...]
    normed, inverse = norm_parts(resid)
    second = (normed * gain + offset).astype(bf16)
    root = math.sqrt(2.0 / math.pi)
    parts = [slice(at, at + chunk) for at in range(0, HIDDEN, chunk)]
    blocks = [(slice(r, r + 592), slice(c, c + 256)) for c in range(0, HIDDEN, 256) for r in range(0, slots * ROWS, 592)]
    second_ref[...] = second

    def products(block):
        rows, cols = block
        return dot(second_ref[rows, :], up_w_ref[:, cols], (1, 0)), dot(cotangent_ref[rows, :], down_w_ref[cols, :], (1, 1))

    up_b_sum = []
    lines = dict()

    def activate(block, up, grad_activated):
        rows, cols = block
        up = up + up_b_ref[:, cols]
        square = up * up
        tanh = jnp.tanh(up * (root + (root * 0.044715) * square))
        half = 0.5 + 0.5 * tanh
        activated_ref[rows, cols] = (up * half).astype(bf16)
        slope = half + (up * (2.0 * half * (1.0 - half))) * (root + (3 * root * 0.044715) * square)
        grad_up = grad_activated * slope
        grad_up_ref[rows, cols] = grad_up.astype(bf16)
        line = jnp.sum(grad_up, axis=0, keepdims=True)
        lines[cols.start] = lines[cols.start] + line if cols.start in lines else line

    ready = products(blocks[0])
    for k, block in enumerate(blocks):
        now = ready
        if True and k + 1 < len(blocks):
            ready = products(blocks[k + 1])
        activate(block, *now)
        if not True and k + 1 < len(blocks):
            ready = products(blocks[k + 1])
    lines = [lines[c] for c in sorted(lines)]
    grad_ups = [grad_up_ref[:, cols] for cols in parts]
    grad_second = sum(dot(grad_up, up_w_ref[:, cols], (1, 1)) for cols, grad_up in zip(parts, grad_ups))
    for cols in parts:
        grad_down_ref[cols, :] = dot(activated_ref[:, cols], grad_branch, (0, 0)).astype(bf16)
    grad_up_weights = [dot(second, grad_up, (0, 0)).astype(bf16) for grad_up in grad_ups]
    scaled = grad_second * gain
    mean_one = jnp.mean(scaled, axis=-1, keepdims=True)
    mean_two = jnp.mean(scaled * normed, axis=-1, keepdims=True)
    grad_full = grad_branch.astype(f32)
    grad_resid = grad_full + inverse * (scaled - mean_one - normed * mean_two)
    grad_resid_ref[...] = grad_resid
    copies.start(grad_resid_ref, grad_resid_far)
    attended = grad_resid.astype(bf16)
    grad_out = jnp.zeros((WIDTH, WIDTH), f32)
    for slot in range(slots):
        part = attended[slot * ROWS : slot * ROWS + ROWS]
        grad_out += dot(mixed_ref[slot, :, :ROWS], part, (1, 0))
        grad_mixed_ref[slot, :, 512:WIDE] = jnp.zeros((WIDTH, WIDE - 512), bf16)
        grad_mixed_ref[slot, :, :ROWS] = dot(out_w_ref[...], part, (1, 1)).astype(bf16)
    copies.start(grad_mixed_ref, grad_mixed_far)
    sums = [attended.astype(f32), grad_second * normed, grad_second, grad_full]
    vectors = jnp.concatenate([jnp.sum(values, axis=0, keepdims=True) for values in sums], 0)

    gathered = jnp.concatenate([grad_out.astype(bf16)] + grad_up_weights, 1)
    packed_ref[:, :1920] = dot(order, gathered, (0, 0)).astype(bf16)
    high, low = two_parts(vectors)
    rows = jnp.concatenate([high, low, jnp.zeros((120, WIDTH), f32)], 0).astype(bf16)
    packed_ref[:, 1920:] = dot(order, rows, (0, 1)).astype(bf16)
    up_b_ref[...] = jnp.concatenate(lines, 1)
    blank = jnp.zeros((CHIPS, 128), bf16)
    for side, ref in ((core, mine_ref), (1 - core, theirs_ref)):
        blocks = [blank] * REST_ROWS
        for r in range(3):
            at = pl.multiple_of(side * 192 + 64 * r, 64)
            for j in range(15):
                blocks[3 * r + j if j < 3 else 6 + 12 * r + j] = packed_ref[pl.ds(at, 64), 128 * j : 128 * j + 128]
            blocks[81 + r] = packed_ref[pl.ds(at, 64), 1920:2048]
        for r in range(12):
            at = pl.multiple_of(side * 768 + 64 * r, 64)
            for j in range(3):
                blocks[45 + 3 * r + j] = grad_down_ref[pl.ds(at, 64), 128 * j : 128 * j + 128]
        high, low = two_parts(up_b_ref[:, pl.ds(pl.multiple_of(side * 768, 128), 768)])
        rows = [part[:, 64 * r : 64 * r + 64] for part in (high, low) for r in range(12)]
        blocks[84] = rows_of(rows, 64, 128).T.astype(bf16)
        ref[...] = jnp.swapaxes(jnp.stack(blocks), 0, 1)
    copies.wait_all()


def run_feed_forward(core, tokens, mixed, cotangent, own, other):
    slots = tokens.shape[0] // ROWS
    arrays = pl.BlockSpec(memory_space=pltpu.VMEM)
    away = pl.BlockSpec(memory_space=pl.ANY)
    return pl.pallas_call(
        feed_forward,
        in_specs=[pl.BlockSpec(memory_space=pltpu.SMEM), away, away, away, arrays, arrays],
        out_specs=[arrays, arrays, arrays, arrays, away, away, arrays, arrays],
        out_shape=[
            pltpu.VMEM((slots * ROWS, HIDDEN), bf16),
            pltpu.VMEM((slots * ROWS, WIDTH), f32),
            pltpu.VMEM((HIDDEN, WIDTH), bf16),
            pltpu.VMEM((8, WIDTH), f32),
            pltpu.HBM((slots * ROWS, WIDTH), f32),
            pltpu.HBM((slots, WIDTH, WIDE), bf16),
            pltpu.VMEM((CHIPS, REST_ROWS, 128), bf16),
            pltpu.VMEM((CHIPS, REST_ROWS, 128), bf16),
        ],
        scratch_shapes=[
            pltpu.VMEM((WIDTH, 2048), bf16),
            pltpu.VMEM((WIDTH, WIDTH), bf16),
            pltpu.VMEM((WIDTH, HIDDEN), bf16),
            pltpu.VMEM((1, HIDDEN), f32),
            pltpu.VMEM((WIDTH, 2048), bf16),
            pltpu.VMEM((HIDDEN, WIDTH), bf16),
            pltpu.VMEM((slots * ROWS, WIDTH), bf16),
            pltpu.VMEM((slots, WIDTH, WIDE), bf16),
            pltpu.VMEM((SPAN, slots, WIDTH), bf16),
            pltpu.VMEM((slots * ROWS, WIDTH), bf16),
            pltpu.VMEM((slots * ROWS, WIDTH), f32),
            pltpu.VMEM((slots, WIDTH, WIDE), bf16),
            pltpu.VMEM((slots * ROWS, WIDTH), bf16),
            pltpu.VMEM((slots * ROWS, HIDDEN), bf16),
            pltpu.SemaphoreType.DMA((5,)),
        ],
        compiler_params=params(46),
        cost_estimate=cost(20),
        name="feed_forward",
    )(core, *far(tokens, mixed, cotangent), *held(own, other))


def feed_forward_output(activated_ref, resid_ref, down_w_ref, row_ref, out_ref):
    slots = out_ref.shape[1]
    result = resid_ref[...] + dot(activated_ref[...], down_w_ref[...], (1, 0)) + row_ref[3:4]
    both = jnp.stack([result[slot * ROWS : slot * ROWS + SPAN] for slot in range(slots)])
    out_ref[...] = jnp.swapaxes(both, 0, 1).astype(bf16)


def run_feed_forward_output(*args):
    slots = args[1].shape[0] // ROWS
    return pl.pallas_call(
        feed_forward_output,
        out_shape=pltpu.HBM((SPAN, slots, WIDTH), bf16),
        compiler_params=params(20),
        cost_estimate=cost(3),
        name="feed_forward_output",
    )(*held(*args))


def backward_slopes(unit, copies, loads, value_ref, mixed_ref, grad_mixed_ref):
    slot, base = unit
    copies.wait(*loads["grad"][slot])
    grads, slopes = [], []
    for h in range(base, base + BACKWARD_BATCH):
        both = slice(48 * (h // 2), 48 * (h // 2) + 48)
        part = slice(HEAD * (h % 2), HEAD * (h % 2) + HEAD)
        grad = grad_mixed_ref[slot, both, :].astype(f32)[part]
        mixed = mixed_ref[slot, both, :].astype(f32)[part]
        shift = jnp.sum(grad * mixed, axis=0, keepdims=True)
        grad = jnp.concatenate([grad, rows_of(three_parts(-shift), WIDE)], 0).astype(bf16)
        value = value_ref[slot, 32 * h : 32 * h + 32, :]
        grads.append(grad)
        slopes.append([dot(grad[:, start:ROWS], value[:, a:b], (0, 0)) for start, a, b in BACKWARD_BLOCKS])
    return grads, slopes


def backward_products(unit, grads, slopes, copies, loads, query_ref, key_ref, probs_refs, turned_ref):
    slot, base = unit
    heads = range(base, base + BACKWARD_BATCH)
    copies.wait(*loads["query"][slot])
    queries = [query_ref[slot, 32 * h : 32 * h + 32, :] for h in heads]
    keys = [key_ref[slot, 32 * h : 32 * h + 32, :] for h in heads]
    if slot < KEPT_SLOTS:
        copies.wait(*loads["probs"][slot][base // LOAD_BATCH])
        probs = [[ref[slot, h].astype(f32) for ref in probs_refs] for h in heads]
    else:
        probs = [
            [jnp.exp2(dot(query[:, start:ROWS], key[:, a:b], (0, 0))) for start, a, b in BACKWARD_BLOCKS]
            for query, key in zip(queries, keys)
        ]
    grad_scores = [[(part * slope).astype(bf16) for part, slope in zip(*pair)] for pair in zip(probs, slopes)]
    probs = [[part.astype(bf16) for part in parts] for parts in probs]
    over = lambda left, parts: jnp.concatenate(
        [dot(left[:, start:ROWS], part, (1, 0)) for part, (start, _, _) in zip(parts, BACKWARD_BLOCKS)], 1)
    grad_v = [over(grad, parts) for grad, parts in zip(grads, probs)]
    grad_k = [over(query, parts) for query, parts in zip(queries, grad_scores)]
    grad_q = [
        [dot(key[:, a:b], part, (1, 1)) for part, (_, a, b) in zip(parts, BACKWARD_BLOCKS)]
        for key, parts in zip(keys, grad_scores)
    ]
    fill = lambda part: jnp.concatenate([jnp.zeros((32, ROWS - part.shape[1]), f32), part], 1) if part.shape[1] < ROWS else part
    lanes = slice(slot * WIDE, slot * WIDE + WIDE)
    blank = jnp.zeros((HEAD, WIDE - ROWS), f32)
    for k, h in enumerate(heads):
        at = h * HEAD
        whole = sum(fill(part) for part in grad_q[k])[:HEAD] * (1.0 / math.sqrt(HEAD))
        turned_ref[at : at + HEAD, lanes] = jnp.concatenate([whole, blank], 1)
        turned_ref[at + WIDTH : at + WIDTH + HEAD, lanes] = grad_k[k][:HEAD] * math.log(2.0)
        turned_ref[at + 2 * WIDTH : at + 2 * WIDTH + HEAD, lanes] = grad_v[k][:HEAD]


def attention_backward(core_ref, query_far, key_far, value_far, mixed_far, grad_mixed_far, low_far, middle_far, high_far, first_far, weight_far,
                       column_ref, turned_far, mine_ref, theirs_ref,
                       turned_ref, bias_ref, packed_ref, turned_low_ref,
                       query_ref, key_ref, value_ref, mixed_ref, grad_mixed_ref, low_ref, middle_ref, high_ref, first_ref, weight_ref, semaphores):
    slots = mixed_ref.shape[0]
    copies = Copies(semaphores)
    loads = {"grad": [], "probs": [], "query": []}
    probs_refs = (low_ref, middle_ref, high_ref)
    for slot in range(slots):
        load = lambda pairs: [copies.start(away.at[slot], near.at[slot]) for away, near in pairs]
        loads["grad"].append(load(((value_far, value_ref), (grad_mixed_far, grad_mixed_ref), (mixed_far, mixed_ref))))
        loads["probs"].append([])
        if slot >= KEPT_SLOTS:
            loads["query"].append(load(((query_far, query_ref), (key_far, key_ref))))
            continue
        for base in range(0, HEADS, LOAD_BATCH):
            part = pl.ds(base, LOAD_BATCH)
            pairs = zip((low_far, middle_far, high_far), probs_refs)
            loads["probs"][slot].append([copies.start(away.at[slot, part], near.at[slot, part]) for away, near in pairs])
            if base == 0:
                loads["query"].append(load(((query_far, query_ref), (key_far, key_ref))))
    weights = [copies.start(first_far, first_ref), copies.start(weight_far, weight_ref)]
    core = core_ref[0]
    sums = jnp.zeros((3 * WIDTH, 1), f32)
    units = [(slot, base) for slot in range(slots) for base in range(0, HEADS, BACKWARD_BATCH)]
    ready = backward_slopes(units[0], copies, loads, value_ref, mixed_ref, grad_mixed_ref)
    for k, unit in enumerate(units):
        slot = unit[0]
        now, ready = ready, None
        if k + 1 < len(units):
            ready = backward_slopes(units[k + 1], copies, loads, value_ref, mixed_ref, grad_mixed_ref)
        backward_products(unit, *now, copies, loads, query_ref, key_ref, probs_refs, turned_ref)
        if unit[1] + BACKWARD_BATCH == HEADS:
            turned = turned_ref[:, slot * WIDE : slot * WIDE + WIDE]
            sums += jnp.sum(turned, axis=1, keepdims=True)
            turned_low_ref[slot] = turned.astype(bf16)
            copies.start(turned_low_ref.at[slot], turned_far.at[slot])
    copies.wait(*weights)
    order = arrival_order()
    turned = jnp.concatenate([turned_low_ref[slot] for slot in range(slots)], 1)
    grad_weight = dot(first_ref[...], turned, (0, 1))
    packed_ref[:, : 3 * WIDTH] = dot(order, grad_weight.astype(bf16), (0, 0)).astype(bf16)
    lane = lax.broadcasted_iota(jnp.int32, (3 * WIDTH, 128), 1)
    high, low = two_parts(sums)
    spread = jnp.where(lane == 0, high, jnp.where(lane == 1, low, 0.0)).astype(bf16)
    against = dot(weight_ref[...], spread, (1, 0))
    grad_offset = against[:, 0:1] + against[:, 1:2]
    along = jnp.sum(grad_weight * weight_ref[...].astype(f32), axis=1, keepdims=True)
    grad_gain = (along - column_ref[:, 1:2] * grad_offset) / column_ref[:, 0:1]
    bias_ref[0:WIDTH] = jnp.broadcast_to(sums[:WIDTH], (WIDTH, 128))
    bias_ref[WIDTH:] = jnp.broadcast_to(sums[2 * WIDTH :], (WIDTH, 128))
    lane = lax.broadcasted_iota(jnp.int32, (WIDTH, 128), 1)
    columns = jnp.zeros((WIDTH, 128), f32)
    for k, values in enumerate((grad_gain, grad_offset, bias_ref[pl.ds(0, WIDTH, stride=2), :], bias_ref[pl.ds(1, WIDTH, stride=2), :])):
        high, low = two_parts(values)
        columns = jnp.where(lane == k, high, jnp.where(lane == 4 + k, low, columns))
    packed_ref[:, 3 * WIDTH :] = dot(order, columns.astype(bf16), (0, 0)).astype(bf16)
    blank = jnp.zeros((CHIPS, 128), bf16)
    for side, ref in ((core, mine_ref), (1 - core, theirs_ref)):
        blocks = []
        for r in range(3):
            at = pl.multiple_of(side * 192 + 64 * r, 64)
            for j in range(10):
                blocks.append(packed_ref[pl.ds(at, 64), 128 * j : 128 * j + 128])
        ref[...] = jnp.swapaxes(jnp.stack(blocks + [blank, blank]), 0, 1)
    copies.wait_all()


def run_backward(core, query, key, value, mixed, grad_mixed, low, middle, high, first, weight, column):
    slots = mixed.shape[0]
    arrays = pl.BlockSpec(memory_space=pltpu.VMEM)
    away = pl.BlockSpec(memory_space=pl.ANY)
    return pl.pallas_call(
        attention_backward,
        in_specs=[pl.BlockSpec(memory_space=pltpu.SMEM)] + [away] * 10 + [arrays],
        out_specs=[away, arrays, arrays],
        out_shape=[
            pltpu.HBM((slots, 3 * WIDTH, WIDE), bf16),
            pltpu.VMEM((CHIPS, FIRST_ROWS, 128), bf16),
            pltpu.VMEM((CHIPS, FIRST_ROWS, 128), bf16),
        ],
        scratch_shapes=[
            pltpu.VMEM((3 * WIDTH, slots * WIDE), f32),
            pltpu.VMEM((2 * WIDTH, 128), f32),
            pltpu.VMEM((WIDTH, 3 * WIDTH + 128), bf16),
            pltpu.VMEM((slots, 3 * WIDTH, WIDE), bf16),
        ]
        + [pltpu.VMEM((slots, rows, WIDE), bf16) for rows in (512, 512, 512, WIDTH, WIDTH)]
        + [pltpu.VMEM((KEPT_SLOTS, HEADS, *shape), bf16) for shape in probs_shapes()]
        + [pltpu.VMEM((slots * WIDE, WIDTH), bf16), pltpu.VMEM((WIDTH, 3 * WIDTH), bf16), pltpu.SemaphoreType.DMA((70,))],
        compiler_params=params(56),
        cost_estimate=cost(22),
        name="attention_backward",
    )(core, *far(query, key, value, mixed, grad_mixed, low, middle, high, first, weight), column)


def input_backward(merged_far, turned_far, grad_resid_far, weight_far, column_ref, out_far,
                   tokens_ref, turned_ref, grad_resid_ref, weight_ref, grad_first_ref, out_ref, semaphores):
    slots = turned_ref.shape[0]
    copies = Copies(semaphores)
    first = [copies.start(weight_far, weight_ref), copies.start(turned_far.at[0], turned_ref.at[0])]
    turns = [copies.start(turned_far.at[slot], turned_ref.at[slot]) for slot in range(1, slots)]
    rest = [copies.start(merged_far, tokens_ref), copies.start(grad_resid_far, grad_resid_ref)]
    gain = column_ref[...].T[0:1]
    copies.wait(*first)
    for slot in range(slots):
        if slot:
            copies.wait(turns[slot - 1])
        grad_first_ref[slot * ROWS : slot * ROWS + ROWS, :] = dot(turned_ref[slot, :, :ROWS], weight_ref[...], (0, 1))
    copies.wait(*rest)
    half = ROWS // 2
    for low, high in ((0, half), (half, SPAN)):
        for slot in range(slots):
            at = slice(slot * ROWS + low, slot * ROWS + low + half)
            normed, inverse = norm_parts(tokens_ref[at, :].astype(f32))
            scaled = grad_first_ref[at, :] * gain
            mean_one = jnp.mean(scaled, axis=-1, keepdims=True)
            mean_two = jnp.mean(scaled * normed, axis=-1, keepdims=True)
            grad = grad_resid_ref[at, :] + inverse * (scaled - mean_one - normed * mean_two)
            out_ref[low:high, slot, :] = grad[: high - low]
        copies.start(out_ref.at[pl.ds(low, high - low)], out_far.at[pl.ds(low, high - low)])
    copies.wait_all()


def run_input_backward(merged, turned, grad_resid, weight, column):
    slots = turned.shape[0]
    arrays = pl.BlockSpec(memory_space=pltpu.VMEM)
    away = pl.BlockSpec(memory_space=pl.ANY)
    return pl.pallas_call(
        input_backward,
        in_specs=[away] * 4 + [arrays],
        out_specs=away,
        out_shape=pltpu.HBM((SPAN, slots, WIDTH), f32),
        scratch_shapes=[
            pltpu.VMEM((slots * ROWS, WIDTH), bf16),
            pltpu.VMEM((slots, 3 * WIDTH, WIDE), bf16),
            pltpu.VMEM((slots * ROWS, WIDTH), f32),
            pltpu.VMEM((WIDTH, 3 * WIDTH), bf16),
            pltpu.VMEM((slots * ROWS, WIDTH), f32),
            pltpu.VMEM((SPAN, slots, WIDTH), f32),
            pltpu.SemaphoreType.DMA((8,)),
        ],
        compiler_params=params(32),
        cost_estimate=cost(6),
        name="input_backward",
    )(*far(merged, turned, grad_resid, weight), column)


def to_chips(message):
    return lax.all_to_all(message, CHIP_AXES, 0, 0, tiled=True)


def to_column(message):
    return lax.all_to_all(message, COLUMN_AXES, 0, 0, tiled=True)


def along_line(message, shift):
    return lax.ppermute(message, LINE_AXIS, [(k, (k + shift) % LINE) for k in range(LINE)])


def across(message):
    return lax.ppermute(message, CORE_AXIS, [(0, 1), (1, 0)])


def shards(tokens, item_frames, ln1_gain, ln1_bias, qkv_weight, qv_bias, out_weight, out_bias, ln2_gain, ln2_bias,
           up_weight, up_bias, down_weight, down_bias, cotangent):
    together = lax.optimization_barrier
    core = lax.axis_index(CORE_AXIS).astype(jnp.int32).reshape(1)
    line = lax.axis_index(LINE_AXIS).astype(jnp.int32).reshape(1)
    first = run_pack_first(qkv_weight, ln1_gain, ln1_bias, qv_bias)
    first, up_weight = together((first, up_weight))
    first = to_chips(first)
    up_sent = up_weight.reshape(3, 16, 2, 4, 12).transpose(0, 2, 4, 1, 3).reshape(3, HIDDEN)
    second = run_pack_second(out_weight, up_sent, down_weight, out_bias, ln2_gain, ln2_bias, down_bias, up_bias)
    tokens, cotangent = tokens.transpose(1, 0, 2), cotangent.transpose(1, 0, 2)
    first, second = together((first, second))
    first_other = across(first)
    second = to_chips(second)
    mixed, query, key, value, weight, normed, merged, low, middle, high, column = run_forward(core, item_frames, tokens, first, first_other)
    second, mixed = together((second, mixed))
    activated, resid, down_w, row, grad_resid, grad_mixed, mine, theirs = run_feed_forward(
        core, merged, mixed, cotangent, second, across(second))
    theirs = across(theirs)
    output = run_feed_forward_output(activated, resid, down_w, row)
    output, mine = together((output, mine))
    output = output.transpose(1, 0, 2)
    rest = run_add_halves(mine, theirs)
    rest, grad_mixed = together((rest, grad_mixed))
    rest = to_column(rest.reshape(CHIPS // LINE, LINE * REST_ROWS, 128))
    turned, mine, theirs = run_backward(core, query, key, value, mixed, grad_mixed, low, middle, high, normed, weight, column)
    theirs = across(theirs)
    own = run_add_halves(mine, theirs)
    own, rest = together((own, rest))
    own, turned = together((own, turned))
    own = to_chips(own)
    keep, *sent = run_sum_column(line, rest)
    sent = [along_line(part, shift + 1) for shift, part in enumerate(sent)]
    grad_out, grad_up, *others = run_unpack_rest(keep, *sent)
    grad_up = grad_up.reshape(3, 2, 12, 16, 4).transpose(0, 3, 1, 4, 2).reshape(3, HIDDEN)
    grad_down, grad_out_b, grad_gain_two, grad_offset_two, grad_down_b, grad_up_b = others
    input_grad = run_input_backward(merged, turned, grad_resid, weight, column).transpose(1, 0, 2)
    grad_qkv, grad_gain, grad_offset, grad_qv = run_unpack_first(own)
    return (output, input_grad, grad_gain, grad_offset, grad_qkv, grad_qv, grad_out, grad_out_b, grad_gain_two, grad_offset_two,
            grad_up, grad_up_b, grad_down, grad_down_b)


def solution(mesh):
    split = Mesh(mesh.devices.reshape(4, 4, 2, mesh.shape["narrow"]), ALL)
    by_rank = lambda n: P(ALL, *([None] * (n - 1)))
    return jax.shard_map(
        shards,
        mesh=split,
        in_specs=tuple(by_rank(n) for n in (3, 2, 1, 1, 2, 1, 2, 1, 1, 1, 2, 1, 2, 1, 3)),
        out_specs=tuple(by_rank(n) for n in (3, 3, 1, 1, 2, 1, 2, 1, 1, 1, 2, 1, 2, 1)),
        check_vma=False,
    )
```

```python
import math

import jax
import jax.numpy as jnp
from jax import lax
from jax.experimental import pallas as pl
from jax.experimental.pallas import tpu as pltpu
from jax.sharding import Mesh
from jax.sharding import PartitionSpec as P

HEADS = 16
HEAD = 24
FRAME = 196
WIDTH = 384
HIDDEN = 1536
WIDE = 640
SPAN = 588
ROWS = 592
CHIPS = 64
FIRST_ROWS = 32
REST_ROWS = 88
EPSILON = 1e-05
NEGATIVE = -1e30
bf16 = jnp.bfloat16
f32 = jnp.float32
FORWARD_BLOCKS = ((0, 128, 208), (128, 384, 400), (384, 640, 592))
FORWARD_BATCH = 8
LOAD_BATCH = 8
KEPT_SLOTS = 2
BACKWARD_BATCH = 8
BACKWARD_BLOCKS = ((0, 0, 256), (128, 256, 512), (384, 512, 640))
ALL = ("wide_0", "wide_1", "wide_2", "narrow")
CHIP_AXES = ("wide_0", "wide_1", "narrow")
COLUMN_AXES = ("wide_0", "wide_1")
LINE_AXIS = "narrow"
LINE = 4
CORE_AXIS = "wide_2"


def dot(left, right, over):
    return lax.dot_general(left, right, (((over[0],), (over[1],)), ((), ())), preferred_element_type=f32)


def norm_parts(values):
    centred = values - jnp.mean(values, axis=-1, keepdims=True)
    inverse = lax.rsqrt(jnp.mean(centred * centred, axis=-1, keepdims=True) + EPSILON)
    return centred * inverse, inverse


def two_parts(values):
    high = values.astype(bf16).astype(f32)
    return high, values - high


def three_parts(values):
    high, rest = two_parts(values)
    middle, low = two_parts(rest)
    return high, middle, low


def rows_of(rows, width, count=8):
    index = lax.broadcasted_iota(jnp.int32, (count, width), 0)
    out = jnp.zeros((count, width), f32)
    for k, row in enumerate(rows):
        out = jnp.where(index == k, row, out)
    return out


def arrival_order():
    place = lax.broadcasted_iota(jnp.int32, (WIDTH, WIDTH), 1)
    feature = lax.broadcasted_iota(jnp.int32, (WIDTH, WIDTH), 0)
    core = (place >= WIDTH // 2).astype(jnp.int32)
    rest = place - core * (WIDTH // 2)
    row = rest >> 6
    chip = rest & 63
    return (feature == 3 * (8 * (chip >> 2) + 4 * core + (chip & 3)) + row).astype(f32).astype(bf16)


def mask_rows(counts_ref, slot):
    lane = lax.broadcasted_iota(jnp.int32, (1, WIDE), 1)
    first_end = counts_ref[slot, 0]
    second_end = first_end + counts_ref[slot, 1]
    third_end = second_end + counts_ref[slot, 2]
    group = [
        (f >= first_end).astype(jnp.int32) + (f >= second_end).astype(jnp.int32) + (f >= third_end).astype(jnp.int32)
        for f in range(3)
    ]
    hidden = []
    for f in range(3):
        row = jnp.full((1, WIDE), NEGATIVE, f32)
        for k in range(f + 1):
            seen = jnp.where(group[f] == group[k], 0.0, NEGATIVE).astype(f32)
            row = jnp.where((lane >= FRAME * k) & (lane < FRAME * (k + 1)), seen, row)
        hidden.append(row)
    frame = [((lane >= FRAME * f) & (lane < FRAME * (f + 1))).astype(f32) for f in range(3)]
    return hidden, frame


def params(mebibytes):
    return pltpu.CompilerParams(vmem_limit_bytes=mebibytes * 2**20)


def cost(microseconds):
    return pl.CostEstimate(flops=int(microseconds * 1.1e9), bytes_accessed=2**20, transcendentals=0)


def shape_of(shape, dtype):
    return jax.ShapeDtypeStruct(shape, dtype)


def held(*arrays):
    return [pltpu.with_memory_space_constraint(a, pltpu.VMEM) for a in arrays]


def far(*arrays):
    return [pltpu.with_memory_space_constraint(a, pltpu.HBM) for a in arrays]


class Copies:
    def __init__(self, semaphores):
        self.semaphores, self.count, self.open = semaphores, 0, []

    def start(self, source, target):
        copy = pltpu.make_async_copy(source, target, self.semaphores.at[self.count])
        self.count += 1
        copy.start()
        self.open.append(copy)
        return copy

    def wait(self, *copies):
        for copy in copies:
            if any(copy is other for other in self.open):
                self.open = [other for other in self.open if other is not copy]
                copy.wait()

    def wait_all(self):
        self.wait(*self.open)


def pack_first(qkv_ref, gain_ref, offset_ref, qv_ref, out_ref, rows_ref):
    rows_ref[...] = jnp.zeros_like(rows_ref)
    weight = qkv_ref[...].astype(f32)
    line = lambda ref, count: ref[...].astype(f32).reshape(1, count)
    gain, offset, qv = line(gain_ref, 3), line(offset_ref, 3), line(qv_ref, 6)
    for r in range(3):
        for j in range(9):
            rows_ref[10 * r + j : 10 * r + j + 1, :] = weight[r : r + 1, 128 * j : 128 * j + 128]
        rows_ref[10 * r + 9 : 10 * r + 10, 0:1] = gain[:, r : r + 1]
        rows_ref[10 * r + 9 : 10 * r + 10, 1:2] = offset[:, r : r + 1]
        rows_ref[10 * r + 9 : 10 * r + 10, 2:4] = qv[:, 2 * r : 2 * r + 2]
    out_ref[...] = jnp.broadcast_to(rows_ref[...].astype(bf16)[None], out_ref.shape)


def pack_second(out_w_ref, up_ref, down_ref, out_b_ref, gain_ref, offset_ref, down_b_ref, up_b_ref, out_ref, rows_ref):
    rows_ref[...] = jnp.zeros_like(rows_ref)
    out_w = out_w_ref[...].astype(f32)
    up = up_ref[...].astype(f32)
    down = down_ref[...].astype(f32)
    line = lambda ref, count: ref[...].astype(f32).reshape(1, count)
    vectors = [line(ref, 3) for ref in (out_b_ref, gain_ref, offset_ref, down_b_ref)]
    for r in range(3):
        for j in range(3):
            rows_ref[3 * r + j : 3 * r + j + 1, :] = out_w[r : r + 1, 128 * j : 128 * j + 128]
        for j in range(12):
            rows_ref[9 + 12 * r + j : 10 + 12 * r + j, :] = up[r : r + 1, 128 * j : 128 * j + 128]
        for k, vector in enumerate(vectors):
            rows_ref[81 + r : 82 + r, k : k + 1] = vector[:, r : r + 1]
    for r in range(12):
        for j in range(3):
            rows_ref[45 + 3 * r + j : 46 + 3 * r + j, :] = down[r : r + 1, 128 * j : 128 * j + 128]
    rows_ref[81:82, 4:16] = line(up_b_ref, 12)
    out_ref[...] = jnp.broadcast_to(rows_ref[...].astype(bf16)[None], out_ref.shape)


def merge_slots(raw_ref, merged_ref):
    both = jnp.swapaxes(raw_ref[...], 0, 1)
    for slot in range(both.shape[0]):
        at = slot * ROWS
        merged_ref[at + ROWS - 16 : at + ROWS, :] = jnp.zeros((16, WIDTH), bf16)
        merged_ref[at : at + SPAN, :] = both[slot]


def run_pack_first(*args):
    return pl.pallas_call(
        pack_first,
        out_shape=pltpu.HBM((CHIPS, FIRST_ROWS, 128), bf16),
        scratch_shapes=[pltpu.VMEM((FIRST_ROWS, 128), f32)],
        compiler_params=params(8),
        cost_estimate=cost(2),
        name="pack_first",
    )(*far(*args))


def run_pack_second(*args):
    return pl.pallas_call(
        pack_second,
        out_shape=pltpu.HBM((CHIPS, REST_ROWS, 128), bf16),
        scratch_shapes=[pltpu.VMEM((REST_ROWS, 128), f32)],
        compiler_params=params(8),
        cost_estimate=cost(2),
        name="pack_second",
    )(*far(*args))


def total(arrived_ref):
    return jnp.sum(arrived_ref[...].astype(f32), axis=0)


def spread_lanes(rows, lane, width):
    index = lax.broadcasted_iota(jnp.int32, (1, width), 1)
    out = jnp.zeros((1, width), f32)
    for k, row in enumerate(rows):
        out = jnp.where(index == k, row[:, lane : lane + 1], out)
    return out.reshape(width)


def unpack_first(arrived_ref, qkv_ref, gain_ref, offset_ref, qv_ref):
    sums = total(arrived_ref)
    more = []
    for r in range(3):
        for j in range(9):
            qkv_ref[r : r + 1, 128 * j : 128 * j + 128] = sums[10 * r + j : 10 * r + j + 1, :]
        row = sums[10 * r + 9 : 10 * r + 10, :]
        more.append(row[:, 0:4] + row[:, 4:8])
    gain_ref[...] = spread_lanes(more, 0, 3)
    offset_ref[...] = spread_lanes(more, 1, 3)
    index = lax.broadcasted_iota(jnp.int32, (1, 6), 1)
    out = jnp.zeros((1, 6), f32)
    for k in range(6):
        out = jnp.where(index == k, more[k // 2][:, 2 + k % 2 : 3 + k % 2], out)
    qv_ref[...] = out.reshape(6)


def run_unpack_first(arrived):
    return pl.pallas_call(
        unpack_first,
        out_shape=[shape_of((3, 3 * WIDTH), f32), shape_of((3,), f32), shape_of((3,), f32), shape_of((6,), f32)],
        compiler_params=params(8),
        cost_estimate=cost(2),
        name="unpack_first",
    )(arrived)


def sum_column(line_ref, arrived_ref, keep_ref, one_ref, two_ref, three_ref, sums_ref):
    sums_ref[...] = total(arrived_ref)
    block = lambda shift: sums_ref[pl.ds(pl.multiple_of(lax.rem(line_ref[0] + shift, LINE) * REST_ROWS, 8), REST_ROWS), :]
    keep_ref[...] = block(0)
    for shift, ref in enumerate((one_ref, two_ref, three_ref)):
        ref[...] = block(shift + 1).astype(bf16)


def run_sum_column(line, arrived):
    arrays = pl.BlockSpec(memory_space=pltpu.VMEM)
    part = shape_of((REST_ROWS, 128), bf16)
    return pl.pallas_call(
        sum_column,
        in_specs=[pl.BlockSpec(memory_space=pltpu.SMEM), arrays],
        out_shape=[shape_of((REST_ROWS, 128), f32), part, part, part],
        scratch_shapes=[pltpu.VMEM((LINE * REST_ROWS, 128), f32)],
        compiler_params=params(12),
        cost_estimate=cost(2),
        name="sum_column",
    )(line, arrived)


def unpack_rest(keep_ref, one_ref, two_ref, three_ref, out_ref, up_ref, down_ref, out_b_ref, gain_ref, offset_ref, down_b_ref, up_b_ref, pairs_ref, turned_ref):
    sums = keep_ref[...] + sum(ref[...].astype(f32) for ref in (one_ref, two_ref, three_ref))
    more = []
    for r in range(3):
        for j in range(3):
            out_ref[r : r + 1, 128 * j : 128 * j + 128] = sums[3 * r + j : 3 * r + j + 1, :]
        line = sums[9 + 12 * r : 21 + 12 * r, :]
        pairs_ref[pl.ds(24 * r, 12, stride=2), 0:64] = line[:, 0:64]
        pairs_ref[pl.ds(24 * r + 1, 12, stride=2), 0:64] = line[:, 64:128]
        row = sums[81 + r : 82 + r, :]
        more.append(row[:, 0:4] + row[:, 4:8])
    turned_ref[...] = pairs_ref[...].T
    by_line = [turned_ref[pl.ds(y, 16, stride=4), :] for y in range(LINE)]
    for r in range(3):
        pieces = [by_line[y][:, 24 * r + 12 * c : 24 * r + 12 * c + 12] for c in range(2) for y in range(LINE)]
        lines = jnp.concatenate(pieces, 1)
        for column in range(16):
            up_ref[r : r + 1, 96 * column : 96 * column + 96] = lines[column : column + 1]
    for r in range(12):
        for j in range(3):
            down_ref[r : r + 1, 128 * j : 128 * j + 128] = sums[45 + 3 * r + j : 46 + 3 * r + j, :]
    for k, ref in enumerate((out_b_ref, gain_ref, offset_ref, down_b_ref)):
        ref[...] = spread_lanes(more, k, 3)
    up_b_ref[...] = (sums[84:85, 0:12] + sums[84:85, 12:24]).reshape(12)


def run_unpack_rest(*parts):
    return pl.pallas_call(
        unpack_rest,
        out_shape=[shape_of((3, WIDTH), f32), shape_of((3, HIDDEN), f32), shape_of((12, WIDTH), f32)]
        + [shape_of((3,), f32)] * 4
        + [shape_of((12,), f32)],
        scratch_shapes=[pltpu.VMEM((128, 128), f32), pltpu.VMEM((128, 128), f32)],
        compiler_params=params(12),
        cost_estimate=cost(2),
        name="unpack_rest",
    )(*parts)


def add_halves(mine_ref, theirs_ref, out_ref):
    out_ref[...] = (mine_ref[...].astype(f32) + theirs_ref[...].astype(f32)).astype(bf16)


def run_add_halves(mine, theirs):
    arrays = pl.BlockSpec(memory_space=pltpu.VMEM)
    return pl.pallas_call(
        add_halves,
        in_specs=[arrays, arrays],
        out_shape=pltpu.HBM(mine.shape, bf16),
        compiler_params=params(12),
        cost_estimate=cost(1),
        name="add_halves",
    )(*held(mine, theirs))


def forward_scores(unit, projected_ref, bias_ref, key_ref, value_ref, more):
    slot, base = unit
    scale = math.log2(math.e) / math.sqrt(HEAD)
    lanes = slice(slot * WIDE, slot * WIDE + WIDE)
    query_more, key_more, value_more = more[slot]
    wide = lambda start: jnp.concatenate([bias_ref[start : start + HEAD, :]] * (WIDE // 128), 1)
    queries, scores = [], []
    for h in range(base, base + FORWARD_BATCH):
        at = h * HEAD
        query = (projected_ref[at : at + HEAD, lanes] + wide(at)) * scale
        key = projected_ref[at + WIDTH : at + WIDTH + HEAD, lanes]
        value = projected_ref[at + 2 * WIDTH : at + 2 * WIDTH + HEAD, lanes] + wide(at + WIDTH)
        query = jnp.concatenate([query, query_more], 0)
        key = jnp.concatenate([key, key_more], 0).astype(bf16)
        key_ref[slot, 32 * h : 32 * h + 32, :] = key
        value_ref[slot, 32 * h : 32 * h + 32, :] = jnp.concatenate([value, value_more], 0).astype(bf16)
        low = query.astype(bf16)
        queries.append(query)
        scores.append([dot(key[:, :count], low[:, a:b], (0, 0)) for a, b, count in FORWARD_BLOCKS])
    return queries, scores


def forward_mixed(unit, queries, scores, mixed_scratch, query_ref, value_ref):
    slot, base = unit
    heads = range(base, base + FORWARD_BATCH)
    peaks = [[jnp.max(part, axis=0, keepdims=True) for part in parts] for parts in scores]
    weights = [[jnp.exp2(part - top).astype(bf16) for part, top in zip(*pair)] for pair in zip(scores, peaks)]
    values = [value_ref[slot, 32 * h : 32 * h + 32, :] for h in heads]
    got = [
        [dot(value[:, :count], part, (1, 0)) for part, (_, _, count) in zip(parts, FORWARD_BLOCKS)]
        for value, parts in zip(values, weights)
    ]
    zero = jnp.zeros((1, WIDE), f32)
    for h, query, tops, parts in zip(heads, queries, peaks, got):
        both = jnp.concatenate(parts, 1)
        row_total = both[HEAD : HEAD + 1]
        mixed_scratch[h * HEAD : h * HEAD + HEAD, :] = both[:HEAD] * (1.0 / row_total)
        logs = jnp.concatenate(tops, 1) + jnp.log2(row_total)
        log_rows = rows_of([zero, zero, zero, *three_parts(-logs)], WIDE)
        query_ref[slot, 32 * h : 32 * h + 32, :] = (query + jnp.concatenate([jnp.zeros((HEAD, WIDE), f32), log_rows], 0)).astype(bf16)


def forward_probs(unit, query_ref, key_ref, refs):
    slot, base = unit
    for h in range(base, base + FORWARD_BATCH):
        query, key = query_ref[slot, 32 * h : 32 * h + 32, :], key_ref[slot, 32 * h : 32 * h + 32, :]
        for ref, (start, a, b) in zip(refs, BACKWARD_BLOCKS):
            ref[h] = jnp.exp2(dot(query[:, start:ROWS], key[:, a:b], (0, 0))).astype(bf16)


def attention_forward(core_ref, counts_ref, tokens_far, own_ref, other_ref,
                      mixed_far, query_far, key_far, value_far, weight_far, first_far, merged_far, low_far, middle_far, high_far, column_ref,
                      first_ref, projected_ref, mixed_scratch, arrived_ref, bias_ref,
                      raw_ref, tokens_ref, mixed_ref, query_ref, key_ref, value_ref, weight_ref, low_ref, middle_ref, high_ref, semaphores):
    slots = mixed_ref.shape[0]
    copies = Copies(semaphores)
    copies.start(tokens_far, raw_ref)
    core = core_ref[0]
    for side, ref in ((core, own_ref), (1 - core, other_ref)):
        blocks = jnp.swapaxes(ref[...], 0, 1)
        for r in range(3):
            at = pl.multiple_of(side * 192 + 64 * r, 64)
            for j in range(10):
                arrived_ref[pl.ds(at, 64), 128 * j : 128 * j + 128] = blocks[10 * r + j]
    order = arrival_order()
    ordered = dot(order, arrived_ref[...], (1, 0))
    weight_ref[...] = ordered[:, : 3 * WIDTH].astype(bf16)
    column_ref[...] = ordered[:, 3 * WIDTH :]
    rows = dot(arrived_ref[:, 3 * WIDTH :], order, (0, 1))
    gain, offset = rows[0:1], rows[1:2]
    for s in range(2):
        column = ordered[:, 3 * WIDTH + 2 + s : 3 * WIDTH + 3 + s]
        bias_ref[pl.ds(s, WIDTH, stride=2), :] = jnp.broadcast_to(column, (WIDTH, 128))
    first_ref[...] = jnp.zeros_like(first_ref)
    copies.wait_all()
    merge_slots(raw_ref, tokens_ref)
    copies.start(tokens_ref, merged_far)
    copies.start(weight_ref, weight_far)
    for slot in range(slots):
        normed, _ = norm_parts(tokens_ref[slot * ROWS : slot * ROWS + ROWS, :].astype(f32))
        first_ref[slot * WIDE : slot * WIDE + ROWS, :] = (normed * gain + offset).astype(bf16)
    copies.start(first_ref, first_far)
    projected_ref[...] = dot(weight_ref[...], first_ref[...], (0, 1))
    one = jnp.ones((1, WIDE), f32)
    more = []
    for slot in range(slots):
        hidden, frame = mask_rows(counts_ref, slot)
        more.append((rows_of(frame, WIDE), rows_of(hidden + [one, one, one], WIDE), rows_of([one, one, one], WIDE)))
    units = [(slot, base) for slot in range(slots) for base in range(0, HEADS, FORWARD_BATCH)]
    refs = (low_ref, middle_ref, high_ref)
    kept = {}

    def probs(unit):
        slot, base = unit
        if slot >= KEPT_SLOTS:
            return
        copies.wait(*kept.get((slot - 1, base // LOAD_BATCH), ()))
        forward_probs(unit, query_ref, key_ref, refs)
        if (base + FORWARD_BATCH) % LOAD_BATCH == 0:
            part = pl.ds(base // LOAD_BATCH * LOAD_BATCH, LOAD_BATCH)
            pairs = zip(refs, (low_far, middle_far, high_far))
            kept[slot, base // LOAD_BATCH] = [copies.start(near.at[part], away.at[slot, part]) for near, away in pairs]

    ready = forward_scores(units[0], projected_ref, bias_ref, key_ref, value_ref, more)
    for k, unit in enumerate(units):
        slot = unit[0]
        now, ready = ready, None
        if k + 1 < len(units):
            ready = forward_scores(units[k + 1], projected_ref, bias_ref, key_ref, value_ref, more)
        forward_mixed(unit, *now, mixed_scratch, query_ref, value_ref)
        if unit[1] + FORWARD_BATCH == HEADS:
            mixed_ref[slot] = mixed_scratch[...].astype(bf16)
            for near, away in ((key_ref, key_far), (value_ref, value_far), (query_ref, query_far), (mixed_ref, mixed_far)):
                copies.start(near.at[slot], away.at[slot])
        if k >= 1:
            probs(units[k - 1])
    probs(units[-1])
    copies.wait_all()


def probs_shapes():
    return [(ROWS - start, b - a) for start, a, b in BACKWARD_BLOCKS]


def run_forward(core, counts, tokens, own, other):
    slots = tokens.shape[1]
    scalars = pl.BlockSpec(memory_space=pltpu.SMEM)
    arrays = pl.BlockSpec(memory_space=pltpu.VMEM)
    away = pl.BlockSpec(memory_space=pl.ANY)
    return pl.pallas_call(
        attention_forward,
        in_specs=[scalars, scalars, away, arrays, arrays],
        out_specs=[away] * 10 + [arrays],
        out_shape=[pltpu.HBM((slots, rows, WIDE), bf16) for rows in (WIDTH, 512, 512, 512)]
        + [pltpu.HBM((WIDTH, 3 * WIDTH), bf16), pltpu.HBM((slots * WIDE, WIDTH), bf16), pltpu.HBM((slots * ROWS, WIDTH), bf16)]
        + [pltpu.HBM((KEPT_SLOTS, HEADS, *shape), bf16) for shape in probs_shapes()]
        + [pltpu.HBM((WIDTH, 128), f32)],
        scratch_shapes=[
            pltpu.VMEM((slots * WIDE, WIDTH), bf16),
            pltpu.VMEM((3 * WIDTH, slots * WIDE), f32),
            pltpu.VMEM((WIDTH, WIDE), f32),
            pltpu.VMEM((WIDTH, 3 * WIDTH + 128), bf16),
            pltpu.VMEM((2 * WIDTH, 128), f32),
            pltpu.VMEM((SPAN, slots, WIDTH), bf16),
            pltpu.VMEM((slots * ROWS, WIDTH), bf16),
        ]
        + [pltpu.VMEM((slots, rows, WIDE), bf16) for rows in (WIDTH, 512, 512, 512)]
        + [pltpu.VMEM((WIDTH, 3 * WIDTH), bf16)]
        + [pltpu.VMEM((HEADS, *shape), bf16) for shape in probs_shapes()]
        + [pltpu.SemaphoreType.DMA((40,))],
        compiler_params=params(48),
        cost_estimate=cost(20),
        name="attention_forward",
    )(core, counts, *far(tokens), *held(own, other))


def feed_forward_early(cotangent_far, merged_far, mixed_far, own_ref,
                       arrived_ref, down_ref, up_b_ref, cotangent_ref, tokens_ref, mixed_ref, slopes_ref, raw_ref, semaphores):
    copies = Copies(semaphores)
    raw = copies.start(cotangent_far, raw_ref)
    copies.start(mixed_far, mixed_ref)
    copies.start(merged_far, tokens_ref)
    unpack_side(own_ref, arrived_ref, down_ref, up_b_ref)
    copies.wait(raw)
    merge_slots(raw_ref, cotangent_ref)
    slopes_ref[...] = dot(cotangent_ref[...], down_ref[...], (1, 1))
    copies.wait_all()


def unpack_side(message_ref, arrived_ref, down_ref, up_b_ref):
    blocks = jnp.swapaxes(message_ref[...], 0, 1)
    for r in range(3):
        rows = slice(64 * r, 64 * r + 64)
        for j in range(15):
            arrived_ref[rows, 128 * j : 128 * j + 128] = blocks[3 * r + j] if j < 3 else blocks[6 + 12 * r + j]
        arrived_ref[rows, 1920:2048] = blocks[81 + r]
    for r in range(12):
        for j in range(3):
            down_ref[64 * r : 64 * r + 64, 128 * j : 128 * j + 128] = blocks[45 + 3 * r + j]
    turned = blocks[81].astype(f32).T
    up_b_ref[0:1, :] = jnp.concatenate([turned[4 + r : 5 + r] for r in range(12)], 1)


def run_feed_forward_early(cotangent, merged, mixed, own):
    _, slots, _ = cotangent.shape
    arrays = pl.BlockSpec(memory_space=pltpu.VMEM)
    away = pl.BlockSpec(memory_space=pl.ANY)
    return pl.pallas_call(
        feed_forward_early,
        in_specs=[away, away, away, arrays],
        out_shape=[
            pltpu.VMEM((WIDTH // 2, 2048), bf16),
            pltpu.VMEM((HIDDEN // 2, WIDTH), bf16),
            pltpu.VMEM((8, HIDDEN // 2), f32),
            pltpu.VMEM((slots * ROWS, WIDTH), bf16),
            pltpu.VMEM((slots * ROWS, WIDTH), bf16),
            pltpu.VMEM((slots, WIDTH, WIDE), bf16),
            pltpu.VMEM((slots * ROWS, HIDDEN // 2), f32),
        ],
        scratch_shapes=[pltpu.VMEM((SPAN, slots, WIDTH), bf16), pltpu.SemaphoreType.DMA((3,))],
        compiler_params=params(16),
        cost_estimate=cost(3),
        name="feed_forward_early",
    )(*far(cotangent, merged, mixed), *held(own))


def feed_forward(core_ref, tokens_ref, mixed_ref, cotangent_ref, own_arrived_ref, own_down_ref, own_up_b_ref, slopes_ref, other_ref,
                 activated_ref, resid_ref, other_down_ref, row_ref, grad_resid_far, grad_mixed_far, mine_ref, theirs_ref,
                 arrived_ref, ordered_ref, up_b_ref, packed_ref, grad_down_ref, grad_resid_ref, grad_mixed_ref, second_ref, grad_up_ref,
                 semaphores):
    slots = mixed_ref.shape[0]
    block = 256
    root = math.sqrt(2.0 / math.pi)
    copies = Copies(semaphores)
    core = core_ref[0]
    sides = (core, 1 - core)
    places = [pl.multiple_of(side * (WIDTH // 2), 64) for side in sides]
    unpack_side(other_ref, arrived_ref, other_down_ref, up_b_ref)
    downs = (own_down_ref, other_down_ref)
    up_bs = (own_up_b_ref, up_b_ref)
    order = arrival_order()
    packed_ref[pl.ds(places[0], WIDTH // 2), :] = own_arrived_ref[...]
    packed_ref[pl.ds(places[1], WIDTH // 2), :] = arrived_ref[...]
    row_ref[...] = dot(packed_ref[:, 1920:], order, (0, 1))[0:8]
    ordered_ref[...] = dot(order, packed_ref[:, :1920], (1, 0)).astype(bf16)
    out_w = ordered_ref[:, :WIDTH]
    up_w = lambda half, at: ordered_ref[:, pl.ds(pl.multiple_of(WIDTH + sides[half] * (HIDDEN // 2) + at, 128), block)]
    out_b, gain, offset = (row_ref[k : k + 1] for k in range(3))
    spans = [slice(slot * ROWS, slot * ROWS + ROWS) for slot in range(slots)]
    norms = {}

    def enter(slot):
        resid = tokens_ref[spans[slot], :].astype(f32) + dot(mixed_ref[slot, :, :ROWS], out_w, (0, 0)) + out_b
        resid_ref[spans[slot], :] = resid
        norms[slot] = norm_parts(resid)
        second_ref[spans[slot], :] = (norms[slot][0] * gain + offset).astype(bf16)

    def products(work):
        slot, half, at = work
        rows = spans[slot]
        up = dot(second_ref[rows, :], up_w(half, at), (1, 0))
        if half == 0:
            return up, slopes_ref[rows, at : at + block]
        return up, dot(cotangent_ref[rows, :], other_down_ref[at : at + block, :], (1, 1))

    lines = {}

    def activate(work, up, grad_activated):
        slot, half, at = work
        rows, cols = spans[slot], slice(half * (HIDDEN // 2) + at, half * (HIDDEN // 2) + at + block)
        up = up + up_bs[half][0:1, at : at + block]
        square = up * up
        tanh = jnp.tanh(up * (root + (root * 0.044715) * square))
        half_tanh = 0.5 + 0.5 * tanh
        activated_ref[rows, cols] = (up * half_tanh).astype(bf16)
        slope = half_tanh + (up * (2.0 * half_tanh * (1.0 - half_tanh))) * (root + (3 * root * 0.044715) * square)
        grad_up = grad_activated * slope
        grad_up_ref[rows, cols] = grad_up.astype(bf16)
        line = jnp.sum(grad_up, axis=0, keepdims=True)
        lines[half, at] = lines[half, at] + line if (half, at) in lines else line

    works = [(slot, half, at) for slot in range(slots) for half in range(2) for at in range(0, HIDDEN // 2, block)]
    enter(0)
    ready = products(works[0])
    for slot in range(1, slots):
        enter(slot)
    for k, work in enumerate(works):
        now = ready
        if k + 1 < len(works):
            ready = products(works[k + 1])
        activate(work, *now)

    grad_branch = cotangent_ref[...]
    halves = [slice(0, HIDDEN // 2), slice(HIDDEN // 2, HIDDEN)]
    side_w = [ordered_ref[:, pl.ds(pl.multiple_of(WIDTH + side * (HIDDEN // 2), 128), HIDDEN // 2)] for side in sides]
    grad_seconds = [sum(dot(grad_up_ref[rows, cols], weight, (1, 1)) for cols, weight in zip(halves, side_w)) for rows in spans]
    attended, sums = [], []

    def leave(slot):
        normed, inverse = norms[slot]
        grad_second = grad_seconds[slot]
        scaled = grad_second * gain
        mean_one = jnp.mean(scaled, axis=-1, keepdims=True)
        mean_two = jnp.mean(scaled * normed, axis=-1, keepdims=True)
        grad_full = cotangent_ref[spans[slot], :].astype(f32)
        grad_resid = grad_full + inverse * (scaled - mean_one - normed * mean_two)
        grad_resid_ref[spans[slot], :] = grad_resid
        low = grad_resid.astype(bf16)
        attended.append(low)
        parts = [low.astype(f32), grad_second * normed, grad_second, grad_full]
        sums.append(jnp.concatenate([jnp.sum(part, axis=0, keepdims=True) for part in parts], 0))

    for slot in range(slots):
        leave(slot)
        cols = halves[slot % 2]
        grad_down_ref[cols, :] = dot(activated_ref[:, cols], grad_branch, (0, 0)).astype(bf16)
    copies.start(grad_resid_ref, grad_resid_far)
    for slot in range(slots):
        grad_mixed_ref[slot, :, 512:WIDE] = jnp.zeros((WIDTH, WIDE - 512), bf16)
        grad_mixed_ref[slot, :, :ROWS] = dot(out_w, attended[slot], (1, 1)).astype(bf16)
    copies.start(grad_mixed_ref, grad_mixed_far)
    grad_out = sum(dot(mixed_ref[slot, :, :ROWS], attended[slot], (1, 0)) for slot in range(slots))
    for side, cols in zip(sides, halves):
        at = pl.multiple_of(WIDTH + side * (HIDDEN // 2), 128)
        ordered_ref[:, pl.ds(at, HIDDEN // 2)] = dot(second_ref[...], grad_up_ref[:, cols], (0, 0)).astype(bf16)
    ordered_ref[:, :WIDTH] = grad_out.astype(bf16)
    packed_ref[:, :1920] = dot(order, ordered_ref[...], (0, 0)).astype(bf16)
    high, low = two_parts(sum(sums))
    rows = jnp.concatenate([high, low, jnp.zeros((120, WIDTH), f32)], 0).astype(bf16)
    packed_ref[:, 1920:] = dot(order, rows, (0, 1)).astype(bf16)
    blank = jnp.zeros((CHIPS, 128), bf16)
    for half, (place, ref) in enumerate(zip(places, (mine_ref, theirs_ref))):
        blocks = [blank] * REST_ROWS
        for r in range(3):
            at = pl.multiple_of(place + 64 * r, 64)
            for j in range(15):
                blocks[3 * r + j if j < 3 else 6 + 12 * r + j] = packed_ref[pl.ds(at, 64), 128 * j : 128 * j + 128]
            blocks[81 + r] = packed_ref[pl.ds(at, 64), 1920:2048]
        for r in range(12):
            at = half * (HIDDEN // 2) + 64 * r
            for j in range(3):
                blocks[45 + 3 * r + j] = grad_down_ref[at : at + 64, 128 * j : 128 * j + 128]
        high, low = two_parts(jnp.concatenate([lines[half, at] for at in range(0, HIDDEN // 2, block)], 1))
        rows = [part[:, 64 * r : 64 * r + 64] for part in (high, low) for r in range(12)]
        blocks[84] = rows_of(rows, 64, 128).T.astype(bf16)
        ref[...] = jnp.swapaxes(jnp.stack(blocks), 0, 1)
    copies.wait_all()


def run_feed_forward(core, tokens, mixed, cotangent, arrived, down, up_b, slopes, other):
    slots = mixed.shape[0]
    arrays = pl.BlockSpec(memory_space=pltpu.VMEM)
    away = pl.BlockSpec(memory_space=pl.ANY)
    return pl.pallas_call(
        feed_forward,
        in_specs=[pl.BlockSpec(memory_space=pltpu.SMEM)] + [arrays] * 8,
        out_specs=[arrays, arrays, arrays, arrays, away, away, arrays, arrays],
        out_shape=[
            pltpu.VMEM((slots * ROWS, HIDDEN), bf16),
            pltpu.VMEM((slots * ROWS, WIDTH), f32),
            pltpu.VMEM((HIDDEN // 2, WIDTH), bf16),
            pltpu.VMEM((8, WIDTH), f32),
            pltpu.HBM((slots * ROWS, WIDTH), f32),
            pltpu.HBM((slots, WIDTH, WIDE), bf16),
            pltpu.VMEM((CHIPS, REST_ROWS, 128), bf16),
            pltpu.VMEM((CHIPS, REST_ROWS, 128), bf16),
        ],
        scratch_shapes=[
            pltpu.VMEM((WIDTH // 2, 2048), bf16),
            pltpu.VMEM((WIDTH, 1920), bf16),
            pltpu.VMEM((8, HIDDEN // 2), f32),
            pltpu.VMEM((WIDTH, 2048), bf16),
            pltpu.VMEM((HIDDEN, WIDTH), bf16),
            pltpu.VMEM((slots * ROWS, WIDTH), f32),
            pltpu.VMEM((slots, WIDTH, WIDE), bf16),
            pltpu.VMEM((slots * ROWS, WIDTH), bf16),
            pltpu.VMEM((slots * ROWS, HIDDEN), bf16),
            pltpu.SemaphoreType.DMA((2,)),
        ],
        compiler_params=params(34),
        cost_estimate=cost(17),
        name="feed_forward",
    )(core, *held(tokens, mixed, cotangent, arrived, down, up_b, slopes, other))


def feed_forward_output(activated_ref, resid_ref, own_down_ref, other_down_ref, row_ref, out_ref):
    slots = out_ref.shape[1]
    half = HIDDEN // 2
    result = resid_ref[...] + row_ref[3:4]
    result += dot(activated_ref[:, :half], own_down_ref[...], (1, 0)) + dot(activated_ref[:, half:], other_down_ref[...], (1, 0))
    both = jnp.stack([result[slot * ROWS : slot * ROWS + SPAN] for slot in range(slots)])
    out_ref[...] = jnp.swapaxes(both, 0, 1).astype(bf16)


def run_feed_forward_output(*args):
    slots = args[1].shape[0] // ROWS
    return pl.pallas_call(
        feed_forward_output,
        out_shape=pltpu.HBM((SPAN, slots, WIDTH), bf16),
        compiler_params=params(20),
        cost_estimate=cost(3),
        name="feed_forward_output",
    )(*held(*args))


def backward_slopes(unit, copies, loads, value_ref, mixed_ref, grad_mixed_ref):
    slot, base = unit
    copies.wait(*loads["grad"][slot])
    grads, slopes = [], []
    for h in range(base, base + BACKWARD_BATCH):
        both = slice(48 * (h // 2), 48 * (h // 2) + 48)
        part = slice(HEAD * (h % 2), HEAD * (h % 2) + HEAD)
        grad = grad_mixed_ref[slot, both, :].astype(f32)[part]
        mixed = mixed_ref[slot, both, :].astype(f32)[part]
        shift = jnp.sum(grad * mixed, axis=0, keepdims=True)
        grad = jnp.concatenate([grad, rows_of(three_parts(-shift), WIDE)], 0).astype(bf16)
        value = value_ref[slot, 32 * h : 32 * h + 32, :]
        grads.append(grad)
        slopes.append([dot(grad[:, start:ROWS], value[:, a:b], (0, 0)) for start, a, b in BACKWARD_BLOCKS])
    return grads, slopes


def backward_products(unit, grads, slopes, copies, loads, query_ref, key_ref, probs_refs, turned_ref):
    slot, base = unit
    heads = range(base, base + BACKWARD_BATCH)
    copies.wait(*loads["query"][slot])
    queries = [query_ref[slot, 32 * h : 32 * h + 32, :] for h in heads]
    keys = [key_ref[slot, 32 * h : 32 * h + 32, :] for h in heads]
    if slot < KEPT_SLOTS:
        copies.wait(*loads["probs"][slot][base // LOAD_BATCH])
        probs = [[ref[slot, h].astype(f32) for ref in probs_refs] for h in heads]
    else:
        probs = [
            [jnp.exp2(dot(query[:, start:ROWS], key[:, a:b], (0, 0))) for start, a, b in BACKWARD_BLOCKS]
            for query, key in zip(queries, keys)
        ]
    grad_scores = [[(part * slope).astype(bf16) for part, slope in zip(*pair)] for pair in zip(probs, slopes)]
    probs = [[part.astype(bf16) for part in parts] for parts in probs]
    over = lambda left, parts: jnp.concatenate(
        [dot(left[:, start:ROWS], part, (1, 0)) for part, (start, _, _) in zip(parts, BACKWARD_BLOCKS)], 1)
    grad_v = [over(grad, parts) for grad, parts in zip(grads, probs)]
    grad_k = [over(query, parts) for query, parts in zip(queries, grad_scores)]
    grad_q = [
        [dot(key[:, a:b], part, (1, 1)) for part, (_, a, b) in zip(parts, BACKWARD_BLOCKS)]
        for key, parts in zip(keys, grad_scores)
    ]
    fill = lambda part: jnp.concatenate([jnp.zeros((32, ROWS - part.shape[1]), f32), part], 1) if part.shape[1] < ROWS else part
    lanes = slice(slot * WIDE, slot * WIDE + WIDE)
    blank = jnp.zeros((HEAD, WIDE - ROWS), f32)
    for k, h in enumerate(heads):
        at = h * HEAD
        whole = sum(fill(part) for part in grad_q[k])[:HEAD] * (1.0 / math.sqrt(HEAD))
        turned_ref[at : at + HEAD, lanes] = jnp.concatenate([whole, blank], 1)
        turned_ref[at + WIDTH : at + WIDTH + HEAD, lanes] = grad_k[k][:HEAD] * math.log(2.0)
        turned_ref[at + 2 * WIDTH : at + 2 * WIDTH + HEAD, lanes] = grad_v[k][:HEAD]


def attention_backward(core_ref, query_far, key_far, value_far, mixed_far, grad_mixed_far, low_far, middle_far, high_far, first_far, weight_far,
                       column_ref, turned_far, mine_ref, theirs_ref,
                       turned_ref, bias_ref, packed_ref, turned_low_ref,
                       query_ref, key_ref, value_ref, mixed_ref, grad_mixed_ref, low_ref, middle_ref, high_ref, first_ref, weight_ref, semaphores):
    slots = mixed_ref.shape[0]
    copies = Copies(semaphores)
    loads = {"grad": [], "probs": [], "query": []}
    probs_refs = (low_ref, middle_ref, high_ref)
    for slot in range(slots):
        load = lambda pairs: [copies.start(away.at[slot], near.at[slot]) for away, near in pairs]
        loads["grad"].append(load(((value_far, value_ref), (grad_mixed_far, grad_mixed_ref), (mixed_far, mixed_ref))))
        loads["probs"].append([])
        if slot >= KEPT_SLOTS:
            loads["query"].append(load(((query_far, query_ref), (key_far, key_ref))))
            continue
        for base in range(0, HEADS, LOAD_BATCH):
            part = pl.ds(base, LOAD_BATCH)
            pairs = zip((low_far, middle_far, high_far), probs_refs)
            loads["probs"][slot].append([copies.start(away.at[slot, part], near.at[slot, part]) for away, near in pairs])
            if base == 0:
                loads["query"].append(load(((query_far, query_ref), (key_far, key_ref))))
    weights = [copies.start(first_far, first_ref), copies.start(weight_far, weight_ref)]
    core = core_ref[0]
    sums = jnp.zeros((3 * WIDTH, 1), f32)
    units = [(slot, base) for slot in range(slots) for base in range(0, HEADS, BACKWARD_BATCH)]
    ready = backward_slopes(units[0], copies, loads, value_ref, mixed_ref, grad_mixed_ref)
    for k, unit in enumerate(units):
        slot = unit[0]
        now, ready = ready, None
        if k + 1 < len(units):
            ready = backward_slopes(units[k + 1], copies, loads, value_ref, mixed_ref, grad_mixed_ref)
        backward_products(unit, *now, copies, loads, query_ref, key_ref, probs_refs, turned_ref)
        if unit[1] + BACKWARD_BATCH == HEADS:
            turned = turned_ref[:, slot * WIDE : slot * WIDE + WIDE]
            sums += jnp.sum(turned, axis=1, keepdims=True)
            turned_low_ref[slot] = turned.astype(bf16)
            copies.start(turned_low_ref.at[slot], turned_far.at[slot])
    copies.wait(*weights)
    order = arrival_order()
    turned = jnp.concatenate([turned_low_ref[slot] for slot in range(slots)], 1)
    grad_weight = dot(first_ref[...], turned, (0, 1))
    packed_ref[:, : 3 * WIDTH] = dot(order, grad_weight.astype(bf16), (0, 0)).astype(bf16)
    lane = lax.broadcasted_iota(jnp.int32, (3 * WIDTH, 128), 1)
    high, low = two_parts(sums)
    spread = jnp.where(lane == 0, high, jnp.where(lane == 1, low, 0.0)).astype(bf16)
    against = dot(weight_ref[...], spread, (1, 0))
    grad_offset = against[:, 0:1] + against[:, 1:2]
    along = jnp.sum(grad_weight * weight_ref[...].astype(f32), axis=1, keepdims=True)
    grad_gain = (along - column_ref[:, 1:2] * grad_offset) / column_ref[:, 0:1]
    bias_ref[0:WIDTH] = jnp.broadcast_to(sums[:WIDTH], (WIDTH, 128))
    bias_ref[WIDTH:] = jnp.broadcast_to(sums[2 * WIDTH :], (WIDTH, 128))
    lane = lax.broadcasted_iota(jnp.int32, (WIDTH, 128), 1)
    columns = jnp.zeros((WIDTH, 128), f32)
    for k, values in enumerate((grad_gain, grad_offset, bias_ref[pl.ds(0, WIDTH, stride=2), :], bias_ref[pl.ds(1, WIDTH, stride=2), :])):
        high, low = two_parts(values)
        columns = jnp.where(lane == k, high, jnp.where(lane == 4 + k, low, columns))
    packed_ref[:, 3 * WIDTH :] = dot(order, columns.astype(bf16), (0, 0)).astype(bf16)
    blank = jnp.zeros((CHIPS, 128), bf16)
    for side, ref in ((core, mine_ref), (1 - core, theirs_ref)):
        blocks = []
        for r in range(3):
            at = pl.multiple_of(side * 192 + 64 * r, 64)
            for j in range(10):
                blocks.append(packed_ref[pl.ds(at, 64), 128 * j : 128 * j + 128])
        ref[...] = jnp.swapaxes(jnp.stack(blocks + [blank, blank]), 0, 1)
    copies.wait_all()


def run_backward(core, query, key, value, mixed, grad_mixed, low, middle, high, first, weight, column):
    slots = mixed.shape[0]
    arrays = pl.BlockSpec(memory_space=pltpu.VMEM)
    away = pl.BlockSpec(memory_space=pl.ANY)
    return pl.pallas_call(
        attention_backward,
        in_specs=[pl.BlockSpec(memory_space=pltpu.SMEM)] + [away] * 10 + [arrays],
        out_specs=[away, arrays, arrays],
        out_shape=[
            pltpu.HBM((slots, 3 * WIDTH, WIDE), bf16),
            pltpu.VMEM((CHIPS, FIRST_ROWS, 128), bf16),
            pltpu.VMEM((CHIPS, FIRST_ROWS, 128), bf16),
        ],
        scratch_shapes=[
            pltpu.VMEM((3 * WIDTH, slots * WIDE), f32),
            pltpu.VMEM((2 * WIDTH, 128), f32),
            pltpu.VMEM((WIDTH, 3 * WIDTH + 128), bf16),
            pltpu.VMEM((slots, 3 * WIDTH, WIDE), bf16),
        ]
        + [pltpu.VMEM((slots, rows, WIDE), bf16) for rows in (512, 512, 512, WIDTH, WIDTH)]
        + [pltpu.VMEM((KEPT_SLOTS, HEADS, *shape), bf16) for shape in probs_shapes()]
        + [pltpu.VMEM((slots * WIDE, WIDTH), bf16), pltpu.VMEM((WIDTH, 3 * WIDTH), bf16), pltpu.SemaphoreType.DMA((70,))],
        compiler_params=params(56),
        cost_estimate=cost(22),
        name="attention_backward",
    )(core, *far(query, key, value, mixed, grad_mixed, low, middle, high, first, weight), column)


def input_backward(merged_far, turned_far, grad_resid_far, weight_far, column_ref, out_far,
                   tokens_ref, turned_ref, grad_resid_ref, weight_ref, grad_first_ref, out_ref, semaphores):
    slots = turned_ref.shape[0]
    copies = Copies(semaphores)
    first = [copies.start(weight_far, weight_ref), copies.start(turned_far.at[0], turned_ref.at[0])]
    turns = [copies.start(turned_far.at[slot], turned_ref.at[slot]) for slot in range(1, slots)]
    rest = [copies.start(merged_far, tokens_ref), copies.start(grad_resid_far, grad_resid_ref)]
    gain = column_ref[...].T[0:1]
    copies.wait(*first)
    for slot in range(slots):
        if slot:
            copies.wait(turns[slot - 1])
        grad_first_ref[slot * ROWS : slot * ROWS + ROWS, :] = dot(turned_ref[slot, :, :ROWS], weight_ref[...], (0, 1))
    copies.wait(*rest)
    half = ROWS // 2
    for low, high in ((0, half), (half, SPAN)):
        for slot in range(slots):
            at = slice(slot * ROWS + low, slot * ROWS + low + half)
            normed, inverse = norm_parts(tokens_ref[at, :].astype(f32))
            scaled = grad_first_ref[at, :] * gain
            mean_one = jnp.mean(scaled, axis=-1, keepdims=True)
            mean_two = jnp.mean(scaled * normed, axis=-1, keepdims=True)
            grad = grad_resid_ref[at, :] + inverse * (scaled - mean_one - normed * mean_two)
            out_ref[low:high, slot, :] = grad[: high - low]
        copies.start(out_ref.at[pl.ds(low, high - low)], out_far.at[pl.ds(low, high - low)])
    copies.wait_all()


def run_input_backward(merged, turned, grad_resid, weight, column):
    slots = turned.shape[0]
    arrays = pl.BlockSpec(memory_space=pltpu.VMEM)
    away = pl.BlockSpec(memory_space=pl.ANY)
    return pl.pallas_call(
        input_backward,
        in_specs=[away] * 4 + [arrays],
        out_specs=away,
        out_shape=pltpu.HBM((SPAN, slots, WIDTH), f32),
        scratch_shapes=[
            pltpu.VMEM((slots * ROWS, WIDTH), bf16),
            pltpu.VMEM((slots, 3 * WIDTH, WIDE), bf16),
            pltpu.VMEM((slots * ROWS, WIDTH), f32),
            pltpu.VMEM((WIDTH, 3 * WIDTH), bf16),
            pltpu.VMEM((slots * ROWS, WIDTH), f32),
            pltpu.VMEM((SPAN, slots, WIDTH), f32),
            pltpu.SemaphoreType.DMA((8,)),
        ],
        compiler_params=params(32),
        cost_estimate=cost(6),
        name="input_backward",
    )(*far(merged, turned, grad_resid, weight), column)


def to_chips(message):
    return lax.all_to_all(message, CHIP_AXES, 0, 0, tiled=True)


def to_column(message):
    return lax.all_to_all(message, COLUMN_AXES, 0, 0, tiled=True)


def along_line(message, shift):
    return lax.ppermute(message, LINE_AXIS, [(k, (k + shift) % LINE) for k in range(LINE)])


def across(message):
    return lax.ppermute(message, CORE_AXIS, [(0, 1), (1, 0)])


def shards(tokens, item_frames, ln1_gain, ln1_bias, qkv_weight, qv_bias, out_weight, out_bias, ln2_gain, ln2_bias,
           up_weight, up_bias, down_weight, down_bias, cotangent):
    together = lax.optimization_barrier
    core = lax.axis_index(CORE_AXIS).astype(jnp.int32).reshape(1)
    line = lax.axis_index(LINE_AXIS).astype(jnp.int32).reshape(1)
    first = run_pack_first(qkv_weight, ln1_gain, ln1_bias, qv_bias)
    first, up_weight = together((first, up_weight))
    first = to_chips(first)
    up_sent = up_weight.reshape(3, 16, 2, 4, 12).transpose(0, 2, 4, 1, 3).reshape(3, HIDDEN)
    second = run_pack_second(out_weight, up_sent, down_weight, out_bias, ln2_gain, ln2_bias, down_bias, up_bias)
    tokens, cotangent = tokens.transpose(1, 0, 2), cotangent.transpose(1, 0, 2)
    first, second = together((first, second))
    first_other = across(first)
    second = to_chips(second)
    mixed, query, key, value, weight, normed, merged, low, middle, high, column = run_forward(core, item_frames, tokens, first, first_other)
    second, mixed = together((second, mixed))
    other = across(second)
    arrived, own_down, up_b, turned_cotangent, near, near_mixed, slopes = run_feed_forward_early(cotangent, merged, mixed, second)
    activated, resid, other_down, row, grad_resid, grad_mixed, mine, theirs = run_feed_forward(
        core, near, near_mixed, turned_cotangent, arrived, own_down, up_b, slopes, other)
    theirs = across(theirs)
    output = run_feed_forward_output(activated, resid, own_down, other_down, row)
    output, mine = together((output, mine))
    output = output.transpose(1, 0, 2)
    rest = run_add_halves(mine, theirs)
    rest, grad_mixed = together((rest, grad_mixed))
    rest = to_column(rest.reshape(CHIPS // LINE, LINE * REST_ROWS, 128))
    turned, mine, theirs = run_backward(core, query, key, value, mixed, grad_mixed, low, middle, high, normed, weight, column)
    theirs = across(theirs)
    own = run_add_halves(mine, theirs)
    own, rest = together((own, rest))
    own, turned = together((own, turned))
    own = to_chips(own)
    keep, *sent = run_sum_column(line, rest)
    sent = [along_line(part, shift + 1) for shift, part in enumerate(sent)]
    grad_out, grad_up, *others = run_unpack_rest(keep, *sent)
    grad_down, grad_out_b, grad_gain_two, grad_offset_two, grad_down_b, grad_up_b = others
    input_grad = run_input_backward(merged, turned, grad_resid, weight, column).transpose(1, 0, 2)
    grad_qkv, grad_gain, grad_offset, grad_qv = run_unpack_first(own)
    return (output, input_grad, grad_gain, grad_offset, grad_qkv, grad_qv, grad_out, grad_out_b, grad_gain_two, grad_offset_two,
            grad_up, grad_up_b, grad_down, grad_down_b)


def solution(mesh):
    split = Mesh(mesh.devices.reshape(4, 4, 2, mesh.shape["narrow"]), ALL)
    by_rank = lambda n: P(ALL, *([None] * (n - 1)))
    return jax.shard_map(
        shards,
        mesh=split,
        in_specs=tuple(by_rank(n) for n in (3, 2, 1, 1, 2, 1, 2, 1, 1, 1, 2, 1, 2, 1, 3)),
        out_specs=tuple(by_rank(n) for n in (3, 3, 1, 1, 2, 1, 2, 1, 1, 1, 2, 1, 2, 1)),
        check_vma=False,
    )
```

```python
import math

import jax
import jax.numpy as jnp
from jax import lax
from jax.experimental import pallas as pl
from jax.experimental.pallas import tpu as pltpu
from jax.sharding import Mesh
from jax.sharding import PartitionSpec as P

HEADS = 16
HEAD = 24
FRAME = 196
WIDTH = 384
HIDDEN = 1536
WIDE = 640
SPAN = 588
ROWS = 592
CHIPS = 64
FIRST_ROWS = 32
REST_ROWS = 88
SECOND_ROWS = 80
EPSILON = 1e-05
NEGATIVE = -1e30
bf16 = jnp.bfloat16
f32 = jnp.float32
FORWARD_BLOCKS = ((0, 128, 208), (128, 384, 400), (384, 640, 592))
FORWARD_BATCH = 8
LOAD_BATCH = 8
KEPT_UNITS = 3
BACKWARD_BATCH = 8
BACKWARD_BLOCKS = ((0, 0, 256), (192, 256, 512), (384, 512, 640))
ALL = ("wide_0", "wide_1", "wide_2", "narrow")
CHIP_AXES = ("wide_0", "wide_1", "narrow")
COLUMN_AXES = ("wide_0", "wide_1")
LINE_AXIS = "narrow"
LINE = 4
CORE_AXIS = "wide_2"


def dot(left, right, over):
    return lax.dot_general(left, right, (((over[0],), (over[1],)), ((), ())), preferred_element_type=f32)


def norm_parts(values):
    centred = values - jnp.mean(values, axis=-1, keepdims=True)
    inverse = lax.rsqrt(jnp.mean(centred * centred, axis=-1, keepdims=True) + EPSILON)
    return centred * inverse, inverse


def two_parts(values):
    high = values.astype(bf16).astype(f32)
    return high, values - high


def three_parts(values):
    high, rest = two_parts(values)
    middle, low = two_parts(rest)
    return high, middle, low


def rows_of(rows, width, count=8):
    index = lax.broadcasted_iota(jnp.int32, (count, width), 0)
    out = jnp.zeros((count, width), f32)
    for k, row in enumerate(rows):
        out = jnp.where(index == k, row, out)
    return out


def arrival_order():
    place = lax.broadcasted_iota(jnp.int32, (WIDTH, WIDTH), 1)
    feature = lax.broadcasted_iota(jnp.int32, (WIDTH, WIDTH), 0)
    core = (place >= WIDTH // 2).astype(jnp.int32)
    rest = place - core * (WIDTH // 2)
    row = rest >> 6
    chip = rest & 63
    return (feature == 3 * (8 * (chip >> 2) + 4 * core + (chip & 3)) + row).astype(f32).astype(bf16)


def mask_rows(counts_ref, slot):
    lane = lax.broadcasted_iota(jnp.int32, (1, WIDE), 1)
    first_end = counts_ref[slot, 0]
    second_end = first_end + counts_ref[slot, 1]
    third_end = second_end + counts_ref[slot, 2]
    group = [
        (f >= first_end).astype(jnp.int32) + (f >= second_end).astype(jnp.int32) + (f >= third_end).astype(jnp.int32)
        for f in range(3)
    ]
    hidden = []
    for f in range(3):
        row = jnp.full((1, WIDE), NEGATIVE, f32)
        for k in range(f + 1):
            seen = jnp.where(group[f] == group[k], 0.0, NEGATIVE).astype(f32)
            row = jnp.where((lane >= FRAME * k) & (lane < FRAME * (k + 1)), seen, row)
        hidden.append(row)
    frame = [((lane >= FRAME * f) & (lane < FRAME * (f + 1))).astype(f32) for f in range(3)]
    return hidden, frame


def params(mebibytes):
    return pltpu.CompilerParams(vmem_limit_bytes=mebibytes * 2**20)


def cost(microseconds):
    return pl.CostEstimate(flops=int(microseconds * 1.1e9), bytes_accessed=2**20, transcendentals=0)


def shape_of(shape, dtype):
    return jax.ShapeDtypeStruct(shape, dtype)


def held(*arrays):
    return [pltpu.with_memory_space_constraint(a, pltpu.VMEM) for a in arrays]


def far(*arrays):
    return [pltpu.with_memory_space_constraint(a, pltpu.HBM) for a in arrays]


class Copies:
    def __init__(self, semaphores):
        self.semaphores, self.count, self.open = semaphores, 0, []

    def start(self, source, target):
        copy = pltpu.make_async_copy(source, target, self.semaphores.at[self.count])
        self.count += 1
        copy.start()
        self.open.append(copy)
        return copy

    def wait(self, *copies):
        for copy in copies:
            if any(copy is other for other in self.open):
                self.open = [other for other in self.open if other is not copy]
                copy.wait()

    def wait_all(self):
        self.wait(*self.open)


def pack_first(qkv_ref, gain_ref, offset_ref, qv_ref, out_w_ref, out_b_ref, gain_two_ref, offset_two_ref, down_b_ref, up_b_ref, out_ref, rows_ref):
    rows_ref[...] = jnp.zeros_like(rows_ref)
    weight = qkv_ref[...].astype(f32)
    line = lambda ref, count: ref[...].astype(f32).reshape(1, count)
    gain, offset, qv = line(gain_ref, 3), line(offset_ref, 3), line(qv_ref, 6)
    for r in range(3):
        for j in range(9):
            rows_ref[10 * r + j : 10 * r + j + 1, :] = weight[r : r + 1, 128 * j : 128 * j + 128]
        rows_ref[10 * r + 9 : 10 * r + 10, 0:1] = gain[:, r : r + 1]
        rows_ref[10 * r + 9 : 10 * r + 10, 1:2] = offset[:, r : r + 1]
        rows_ref[10 * r + 9 : 10 * r + 10, 2:4] = qv[:, 2 * r : 2 * r + 2]
    for k, ref in enumerate((out_b_ref, gain_two_ref, offset_two_ref, down_b_ref)):
        values = line(ref, 3)
        for r in range(3):
            rows_ref[30:31, 4 * r + k : 4 * r + k + 1] = values[:, r : r + 1]
    rows_ref[30:31, 12:24] = line(up_b_ref, 12)
    rows_ref[31:32, :] = out_w_ref[...].astype(f32)[2:3, 256:384]
    out_ref[...] = jnp.broadcast_to(rows_ref[...].astype(bf16)[None], out_ref.shape)


def pack_second(out_w_ref, up_ref, down_ref, out_ref, rows_ref):
    out_w = out_w_ref[...].astype(f32)
    up = up_ref[...].astype(f32)
    down = down_ref[...].astype(f32)
    for k in range(8):
        rows_ref[k : k + 1, :] = out_w[k // 3 : k // 3 + 1, 128 * (k % 3) : 128 * (k % 3) + 128]
    for k in range(36):
        rows_ref[8 + k : 9 + k, :] = up[k // 12 : k // 12 + 1, 128 * (k % 12) : 128 * (k % 12) + 128]
        rows_ref[44 + k : 45 + k, :] = down[k // 3 : k // 3 + 1, 128 * (k % 3) : 128 * (k % 3) + 128]
    out_ref[...] = jnp.broadcast_to(rows_ref[...].astype(bf16)[None], out_ref.shape)


def merge_slots(raw_ref, merged_ref):
    both = jnp.swapaxes(raw_ref[...], 0, 1)
    for slot in range(both.shape[0]):
        at = slot * ROWS
        merged_ref[at + ROWS - 16 : at + ROWS, :] = jnp.zeros((16, WIDTH), bf16)
        merged_ref[at : at + SPAN, :] = both[slot]


def run_pack_first(*args):
    return pl.pallas_call(
        pack_first,
        out_shape=pltpu.HBM((CHIPS, FIRST_ROWS, 128), bf16),
        scratch_shapes=[pltpu.VMEM((FIRST_ROWS, 128), f32)],
        compiler_params=params(8),
        cost_estimate=cost(2),
        name="pack_first",
    )(*far(*args))


def run_pack_second(*args):
    return pl.pallas_call(
        pack_second,
        out_shape=pltpu.HBM((CHIPS, SECOND_ROWS, 128), bf16),
        scratch_shapes=[pltpu.VMEM((SECOND_ROWS, 128), f32)],
        compiler_params=params(8),
        cost_estimate=cost(2),
        name="pack_second",
    )(*far(*args))


def total(arrived_ref):
    return jnp.sum(arrived_ref[...].astype(f32), axis=0)


def spread_lanes(rows, lane, width):
    index = lax.broadcasted_iota(jnp.int32, (1, width), 1)
    out = jnp.zeros((1, width), f32)
    for k, row in enumerate(rows):
        out = jnp.where(index == k, row[:, lane : lane + 1], out)
    return out.reshape(width)


def unpack_first(arrived_ref, qkv_ref, gain_ref, offset_ref, qv_ref):
    sums = total(arrived_ref)
    more = []
    for r in range(3):
        for j in range(9):
            qkv_ref[r : r + 1, 128 * j : 128 * j + 128] = sums[10 * r + j : 10 * r + j + 1, :]
        row = sums[10 * r + 9 : 10 * r + 10, :]
        more.append(row[:, 0:4] + row[:, 4:8])
    gain_ref[...] = spread_lanes(more, 0, 3)
    offset_ref[...] = spread_lanes(more, 1, 3)
    index = lax.broadcasted_iota(jnp.int32, (1, 6), 1)
    out = jnp.zeros((1, 6), f32)
    for k in range(6):
        out = jnp.where(index == k, more[k // 2][:, 2 + k % 2 : 3 + k % 2], out)
    qv_ref[...] = out.reshape(6)


def run_unpack_first(arrived):
    return pl.pallas_call(
        unpack_first,
        out_shape=[shape_of((3, 3 * WIDTH), f32), shape_of((3,), f32), shape_of((3,), f32), shape_of((6,), f32)],
        compiler_params=params(8),
        cost_estimate=cost(2),
        name="unpack_first",
    )(arrived)


def sum_column(line_ref, arrived_ref, keep_ref, one_ref, two_ref, three_ref, sums_ref):
    sums_ref[...] = total(arrived_ref)
    block = lambda shift: sums_ref[pl.ds(pl.multiple_of(lax.rem(line_ref[0] + shift, LINE) * REST_ROWS, 8), REST_ROWS), :]
    keep_ref[...] = block(0)
    for shift, ref in enumerate((one_ref, two_ref, three_ref)):
        ref[...] = block(shift + 1).astype(bf16)


def run_sum_column(line, arrived):
    arrays = pl.BlockSpec(memory_space=pltpu.VMEM)
    part = shape_of((REST_ROWS, 128), bf16)
    return pl.pallas_call(
        sum_column,
        in_specs=[pl.BlockSpec(memory_space=pltpu.SMEM), arrays],
        out_shape=[shape_of((REST_ROWS, 128), f32), part, part, part],
        scratch_shapes=[pltpu.VMEM((LINE * REST_ROWS, 128), f32)],
        compiler_params=params(12),
        cost_estimate=cost(2),
        name="sum_column",
    )(line, arrived)


def unpack_rest(keep_ref, one_ref, two_ref, three_ref, out_ref, up_ref, down_ref, out_b_ref, gain_ref, offset_ref, down_b_ref, up_b_ref, pairs_ref, turned_ref):
    sums = keep_ref[...] + sum(ref[...].astype(f32) for ref in (one_ref, two_ref, three_ref))
    more = []
    for r in range(3):
        for j in range(3):
            out_ref[r : r + 1, 128 * j : 128 * j + 128] = sums[3 * r + j : 3 * r + j + 1, :]
        line = sums[9 + 12 * r : 21 + 12 * r, :]
        pairs_ref[pl.ds(24 * r, 12, stride=2), 0:64] = line[:, 0:64]
        pairs_ref[pl.ds(24 * r + 1, 12, stride=2), 0:64] = line[:, 64:128]
        row = sums[81 + r : 82 + r, :]
        more.append(row[:, 0:4] + row[:, 4:8])
    turned_ref[...] = pairs_ref[...].T
    by_line = [turned_ref[pl.ds(y, 16, stride=4), :] for y in range(LINE)]
    for r in range(3):
        pieces = [by_line[y][:, 24 * r + 12 * c : 24 * r + 12 * c + 12] for c in range(2) for y in range(LINE)]
        lines = jnp.concatenate(pieces, 1)
        for column in range(16):
            up_ref[r : r + 1, 96 * column : 96 * column + 96] = lines[column : column + 1]
    for r in range(12):
        for j in range(3):
            down_ref[r : r + 1, 128 * j : 128 * j + 128] = sums[45 + 3 * r + j : 46 + 3 * r + j, :]
    for k, ref in enumerate((out_b_ref, gain_ref, offset_ref, down_b_ref)):
        ref[...] = spread_lanes(more, k, 3)
    up_b_ref[...] = (sums[84:85, 0:12] + sums[84:85, 12:24]).reshape(12)


def run_unpack_rest(*parts):
    return pl.pallas_call(
        unpack_rest,
        out_shape=[shape_of((3, WIDTH), f32), shape_of((3, HIDDEN), f32), shape_of((12, WIDTH), f32)]
        + [shape_of((3,), f32)] * 4
        + [shape_of((12,), f32)],
        scratch_shapes=[pltpu.VMEM((128, 128), f32), pltpu.VMEM((128, 128), f32)],
        compiler_params=params(12),
        cost_estimate=cost(2),
        name="unpack_rest",
    )(*parts)


def add_halves(mine_ref, theirs_ref, out_ref):
    out_ref[...] = (mine_ref[...].astype(f32) + theirs_ref[...].astype(f32)).astype(bf16)


def run_add_halves(mine, theirs):
    arrays = pl.BlockSpec(memory_space=pltpu.VMEM)
    return pl.pallas_call(
        add_halves,
        in_specs=[arrays, arrays],
        out_shape=pltpu.HBM(mine.shape, bf16),
        compiler_params=params(12),
        cost_estimate=cost(1),
        name="add_halves",
    )(*held(mine, theirs))


def forward_scores(unit, projected_ref, bias_ref, key_ref, value_ref, more):
    slot, base = unit
    scale = math.log2(math.e) / math.sqrt(HEAD)
    lanes = slice(slot * WIDE, slot * WIDE + WIDE)
    query_more, key_more, value_more = more[slot]
    wide = lambda start: jnp.concatenate([bias_ref[start : start + HEAD, :]] * (WIDE // 128), 1)
    queries, scores = [], []
    for h in range(base, base + FORWARD_BATCH):
        at = h * HEAD
        query = (projected_ref[at : at + HEAD, lanes] + wide(at)) * scale
        key = projected_ref[at + WIDTH : at + WIDTH + HEAD, lanes]
        value = projected_ref[at + 2 * WIDTH : at + 2 * WIDTH + HEAD, lanes] + wide(at + WIDTH)
        query = jnp.concatenate([query, query_more], 0)
        key = jnp.concatenate([key, key_more], 0).astype(bf16)
        key_ref[slot, 32 * h : 32 * h + 32, :] = key
        value_ref[slot, 32 * h : 32 * h + 32, :] = jnp.concatenate([value, value_more], 0).astype(bf16)
        low = query.astype(bf16)
        queries.append(query)
        scores.append([dot(key[:, :count], low[:, a:b], (0, 0)) for a, b, count in FORWARD_BLOCKS])
    return queries, scores


def forward_mixed(unit, queries, scores, mixed_scratch, query_ref, value_ref):
    slot, base = unit
    heads = range(base, base + FORWARD_BATCH)
    peaks = [[jnp.max(part, axis=0, keepdims=True) for part in parts] for parts in scores]
    weights = [[jnp.exp2(part - top).astype(bf16) for part, top in zip(*pair)] for pair in zip(scores, peaks)]
    values = [value_ref[slot, 32 * h : 32 * h + 32, :] for h in heads]
    got = [
        [dot(value[:, :count], part, (1, 0)) for part, (_, _, count) in zip(parts, FORWARD_BLOCKS)]
        for value, parts in zip(values, weights)
    ]
    zero = jnp.zeros((1, WIDE), f32)
    for h, query, tops, parts in zip(heads, queries, peaks, got):
        both = jnp.concatenate(parts, 1)
        row_total = both[HEAD : HEAD + 1]
        mixed_scratch[h * HEAD : h * HEAD + HEAD, :] = both[:HEAD] * (1.0 / row_total)
        logs = jnp.concatenate(tops, 1) + jnp.log2(row_total)
        log_rows = rows_of([zero, zero, zero, *three_parts(-logs)], WIDE)
        query_ref[slot, 32 * h : 32 * h + 32, :] = (query + jnp.concatenate([jnp.zeros((HEAD, WIDE), f32), log_rows], 0)).astype(bf16)


def forward_probs(unit, query_ref, key_ref, refs):
    slot, base = unit
    for h in range(base, base + FORWARD_BATCH):
        query, key = query_ref[slot, 32 * h : 32 * h + 32, :], key_ref[slot, 32 * h : 32 * h + 32, :]
        for ref, (start, a, b) in zip(refs, BACKWARD_BLOCKS):
            ref[h] = jnp.exp2(dot(query[:, start:ROWS], key[:, a:b], (0, 0))).astype(bf16)


def attention_forward(core_ref, counts_ref, tokens_far, own_ref, other_ref,
                      mixed_far, query_far, key_far, value_far, weight_far, first_far, merged_far, low_far, middle_far, high_far, column_far, extra_far,
                      first_ref, projected_ref, mixed_scratch, arrived_ref, bias_ref,
                      raw_ref, tokens_ref, mixed_ref, query_ref, key_ref, value_ref, weight_ref, low_ref, middle_ref, high_ref, column_ref, extra_ref, semaphores):
    slots = mixed_ref.shape[0]
    copies = Copies(semaphores)
    copies.start(tokens_far, raw_ref)
    core = core_ref[0]
    for k, (side, ref) in enumerate(((core, own_ref), (1 - core, other_ref))):
        blocks = jnp.swapaxes(ref[...], 0, 1)
        for r in range(3):
            at = pl.multiple_of(side * 192 + 64 * r, 64)
            for j in range(10):
                arrived_ref[pl.ds(at, 64), 128 * j : 128 * j + 128] = blocks[10 * r + j]
        extra_ref[2 * k] = blocks[30]
        extra_ref[2 * k + 1] = blocks[31]
    order = arrival_order()
    ordered = dot(order, arrived_ref[...], (1, 0))
    weight_ref[...] = ordered[:, : 3 * WIDTH].astype(bf16)
    column_ref[...] = ordered[:, 3 * WIDTH :]
    rows = dot(arrived_ref[:, 3 * WIDTH :], order, (0, 1))
    gain, offset = rows[0:1], rows[1:2]
    for s in range(2):
        column = ordered[:, 3 * WIDTH + 2 + s : 3 * WIDTH + 3 + s]
        bias_ref[pl.ds(s, WIDTH, stride=2), :] = jnp.broadcast_to(column, (WIDTH, 128))
    first_ref[...] = jnp.zeros_like(first_ref)
    copies.wait_all()
    merge_slots(raw_ref, tokens_ref)
    copies.start(tokens_ref, merged_far)
    copies.start(weight_ref, weight_far)
    copies.start(column_ref, column_far)
    copies.start(extra_ref, extra_far)
    for slot in range(slots):
        normed, _ = norm_parts(tokens_ref[slot * ROWS : slot * ROWS + ROWS, :].astype(f32))
        first_ref[slot * WIDE : slot * WIDE + ROWS, :] = (normed * gain + offset).astype(bf16)
    copies.start(first_ref, first_far)
    projected_ref[...] = dot(weight_ref[...], first_ref[...], (0, 1))
    one = jnp.ones((1, WIDE), f32)
    more = []
    for slot in range(slots):
        hidden, frame = mask_rows(counts_ref, slot)
        more.append((rows_of(frame, WIDE), rows_of(hidden + [one, one, one], WIDE), rows_of([one, one, one], WIDE)))
    units = [(slot, base) for slot in range(slots) for base in range(0, HEADS, FORWARD_BATCH)]
    refs = (low_ref, middle_ref, high_ref)
    kept = {}

    def probs(unit):
        slot, base = unit
        if units.index(unit) >= KEPT_UNITS:
            return
        copies.wait(*kept.get((slot - 1, base // LOAD_BATCH), ()))
        forward_probs(unit, query_ref, key_ref, refs)
        if (base + FORWARD_BATCH) % LOAD_BATCH == 0:
            part = pl.ds(base // LOAD_BATCH * LOAD_BATCH, LOAD_BATCH)
            pairs = zip(refs, (low_far, middle_far, high_far))
            kept[slot, base // LOAD_BATCH] = [copies.start(near.at[part], away.at[slot, part]) for near, away in pairs]

    ready = forward_scores(units[0], projected_ref, bias_ref, key_ref, value_ref, more)
    for k, unit in enumerate(units):
        slot = unit[0]
        now, ready = ready, None
        if k + 1 < len(units):
            ready = forward_scores(units[k + 1], projected_ref, bias_ref, key_ref, value_ref, more)
        forward_mixed(unit, *now, mixed_scratch, query_ref, value_ref)
        if unit[1] + FORWARD_BATCH == HEADS:
            mixed_ref[slot] = mixed_scratch[...].astype(bf16)
            for near, away in ((key_ref, key_far), (value_ref, value_far), (query_ref, query_far), (mixed_ref, mixed_far)):
                copies.start(near.at[slot], away.at[slot])
        if k >= 1:
            probs(units[k - 1])
    probs(units[-1])
    copies.wait_all()


def probs_shapes():
    return [(ROWS - start, b - a) for start, a, b in BACKWARD_BLOCKS]


def run_forward(core, counts, tokens, own, other):
    slots = tokens.shape[1]
    scalars = pl.BlockSpec(memory_space=pltpu.SMEM)
    arrays = pl.BlockSpec(memory_space=pltpu.VMEM)
    away = pl.BlockSpec(memory_space=pl.ANY)
    return pl.pallas_call(
        attention_forward,
        in_specs=[scalars, scalars, away, arrays, arrays],
        out_specs=[away] * 12,
        out_shape=[pltpu.HBM((slots, rows, WIDE), bf16) for rows in (WIDTH, 512, 512, 512)]
        + [pltpu.HBM((WIDTH, 3 * WIDTH), bf16), pltpu.HBM((slots * WIDE, WIDTH), bf16), pltpu.HBM((slots * ROWS, WIDTH), bf16)]
        + [pltpu.HBM((slots, HEADS, *shape), bf16) for shape in probs_shapes()]
        + [pltpu.HBM((WIDTH, 128), f32), pltpu.HBM((4, 64, 128), bf16)],
        scratch_shapes=[
            pltpu.VMEM((slots * WIDE, WIDTH), bf16),
            pltpu.VMEM((3 * WIDTH, slots * WIDE), f32),
            pltpu.VMEM((WIDTH, WIDE), f32),
            pltpu.VMEM((WIDTH, 3 * WIDTH + 128), bf16),
            pltpu.VMEM((2 * WIDTH + 8, 128), f32),
            pltpu.VMEM((SPAN, slots, WIDTH), bf16),
            pltpu.VMEM((slots * ROWS, WIDTH), bf16),
        ]
        + [pltpu.VMEM((slots, rows, WIDE), bf16) for rows in (WIDTH, 512, 512, 512)]
        + [pltpu.VMEM((WIDTH, 3 * WIDTH), bf16)]
        + [pltpu.VMEM((HEADS, *shape), bf16) for shape in probs_shapes()]
        + [pltpu.VMEM((WIDTH, 128), f32), pltpu.VMEM((4, 64, 128), bf16), pltpu.SemaphoreType.DMA((40,))],
        compiler_params=params(48),
        cost_estimate=cost(20),
        name="attention_forward",
    )(core, counts, *far(tokens), *held(own, other))


def feed_forward_early(cotangent_far, merged_far, mixed_far, extra_far, own_ref,
                       arrived_ref, down_ref, up_b_ref, cotangent_ref, tokens_ref, mixed_ref, slopes_ref, extra_ref, raw_ref, semaphores):
    copies = Copies(semaphores)
    extra = copies.start(extra_far, extra_ref)
    raw = copies.start(cotangent_far, raw_ref)
    copies.start(mixed_far, mixed_ref)
    copies.start(merged_far, tokens_ref)
    unpack_side(own_ref, lambda: (copies.wait(extra), extra_ref[0], extra_ref[1])[1:], arrived_ref, down_ref, up_b_ref)
    copies.wait(raw)
    merge_slots(raw_ref, cotangent_ref)
    slopes_ref[...] = dot(cotangent_ref[...], down_ref[...], (1, 1))
    copies.wait_all()


def unpack_side(message_ref, extra, arrived_ref, down_ref, up_b_ref):
    blocks = jnp.swapaxes(message_ref[...], 0, 1)
    for r in range(12):
        for j in range(3):
            down_ref[64 * r : 64 * r + 64, 128 * j : 128 * j + 128] = blocks[44 + 3 * r + j]
    for r in range(3):
        for j in range(12):
            arrived_ref[64 * r : 64 * r + 64, 384 + 128 * j : 512 + 128 * j] = blocks[8 + 12 * r + j]
    vectors, tile = extra()
    vectors = vectors.astype(f32)
    for r in range(3):
        rows = slice(64 * r, 64 * r + 64)
        for j in range(3):
            arrived_ref[rows, 128 * j : 128 * j + 128] = tile if 3 * r + j == 8 else blocks[3 * r + j]
        arrived_ref[rows, 1920:2048] = (pltpu.roll(vectors, 128 - 4 * r, 1) if r else vectors).astype(bf16)
    turned = vectors.T
    up_b_ref[0:1, :] = jnp.concatenate([turned[12 + r : 13 + r] for r in range(12)], 1)


def run_feed_forward_early(cotangent, merged, mixed, own, extra):
    _, slots, _ = cotangent.shape
    arrays = pl.BlockSpec(memory_space=pltpu.VMEM)
    away = pl.BlockSpec(memory_space=pl.ANY)
    return pl.pallas_call(
        feed_forward_early,
        in_specs=[away, away, away, away, arrays],
        out_shape=[
            pltpu.VMEM((WIDTH // 2, 2048), bf16),
            pltpu.VMEM((HIDDEN // 2, WIDTH), bf16),
            pltpu.VMEM((8, HIDDEN // 2), f32),
            pltpu.VMEM((slots * ROWS, WIDTH), bf16),
            pltpu.VMEM((slots * ROWS, WIDTH), bf16),
            pltpu.VMEM((slots, WIDTH, WIDE), bf16),
            pltpu.VMEM((slots * ROWS, HIDDEN // 2), f32),
            pltpu.VMEM((4, 64, 128), bf16),
        ],
        scratch_shapes=[pltpu.VMEM((SPAN, slots, WIDTH), bf16), pltpu.SemaphoreType.DMA((4,))],
        compiler_params=params(16),
        cost_estimate=cost(3),
        name="feed_forward_early",
    )(*far(cotangent, merged, mixed, extra), *held(own))


def feed_forward(core_ref, tokens_ref, mixed_ref, cotangent_ref, own_arrived_ref, own_down_ref, own_up_b_ref, slopes_ref, other_ref, extra_ref,
                 activated_ref, resid_ref, other_down_ref, row_ref, grad_resid_far, grad_mixed_far, mine_ref, theirs_ref,
                 arrived_ref, ordered_ref, up_b_ref, packed_ref, grad_down_ref, grad_resid_ref, grad_mixed_ref, second_ref, grad_up_ref,
                 semaphores):
    slots = mixed_ref.shape[0]
    block = 256
    root = math.sqrt(2.0 / math.pi)
    copies = Copies(semaphores)
    core = core_ref[0]
    sides = (core, 1 - core)
    places = [pl.multiple_of(side * (WIDTH // 2), 64) for side in sides]
    unpack_side(other_ref, lambda: (extra_ref[2], extra_ref[3]), arrived_ref, other_down_ref, up_b_ref)
    downs = (own_down_ref, other_down_ref)
    up_bs = (own_up_b_ref, up_b_ref)
    order = arrival_order()
    packed_ref[pl.ds(places[0], WIDTH // 2), :] = own_arrived_ref[...]
    packed_ref[pl.ds(places[1], WIDTH // 2), :] = arrived_ref[...]
    row_ref[...] = dot(packed_ref[:, 1920:], order, (0, 1))[0:8]
    ordered_ref[...] = dot(order, packed_ref[:, :1920], (1, 0)).astype(bf16)
    out_w = ordered_ref[:, :WIDTH]
    up_w = lambda half, at: ordered_ref[:, pl.ds(pl.multiple_of(WIDTH + sides[half] * (HIDDEN // 2) + at, 128), block)]
    out_b, gain, offset = (row_ref[k : k + 1] for k in range(3))
    spans = [slice(slot * ROWS, slot * ROWS + ROWS) for slot in range(slots)]
    norms = {}

    def enter(slot):
        resid = tokens_ref[spans[slot], :].astype(f32) + dot(mixed_ref[slot, :, :ROWS], out_w, (0, 0)) + out_b
        resid_ref[spans[slot], :] = resid
        norms[slot] = norm_parts(resid)
        second_ref[spans[slot], :] = (norms[slot][0] * gain + offset).astype(bf16)

    def products(work):
        slot, half, at = work
        rows = spans[slot]
        up = dot(second_ref[rows, :], up_w(half, at), (1, 0))
        if half == 0:
            return up, slopes_ref[rows, at : at + block]
        return up, dot(cotangent_ref[rows, :], other_down_ref[at : at + block, :], (1, 1))

    lines = {}

    def activate(work, up, grad_activated):
        slot, half, at = work
        rows, cols = spans[slot], slice(half * (HIDDEN // 2) + at, half * (HIDDEN // 2) + at + block)
        up = up + up_bs[half][0:1, at : at + block]
        square = up * up
        tanh = jnp.tanh(up * (root + (root * 0.044715) * square))
        half_tanh = 0.5 + 0.5 * tanh
        activated_ref[rows, cols] = (up * half_tanh).astype(bf16)
        slope = half_tanh + (up * (2.0 * half_tanh * (1.0 - half_tanh))) * (root + (3 * root * 0.044715) * square)
        grad_up = grad_activated * slope
        grad_up_ref[rows, cols] = grad_up.astype(bf16)
        line = jnp.sum(grad_up, axis=0, keepdims=True)
        lines[half, at] = lines[half, at] + line if (half, at) in lines else line

    works = [(slot, half, at) for slot in range(slots) for half in range(2) for at in range(0, HIDDEN // 2, block)]
    enter(0)
    ready = products(works[0])
    for slot in range(1, slots):
        enter(slot)
    for k, work in enumerate(works):
        now = ready
        if k + 1 < len(works):
            ready = products(works[k + 1])
        activate(work, *now)

    grad_branch = cotangent_ref[...]
    halves = [slice(0, HIDDEN // 2), slice(HIDDEN // 2, HIDDEN)]
    side_w = [ordered_ref[:, pl.ds(pl.multiple_of(WIDTH + side * (HIDDEN // 2), 128), HIDDEN // 2)] for side in sides]
    grad_seconds = [sum(dot(grad_up_ref[rows, cols], weight, (1, 1)) for cols, weight in zip(halves, side_w)) for rows in spans]
    attended, sums = [], []

    def leave(slot):
        normed, inverse = norms[slot]
        grad_second = grad_seconds[slot]
        scaled = grad_second * gain
        mean_one = jnp.mean(scaled, axis=-1, keepdims=True)
        mean_two = jnp.mean(scaled * normed, axis=-1, keepdims=True)
        grad_full = cotangent_ref[spans[slot], :].astype(f32)
        grad_resid = grad_full + inverse * (scaled - mean_one - normed * mean_two)
        grad_resid_ref[spans[slot], :] = grad_resid
        low = grad_resid.astype(bf16)
        attended.append(low)
        parts = [low.astype(f32), grad_second * normed, grad_second, grad_full]
        sums.append(jnp.concatenate([jnp.sum(part, axis=0, keepdims=True) for part in parts], 0))

    for slot in range(slots):
        leave(slot)
        cols = halves[slot % 2]
        grad_down_ref[cols, :] = dot(activated_ref[:, cols], grad_branch, (0, 0)).astype(bf16)
    copies.start(grad_resid_ref, grad_resid_far)
    for slot in range(slots):
        grad_mixed_ref[slot, :, 512:WIDE] = jnp.zeros((WIDTH, WIDE - 512), bf16)
        grad_mixed_ref[slot, :, :ROWS] = dot(out_w, attended[slot], (1, 1)).astype(bf16)
    copies.start(grad_mixed_ref, grad_mixed_far)
    grad_out = sum(dot(mixed_ref[slot, :, :ROWS], attended[slot], (1, 0)) for slot in range(slots))
    for side, cols in zip(sides, halves):
        at = pl.multiple_of(WIDTH + side * (HIDDEN // 2), 128)
        ordered_ref[:, pl.ds(at, HIDDEN // 2)] = dot(second_ref[...], grad_up_ref[:, cols], (0, 0)).astype(bf16)
    ordered_ref[:, :WIDTH] = grad_out.astype(bf16)
    packed_ref[:, :1920] = dot(order, ordered_ref[...], (0, 0)).astype(bf16)
    high, low = two_parts(sum(sums))
    rows = jnp.concatenate([high, low, jnp.zeros((120, WIDTH), f32)], 0).astype(bf16)
    packed_ref[:, 1920:] = dot(order, rows, (0, 1)).astype(bf16)
    blank = jnp.zeros((CHIPS, 128), bf16)
    for half, (place, ref) in enumerate(zip(places, (mine_ref, theirs_ref))):
        blocks = [blank] * REST_ROWS
        for r in range(3):
            at = pl.multiple_of(place + 64 * r, 64)
            for j in range(15):
                blocks[3 * r + j if j < 3 else 6 + 12 * r + j] = packed_ref[pl.ds(at, 64), 128 * j : 128 * j + 128]
            blocks[81 + r] = packed_ref[pl.ds(at, 64), 1920:2048]
        for r in range(12):
            at = half * (HIDDEN // 2) + 64 * r
            for j in range(3):
                blocks[45 + 3 * r + j] = grad_down_ref[at : at + 64, 128 * j : 128 * j + 128]
        high, low = two_parts(jnp.concatenate([lines[half, at] for at in range(0, HIDDEN // 2, block)], 1))
        rows = [part[:, 64 * r : 64 * r + 64] for part in (high, low) for r in range(12)]
        blocks[84] = rows_of(rows, 64, 128).T.astype(bf16)
        ref[...] = jnp.swapaxes(jnp.stack(blocks), 0, 1)
    copies.wait_all()


def run_feed_forward(core, tokens, mixed, cotangent, arrived, down, up_b, slopes, other, extra):
    slots = mixed.shape[0]
    arrays = pl.BlockSpec(memory_space=pltpu.VMEM)
    away = pl.BlockSpec(memory_space=pl.ANY)
    return pl.pallas_call(
        feed_forward,
        in_specs=[pl.BlockSpec(memory_space=pltpu.SMEM)] + [arrays] * 9,
        out_specs=[arrays, arrays, arrays, arrays, away, away, arrays, arrays],
        out_shape=[
            pltpu.VMEM((slots * ROWS, HIDDEN), bf16),
            pltpu.VMEM((slots * ROWS, WIDTH), f32),
            pltpu.VMEM((HIDDEN // 2, WIDTH), bf16),
            pltpu.VMEM((8, WIDTH), f32),
            pltpu.HBM((slots * ROWS, WIDTH), f32),
            pltpu.HBM((slots, WIDTH, WIDE), bf16),
            pltpu.VMEM((CHIPS, REST_ROWS, 128), bf16),
            pltpu.VMEM((CHIPS, REST_ROWS, 128), bf16),
        ],
        scratch_shapes=[
            pltpu.VMEM((WIDTH // 2, 2048), bf16),
            pltpu.VMEM((WIDTH, 1920), bf16),
            pltpu.VMEM((8, HIDDEN // 2), f32),
            pltpu.VMEM((WIDTH, 2048), bf16),
            pltpu.VMEM((HIDDEN, WIDTH), bf16),
            pltpu.VMEM((slots * ROWS, WIDTH), f32),
            pltpu.VMEM((slots, WIDTH, WIDE), bf16),
            pltpu.VMEM((slots * ROWS, WIDTH), bf16),
            pltpu.VMEM((slots * ROWS, HIDDEN), bf16),
            pltpu.SemaphoreType.DMA((2,)),
        ],
        compiler_params=params(34),
        cost_estimate=cost(17),
        name="feed_forward",
    )(core, *held(tokens, mixed, cotangent, arrived, down, up_b, slopes, other, extra))


def feed_forward_output(activated_ref, resid_ref, own_down_ref, other_down_ref, row_ref, out_ref):
    slots = out_ref.shape[1]
    half = HIDDEN // 2
    result = resid_ref[...] + row_ref[3:4]
    result += dot(activated_ref[:, :half], own_down_ref[...], (1, 0)) + dot(activated_ref[:, half:], other_down_ref[...], (1, 0))
    both = jnp.stack([result[slot * ROWS : slot * ROWS + SPAN] for slot in range(slots)])
    out_ref[...] = jnp.swapaxes(both, 0, 1).astype(bf16)


def run_feed_forward_output(*args):
    slots = args[1].shape[0] // ROWS
    return pl.pallas_call(
        feed_forward_output,
        out_shape=pltpu.HBM((SPAN, slots, WIDTH), bf16),
        compiler_params=params(20),
        cost_estimate=cost(3),
        name="feed_forward_output",
    )(*held(*args))


def backward_slopes(unit, copies, loads, value_ref, mixed_ref, grad_mixed_ref):
    slot, base = unit
    copies.wait(*loads["grad"][slot])
    grads, slopes = [], []
    for h in range(base, base + BACKWARD_BATCH):
        both = slice(48 * (h // 2), 48 * (h // 2) + 48)
        part = slice(HEAD * (h % 2), HEAD * (h % 2) + HEAD)
        grad = grad_mixed_ref[slot, both, :].astype(f32)[part]
        mixed = mixed_ref[slot, both, :].astype(f32)[part]
        shift = jnp.sum(grad * mixed, axis=0, keepdims=True)
        grad = jnp.concatenate([grad, rows_of(three_parts(-shift), WIDE)], 0).astype(bf16)
        value = value_ref[slot, 32 * h : 32 * h + 32, :]
        grads.append(grad)
        slopes.append([dot(grad[:, start:ROWS], value[:, a:b], (0, 0)) for start, a, b in BACKWARD_BLOCKS])
    return grads, slopes


def backward_products(unit, grads, slopes, copies, loads, query_ref, key_ref, probs_refs, turned_ref):
    slot, base = unit
    heads = range(base, base + BACKWARD_BATCH)
    copies.wait(*loads["query"][slot])
    queries = [query_ref[slot, 32 * h : 32 * h + 32, :] for h in heads]
    keys = [key_ref[slot, 32 * h : 32 * h + 32, :] for h in heads]
    if (slot * HEADS + base) // LOAD_BATCH < KEPT_UNITS:
        copies.wait(*loads["probs"][slot][base // LOAD_BATCH])
        probs = [[ref[slot, h].astype(f32) for ref in probs_refs] for h in heads]
    else:
        probs = [
            [jnp.exp2(dot(query[:, start:ROWS], key[:, a:b], (0, 0))) for start, a, b in BACKWARD_BLOCKS]
            for query, key in zip(queries, keys)
        ]
    grad_scores = [[(part * slope).astype(bf16) for part, slope in zip(*pair)] for pair in zip(probs, slopes)]
    probs = [[part.astype(bf16) for part in parts] for parts in probs]
    over = lambda left, parts: jnp.concatenate(
        [dot(left[:, start:ROWS], part, (1, 0)) for part, (start, _, _) in zip(parts, BACKWARD_BLOCKS)], 1)
    grad_v = [over(grad, parts) for grad, parts in zip(grads, probs)]
    grad_k = [over(query, parts) for query, parts in zip(queries, grad_scores)]
    grad_q = [
        [dot(key[:, a:b], part, (1, 1)) for part, (_, a, b) in zip(parts, BACKWARD_BLOCKS)]
        for key, parts in zip(keys, grad_scores)
    ]
    fill = lambda part: jnp.concatenate([jnp.zeros((32, ROWS - part.shape[1]), f32), part], 1) if part.shape[1] < ROWS else part
    lanes = slice(slot * WIDE, slot * WIDE + WIDE)
    blank = jnp.zeros((HEAD, WIDE - ROWS), f32)
    for k, h in enumerate(heads):
        at = h * HEAD
        whole = sum(fill(part) for part in grad_q[k])[:HEAD] * (1.0 / math.sqrt(HEAD))
        turned_ref[at : at + HEAD, lanes] = jnp.concatenate([whole, blank], 1)
        turned_ref[at + WIDTH : at + WIDTH + HEAD, lanes] = grad_k[k][:HEAD] * math.log(2.0)
        turned_ref[at + 2 * WIDTH : at + 2 * WIDTH + HEAD, lanes] = grad_v[k][:HEAD]


def attention_backward(core_ref, query_far, key_far, value_far, mixed_far, grad_mixed_far, low_far, middle_far, high_far, first_far, weight_far,
                       column_far, turned_far, mine_ref, theirs_ref,
                       turned_ref, bias_ref, packed_ref, turned_low_ref,
                       query_ref, key_ref, value_ref, mixed_ref, grad_mixed_ref, low_ref, middle_ref, high_ref, first_ref, weight_ref, column_ref, semaphores):
    slots = mixed_ref.shape[0]
    copies = Copies(semaphores)
    loads = {"grad": [], "probs": [], "query": []}
    probs_refs = (low_ref, middle_ref, high_ref)
    for slot in range(slots):
        load = lambda pairs: [copies.start(away.at[slot], near.at[slot]) for away, near in pairs]
        loads["grad"].append(load(((value_far, value_ref), (grad_mixed_far, grad_mixed_ref), (mixed_far, mixed_ref))))
        loads["probs"].append([])
        for base in range(0, HEADS, LOAD_BATCH):
            if (slot * HEADS + base) // LOAD_BATCH < KEPT_UNITS:
                part = pl.ds(base, LOAD_BATCH)
                pairs = zip((low_far, middle_far, high_far), probs_refs)
                loads["probs"][slot].append([copies.start(away.at[slot, part], near.at[slot, part]) for away, near in pairs])
            if base == 0:
                loads["query"].append(load(((query_far, query_ref), (key_far, key_ref))))
    weights = [copies.start(first_far, first_ref), copies.start(weight_far, weight_ref), copies.start(column_far, column_ref)]
    core = core_ref[0]
    sums = jnp.zeros((3 * WIDTH, 1), f32)
    units = [(slot, base) for slot in range(slots) for base in range(0, HEADS, BACKWARD_BATCH)]
    ready = backward_slopes(units[0], copies, loads, value_ref, mixed_ref, grad_mixed_ref)
    for k, unit in enumerate(units):
        slot = unit[0]
        now, ready = ready, None
        if k + 1 < len(units):
            ready = backward_slopes(units[k + 1], copies, loads, value_ref, mixed_ref, grad_mixed_ref)
        backward_products(unit, *now, copies, loads, query_ref, key_ref, probs_refs, turned_ref)
        if unit[1] + BACKWARD_BATCH == HEADS:
            turned = turned_ref[:, slot * WIDE : slot * WIDE + WIDE]
            sums += jnp.sum(turned, axis=1, keepdims=True)
            turned_low_ref[slot] = turned.astype(bf16)
            copies.start(turned_low_ref.at[slot], turned_far.at[slot])
    copies.wait(*weights)
    order = arrival_order()
    turned = jnp.concatenate([turned_low_ref[slot] for slot in range(slots)], 1)
    grad_weight = dot(first_ref[...], turned, (0, 1))
    packed_ref[:, : 3 * WIDTH] = dot(order, grad_weight.astype(bf16), (0, 0)).astype(bf16)
    lane = lax.broadcasted_iota(jnp.int32, (3 * WIDTH, 128), 1)
    high, low = two_parts(sums)
    spread = jnp.where(lane == 0, high, jnp.where(lane == 1, low, 0.0)).astype(bf16)
    against = dot(weight_ref[...], spread, (1, 0))
    grad_offset = against[:, 0:1] + against[:, 1:2]
    along = jnp.sum(grad_weight * weight_ref[...].astype(f32), axis=1, keepdims=True)
    grad_gain = (along - column_ref[:, 1:2] * grad_offset) / column_ref[:, 0:1]
    bias_ref[0:WIDTH] = jnp.broadcast_to(sums[:WIDTH], (WIDTH, 128))
    bias_ref[WIDTH : 2 * WIDTH] = jnp.broadcast_to(sums[2 * WIDTH :], (WIDTH, 128))
    lane = lax.broadcasted_iota(jnp.int32, (WIDTH, 128), 1)
    columns = jnp.zeros((WIDTH, 128), f32)
    for k, values in enumerate((grad_gain, grad_offset, bias_ref[pl.ds(0, WIDTH, stride=2), :], bias_ref[pl.ds(1, WIDTH, stride=2), :])):
        high, low = two_parts(values)
        columns = jnp.where(lane == k, high, jnp.where(lane == 4 + k, low, columns))
    packed_ref[:, 3 * WIDTH :] = dot(order, columns.astype(bf16), (0, 0)).astype(bf16)
    blank = jnp.zeros((CHIPS, 128), bf16)
    for side, ref in ((core, mine_ref), (1 - core, theirs_ref)):
        blocks = []
        for r in range(3):
            at = pl.multiple_of(side * 192 + 64 * r, 64)
            for j in range(10):
                blocks.append(packed_ref[pl.ds(at, 64), 128 * j : 128 * j + 128])
        ref[...] = jnp.swapaxes(jnp.stack(blocks + [blank, blank]), 0, 1)
    copies.wait_all()


def run_backward(core, query, key, value, mixed, grad_mixed, low, middle, high, first, weight, column):
    slots = mixed.shape[0]
    arrays = pl.BlockSpec(memory_space=pltpu.VMEM)
    away = pl.BlockSpec(memory_space=pl.ANY)
    return pl.pallas_call(
        attention_backward,
        in_specs=[pl.BlockSpec(memory_space=pltpu.SMEM)] + [away] * 11,
        out_specs=[away, arrays, arrays],
        out_shape=[
            pltpu.HBM((slots, 3 * WIDTH, WIDE), bf16),
            pltpu.VMEM((CHIPS, FIRST_ROWS, 128), bf16),
            pltpu.VMEM((CHIPS, FIRST_ROWS, 128), bf16),
        ],
        scratch_shapes=[
            pltpu.VMEM((3 * WIDTH, slots * WIDE), f32),
            pltpu.VMEM((2 * WIDTH + 8, 128), f32),
            pltpu.VMEM((WIDTH, 3 * WIDTH + 128), bf16),
            pltpu.VMEM((slots, 3 * WIDTH, WIDE), bf16),
        ]
        + [pltpu.VMEM((slots, rows, WIDE), bf16) for rows in (512, 512, 512, WIDTH, WIDTH)]
        + [pltpu.VMEM((slots, HEADS, *shape), bf16) for shape in probs_shapes()]
        + [pltpu.VMEM((slots * WIDE, WIDTH), bf16), pltpu.VMEM((WIDTH, 3 * WIDTH), bf16), pltpu.VMEM((WIDTH, 128), f32), pltpu.SemaphoreType.DMA((70,))],
        compiler_params=params(56),
        cost_estimate=cost(22),
        name="attention_backward",
    )(core, *far(query, key, value, mixed, grad_mixed, low, middle, high, first, weight, column))


def input_backward(merged_far, turned_far, grad_resid_far, weight_far, column_far, out_far,
                   tokens_ref, turned_ref, grad_resid_ref, weight_ref, grad_first_ref, out_ref, column_ref, semaphores):
    slots = turned_ref.shape[0]
    copies = Copies(semaphores)
    first = [copies.start(weight_far, weight_ref), copies.start(turned_far.at[0], turned_ref.at[0])]
    turns = [copies.start(turned_far.at[slot], turned_ref.at[slot]) for slot in range(1, slots)]
    rest = [copies.start(column_far, column_ref), copies.start(merged_far, tokens_ref), copies.start(grad_resid_far, grad_resid_ref)]
    copies.wait(*first)
    for slot in range(slots):
        if slot:
            copies.wait(turns[slot - 1])
        grad_first_ref[slot * ROWS : slot * ROWS + ROWS, :] = dot(turned_ref[slot, :, :ROWS], weight_ref[...], (0, 1))
    copies.wait(*rest)
    gain = column_ref[...].T[0:1]
    half = ROWS // 2
    for low, high in ((0, half), (half, SPAN)):
        for slot in range(slots):
            at = slice(slot * ROWS + low, slot * ROWS + low + half)
            normed, inverse = norm_parts(tokens_ref[at, :].astype(f32))
            scaled = grad_first_ref[at, :] * gain
            mean_one = jnp.mean(scaled, axis=-1, keepdims=True)
            mean_two = jnp.mean(scaled * normed, axis=-1, keepdims=True)
            grad = grad_resid_ref[at, :] + inverse * (scaled - mean_one - normed * mean_two)
            out_ref[low:high, slot, :] = grad[: high - low]
        copies.start(out_ref.at[pl.ds(low, high - low)], out_far.at[pl.ds(low, high - low)])
    copies.wait_all()


def run_input_backward(merged, turned, grad_resid, weight, column):
    slots = turned.shape[0]
    arrays = pl.BlockSpec(memory_space=pltpu.VMEM)
    away = pl.BlockSpec(memory_space=pl.ANY)
    return pl.pallas_call(
        input_backward,
        in_specs=[away] * 5,
        out_specs=away,
        out_shape=pltpu.HBM((SPAN, slots, WIDTH), f32),
        scratch_shapes=[
            pltpu.VMEM((slots * ROWS, WIDTH), bf16),
            pltpu.VMEM((slots, 3 * WIDTH, WIDE), bf16),
            pltpu.VMEM((slots * ROWS, WIDTH), f32),
            pltpu.VMEM((WIDTH, 3 * WIDTH), bf16),
            pltpu.VMEM((slots * ROWS, WIDTH), f32),
            pltpu.VMEM((SPAN, slots, WIDTH), f32),
            pltpu.VMEM((WIDTH, 128), f32),
            pltpu.SemaphoreType.DMA((8,)),
        ],
        compiler_params=params(32),
        cost_estimate=cost(6),
        name="input_backward",
    )(*far(merged, turned, grad_resid, weight, column))


def to_chips(message):
    return lax.all_to_all(message, CHIP_AXES, 0, 0, tiled=True)


def to_column(message):
    return lax.all_to_all(message, COLUMN_AXES, 0, 0, tiled=True)


def along_line(message, shift):
    return lax.ppermute(message, LINE_AXIS, [(k, (k + shift) % LINE) for k in range(LINE)])


def across(message):
    return lax.ppermute(message, CORE_AXIS, [(0, 1), (1, 0)])


def shards(tokens, item_frames, ln1_gain, ln1_bias, qkv_weight, qv_bias, out_weight, out_bias, ln2_gain, ln2_bias,
           up_weight, up_bias, down_weight, down_bias, cotangent):
    together = lax.optimization_barrier
    core = lax.axis_index(CORE_AXIS).astype(jnp.int32).reshape(1)
    line = lax.axis_index(LINE_AXIS).astype(jnp.int32).reshape(1)
    first = run_pack_first(qkv_weight, ln1_gain, ln1_bias, qv_bias, out_weight, out_bias, ln2_gain, ln2_bias, down_bias, up_bias)
    first, up_weight = together((first, up_weight))
    first = to_chips(first)
    up_sent = up_weight.reshape(3, 16, 2, 4, 12).transpose(0, 2, 4, 1, 3).reshape(3, HIDDEN)
    second = run_pack_second(out_weight, up_sent, down_weight)
    tokens, cotangent = tokens.transpose(1, 0, 2), cotangent.transpose(1, 0, 2)
    first, second = together((first, second))
    first_other = across(first)
    second = to_chips(second)
    mixed, query, key, value, weight, normed, merged, low, middle, high, column, extra = run_forward(core, item_frames, tokens, first, first_other)
    second, mixed = together((second, mixed))
    other = across(second)
    arrived, own_down, up_b, turned_cotangent, near, near_mixed, slopes, extra = run_feed_forward_early(cotangent, merged, mixed, second, extra)
    activated, resid, other_down, row, grad_resid, grad_mixed, mine, theirs = run_feed_forward(
        core, near, near_mixed, turned_cotangent, arrived, own_down, up_b, slopes, other, extra)
    theirs = across(theirs)
    output = run_feed_forward_output(activated, resid, own_down, other_down, row)
    output, mine = together((output, mine))
    output = output.transpose(1, 0, 2)
    rest = run_add_halves(mine, theirs)
    rest, grad_mixed = together((rest, grad_mixed))
    rest = to_column(rest.reshape(CHIPS // LINE, LINE * REST_ROWS, 128))
    turned, mine, theirs = run_backward(core, query, key, value, mixed, grad_mixed, low, middle, high, normed, weight, column)
    theirs = across(theirs)
    own = run_add_halves(mine, theirs)
    own, rest = together((own, rest))
    own, turned = together((own, turned))
    own = to_chips(own)
    keep, *sent = run_sum_column(line, rest)
    sent = [along_line(part, shift + 1) for shift, part in enumerate(sent)]
    grad_out, grad_up, *others = run_unpack_rest(keep, *sent)
    grad_down, grad_out_b, grad_gain_two, grad_offset_two, grad_down_b, grad_up_b = others
    input_grad = run_input_backward(merged, turned, grad_resid, weight, column).transpose(1, 0, 2)
    grad_qkv, grad_gain, grad_offset, grad_qv = run_unpack_first(own)
    return (output, input_grad, grad_gain, grad_offset, grad_qkv, grad_qv, grad_out, grad_out_b, grad_gain_two, grad_offset_two,
            grad_up, grad_up_b, grad_down, grad_down_b)


def solution(mesh):
    split = Mesh(mesh.devices.reshape(4, 4, 2, mesh.shape["narrow"]), ALL)
    by_rank = lambda n: P(ALL, *([None] * (n - 1)))
    return jax.shard_map(
        shards,
        mesh=split,
        in_specs=tuple(by_rank(n) for n in (3, 2, 1, 1, 2, 1, 2, 1, 1, 1, 2, 1, 2, 1, 3)),
        out_specs=tuple(by_rank(n) for n in (3, 3, 1, 1, 2, 1, 2, 1, 1, 1, 2, 1, 2, 1)),
        check_vma=False,
    )
```

```python
import math

import jax
import jax.numpy as jnp
from jax import lax
from jax.experimental import pallas as pl
from jax.experimental.pallas import tpu as pltpu
from jax.sharding import Mesh
from jax.sharding import PartitionSpec as P

HEADS = 16
HEAD = 24
FRAME = 196
WIDTH = 384
HIDDEN = 1536
WIDE = 640
SPAN = 588
ROWS = 592
CHIPS = 64
FIRST_ROWS = 32
REST_ROWS = 88
SECOND_ROWS = 80
EPSILON = 1e-05
NEGATIVE = -1e30
bf16 = jnp.bfloat16
f32 = jnp.float32
FORWARD_BLOCKS = ((0, 128, 208), (128, 384, 400), (384, 640, 592))
FORWARD_BATCH = 8
LOAD_BATCH = 8
KEPT_HEADS = 24
BACKWARD_BATCH = 8
BACKWARD_BLOCKS = ((0, 0, 256), (192, 256, 512), (384, 512, 640))
ALL = ("wide_0", "wide_1", "wide_2", "narrow")
CHIP_AXES = ("wide_0", "wide_1", "narrow")
COLUMN_AXES = ("wide_0", "wide_1")
LINE_AXIS = "narrow"
LINE = 4
CORE_AXIS = "wide_2"


def dot(left, right, over):
    return lax.dot_general(left, right, (((over[0],), (over[1],)), ((), ())), preferred_element_type=f32)


def norm_parts(values):
    centred = values - jnp.mean(values, axis=-1, keepdims=True)
    inverse = lax.rsqrt(jnp.mean(centred * centred, axis=-1, keepdims=True) + EPSILON)
    return centred * inverse, inverse


def two_parts(values):
    high = values.astype(bf16).astype(f32)
    return high, values - high


def three_parts(values):
    high, rest = two_parts(values)
    middle, low = two_parts(rest)
    return high, middle, low


def rows_of(rows, width, count=8):
    index = lax.broadcasted_iota(jnp.int32, (count, width), 0)
    out = jnp.zeros((count, width), f32)
    for k, row in enumerate(rows):
        out = jnp.where(index == k, row, out)
    return out


def arrival_order():
    place = lax.broadcasted_iota(jnp.int32, (WIDTH, WIDTH), 1)
    feature = lax.broadcasted_iota(jnp.int32, (WIDTH, WIDTH), 0)
    core = (place >= WIDTH // 2).astype(jnp.int32)
    rest = place - core * (WIDTH // 2)
    row = rest >> 6
    chip = rest & 63
    return (feature == 3 * (8 * (chip >> 2) + 4 * core + (chip & 3)) + row).astype(f32).astype(bf16)


def mask_rows(counts_ref, slot):
    lane = lax.broadcasted_iota(jnp.int32, (1, WIDE), 1)
    first_end = counts_ref[slot, 0]
    second_end = first_end + counts_ref[slot, 1]
    third_end = second_end + counts_ref[slot, 2]
    group = [
        (f >= first_end).astype(jnp.int32) + (f >= second_end).astype(jnp.int32) + (f >= third_end).astype(jnp.int32)
        for f in range(3)
    ]
    hidden = []
    for f in range(3):
        row = jnp.full((1, WIDE), NEGATIVE, f32)
        for k in range(f + 1):
            seen = jnp.where(group[f] == group[k], 0.0, NEGATIVE).astype(f32)
            row = jnp.where((lane >= FRAME * k) & (lane < FRAME * (k + 1)), seen, row)
        hidden.append(row)
    frame = [((lane >= FRAME * f) & (lane < FRAME * (f + 1))).astype(f32) for f in range(3)]
    return hidden, frame


def params(mebibytes):
    return pltpu.CompilerParams(vmem_limit_bytes=mebibytes * 2**20)


def cost(microseconds):
    return pl.CostEstimate(flops=int(microseconds * 1.1e9), bytes_accessed=2**20, transcendentals=0)


def shape_of(shape, dtype):
    return jax.ShapeDtypeStruct(shape, dtype)


def held(*arrays):
    return [pltpu.with_memory_space_constraint(a, pltpu.VMEM) for a in arrays]


def far(*arrays):
    return [pltpu.with_memory_space_constraint(a, pltpu.HBM) for a in arrays]


class Copies:
    def __init__(self, semaphores):
        self.semaphores, self.count, self.open = semaphores, 0, []

    def start(self, source, target):
        copy = pltpu.make_async_copy(source, target, self.semaphores.at[self.count])
        self.count += 1
        copy.start()
        self.open.append(copy)
        return copy

    def wait(self, *copies):
        for copy in copies:
            if any(copy is other for other in self.open):
                self.open = [other for other in self.open if other is not copy]
                copy.wait()

    def wait_all(self):
        self.wait(*self.open)


def pack_first(qkv_ref, gain_ref, offset_ref, qv_ref, out_w_ref, out_b_ref, gain_two_ref, offset_two_ref, down_b_ref, up_b_ref, out_ref, rows_ref):
    rows_ref[...] = jnp.zeros_like(rows_ref)
    weight = qkv_ref[...].astype(f32)
    line = lambda ref, count: ref[...].astype(f32).reshape(1, count)
    gain, offset, qv = line(gain_ref, 3), line(offset_ref, 3), line(qv_ref, 6)
    for r in range(3):
        for j in range(9):
            rows_ref[10 * r + j : 10 * r + j + 1, :] = weight[r : r + 1, 128 * j : 128 * j + 128]
        rows_ref[10 * r + 9 : 10 * r + 10, 0:1] = gain[:, r : r + 1]
        rows_ref[10 * r + 9 : 10 * r + 10, 1:2] = offset[:, r : r + 1]
        rows_ref[10 * r + 9 : 10 * r + 10, 2:4] = qv[:, 2 * r : 2 * r + 2]
    for k, ref in enumerate((out_b_ref, gain_two_ref, offset_two_ref, down_b_ref)):
        values = line(ref, 3)
        for r in range(3):
            rows_ref[30:31, 4 * r + k : 4 * r + k + 1] = values[:, r : r + 1]
    rows_ref[30:31, 12:24] = line(up_b_ref, 12)
    rows_ref[31:32, :] = out_w_ref[...].astype(f32)[2:3, 256:384]
    out_ref[...] = jnp.broadcast_to(rows_ref[...].astype(bf16)[None], out_ref.shape)


def pack_second(out_w_ref, up_ref, down_ref, out_ref, rows_ref):
    out_w = out_w_ref[...].astype(f32)
    up = up_ref[...].astype(f32)
    down = down_ref[...].astype(f32)
    for k in range(8):
        rows_ref[k : k + 1, :] = out_w[k // 3 : k // 3 + 1, 128 * (k % 3) : 128 * (k % 3) + 128]
    for k in range(36):
        rows_ref[8 + k : 9 + k, :] = up[k // 12 : k // 12 + 1, 128 * (k % 12) : 128 * (k % 12) + 128]
        rows_ref[44 + k : 45 + k, :] = down[k // 3 : k // 3 + 1, 128 * (k % 3) : 128 * (k % 3) + 128]
    out_ref[...] = jnp.broadcast_to(rows_ref[...].astype(bf16)[None], out_ref.shape)


def merge_slots(raw_ref, merged_ref):
    both = jnp.swapaxes(raw_ref[...], 0, 1)
    for slot in range(both.shape[0]):
        at = slot * ROWS
        merged_ref[at + ROWS - 16 : at + ROWS, :] = jnp.zeros((16, WIDTH), bf16)
        merged_ref[at : at + SPAN, :] = both[slot]


def run_pack_first(*args):
    return pl.pallas_call(
        pack_first,
        out_shape=pltpu.HBM((CHIPS, FIRST_ROWS, 128), bf16),
        scratch_shapes=[pltpu.VMEM((FIRST_ROWS, 128), f32)],
        compiler_params=params(8),
        cost_estimate=cost(2),
        name="pack_first",
    )(*far(*args))


def run_pack_second(*args):
    return pl.pallas_call(
        pack_second,
        out_shape=pltpu.HBM((CHIPS, SECOND_ROWS, 128), bf16),
        scratch_shapes=[pltpu.VMEM((SECOND_ROWS, 128), f32)],
        compiler_params=params(8),
        cost_estimate=cost(2),
        name="pack_second",
    )(*far(*args))


def total(arrived_ref):
    return jnp.sum(arrived_ref[...].astype(f32), axis=0)


def spread_lanes(rows, lane, width):
    index = lax.broadcasted_iota(jnp.int32, (1, width), 1)
    out = jnp.zeros((1, width), f32)
    for k, row in enumerate(rows):
        out = jnp.where(index == k, row[:, lane : lane + 1], out)
    return out.reshape(width)


def unpack_first(arrived_ref, qkv_ref, gain_ref, offset_ref, qv_ref):
    sums = total(arrived_ref)
    more = []
    for r in range(3):
        for j in range(9):
            qkv_ref[r : r + 1, 128 * j : 128 * j + 128] = sums[10 * r + j : 10 * r + j + 1, :]
        row = sums[10 * r + 9 : 10 * r + 10, :]
        more.append(row[:, 0:4] + row[:, 4:8])
    gain_ref[...] = spread_lanes(more, 0, 3)
    offset_ref[...] = spread_lanes(more, 1, 3)
    index = lax.broadcasted_iota(jnp.int32, (1, 6), 1)
    out = jnp.zeros((1, 6), f32)
    for k in range(6):
        out = jnp.where(index == k, more[k // 2][:, 2 + k % 2 : 3 + k % 2], out)
    qv_ref[...] = out.reshape(6)


def run_unpack_first(arrived):
    return pl.pallas_call(
        unpack_first,
        out_shape=[shape_of((3, 3 * WIDTH), f32), shape_of((3,), f32), shape_of((3,), f32), shape_of((6,), f32)],
        compiler_params=params(8),
        cost_estimate=cost(2),
        name="unpack_first",
    )(arrived)


def sum_column(line_ref, arrived_ref, keep_ref, one_ref, two_ref, three_ref, sums_ref):
    sums_ref[...] = total(arrived_ref)
    block = lambda shift: sums_ref[pl.ds(pl.multiple_of(lax.rem(line_ref[0] + shift, LINE) * REST_ROWS, 8), REST_ROWS), :]
    keep_ref[...] = block(0)
    for shift, ref in enumerate((one_ref, two_ref, three_ref)):
        ref[...] = block(shift + 1).astype(bf16)


def run_sum_column(line, arrived):
    arrays = pl.BlockSpec(memory_space=pltpu.VMEM)
    part = shape_of((REST_ROWS, 128), bf16)
    return pl.pallas_call(
        sum_column,
        in_specs=[pl.BlockSpec(memory_space=pltpu.SMEM), arrays],
        out_shape=[shape_of((REST_ROWS, 128), f32), part, part, part],
        scratch_shapes=[pltpu.VMEM((LINE * REST_ROWS, 128), f32)],
        compiler_params=params(12),
        cost_estimate=cost(2),
        name="sum_column",
    )(line, arrived)


def unpack_rest(keep_ref, one_ref, two_ref, three_ref, out_ref, up_ref, down_ref, out_b_ref, gain_ref, offset_ref, down_b_ref, up_b_ref, pairs_ref, turned_ref):
    sums = keep_ref[...] + sum(ref[...].astype(f32) for ref in (one_ref, two_ref, three_ref))
    more = []
    for r in range(3):
        for j in range(3):
            out_ref[r : r + 1, 128 * j : 128 * j + 128] = sums[3 * r + j : 3 * r + j + 1, :]
        line = sums[9 + 12 * r : 21 + 12 * r, :]
        pairs_ref[pl.ds(24 * r, 12, stride=2), 0:64] = line[:, 0:64]
        pairs_ref[pl.ds(24 * r + 1, 12, stride=2), 0:64] = line[:, 64:128]
        row = sums[81 + r : 82 + r, :]
        more.append(row[:, 0:4] + row[:, 4:8])
    turned_ref[...] = pairs_ref[...].T
    by_line = [turned_ref[pl.ds(y, 16, stride=4), :] for y in range(LINE)]
    for r in range(3):
        pieces = [by_line[y][:, 24 * r + 12 * c : 24 * r + 12 * c + 12] for c in range(2) for y in range(LINE)]
        lines = jnp.concatenate(pieces, 1)
        for column in range(16):
            up_ref[r : r + 1, 96 * column : 96 * column + 96] = lines[column : column + 1]
    for r in range(12):
        for j in range(3):
            down_ref[r : r + 1, 128 * j : 128 * j + 128] = sums[45 + 3 * r + j : 46 + 3 * r + j, :]
    for k, ref in enumerate((out_b_ref, gain_ref, offset_ref, down_b_ref)):
        ref[...] = spread_lanes(more, k, 3)
    up_b_ref[...] = (sums[84:85, 0:12] + sums[84:85, 12:24]).reshape(12)


def run_unpack_rest(*parts):
    return pl.pallas_call(
        unpack_rest,
        out_shape=[shape_of((3, WIDTH), f32), shape_of((3, HIDDEN), f32), shape_of((12, WIDTH), f32)]
        + [shape_of((3,), f32)] * 4
        + [shape_of((12,), f32)],
        scratch_shapes=[pltpu.VMEM((128, 128), f32), pltpu.VMEM((128, 128), f32)],
        compiler_params=params(12),
        cost_estimate=cost(2),
        name="unpack_rest",
    )(*parts)


def add_halves(mine_ref, theirs_ref, out_far, out_ref, semaphores):
    copies = Copies(semaphores)
    count = CHIPS // 4
    for at in range(0, CHIPS, count):
        out_ref[at : at + count] = mine_ref[at : at + count] + theirs_ref[at : at + count]
        part = pl.ds(at, count)
        copies.start(out_ref.at[part], out_far.at[part])
    copies.wait_all()


def run_add_halves(mine, theirs):
    arrays = pl.BlockSpec(memory_space=pltpu.VMEM)
    return pl.pallas_call(
        add_halves,
        in_specs=[arrays, arrays],
        out_specs=pl.BlockSpec(memory_space=pl.ANY),
        out_shape=pltpu.HBM(mine.shape, bf16),
        scratch_shapes=[pltpu.VMEM(mine.shape, bf16), pltpu.SemaphoreType.DMA((4,))],
        compiler_params=params(12),
        cost_estimate=cost(1),
        name="add_halves",
    )(*held(mine, theirs))


def forward_scores(unit, projected_ref, bias_ref, key_ref, value_ref, more):
    slot, base = unit
    scale = math.log2(math.e) / math.sqrt(HEAD)
    lanes = slice(slot * WIDE, slot * WIDE + WIDE)
    query_more, key_more, value_more = more[slot]
    wide = lambda start: jnp.concatenate([bias_ref[start : start + HEAD, :]] * (WIDE // 128), 1)
    queries, scores = [], []
    for h in range(base, base + FORWARD_BATCH):
        at = h * HEAD
        query = (projected_ref[at : at + HEAD, lanes] + wide(at)) * scale
        key = projected_ref[at + WIDTH : at + WIDTH + HEAD, lanes]
        value = projected_ref[at + 2 * WIDTH : at + 2 * WIDTH + HEAD, lanes] + wide(at + WIDTH)
        query = jnp.concatenate([query, query_more], 0)
        key = jnp.concatenate([key, key_more], 0).astype(bf16)
        key_ref[slot, 32 * h : 32 * h + 32, :] = key
        value_ref[slot, 32 * h : 32 * h + 32, :] = jnp.concatenate([value, value_more], 0).astype(bf16)
        low = query.astype(bf16)
        queries.append(query)
        scores.append([dot(key[:, :count], low[:, a:b], (0, 0)) for a, b, count in FORWARD_BLOCKS])
    return queries, scores


def forward_mixed(unit, queries, scores, mixed_scratch, query_ref, value_ref):
    slot, base = unit
    heads = range(base, base + FORWARD_BATCH)
    peaks = [[jnp.max(part, axis=0, keepdims=True) for part in parts] for parts in scores]
    weights = [[jnp.exp2(part - top).astype(bf16) for part, top in zip(*pair)] for pair in zip(scores, peaks)]
    values = [value_ref[slot, 32 * h : 32 * h + 32, :] for h in heads]
    got = [
        [dot(value[:, :count], part, (1, 0)) for part, (_, _, count) in zip(parts, FORWARD_BLOCKS)]
        for value, parts in zip(values, weights)
    ]
    zero = jnp.zeros((1, WIDE), f32)
    for h, query, tops, parts in zip(heads, queries, peaks, got):
        both = jnp.concatenate(parts, 1)
        row_total = both[HEAD : HEAD + 1]
        mixed_scratch[h * HEAD : h * HEAD + HEAD, :] = both[:HEAD] * (1.0 / row_total)
        logs = jnp.concatenate(tops, 1) + jnp.log2(row_total)
        log_rows = rows_of([zero, zero, zero, *three_parts(-logs)], WIDE)
        query_ref[slot, 32 * h : 32 * h + 32, :] = (query + jnp.concatenate([jnp.zeros((HEAD, WIDE), f32), log_rows], 0)).astype(bf16)


def forward_probs(unit, query_ref, key_ref, refs):
    slot, base = unit
    for h in range(base, base + FORWARD_BATCH):
        query, key = query_ref[slot, 32 * h : 32 * h + 32, :], key_ref[slot, 32 * h : 32 * h + 32, :]
        for ref, (start, a, b) in zip(refs, BACKWARD_BLOCKS):
            ref[h] = jnp.exp2(dot(query[:, start:ROWS], key[:, a:b], (0, 0))).astype(bf16)


def attention_forward(core_ref, counts_ref, tokens_far, own_ref, other_ref,
                      mixed_far, query_far, key_far, value_far, weight_far, first_far, merged_far, low_far, middle_far, high_far, column_far, extra_far,
                      first_ref, projected_ref, mixed_scratch, arrived_ref, bias_ref,
                      raw_ref, tokens_ref, mixed_ref, query_ref, key_ref, value_ref, weight_ref, low_ref, middle_ref, high_ref, column_ref, extra_ref, semaphores):
    slots = mixed_ref.shape[0]
    copies = Copies(semaphores)
    copies.start(tokens_far, raw_ref)
    core = core_ref[0]
    for k, (side, ref) in enumerate(((core, own_ref), (1 - core, other_ref))):
        blocks = jnp.swapaxes(ref[...], 0, 1)
        for r in range(3):
            at = pl.multiple_of(side * 192 + 64 * r, 64)
            for j in range(10):
                arrived_ref[pl.ds(at, 64), 128 * j : 128 * j + 128] = blocks[10 * r + j]
        extra_ref[2 * k] = blocks[30]
        extra_ref[2 * k + 1] = blocks[31]
    order = arrival_order()
    ordered = dot(order, arrived_ref[...], (1, 0))
    weight_ref[...] = ordered[:, : 3 * WIDTH].astype(bf16)
    column_ref[...] = ordered[:, 3 * WIDTH :]
    rows = dot(arrived_ref[:, 3 * WIDTH :], order, (0, 1))
    gain, offset = rows[0:1], rows[1:2]
    for s in range(2):
        column = ordered[:, 3 * WIDTH + 2 + s : 3 * WIDTH + 3 + s]
        bias_ref[pl.ds(s, WIDTH, stride=2), :] = jnp.broadcast_to(column, (WIDTH, 128))
    first_ref[...] = jnp.zeros_like(first_ref)
    copies.wait_all()
    merge_slots(raw_ref, tokens_ref)
    copies.start(tokens_ref, merged_far)
    copies.start(weight_ref, weight_far)
    copies.start(column_ref, column_far)
    copies.start(extra_ref, extra_far)
    for slot in range(slots):
        normed, _ = norm_parts(tokens_ref[slot * ROWS : slot * ROWS + ROWS, :].astype(f32))
        first_ref[slot * WIDE : slot * WIDE + ROWS, :] = (normed * gain + offset).astype(bf16)
    copies.start(first_ref, first_far)
    projected_ref[...] = dot(weight_ref[...], first_ref[...], (0, 1))
    one = jnp.ones((1, WIDE), f32)
    more = []
    for slot in range(slots):
        hidden, frame = mask_rows(counts_ref, slot)
        more.append((rows_of(frame, WIDE), rows_of(hidden + [one, one, one], WIDE), rows_of([one, one, one], WIDE)))
    units = [(slot, base) for slot in range(slots) for base in range(0, HEADS, FORWARD_BATCH)]
    refs = (low_ref, middle_ref, high_ref)
    kept = {}

    def probs(unit):
        slot, base = unit
        if slot * HEADS + base >= KEPT_HEADS:
            return
        copies.wait(*kept.get((slot - 1, base // LOAD_BATCH), ()))
        forward_probs(unit, query_ref, key_ref, refs)
        if (base + FORWARD_BATCH) % LOAD_BATCH == 0:
            part = pl.ds(base // LOAD_BATCH * LOAD_BATCH, LOAD_BATCH)
            pairs = zip(refs, (low_far, middle_far, high_far))
            kept[slot, base // LOAD_BATCH] = [copies.start(near.at[part], away.at[slot, part]) for near, away in pairs]

    def scores(unit):
        slot, base = unit
        got = forward_scores(unit, projected_ref, bias_ref, key_ref, value_ref, more)
        if base + FORWARD_BATCH == HEADS:
            for near, away in ((key_ref, key_far), (value_ref, value_far)):
                copies.start(near.at[slot], away.at[slot])
        return got

    ready = scores(units[0])
    for k, unit in enumerate(units):
        slot = unit[0]
        now, ready = ready, None
        if k + 1 < len(units):
            ready = scores(units[k + 1])
        if k >= 1:
            probs(units[k - 1])
        forward_mixed(unit, *now, mixed_scratch, query_ref, value_ref)
        if unit[1] + FORWARD_BATCH == HEADS:
            mixed_ref[slot] = mixed_scratch[...].astype(bf16)
            for near, away in ((query_ref, query_far), (mixed_ref, mixed_far)):
                copies.start(near.at[slot], away.at[slot])
    probs(units[-1])
    copies.wait_all()


def probs_shapes():
    return [(ROWS - start, b - a) for start, a, b in BACKWARD_BLOCKS]


def run_forward(core, counts, tokens, own, other):
    slots = tokens.shape[1]
    scalars = pl.BlockSpec(memory_space=pltpu.SMEM)
    arrays = pl.BlockSpec(memory_space=pltpu.VMEM)
    away = pl.BlockSpec(memory_space=pl.ANY)
    return pl.pallas_call(
        attention_forward,
        in_specs=[scalars, scalars, away, arrays, arrays],
        out_specs=[away] * 12,
        out_shape=[pltpu.HBM((slots, rows, WIDE), bf16) for rows in (WIDTH, 512, 512, 512)]
        + [pltpu.HBM((WIDTH, 3 * WIDTH), bf16), pltpu.HBM((slots * WIDE, WIDTH), bf16), pltpu.HBM((slots * ROWS, WIDTH), bf16)]
        + [pltpu.HBM((slots, HEADS, *shape), bf16) for shape in probs_shapes()]
        + [pltpu.HBM((WIDTH, 128), f32), pltpu.HBM((4, 64, 128), bf16)],
        scratch_shapes=[
            pltpu.VMEM((slots * WIDE, WIDTH), bf16),
            pltpu.VMEM((3 * WIDTH, slots * WIDE), f32),
            pltpu.VMEM((WIDTH, WIDE), f32),
            pltpu.VMEM((WIDTH, 3 * WIDTH + 128), bf16),
            pltpu.VMEM((2 * WIDTH + 8, 128), f32),
            pltpu.VMEM((SPAN, slots, WIDTH), bf16),
            pltpu.VMEM((slots * ROWS, WIDTH), bf16),
        ]
        + [pltpu.VMEM((slots, rows, WIDE), bf16) for rows in (WIDTH, 512, 512, 512)]
        + [pltpu.VMEM((WIDTH, 3 * WIDTH), bf16)]
        + [pltpu.VMEM((HEADS, *shape), bf16) for shape in probs_shapes()]
        + [pltpu.VMEM((WIDTH, 128), f32), pltpu.VMEM((4, 64, 128), bf16), pltpu.SemaphoreType.DMA((40,))],
        compiler_params=params(48),
        cost_estimate=cost(20),
        name="attention_forward",
    )(core, counts, *far(tokens), *held(own, other))


def feed_forward_early(cotangent_far, merged_far, mixed_far, extra_far, own_ref,
                       arrived_ref, down_ref, up_b_ref, cotangent_ref, tokens_ref, mixed_ref, slopes_ref, extra_ref, raw_ref, semaphores):
    copies = Copies(semaphores)
    extra = copies.start(extra_far, extra_ref)
    raw = copies.start(cotangent_far, raw_ref)
    copies.start(mixed_far, mixed_ref)
    copies.start(merged_far, tokens_ref)
    unpack_side(own_ref, lambda: (copies.wait(extra), extra_ref[0], extra_ref[1])[1:], arrived_ref, down_ref, up_b_ref)
    copies.wait(raw)
    merge_slots(raw_ref, cotangent_ref)
    slopes_ref[...] = dot(cotangent_ref[...], down_ref[...], (1, 1))
    copies.wait_all()


def unpack_side(message_ref, extra, arrived_ref, down_ref, up_b_ref):
    blocks = jnp.swapaxes(message_ref[...], 0, 1)
    for r in range(12):
        for j in range(3):
            down_ref[64 * r : 64 * r + 64, 128 * j : 128 * j + 128] = blocks[44 + 3 * r + j]
    for r in range(3):
        for j in range(12):
            arrived_ref[64 * r : 64 * r + 64, 384 + 128 * j : 512 + 128 * j] = blocks[8 + 12 * r + j]
    vectors, tile = extra()
    vectors = vectors.astype(f32)
    for r in range(3):
        rows = slice(64 * r, 64 * r + 64)
        for j in range(3):
            arrived_ref[rows, 128 * j : 128 * j + 128] = tile if 3 * r + j == 8 else blocks[3 * r + j]
        arrived_ref[rows, 1920:2048] = (pltpu.roll(vectors, 128 - 4 * r, 1) if r else vectors).astype(bf16)
    turned = vectors.T
    up_b_ref[0:1, :] = jnp.concatenate([turned[12 + r : 13 + r] for r in range(12)], 1)


def run_feed_forward_early(cotangent, merged, mixed, own, extra):
    _, slots, _ = cotangent.shape
    arrays = pl.BlockSpec(memory_space=pltpu.VMEM)
    away = pl.BlockSpec(memory_space=pl.ANY)
    return pl.pallas_call(
        feed_forward_early,
        in_specs=[away, away, away, away, arrays],
        out_shape=[
            pltpu.VMEM((WIDTH // 2, 2048), bf16),
            pltpu.VMEM((HIDDEN // 2, WIDTH), bf16),
            pltpu.VMEM((8, HIDDEN // 2), f32),
            pltpu.VMEM((slots * ROWS, WIDTH), bf16),
            pltpu.VMEM((slots * ROWS, WIDTH), bf16),
            pltpu.VMEM((slots, WIDTH, WIDE), bf16),
            pltpu.VMEM((slots * ROWS, HIDDEN // 2), f32),
            pltpu.VMEM((4, 64, 128), bf16),
        ],
        scratch_shapes=[pltpu.VMEM((SPAN, slots, WIDTH), bf16), pltpu.SemaphoreType.DMA((4,))],
        compiler_params=params(16),
        cost_estimate=cost(3),
        name="feed_forward_early",
    )(*far(cotangent, merged, mixed, extra), *held(own))


def feed_forward(core_ref, tokens_ref, mixed_ref, cotangent_ref, own_arrived_ref, own_down_ref, own_up_b_ref, slopes_ref, other_ref, extra_ref,
                 activated_ref, resid_ref, other_down_ref, row_ref, grad_resid_far, grad_mixed_far, mine_ref, theirs_ref,
                 arrived_ref, ordered_ref, up_b_ref, packed_ref, grad_down_ref, grad_resid_ref, grad_mixed_ref, second_ref, grad_up_ref,
                 semaphores):
    slots = mixed_ref.shape[0]
    block = 768
    root = math.sqrt(2.0 / math.pi)
    copies = Copies(semaphores)
    core = core_ref[0]
    sides = (core, 1 - core)
    places = [pl.multiple_of(side * (WIDTH // 2), 64) for side in sides]
    unpack_side(other_ref, lambda: (extra_ref[2], extra_ref[3]), arrived_ref, other_down_ref, up_b_ref)
    downs = (own_down_ref, other_down_ref)
    up_bs = (own_up_b_ref, up_b_ref)
    order = arrival_order()
    packed_ref[pl.ds(places[0], WIDTH // 2), :] = own_arrived_ref[...]
    packed_ref[pl.ds(places[1], WIDTH // 2), :] = arrived_ref[...]
    row_ref[...] = dot(packed_ref[:, 1920:], order, (0, 1))[0:8]
    ordered_ref[...] = dot(order, packed_ref[:, :1920], (1, 0)).astype(bf16)
    out_w = ordered_ref[:, :WIDTH]
    up_w = lambda half, at: ordered_ref[:, pl.ds(pl.multiple_of(WIDTH + sides[half] * (HIDDEN // 2) + at, 128), block)]
    out_b, gain, offset = (row_ref[k : k + 1] for k in range(3))
    spans = [slice(slot * ROWS, slot * ROWS + ROWS) for slot in range(slots)]
    norms = {}

    def enter(slot):
        resid = tokens_ref[spans[slot], :].astype(f32) + dot(mixed_ref[slot, :, :ROWS], out_w, (0, 0)) + out_b
        resid_ref[spans[slot], :] = resid
        norms[slot] = norm_parts(resid)
        second_ref[spans[slot], :] = (norms[slot][0] * gain + offset).astype(bf16)

    def products(work):
        slot, half, at = work
        rows = spans[slot]
        up = dot(second_ref[rows, :], up_w(half, at), (1, 0))
        if half == 0:
            return up, slopes_ref[rows, at : at + block]
        return up, dot(cotangent_ref[rows, :], other_down_ref[at : at + block, :], (1, 1))

    lines = {}

    def activate(work, up, grad_activated):
        slot, half, at = work
        rows, cols = spans[slot], slice(half * (HIDDEN // 2) + at, half * (HIDDEN // 2) + at + block)
        up = up + up_bs[half][0:1, at : at + block]
        square = up * up
        tanh = jnp.tanh(up * (root + (root * 0.044715) * square))
        half_tanh = 0.5 + 0.5 * tanh
        activated_ref[rows, cols] = (up * half_tanh).astype(bf16)
        slope = half_tanh + (up * (2.0 * half_tanh * (1.0 - half_tanh))) * (root + (3 * root * 0.044715) * square)
        grad_up = grad_activated * slope
        grad_up_ref[rows, cols] = grad_up.astype(bf16)
        line = jnp.sum(grad_up, axis=0, keepdims=True)
        lines[half, at] = lines[half, at] + line if (half, at) in lines else line

    works = [(slot, half, at) for slot in range(slots) for half in range(2) for at in range(0, HIDDEN // 2, block)]
    enter(0)
    ready = products(works[0])
    for slot in range(1, slots):
        enter(slot)
    for k, work in enumerate(works):
        now = ready
        if k + 1 < len(works):
            ready = products(works[k + 1])
        activate(work, *now)

    grad_branch = cotangent_ref[...]
    halves = [slice(0, HIDDEN // 2), slice(HIDDEN // 2, HIDDEN)]
    side_w = [ordered_ref[:, pl.ds(pl.multiple_of(WIDTH + side * (HIDDEN // 2), 128), HIDDEN // 2)] for side in sides]
    grad_seconds = [sum(dot(grad_up_ref[rows, cols], weight, (1, 1)) for cols, weight in zip(halves, side_w)) for rows in spans]
    attended, sums = [], []

    def leave(slot):
        normed, inverse = norms[slot]
        grad_second = grad_seconds[slot]
        scaled = grad_second * gain
        mean_one = jnp.mean(scaled, axis=-1, keepdims=True)
        mean_two = jnp.mean(scaled * normed, axis=-1, keepdims=True)
        grad_full = cotangent_ref[spans[slot], :].astype(f32)
        grad_resid = grad_full + inverse * (scaled - mean_one - normed * mean_two)
        grad_resid_ref[spans[slot], :] = grad_resid
        low = grad_resid.astype(bf16)
        attended.append(low)
        parts = [low.astype(f32), grad_second * normed, grad_second, grad_full]
        sums.append(jnp.concatenate([jnp.sum(part, axis=0, keepdims=True) for part in parts], 0))

    for slot in range(slots):
        leave(slot)
        cols = halves[slot % 2]
        grad_down_ref[cols, :] = dot(activated_ref[:, cols], grad_branch, (0, 0)).astype(bf16)
    copies.start(grad_resid_ref, grad_resid_far)
    for slot in range(slots):
        grad_mixed_ref[slot, :, 512:WIDE] = jnp.zeros((WIDTH, WIDE - 512), bf16)
        grad_mixed_ref[slot, :, :ROWS] = dot(out_w, attended[slot], (1, 1)).astype(bf16)
    copies.start(grad_mixed_ref, grad_mixed_far)
    grad_out = sum(dot(mixed_ref[slot, :, :ROWS], attended[slot], (1, 0)) for slot in range(slots))
    for side, cols in zip(sides, halves):
        at = pl.multiple_of(WIDTH + side * (HIDDEN // 2), 128)
        ordered_ref[:, pl.ds(at, HIDDEN // 2)] = dot(second_ref[...], grad_up_ref[:, cols], (0, 0)).astype(bf16)
    ordered_ref[:, :WIDTH] = grad_out.astype(bf16)
    packed_ref[:, :1920] = dot(order, ordered_ref[...], (0, 0)).astype(bf16)
    high, low = two_parts(sum(sums))
    rows = jnp.concatenate([high, low, jnp.zeros((120, WIDTH), f32)], 0).astype(bf16)
    packed_ref[:, 1920:] = dot(order, rows, (0, 1)).astype(bf16)
    blank = jnp.zeros((CHIPS, 128), bf16)
    for half, (place, ref) in enumerate(zip(places, (mine_ref, theirs_ref))):
        blocks = [blank] * REST_ROWS
        for r in range(3):
            at = pl.multiple_of(place + 64 * r, 64)
            for j in range(15):
                blocks[3 * r + j if j < 3 else 6 + 12 * r + j] = packed_ref[pl.ds(at, 64), 128 * j : 128 * j + 128]
            blocks[81 + r] = packed_ref[pl.ds(at, 64), 1920:2048]
        for r in range(12):
            at = half * (HIDDEN // 2) + 64 * r
            for j in range(3):
                blocks[45 + 3 * r + j] = grad_down_ref[at : at + 64, 128 * j : 128 * j + 128]
        high, low = two_parts(jnp.concatenate([lines[half, at] for at in range(0, HIDDEN // 2, block)], 1))
        rows = [part[:, 64 * r : 64 * r + 64] for part in (high, low) for r in range(12)]
        blocks[84] = rows_of(rows, 64, 128).T.astype(bf16)
        ref[...] = jnp.swapaxes(jnp.stack(blocks), 0, 1)
    copies.wait_all()


def run_feed_forward(core, tokens, mixed, cotangent, arrived, down, up_b, slopes, other, extra):
    slots = mixed.shape[0]
    arrays = pl.BlockSpec(memory_space=pltpu.VMEM)
    away = pl.BlockSpec(memory_space=pl.ANY)
    return pl.pallas_call(
        feed_forward,
        in_specs=[pl.BlockSpec(memory_space=pltpu.SMEM)] + [arrays] * 9,
        out_specs=[arrays, arrays, arrays, arrays, away, away, arrays, arrays],
        out_shape=[
            pltpu.VMEM((slots * ROWS, HIDDEN), bf16),
            pltpu.VMEM((slots * ROWS, WIDTH), f32),
            pltpu.VMEM((HIDDEN // 2, WIDTH), bf16),
            pltpu.VMEM((8, WIDTH), f32),
            pltpu.HBM((slots * ROWS, WIDTH), f32),
            pltpu.HBM((slots, WIDTH, WIDE), bf16),
            pltpu.VMEM((CHIPS, REST_ROWS, 128), bf16),
            pltpu.VMEM((CHIPS, REST_ROWS, 128), bf16),
        ],
        scratch_shapes=[
            pltpu.VMEM((WIDTH // 2, 2048), bf16),
            pltpu.VMEM((WIDTH, 1920), bf16),
            pltpu.VMEM((8, HIDDEN // 2), f32),
            pltpu.VMEM((WIDTH, 2048), bf16),
            pltpu.VMEM((HIDDEN, WIDTH), bf16),
            pltpu.VMEM((slots * ROWS, WIDTH), f32),
            pltpu.VMEM((slots, WIDTH, WIDE), bf16),
            pltpu.VMEM((slots * ROWS, WIDTH), bf16),
            pltpu.VMEM((slots * ROWS, HIDDEN), bf16),
            pltpu.SemaphoreType.DMA((2,)),
        ],
        compiler_params=params(34),
        cost_estimate=cost(17),
        name="feed_forward",
    )(core, *held(tokens, mixed, cotangent, arrived, down, up_b, slopes, other, extra))


def feed_forward_output(activated_ref, resid_ref, own_down_ref, other_down_ref, row_ref, out_far, out_ref, semaphores):
    slots = out_ref.shape[1]
    copies = Copies(semaphores)
    half, middle = HIDDEN // 2, ROWS // 2
    for low, high in ((0, middle), (middle, SPAN)):
        both = []
        for slot in range(slots):
            at = slice(slot * ROWS + low, slot * ROWS + low + middle)
            result = resid_ref[at, :] + row_ref[3:4]
            result += dot(activated_ref[at, :half], own_down_ref[...], (1, 0)) + dot(activated_ref[at, half:], other_down_ref[...], (1, 0))
            both.append(result[: high - low])
        out_ref[low:high] = jnp.swapaxes(jnp.stack(both), 0, 1).astype(bf16)
        part = pl.ds(low, high - low)
        copies.start(out_ref.at[part], out_far.at[part])
    copies.wait_all()


def run_feed_forward_output(*args):
    slots = args[1].shape[0] // ROWS
    return pl.pallas_call(
        feed_forward_output,
        out_specs=pl.BlockSpec(memory_space=pl.ANY),
        out_shape=pltpu.HBM((SPAN, slots, WIDTH), bf16),
        scratch_shapes=[pltpu.VMEM((SPAN, slots, WIDTH), bf16), pltpu.SemaphoreType.DMA((2,))],
        compiler_params=params(20),
        cost_estimate=cost(3),
        name="feed_forward_output",
    )(*held(*args))


def backward_slopes(unit, copies, loads, value_ref, mixed_ref, grad_mixed_ref):
    slot, base = unit
    copies.wait(*loads["grad"][slot])
    grads, slopes = [], []
    for h in range(base, base + BACKWARD_BATCH):
        both = slice(48 * (h // 2), 48 * (h // 2) + 48)
        part = slice(HEAD * (h % 2), HEAD * (h % 2) + HEAD)
        grad = grad_mixed_ref[slot, both, :].astype(f32)[part]
        mixed = mixed_ref[slot, both, :].astype(f32)[part]
        shift = jnp.sum(grad * mixed, axis=0, keepdims=True)
        grad = jnp.concatenate([grad, rows_of(three_parts(-shift), WIDE)], 0).astype(bf16)
        value = value_ref[slot, 32 * h : 32 * h + 32, :]
        grads.append(grad)
        slopes.append([dot(grad[:, start:ROWS], value[:, a:b], (0, 0)) for start, a, b in BACKWARD_BLOCKS])
    return grads, slopes


def backward_products(unit, grads, slopes, copies, loads, query_ref, key_ref, probs_refs, turned_ref):
    slot, base = unit
    heads = range(base, base + BACKWARD_BATCH)
    copies.wait(*loads["query"][slot])
    queries = [query_ref[slot, 32 * h : 32 * h + 32, :] for h in heads]
    keys = [key_ref[slot, 32 * h : 32 * h + 32, :] for h in heads]
    if slot * HEADS + base < KEPT_HEADS:
        copies.wait(*loads["probs"][slot][base // LOAD_BATCH])
        probs = [[ref[slot, h].astype(f32) for ref in probs_refs] for h in heads]
    else:
        probs = [
            [jnp.exp2(dot(query[:, start:ROWS], key[:, a:b], (0, 0))) for start, a, b in BACKWARD_BLOCKS]
            for query, key in zip(queries, keys)
        ]
    grad_scores = [[(part * slope).astype(bf16) for part, slope in zip(*pair)] for pair in zip(probs, slopes)]
    probs = [[part.astype(bf16) for part in parts] for parts in probs]
    over = lambda left, parts: jnp.concatenate(
        [dot(left[:, start:ROWS], part, (1, 0)) for part, (start, _, _) in zip(parts, BACKWARD_BLOCKS)], 1)
    grad_v = [over(grad, parts) for grad, parts in zip(grads, probs)]
    grad_k = [over(query, parts) for query, parts in zip(queries, grad_scores)]
    grad_q = [
        [dot(key[:, a:b], part, (1, 1)) for part, (_, a, b) in zip(parts, BACKWARD_BLOCKS)]
        for key, parts in zip(keys, grad_scores)
    ]
    fill = lambda part: jnp.concatenate([jnp.zeros((32, ROWS - part.shape[1]), f32), part], 1) if part.shape[1] < ROWS else part
    blank = jnp.zeros((HEAD, WIDE - ROWS), f32)
    whole_q = [jnp.concatenate([sum(fill(part) for part in parts)[:HEAD] * (1.0 / math.sqrt(HEAD)), blank], 1) for parts in grad_q]
    whole_k = [part[:HEAD] * math.log(2.0) for part in grad_k]
    whole_v = [part[:HEAD] for part in grad_v]
    for k in range(0, BACKWARD_BATCH, 2):
        at = (base + k) * HEAD
        for offset, parts in ((0, whole_q), (WIDTH, whole_k), (2 * WIDTH, whole_v)):
            turned_ref[slot, offset + at : offset + at + 2 * HEAD, :] = jnp.concatenate(parts[k : k + 2], 0).astype(bf16)


def attention_backward(core_ref, query_far, key_far, value_far, mixed_far, grad_mixed_far, low_far, middle_far, high_far, first_far, weight_far,
                       column_far, turned_far, mine_ref, theirs_ref,
                       bias_ref, packed_ref, turned_ref,
                       query_ref, key_ref, value_ref, mixed_ref, grad_mixed_ref, low_ref, middle_ref, high_ref, first_ref, weight_ref, column_ref, semaphores):
    slots = mixed_ref.shape[0]
    copies = Copies(semaphores)
    loads = {"grad": [], "probs": [], "query": []}
    probs_refs = (low_ref, middle_ref, high_ref)
    for slot in range(slots):
        load = lambda pairs: [copies.start(away.at[slot], near.at[slot]) for away, near in pairs]
        loads["grad"].append(load(((value_far, value_ref), (grad_mixed_far, grad_mixed_ref), (mixed_far, mixed_ref))))
        loads["probs"].append([])
        for base in range(0, HEADS, LOAD_BATCH):
            if slot * HEADS + base < KEPT_HEADS:
                part = pl.ds(base, LOAD_BATCH)
                pairs = zip((low_far, middle_far, high_far), probs_refs)
                loads["probs"][slot].append([copies.start(away.at[slot, part], near.at[slot, part]) for away, near in pairs])
            if base == 0:
                loads["query"].append(load(((query_far, query_ref), (key_far, key_ref))))
    weights = [copies.start(first_far, first_ref.at[:, pl.ds(0, WIDTH)]), copies.start(weight_far, weight_ref), copies.start(column_far, column_ref)]
    core = core_ref[0]
    units = [(slot, base) for slot in range(slots) for base in range(0, HEADS, BACKWARD_BATCH)]
    ready = backward_slopes(units[0], copies, loads, value_ref, mixed_ref, grad_mixed_ref)
    for k, unit in enumerate(units):
        slot = unit[0]
        now, ready = ready, None
        if k + 1 < len(units):
            ready = backward_slopes(units[k + 1], copies, loads, value_ref, mixed_ref, grad_mixed_ref)
        backward_products(unit, *now, copies, loads, query_ref, key_ref, probs_refs, turned_ref)
        if unit[1] + BACKWARD_BATCH == HEADS:
            copies.start(turned_ref.at[slot], turned_far.at[slot])
    copies.wait(*weights)
    order = arrival_order()
    turned = jnp.concatenate([turned_ref[slot] for slot in range(slots)], 1)
    first_ref[:, WIDTH:] = jnp.ones((slots * WIDE, 128), bf16)
    grad_more = dot(first_ref[:, : WIDTH + 16], turned, (0, 1))
    grad_weight, sums = grad_more[:WIDTH], grad_more[WIDTH : WIDTH + 1]
    packed_ref[:, : 3 * WIDTH] = dot(order, grad_weight.astype(bf16), (0, 0)).astype(bf16)
    weight = weight_ref[...].astype(f32)
    grad_offset = jnp.sum(weight * sums, axis=1, keepdims=True)
    along = jnp.sum(grad_weight * weight, axis=1, keepdims=True)
    grad_gain = (along - column_ref[:, 1:2] * grad_offset) / column_ref[:, 0:1]
    bias_ref[0:WIDTH] = jnp.broadcast_to(sums[:, :WIDTH], (128, WIDTH)).T
    bias_ref[WIDTH : 2 * WIDTH] = jnp.broadcast_to(sums[:, 2 * WIDTH :], (128, WIDTH)).T
    lane = lax.broadcasted_iota(jnp.int32, (WIDTH, 128), 1)
    columns = jnp.zeros((WIDTH, 128), f32)
    for k, values in enumerate((grad_gain, grad_offset, bias_ref[pl.ds(0, WIDTH, stride=2), :], bias_ref[pl.ds(1, WIDTH, stride=2), :])):
        high, low = two_parts(values)
        columns = jnp.where(lane == k, high, jnp.where(lane == 4 + k, low, columns))
    packed_ref[:, 3 * WIDTH :] = dot(order, columns.astype(bf16), (0, 0)).astype(bf16)
    blank = jnp.zeros((CHIPS, 128), bf16)
    for side, ref in ((core, mine_ref), (1 - core, theirs_ref)):
        blocks = []
        for r in range(3):
            at = pl.multiple_of(side * 192 + 64 * r, 64)
            for j in range(10):
                blocks.append(packed_ref[pl.ds(at, 64), 128 * j : 128 * j + 128])
        ref[...] = jnp.swapaxes(jnp.stack(blocks + [blank, blank]), 0, 1)
    copies.wait_all()


def run_backward(core, query, key, value, mixed, grad_mixed, low, middle, high, first, weight, column):
    slots = mixed.shape[0]
    arrays = pl.BlockSpec(memory_space=pltpu.VMEM)
    away = pl.BlockSpec(memory_space=pl.ANY)
    return pl.pallas_call(
        attention_backward,
        in_specs=[pl.BlockSpec(memory_space=pltpu.SMEM)] + [away] * 11,
        out_specs=[away, arrays, arrays],
        out_shape=[
            pltpu.HBM((slots, 3 * WIDTH, WIDE), bf16),
            pltpu.VMEM((CHIPS, FIRST_ROWS, 128), bf16),
            pltpu.VMEM((CHIPS, FIRST_ROWS, 128), bf16),
        ],
        scratch_shapes=[
            pltpu.VMEM((2 * WIDTH + 8, 128), f32),
            pltpu.VMEM((WIDTH, 3 * WIDTH + 128), bf16),
            pltpu.VMEM((slots, 3 * WIDTH, WIDE), bf16),
        ]
        + [pltpu.VMEM((slots, rows, WIDE), bf16) for rows in (512, 512, 512, WIDTH, WIDTH)]
        + [pltpu.VMEM((slots, HEADS, *shape), bf16) for shape in probs_shapes()]
        + [pltpu.VMEM((slots * WIDE, WIDTH + 128), bf16), pltpu.VMEM((WIDTH, 3 * WIDTH), bf16), pltpu.VMEM((WIDTH, 128), f32), pltpu.SemaphoreType.DMA((70,))],
        compiler_params=params(56),
        cost_estimate=cost(22),
        name="attention_backward",
    )(core, *far(query, key, value, mixed, grad_mixed, low, middle, high, first, weight, column))


def input_backward(merged_far, turned_far, grad_resid_far, weight_far, column_far, out_far,
                   tokens_ref, turned_ref, grad_resid_ref, weight_ref, grad_first_ref, out_ref, column_ref, semaphores):
    slots = turned_ref.shape[0]
    copies = Copies(semaphores)
    first = [copies.start(weight_far, weight_ref), copies.start(turned_far.at[0], turned_ref.at[0])]
    turns = [copies.start(turned_far.at[slot], turned_ref.at[slot]) for slot in range(1, slots)]
    rest = [copies.start(column_far, column_ref), copies.start(merged_far, tokens_ref), copies.start(grad_resid_far, grad_resid_ref)]
    copies.wait(*first)
    for slot in range(slots):
        if slot:
            copies.wait(turns[slot - 1])
        grad_first_ref[slot * ROWS : slot * ROWS + ROWS, :] = dot(turned_ref[slot, :, :ROWS], weight_ref[...], (0, 1))
    copies.wait(*rest)
    gain = column_ref[...].T[0:1]
    half = ROWS // 2
    for low, high in ((0, half), (half, SPAN)):
        for slot in range(slots):
            at = slice(slot * ROWS + low, slot * ROWS + low + half)
            normed, inverse = norm_parts(tokens_ref[at, :].astype(f32))
            scaled = grad_first_ref[at, :] * gain
            mean_one = jnp.mean(scaled, axis=-1, keepdims=True)
            mean_two = jnp.mean(scaled * normed, axis=-1, keepdims=True)
            grad = grad_resid_ref[at, :] + inverse * (scaled - mean_one - normed * mean_two)
            out_ref[low:high, slot, :] = grad[: high - low]
        copies.start(out_ref.at[pl.ds(low, high - low)], out_far.at[pl.ds(low, high - low)])
    copies.wait_all()


def run_input_backward(merged, turned, grad_resid, weight, column):
    slots = turned.shape[0]
    arrays = pl.BlockSpec(memory_space=pltpu.VMEM)
    away = pl.BlockSpec(memory_space=pl.ANY)
    return pl.pallas_call(
        input_backward,
        in_specs=[away] * 5,
        out_specs=away,
        out_shape=pltpu.HBM((SPAN, slots, WIDTH), f32),
        scratch_shapes=[
            pltpu.VMEM((slots * ROWS, WIDTH), bf16),
            pltpu.VMEM((slots, 3 * WIDTH, WIDE), bf16),
            pltpu.VMEM((slots * ROWS, WIDTH), f32),
            pltpu.VMEM((WIDTH, 3 * WIDTH), bf16),
            pltpu.VMEM((slots * ROWS, WIDTH), f32),
            pltpu.VMEM((SPAN, slots, WIDTH), f32),
            pltpu.VMEM((WIDTH, 128), f32),
            pltpu.SemaphoreType.DMA((8,)),
        ],
        compiler_params=params(32),
        cost_estimate=cost(6),
        name="input_backward",
    )(*far(merged, turned, grad_resid, weight, column))


def to_chips(message):
    return lax.all_to_all(message, CHIP_AXES, 0, 0, tiled=True)


def to_column(message):
    return lax.all_to_all(message, COLUMN_AXES, 0, 0, tiled=True)


def along_line(message, shift):
    return lax.ppermute(message, LINE_AXIS, [(k, (k + shift) % LINE) for k in range(LINE)])


def across(message):
    return lax.ppermute(message, CORE_AXIS, [(0, 1), (1, 0)])


def shards(tokens, item_frames, ln1_gain, ln1_bias, qkv_weight, qv_bias, out_weight, out_bias, ln2_gain, ln2_bias,
           up_weight, up_bias, down_weight, down_bias, cotangent):
    together = lax.optimization_barrier
    core = lax.axis_index(CORE_AXIS).astype(jnp.int32).reshape(1)
    line = lax.axis_index(LINE_AXIS).astype(jnp.int32).reshape(1)
    first = run_pack_first(qkv_weight, ln1_gain, ln1_bias, qv_bias, out_weight, out_bias, ln2_gain, ln2_bias, down_bias, up_bias)
    first, up_weight = together((first, up_weight))
    first = to_chips(first)
    up_sent = up_weight.reshape(3, 16, 2, 4, 12).transpose(0, 2, 4, 1, 3).reshape(3, HIDDEN)
    second = run_pack_second(out_weight, up_sent, down_weight)
    tokens, cotangent = tokens.transpose(1, 0, 2), cotangent.transpose(1, 0, 2)
    first, second = together((first, second))
    first_other = across(first)
    second = to_chips(second)
    mixed, query, key, value, weight, normed, merged, low, middle, high, column, extra = run_forward(core, item_frames, tokens, first, first_other)
    second, mixed = together((second, mixed))
    other = across(second)
    arrived, own_down, up_b, turned_cotangent, near, near_mixed, slopes, extra = run_feed_forward_early(cotangent, merged, mixed, second, extra)
    activated, resid, other_down, row, grad_resid, grad_mixed, mine, theirs = run_feed_forward(
        core, near, near_mixed, turned_cotangent, arrived, own_down, up_b, slopes, other, extra)
    theirs = across(theirs)
    output = run_feed_forward_output(activated, resid, own_down, other_down, row)
    output, mine = together((output, mine))
    output = output.transpose(1, 0, 2)
    rest = run_add_halves(mine, theirs)
    rest, grad_mixed = together((rest, grad_mixed))
    rest = to_column(rest.reshape(CHIPS // LINE, LINE * REST_ROWS, 128))
    turned, mine, theirs = run_backward(core, query, key, value, mixed, grad_mixed, low, middle, high, normed, weight, column)
    theirs = across(theirs)
    own = run_add_halves(mine, theirs)
    own, rest = together((own, rest))
    own, turned = together((own, turned))
    own = to_chips(own)
    keep, *sent = run_sum_column(line, rest)
    sent = [along_line(part, shift + 1) for shift, part in enumerate(sent)]
    grad_out, grad_up, *others = run_unpack_rest(keep, *sent)
    grad_down, grad_out_b, grad_gain_two, grad_offset_two, grad_down_b, grad_up_b = others
    input_grad = run_input_backward(merged, turned, grad_resid, weight, column).transpose(1, 0, 2)
    grad_qkv, grad_gain, grad_offset, grad_qv = run_unpack_first(own)
    return (output, input_grad, grad_gain, grad_offset, grad_qkv, grad_qv, grad_out, grad_out_b, grad_gain_two, grad_offset_two,
            grad_up, grad_up_b, grad_down, grad_down_b)


def solution(mesh):
    split = Mesh(mesh.devices.reshape(4, 4, 2, mesh.shape["narrow"]), ALL)
    by_rank = lambda n: P(ALL, *([None] * (n - 1)))
    return jax.shard_map(
        shards,
        mesh=split,
        in_specs=tuple(by_rank(n) for n in (3, 2, 1, 1, 2, 1, 2, 1, 1, 1, 2, 1, 2, 1, 3)),
        out_specs=tuple(by_rank(n) for n in (3, 3, 1, 1, 2, 1, 2, 1, 1, 1, 2, 1, 2, 1)),
        check_vma=False,
    )
```

```python
import math

import jax
import jax.numpy as jnp
from jax import lax
from jax.experimental import pallas as pl
from jax.experimental.pallas import tpu as pltpu
from jax.sharding import Mesh
from jax.sharding import PartitionSpec as P

HEADS = 16
HEAD = 24
FRAME = 196
WIDTH = 384
HIDDEN = 1536
WIDE = 640
SPAN = 588
ROWS = 592
CHIPS = 64
FIRST_ROWS = 32
REST_ROWS = 88
SECOND_ROWS = 80
EPSILON = 1e-05
NEGATIVE = -1e30
bf16 = jnp.bfloat16
f32 = jnp.float32
FORWARD_BLOCKS = ((0, 128, 208), (128, 384, 400), (384, 640, 592))
FORWARD_BATCH = 8
LOAD_BATCH = 8
KEPT_HEADS = 24
BACKWARD_BATCH = 4
BACKWARD_BLOCKS = ((0, 0, 256), (192, 256, 512), (384, 512, 640))
ALL = ("wide_0", "wide_1", "wide_2", "narrow")
CHIP_AXES = ("wide_0", "wide_1", "narrow")
COLUMN_AXES = ("wide_0", "wide_1")
LINE_AXIS = "narrow"
LINE = 4
CORE_AXIS = "wide_2"


def dot(left, right, over):
    return lax.dot_general(left, right, (((over[0],), (over[1],)), ((), ())), preferred_element_type=f32)


def norm_parts(values):
    centred = values - jnp.mean(values, axis=-1, keepdims=True)
    inverse = lax.rsqrt(jnp.mean(centred * centred, axis=-1, keepdims=True) + EPSILON)
    return centred * inverse, inverse


def two_parts(values):
    high = values.astype(bf16).astype(f32)
    return high, values - high


def three_parts(values):
    high, rest = two_parts(values)
    middle, low = two_parts(rest)
    return high, middle, low


def rows_of(rows, width, count=8):
    index = lax.broadcasted_iota(jnp.int32, (count, width), 0)
    out = jnp.zeros((count, width), f32)
    for k, row in enumerate(rows):
        out = jnp.where(index == k, row, out)
    return out


def arrival_order():
    place = lax.broadcasted_iota(jnp.int32, (WIDTH, WIDTH), 1)
    feature = lax.broadcasted_iota(jnp.int32, (WIDTH, WIDTH), 0)
    core = (place >= WIDTH // 2).astype(jnp.int32)
    rest = place - core * (WIDTH // 2)
    row = rest >> 6
    chip = rest & 63
    return (feature == 3 * (8 * (chip >> 2) + 4 * core + (chip & 3)) + row).astype(f32).astype(bf16)


def mask_rows(counts_ref, slot):
    lane = lax.broadcasted_iota(jnp.int32, (1, WIDE), 1)
    first_end = counts_ref[slot, 0]
    second_end = first_end + counts_ref[slot, 1]
    third_end = second_end + counts_ref[slot, 2]
    group = [
        (f >= first_end).astype(jnp.int32) + (f >= second_end).astype(jnp.int32) + (f >= third_end).astype(jnp.int32)
        for f in range(3)
    ]
    hidden = []
    for f in range(3):
        row = jnp.full((1, WIDE), NEGATIVE, f32)
        for k in range(f + 1):
            seen = jnp.where(group[f] == group[k], 0.0, NEGATIVE).astype(f32)
            row = jnp.where((lane >= FRAME * k) & (lane < FRAME * (k + 1)), seen, row)
        hidden.append(row)
    frame = [((lane >= FRAME * f) & ((lane < FRAME * (f + 1)) | (f == 2))).astype(f32) for f in range(3)]
    return hidden, frame


def params(mebibytes):
    return pltpu.CompilerParams(vmem_limit_bytes=mebibytes * 2**20)


def cost(microseconds):
    return pl.CostEstimate(flops=int(microseconds * 1.1e9), bytes_accessed=2**20, transcendentals=0)


def shape_of(shape, dtype):
    return jax.ShapeDtypeStruct(shape, dtype)


def held(*arrays):
    return [pltpu.with_memory_space_constraint(a, pltpu.VMEM) for a in arrays]


def far(*arrays):
    return [pltpu.with_memory_space_constraint(a, pltpu.HBM) for a in arrays]


class Copies:
    def __init__(self, semaphores):
        self.semaphores, self.count, self.open = semaphores, 0, []

    def start(self, source, target):
        copy = pltpu.make_async_copy(source, target, self.semaphores.at[self.count])
        self.count += 1
        copy.start()
        self.open.append(copy)
        return copy

    def wait(self, *copies):
        for copy in copies:
            if any(copy is other for other in self.open):
                self.open = [other for other in self.open if other is not copy]
                copy.wait()

    def wait_all(self):
        self.wait(*self.open)


def pack_first(qkv_ref, gain_ref, offset_ref, qv_ref, out_w_ref, out_b_ref, gain_two_ref, offset_two_ref, down_b_ref, up_b_ref, out_ref, rows_ref):
    rows_ref[...] = jnp.zeros_like(rows_ref)
    weight = qkv_ref[...].astype(f32)
    line = lambda ref, count: ref[...].astype(f32).reshape(1, count)
    gain, offset, qv = line(gain_ref, 3), line(offset_ref, 3), line(qv_ref, 6)
    for r in range(3):
        for j in range(9):
            rows_ref[10 * r + j : 10 * r + j + 1, :] = weight[r : r + 1, 128 * j : 128 * j + 128]
        rows_ref[10 * r + 9 : 10 * r + 10, 0:1] = gain[:, r : r + 1]
        rows_ref[10 * r + 9 : 10 * r + 10, 1:2] = offset[:, r : r + 1]
        rows_ref[10 * r + 9 : 10 * r + 10, 2:4] = qv[:, 2 * r : 2 * r + 2]
    for k, ref in enumerate((out_b_ref, gain_two_ref, offset_two_ref, down_b_ref)):
        values = line(ref, 3)
        for r in range(3):
            rows_ref[30:31, 4 * r + k : 4 * r + k + 1] = values[:, r : r + 1]
    rows_ref[30:31, 12:24] = line(up_b_ref, 12)
    rows_ref[31:32, :] = out_w_ref[...].astype(f32)[2:3, 256:384]
    out_ref[...] = jnp.broadcast_to(rows_ref[...].astype(bf16)[None], out_ref.shape)


def pack_second(out_w_ref, up_ref, down_ref, out_ref, rows_ref):
    out_w = out_w_ref[...].astype(f32)
    up = up_ref[...].astype(f32)
    down = down_ref[...].astype(f32)
    for k in range(8):
        rows_ref[k : k + 1, :] = out_w[k // 3 : k // 3 + 1, 128 * (k % 3) : 128 * (k % 3) + 128]
    for k in range(36):
        rows_ref[8 + k : 9 + k, :] = up[k // 12 : k // 12 + 1, 128 * (k % 12) : 128 * (k % 12) + 128]
        rows_ref[44 + k : 45 + k, :] = down[k // 3 : k // 3 + 1, 128 * (k % 3) : 128 * (k % 3) + 128]
    out_ref[...] = jnp.broadcast_to(rows_ref[...].astype(bf16)[None], out_ref.shape)


def merge_slots(raw_ref, merged_ref):
    both = jnp.swapaxes(raw_ref[...], 0, 1)
    for slot in range(both.shape[0]):
        at = slot * ROWS
        merged_ref[at + ROWS - 16 : at + ROWS, :] = jnp.zeros((16, WIDTH), bf16)
        merged_ref[at : at + SPAN, :] = both[slot]


def run_pack_first(*args):
    return pl.pallas_call(
        pack_first,
        out_shape=pltpu.HBM((CHIPS, FIRST_ROWS, 128), bf16),
        scratch_shapes=[pltpu.VMEM((FIRST_ROWS, 128), f32)],
        compiler_params=params(8),
        cost_estimate=cost(2),
        name="pack_first",
    )(*far(*args))


def run_pack_second(*args):
    return pl.pallas_call(
        pack_second,
        out_shape=pltpu.HBM((CHIPS, SECOND_ROWS, 128), bf16),
        scratch_shapes=[pltpu.VMEM((SECOND_ROWS, 128), f32)],
        compiler_params=params(8),
        cost_estimate=cost(2),
        name="pack_second",
    )(*far(*args))


def total(arrived_ref):
    return jnp.sum(arrived_ref[...].astype(f32), axis=0)


def spread_lanes(rows, lane, width):
    index = lax.broadcasted_iota(jnp.int32, (1, width), 1)
    out = jnp.zeros((1, width), f32)
    for k, row in enumerate(rows):
        out = jnp.where(index == k, row[:, lane : lane + 1], out)
    return out.reshape(width)


def unpack_first(arrived_ref, qkv_ref, gain_ref, offset_ref, qv_ref):
    sums = total(arrived_ref)
    more = []
    for r in range(3):
        for j in range(9):
            qkv_ref[r : r + 1, 128 * j : 128 * j + 128] = sums[10 * r + j : 10 * r + j + 1, :]
        row = sums[10 * r + 9 : 10 * r + 10, :]
        more.append(row[:, 0:4] + row[:, 4:8])
    gain_ref[...] = spread_lanes(more, 0, 3)
    offset_ref[...] = spread_lanes(more, 1, 3)
    index = lax.broadcasted_iota(jnp.int32, (1, 6), 1)
    out = jnp.zeros((1, 6), f32)
    for k in range(6):
        out = jnp.where(index == k, more[k // 2][:, 2 + k % 2 : 3 + k % 2], out)
    qv_ref[...] = out.reshape(6)


def run_unpack_first(arrived):
    return pl.pallas_call(
        unpack_first,
        out_shape=[shape_of((3, 3 * WIDTH), f32), shape_of((3,), f32), shape_of((3,), f32), shape_of((6,), f32)],
        compiler_params=params(8),
        cost_estimate=cost(2),
        name="unpack_first",
    )(arrived)


def sum_column(line_ref, arrived_ref, keep_ref, one_ref, two_ref, three_ref, sums_ref):
    sums_ref[...] = total(arrived_ref)
    block = lambda shift: sums_ref[pl.ds(pl.multiple_of(lax.rem(line_ref[0] + shift, LINE) * REST_ROWS, 8), REST_ROWS), :]
    keep_ref[...] = block(0)
    for shift, ref in enumerate((one_ref, two_ref, three_ref)):
        ref[...] = block(shift + 1).astype(bf16)


def run_sum_column(line, arrived):
    arrays = pl.BlockSpec(memory_space=pltpu.VMEM)
    part = shape_of((REST_ROWS, 128), bf16)
    return pl.pallas_call(
        sum_column,
        in_specs=[pl.BlockSpec(memory_space=pltpu.SMEM), arrays],
        out_shape=[shape_of((REST_ROWS, 128), f32), part, part, part],
        scratch_shapes=[pltpu.VMEM((LINE * REST_ROWS, 128), f32)],
        compiler_params=params(12),
        cost_estimate=cost(2),
        name="sum_column",
    )(line, arrived)


def unpack_rest(keep_ref, one_ref, two_ref, three_ref, out_ref, up_ref, down_ref, out_b_ref, gain_ref, offset_ref, down_b_ref, up_b_ref, pairs_ref, turned_ref):
    sums = keep_ref[...] + sum(ref[...].astype(f32) for ref in (one_ref, two_ref, three_ref))
    more = []
    for r in range(3):
        for j in range(3):
            out_ref[r : r + 1, 128 * j : 128 * j + 128] = sums[3 * r + j : 3 * r + j + 1, :]
        line = sums[9 + 12 * r : 21 + 12 * r, :]
        pairs_ref[pl.ds(24 * r, 12, stride=2), 0:64] = line[:, 0:64]
        pairs_ref[pl.ds(24 * r + 1, 12, stride=2), 0:64] = line[:, 64:128]
        row = sums[81 + r : 82 + r, :]
        more.append(row[:, 0:4] + row[:, 4:8])
    turned_ref[...] = pairs_ref[...].T
    by_line = [turned_ref[pl.ds(y, 16, stride=4), :] for y in range(LINE)]
    for r in range(3):
        pieces = [by_line[y][:, 24 * r + 12 * c : 24 * r + 12 * c + 12] for c in range(2) for y in range(LINE)]
        lines = jnp.concatenate(pieces, 1)
        for column in range(16):
            up_ref[r : r + 1, 96 * column : 96 * column + 96] = lines[column : column + 1]
    for r in range(12):
        for j in range(3):
            down_ref[r : r + 1, 128 * j : 128 * j + 128] = sums[45 + 3 * r + j : 46 + 3 * r + j, :]
    for k, ref in enumerate((out_b_ref, gain_ref, offset_ref, down_b_ref)):
        ref[...] = spread_lanes(more, k, 3)
    up_b_ref[...] = (sums[84:85, 0:12] + sums[84:85, 12:24]).reshape(12)


def run_unpack_rest(*parts):
    return pl.pallas_call(
        unpack_rest,
        out_shape=[shape_of((3, WIDTH), f32), shape_of((3, HIDDEN), f32), shape_of((12, WIDTH), f32)]
        + [shape_of((3,), f32)] * 4
        + [shape_of((12,), f32)],
        scratch_shapes=[pltpu.VMEM((128, 128), f32), pltpu.VMEM((128, 128), f32)],
        compiler_params=params(12),
        cost_estimate=cost(2),
        name="unpack_rest",
    )(*parts)


def add_halves(mine_ref, theirs_ref, out_far, out_ref, semaphores):
    copies = Copies(semaphores)
    count = CHIPS // 4
    for at in range(0, CHIPS, count):
        out_ref[at : at + count] = mine_ref[at : at + count] + theirs_ref[at : at + count]
        part = pl.ds(at, count)
        copies.start(out_ref.at[part], out_far.at[part])
    copies.wait_all()


def run_add_halves(mine, theirs):
    arrays = pl.BlockSpec(memory_space=pltpu.VMEM)
    return pl.pallas_call(
        add_halves,
        in_specs=[arrays, arrays],
        out_specs=pl.BlockSpec(memory_space=pl.ANY),
        out_shape=pltpu.HBM(mine.shape, bf16),
        scratch_shapes=[pltpu.VMEM(mine.shape, bf16), pltpu.SemaphoreType.DMA((4,))],
        compiler_params=params(12),
        cost_estimate=cost(1),
        name="add_halves",
    )(*held(mine, theirs))


def forward_scores(unit, projected_ref, bias_ref, key_ref, value_ref, more):
    slot, base = unit
    scale = math.log2(math.e) / math.sqrt(HEAD)
    lanes = slice(slot * WIDE, slot * WIDE + WIDE)
    query_more, key_more, value_more = more[slot]
    wide = lambda start: jnp.concatenate([bias_ref[start : start + HEAD, :]] * (WIDE // 128), 1)
    queries, scores = [], []
    for h in range(base, base + FORWARD_BATCH):
        at = h * HEAD
        query = (projected_ref[at : at + HEAD, lanes] + wide(at)) * scale
        key = projected_ref[at + WIDTH : at + WIDTH + HEAD, lanes]
        value = projected_ref[at + 2 * WIDTH : at + 2 * WIDTH + HEAD, lanes] + wide(at + WIDTH)
        query = jnp.concatenate([query, query_more], 0)
        key = jnp.concatenate([key, key_more], 0).astype(bf16)
        key_ref[slot, 32 * h : 32 * h + 32, :] = key
        value_ref[slot, 32 * h : 32 * h + 32, :] = jnp.concatenate([value, value_more], 0).astype(bf16)
        low = query.astype(bf16)
        queries.append(query)
        scores.append([dot(key[:, :count], low[:, a:b], (0, 0)) for a, b, count in FORWARD_BLOCKS])
    return queries, scores


def forward_mixed(unit, queries, scores, mixed_scratch, query_ref, value_ref):
    slot, base = unit
    heads = range(base, base + FORWARD_BATCH)
    peaks = [[jnp.max(part, axis=0, keepdims=True) for part in parts] for parts in scores]
    weights = [[jnp.exp2(part - top).astype(bf16) for part, top in zip(*pair)] for pair in zip(scores, peaks)]
    values = [value_ref[slot, 32 * h : 32 * h + 32, :] for h in heads]
    got = [
        [dot(value[:, :count], part, (1, 0)) for part, (_, _, count) in zip(parts, FORWARD_BLOCKS)]
        for value, parts in zip(values, weights)
    ]
    zero = jnp.zeros((1, WIDE), f32)
    for h, query, tops, parts in zip(heads, queries, peaks, got):
        both = jnp.concatenate(parts, 1)
        row_total = both[HEAD : HEAD + 1]
        mixed_scratch[h * HEAD : h * HEAD + HEAD, :] = both[:HEAD] * (1.0 / row_total)
        logs = jnp.concatenate(tops, 1) + jnp.log2(row_total)
        log_rows = rows_of([zero, zero, zero, *three_parts(-logs)], WIDE)
        query_ref[slot, 32 * h : 32 * h + 32, :] = (query + jnp.concatenate([jnp.zeros((HEAD, WIDE), f32), log_rows], 0)).astype(bf16)


def forward_probs(unit, query_ref, key_ref, refs):
    slot, base = unit
    for h in range(base, base + FORWARD_BATCH):
        query, key = query_ref[slot, 32 * h : 32 * h + 32, :], key_ref[slot, 32 * h : 32 * h + 32, :]
        for ref, (start, a, b) in zip(refs, BACKWARD_BLOCKS):
            ref[h] = jnp.exp2(dot(query[:, start:ROWS], key[:, a:b], (0, 0))).astype(bf16)


def attention_forward(core_ref, counts_ref, tokens_far, own_ref, other_ref,
                      mixed_far, query_far, key_far, value_far, weight_far, first_far, merged_far, low_far, middle_far, high_far, column_far, extra_far,
                      first_ref, projected_ref, mixed_scratch, arrived_ref, bias_ref,
                      raw_ref, tokens_ref, mixed_ref, query_ref, key_ref, value_ref, weight_ref, low_ref, middle_ref, high_ref, column_ref, extra_ref, semaphores):
    slots = mixed_ref.shape[0]
    copies = Copies(semaphores)
    copies.start(tokens_far, raw_ref)
    core = core_ref[0]
    for k, (side, ref) in enumerate(((core, own_ref), (1 - core, other_ref))):
        blocks = jnp.swapaxes(ref[...], 0, 1)
        for r in range(3):
            at = pl.multiple_of(side * 192 + 64 * r, 64)
            for j in range(10):
                arrived_ref[pl.ds(at, 64), 128 * j : 128 * j + 128] = blocks[10 * r + j]
        extra_ref[2 * k] = blocks[30]
        extra_ref[2 * k + 1] = blocks[31]
    order = arrival_order()
    ordered = dot(order, arrived_ref[...], (1, 0))
    weight_ref[...] = ordered[:, : 3 * WIDTH].astype(bf16)
    column_ref[...] = ordered[:, 3 * WIDTH :]
    rows = dot(arrived_ref[:, 3 * WIDTH :], order, (0, 1))
    gain, offset = rows[0:1], rows[1:2]
    for s in range(2):
        column = ordered[:, 3 * WIDTH + 2 + s : 3 * WIDTH + 3 + s]
        bias_ref[pl.ds(s, WIDTH, stride=2), :] = jnp.broadcast_to(column, (WIDTH, 128))
    first_ref[...] = jnp.zeros_like(first_ref)
    copies.wait_all()
    merge_slots(raw_ref, tokens_ref)
    copies.start(tokens_ref, merged_far)
    copies.start(weight_ref, weight_far)
    copies.start(column_ref, column_far)
    copies.start(extra_ref, extra_far)
    for slot in range(slots):
        normed, _ = norm_parts(tokens_ref[slot * ROWS : slot * ROWS + ROWS, :].astype(f32))
        first_ref[slot * WIDE : slot * WIDE + ROWS, :] = (normed * gain + offset).astype(bf16)
    copies.start(first_ref, first_far)
    projected_ref[...] = dot(weight_ref[...], first_ref[...], (0, 1))
    one = jnp.ones((1, WIDE), f32)
    more = []
    for slot in range(slots):
        hidden, frame = mask_rows(counts_ref, slot)
        more.append((rows_of(frame, WIDE), rows_of(hidden + [one, one, one], WIDE), rows_of([one, one, one], WIDE)))
    units = [(slot, base) for slot in range(slots) for base in range(0, HEADS, FORWARD_BATCH)]
    refs = (low_ref, middle_ref, high_ref)
    kept = {}

    def probs(unit):
        slot, base = unit
        if slot * HEADS + base >= KEPT_HEADS:
            return
        copies.wait(*kept.get((slot - 1, base // LOAD_BATCH), ()))
        forward_probs(unit, query_ref, key_ref, refs)
        if (base + FORWARD_BATCH) % LOAD_BATCH == 0:
            part = pl.ds(base // LOAD_BATCH * LOAD_BATCH, LOAD_BATCH)
            pairs = zip(refs, (low_far, middle_far, high_far))
            kept[slot, base // LOAD_BATCH] = [copies.start(near.at[part], away.at[slot, part]) for near, away in pairs]

    def scores(unit):
        slot, base = unit
        got = forward_scores(unit, projected_ref, bias_ref, key_ref, value_ref, more)
        if base + FORWARD_BATCH == HEADS:
            for near, away in ((key_ref, key_far), (value_ref, value_far)):
                copies.start(near.at[slot], away.at[slot])
        return got

    ready = scores(units[0])
    for k, unit in enumerate(units):
        slot = unit[0]
        now, ready = ready, None
        if k + 1 < len(units):
            ready = scores(units[k + 1])
        if k >= 1:
            probs(units[k - 1])
        forward_mixed(unit, *now, mixed_scratch, query_ref, value_ref)
        if unit[1] + FORWARD_BATCH == HEADS:
            mixed_ref[slot] = mixed_scratch[...].astype(bf16)
            for near, away in ((query_ref, query_far), (mixed_ref, mixed_far)):
                copies.start(near.at[slot], away.at[slot])
    probs(units[-1])
    copies.wait_all()


def probs_shapes():
    return [(ROWS - start, b - a) for start, a, b in BACKWARD_BLOCKS]


def run_forward(core, counts, tokens, own, other):
    slots = tokens.shape[1]
    scalars = pl.BlockSpec(memory_space=pltpu.SMEM)
    arrays = pl.BlockSpec(memory_space=pltpu.VMEM)
    away = pl.BlockSpec(memory_space=pl.ANY)
    return pl.pallas_call(
        attention_forward,
        in_specs=[scalars, scalars, away, arrays, arrays],
        out_specs=[away] * 12,
        out_shape=[pltpu.HBM((slots, rows, WIDE), bf16) for rows in (WIDTH, 512, 512, 512)]
        + [pltpu.HBM((WIDTH, 3 * WIDTH), bf16), pltpu.HBM((slots * WIDE, WIDTH), bf16), pltpu.HBM((slots * ROWS, WIDTH), bf16)]
        + [pltpu.HBM((slots, HEADS, *shape), bf16) for shape in probs_shapes()]
        + [pltpu.HBM((WIDTH, 128), f32), pltpu.HBM((4, 64, 128), bf16)],
        scratch_shapes=[
            pltpu.VMEM((slots * WIDE, WIDTH), bf16),
            pltpu.VMEM((3 * WIDTH, slots * WIDE), f32),
            pltpu.VMEM((WIDTH, WIDE), f32),
            pltpu.VMEM((WIDTH, 3 * WIDTH + 128), bf16),
            pltpu.VMEM((2 * WIDTH + 8, 128), f32),
            pltpu.VMEM((SPAN, slots, WIDTH), bf16),
            pltpu.VMEM((slots * ROWS, WIDTH), bf16),
        ]
        + [pltpu.VMEM((slots, rows, WIDE), bf16) for rows in (WIDTH, 512, 512, 512)]
        + [pltpu.VMEM((WIDTH, 3 * WIDTH), bf16)]
        + [pltpu.VMEM((HEADS, *shape), bf16) for shape in probs_shapes()]
        + [pltpu.VMEM((WIDTH, 128), f32), pltpu.VMEM((4, 64, 128), bf16), pltpu.SemaphoreType.DMA((40,))],
        compiler_params=params(48),
        cost_estimate=cost(20),
        name="attention_forward",
    )(core, counts, *far(tokens), *held(own, other))


def feed_forward_early(cotangent_far, merged_far, mixed_far, extra_far, own_ref,
                       arrived_ref, down_ref, up_b_ref, cotangent_ref, tokens_ref, mixed_ref, slopes_ref, extra_ref, raw_ref, semaphores):
    copies = Copies(semaphores)
    extra = copies.start(extra_far, extra_ref)
    raw = copies.start(cotangent_far, raw_ref)
    copies.start(mixed_far, mixed_ref)
    copies.start(merged_far, tokens_ref)
    unpack_side(own_ref, lambda: (copies.wait(extra), extra_ref[0], extra_ref[1])[1:], arrived_ref, down_ref, up_b_ref)
    copies.wait(raw)
    merge_slots(raw_ref, cotangent_ref)
    slopes_ref[...] = dot(cotangent_ref[...], down_ref[...], (1, 1))
    copies.wait_all()


def unpack_side(message_ref, extra, arrived_ref, down_ref, up_b_ref):
    blocks = jnp.swapaxes(message_ref[...], 0, 1)
    for r in range(12):
        for j in range(3):
            down_ref[64 * r : 64 * r + 64, 128 * j : 128 * j + 128] = blocks[44 + 3 * r + j]
    for r in range(3):
        for j in range(12):
            arrived_ref[64 * r : 64 * r + 64, 384 + 128 * j : 512 + 128 * j] = blocks[8 + 12 * r + j]
    vectors, tile = extra()
    vectors = vectors.astype(f32)
    for r in range(3):
        rows = slice(64 * r, 64 * r + 64)
        for j in range(3):
            arrived_ref[rows, 128 * j : 128 * j + 128] = tile if 3 * r + j == 8 else blocks[3 * r + j]
        arrived_ref[rows, 1920:2048] = (pltpu.roll(vectors, 128 - 4 * r, 1) if r else vectors).astype(bf16)
    turned = vectors.T
    up_b_ref[0:1, :] = jnp.concatenate([turned[12 + r : 13 + r] for r in range(12)], 1)


def run_feed_forward_early(cotangent, merged, mixed, own, extra):
    _, slots, _ = cotangent.shape
    arrays = pl.BlockSpec(memory_space=pltpu.VMEM)
    away = pl.BlockSpec(memory_space=pl.ANY)
    return pl.pallas_call(
        feed_forward_early,
        in_specs=[away, away, away, away, arrays],
        out_shape=[
            pltpu.VMEM((WIDTH // 2, 2048), bf16),
            pltpu.VMEM((HIDDEN // 2, WIDTH), bf16),
            pltpu.VMEM((8, HIDDEN // 2), f32),
            pltpu.VMEM((slots * ROWS, WIDTH), bf16),
            pltpu.VMEM((slots * ROWS, WIDTH), bf16),
            pltpu.VMEM((slots, WIDTH, WIDE), bf16),
            pltpu.VMEM((slots * ROWS, HIDDEN // 2), f32),
            pltpu.VMEM((4, 64, 128), bf16),
        ],
        scratch_shapes=[pltpu.VMEM((SPAN, slots, WIDTH), bf16), pltpu.SemaphoreType.DMA((4,))],
        compiler_params=params(16),
        cost_estimate=cost(3),
        name="feed_forward_early",
    )(*far(cotangent, merged, mixed, extra), *held(own))


def feed_forward(core_ref, tokens_ref, mixed_ref, cotangent_ref, own_arrived_ref, own_down_ref, own_up_b_ref, slopes_ref, other_ref, extra_ref,
                 activated_ref, resid_ref, other_down_ref, row_ref, grad_resid_far, grad_mixed_far, mine_ref, theirs_ref,
                 arrived_ref, ordered_ref, up_b_ref, packed_ref, grad_down_ref, grad_resid_ref, grad_mixed_ref, second_ref, grad_up_ref,
                 semaphores):
    slots = mixed_ref.shape[0]
    block = 768
    root = math.sqrt(2.0 / math.pi)
    copies = Copies(semaphores)
    core = core_ref[0]
    sides = (core, 1 - core)
    places = [pl.multiple_of(side * (WIDTH // 2), 64) for side in sides]
    unpack_side(other_ref, lambda: (extra_ref[2], extra_ref[3]), arrived_ref, other_down_ref, up_b_ref)
    downs = (own_down_ref, other_down_ref)
    up_bs = (own_up_b_ref, up_b_ref)
    order = arrival_order()
    packed_ref[pl.ds(places[0], WIDTH // 2), :] = own_arrived_ref[...]
    packed_ref[pl.ds(places[1], WIDTH // 2), :] = arrived_ref[...]
    row_ref[...] = dot(packed_ref[:, 1920:], order, (0, 1))[0:8]
    ordered_ref[...] = dot(order, packed_ref[:, :1920], (1, 0)).astype(bf16)
    out_w = ordered_ref[:, :WIDTH]
    up_w = lambda half, at: ordered_ref[:, pl.ds(pl.multiple_of(WIDTH + sides[half] * (HIDDEN // 2) + at, 128), block)]
    out_b, gain, offset = (row_ref[k : k + 1] for k in range(3))
    spans = [slice(slot * ROWS, slot * ROWS + ROWS) for slot in range(slots)]
    norms = {}

    def enter(slot):
        resid = tokens_ref[spans[slot], :].astype(f32) + dot(mixed_ref[slot, :, :ROWS], out_w, (0, 0)) + out_b
        resid_ref[spans[slot], :] = resid
        norms[slot] = norm_parts(resid)
        second_ref[spans[slot], :] = (norms[slot][0] * gain + offset).astype(bf16)

    def products(work):
        slot, half, at = work
        rows = spans[slot]
        up = dot(second_ref[rows, :], up_w(half, at), (1, 0))
        if half == 0:
            return up, slopes_ref[rows, at : at + block]
        return up, dot(cotangent_ref[rows, :], other_down_ref[at : at + block, :], (1, 1))

    lines = {}

    def activate(work, up, grad_activated):
        slot, half, at = work
        rows, cols = spans[slot], slice(half * (HIDDEN // 2) + at, half * (HIDDEN // 2) + at + block)
        up = up + up_bs[half][0:1, at : at + block]
        square = up * up
        tanh = jnp.tanh(up * (root + (root * 0.044715) * square))
        half_tanh = 0.5 + 0.5 * tanh
        activated_ref[rows, cols] = (up * half_tanh).astype(bf16)
        slope = half_tanh + (up * (2.0 * half_tanh * (1.0 - half_tanh))) * (root + (3 * root * 0.044715) * square)
        grad_up = grad_activated * slope
        grad_up_ref[rows, cols] = grad_up.astype(bf16)
        line = jnp.sum(grad_up, axis=0, keepdims=True)
        lines[half, at] = lines[half, at] + line if (half, at) in lines else line

    works = [(slot, half, at) for slot in range(slots) for half in range(2) for at in range(0, HIDDEN // 2, block)]
    enter(0)
    ready = products(works[0])
    for slot in range(1, slots):
        enter(slot)
    for k, work in enumerate(works):
        now = ready
        if k + 1 < len(works):
            ready = products(works[k + 1])
        activate(work, *now)

    grad_branch = cotangent_ref[...]
    halves = [slice(0, HIDDEN // 2), slice(HIDDEN // 2, HIDDEN)]
    side_w = [ordered_ref[:, pl.ds(pl.multiple_of(WIDTH + side * (HIDDEN // 2), 128), HIDDEN // 2)] for side in sides]
    grad_seconds = [sum(dot(grad_up_ref[rows, cols], weight, (1, 1)) for cols, weight in zip(halves, side_w)) for rows in spans]
    attended, sums = [], []

    def leave(slot):
        normed, inverse = norms[slot]
        grad_second = grad_seconds[slot]
        scaled = grad_second * gain
        mean_one = jnp.mean(scaled, axis=-1, keepdims=True)
        mean_two = jnp.mean(scaled * normed, axis=-1, keepdims=True)
        grad_full = cotangent_ref[spans[slot], :].astype(f32)
        grad_resid = grad_full + inverse * (scaled - mean_one - normed * mean_two)
        grad_resid_ref[spans[slot], :] = grad_resid
        low = grad_resid.astype(bf16)
        attended.append(low)
        parts = [low.astype(f32), grad_second * normed, grad_second, grad_full]
        sums.append(jnp.concatenate([jnp.sum(part, axis=0, keepdims=True) for part in parts], 0))

    for slot in range(slots):
        leave(slot)
        cols = halves[slot % 2]
        grad_down_ref[cols, :] = dot(activated_ref[:, cols], grad_branch, (0, 0)).astype(bf16)
    copies.start(grad_resid_ref, grad_resid_far)
    for slot in range(slots):
        grad_mixed_ref[slot, :, 512:WIDE] = jnp.zeros((WIDTH, WIDE - 512), bf16)
        grad_mixed_ref[slot, :, :ROWS] = dot(out_w, attended[slot], (1, 1)).astype(bf16)
    copies.start(grad_mixed_ref, grad_mixed_far)
    grad_out = sum(dot(mixed_ref[slot, :, :ROWS], attended[slot], (1, 0)) for slot in range(slots))
    for side, cols in zip(sides, halves):
        at = pl.multiple_of(WIDTH + side * (HIDDEN // 2), 128)
        ordered_ref[:, pl.ds(at, HIDDEN // 2)] = dot(second_ref[...], grad_up_ref[:, cols], (0, 0)).astype(bf16)
    ordered_ref[:, :WIDTH] = grad_out.astype(bf16)
    packed_ref[:, :1920] = dot(order, ordered_ref[...], (0, 0)).astype(bf16)
    high, low = two_parts(sum(sums))
    rows = jnp.concatenate([high, low, jnp.zeros((120, WIDTH), f32)], 0).astype(bf16)
    packed_ref[:, 1920:] = dot(order, rows, (0, 1)).astype(bf16)
    blank = jnp.zeros((CHIPS, 128), bf16)
    for half, (place, ref) in enumerate(zip(places, (mine_ref, theirs_ref))):
        blocks = [blank] * REST_ROWS
        for r in range(3):
            at = pl.multiple_of(place + 64 * r, 64)
            for j in range(15):
                blocks[3 * r + j if j < 3 else 6 + 12 * r + j] = packed_ref[pl.ds(at, 64), 128 * j : 128 * j + 128]
            blocks[81 + r] = packed_ref[pl.ds(at, 64), 1920:2048]
        for r in range(12):
            at = half * (HIDDEN // 2) + 64 * r
            for j in range(3):
                blocks[45 + 3 * r + j] = grad_down_ref[at : at + 64, 128 * j : 128 * j + 128]
        high, low = two_parts(jnp.concatenate([lines[half, at] for at in range(0, HIDDEN // 2, block)], 1))
        rows = [part[:, 64 * r : 64 * r + 64] for part in (high, low) for r in range(12)]
        blocks[84] = rows_of(rows, 64, 128).T.astype(bf16)
        ref[...] = jnp.swapaxes(jnp.stack(blocks), 0, 1)
    copies.wait_all()


def run_feed_forward(core, tokens, mixed, cotangent, arrived, down, up_b, slopes, other, extra):
    slots = mixed.shape[0]
    arrays = pl.BlockSpec(memory_space=pltpu.VMEM)
    away = pl.BlockSpec(memory_space=pl.ANY)
    return pl.pallas_call(
        feed_forward,
        in_specs=[pl.BlockSpec(memory_space=pltpu.SMEM)] + [arrays] * 9,
        out_specs=[arrays, arrays, arrays, arrays, away, away, arrays, arrays],
        out_shape=[
            pltpu.VMEM((slots * ROWS, HIDDEN), bf16),
            pltpu.VMEM((slots * ROWS, WIDTH), f32),
            pltpu.VMEM((HIDDEN // 2, WIDTH), bf16),
            pltpu.VMEM((8, WIDTH), f32),
            pltpu.HBM((slots * ROWS, WIDTH), f32),
            pltpu.HBM((slots, WIDTH, WIDE), bf16),
            pltpu.VMEM((CHIPS, REST_ROWS, 128), bf16),
            pltpu.VMEM((CHIPS, REST_ROWS, 128), bf16),
        ],
        scratch_shapes=[
            pltpu.VMEM((WIDTH // 2, 2048), bf16),
            pltpu.VMEM((WIDTH, 1920), bf16),
            pltpu.VMEM((8, HIDDEN // 2), f32),
            pltpu.VMEM((WIDTH, 2048), bf16),
            pltpu.VMEM((HIDDEN, WIDTH), bf16),
            pltpu.VMEM((slots * ROWS, WIDTH), f32),
            pltpu.VMEM((slots, WIDTH, WIDE), bf16),
            pltpu.VMEM((slots * ROWS, WIDTH), bf16),
            pltpu.VMEM((slots * ROWS, HIDDEN), bf16),
            pltpu.SemaphoreType.DMA((2,)),
        ],
        compiler_params=params(34),
        cost_estimate=cost(17),
        name="feed_forward",
    )(core, *held(tokens, mixed, cotangent, arrived, down, up_b, slopes, other, extra))


def feed_forward_output(activated_ref, resid_ref, own_down_ref, other_down_ref, row_ref, out_far, out_ref, semaphores):
    slots = out_ref.shape[1]
    copies = Copies(semaphores)
    half, middle = HIDDEN // 2, ROWS // 2
    for low, high in ((0, middle), (middle, SPAN)):
        both = []
        for slot in range(slots):
            at = slice(slot * ROWS + low, slot * ROWS + low + middle)
            result = resid_ref[at, :] + row_ref[3:4]
            result += dot(activated_ref[at, :half], own_down_ref[...], (1, 0)) + dot(activated_ref[at, half:], other_down_ref[...], (1, 0))
            both.append(result[: high - low])
        out_ref[low:high] = jnp.swapaxes(jnp.stack(both), 0, 1).astype(bf16)
        part = pl.ds(low, high - low)
        copies.start(out_ref.at[part], out_far.at[part])
    copies.wait_all()


def run_feed_forward_output(*args):
    slots = args[1].shape[0] // ROWS
    return pl.pallas_call(
        feed_forward_output,
        out_specs=pl.BlockSpec(memory_space=pl.ANY),
        out_shape=pltpu.HBM((SPAN, slots, WIDTH), bf16),
        scratch_shapes=[pltpu.VMEM((SPAN, slots, WIDTH), bf16), pltpu.SemaphoreType.DMA((2,))],
        compiler_params=params(20),
        cost_estimate=cost(3),
        name="feed_forward_output",
    )(*held(*args))


def backward_slopes(unit, copies, loads, value_ref, mixed_ref, grad_mixed_ref):
    slot, base = unit
    copies.wait(*loads["grad"][slot])
    grads, slopes = [], []
    for h in range(base, base + BACKWARD_BATCH):
        both = slice(48 * (h // 2), 48 * (h // 2) + 48)
        part = slice(HEAD * (h % 2), HEAD * (h % 2) + HEAD)
        grad = grad_mixed_ref[slot, both, :].astype(f32)[part]
        mixed = mixed_ref[slot, both, :].astype(f32)[part]
        shift = jnp.sum(grad * mixed, axis=0, keepdims=True)
        grad = jnp.concatenate([grad, rows_of(three_parts(-shift), WIDE)], 0).astype(bf16)
        value = value_ref[slot, 32 * h : 32 * h + 32, :]
        grads.append(grad)
        slopes.append([dot(grad[:, start:ROWS], value[:, a:b], (0, 0)) for start, a, b in BACKWARD_BLOCKS])
    return grads, slopes


def backward_products(unit, grads, slopes, copies, loads, query_ref, key_ref, probs_refs, turned_ref):
    slot, base = unit
    heads = range(base, base + BACKWARD_BATCH)
    copies.wait(*loads["query"][slot])
    queries = [query_ref[slot, 32 * h : 32 * h + 32, :] for h in heads]
    keys = [key_ref[slot, 32 * h : 32 * h + 32, :] for h in heads]
    if slot * HEADS + base < KEPT_HEADS:
        copies.wait(*loads["probs"][slot][base // LOAD_BATCH])
        probs = [[ref[slot, h].astype(f32) for ref in probs_refs] for h in heads]
    else:
        probs = [
            [jnp.exp2(dot(query[:, start:ROWS], key[:, a:b], (0, 0))) for start, a, b in BACKWARD_BLOCKS]
            for query, key in zip(queries, keys)
        ]
    grad_scores = [[(part * slope).astype(bf16) for part, slope in zip(*pair)] for pair in zip(probs, slopes)]
    probs = [[part.astype(bf16) for part in parts] for parts in probs]
    over = lambda left, parts: jnp.concatenate(
        [dot(left[:, start:ROWS], part, (1, 0)) for part, (start, _, _) in zip(parts, BACKWARD_BLOCKS)], 1)
    grad_v = [over(grad, parts) for grad, parts in zip(grads, probs)]
    grad_k = [over(query, parts) for query, parts in zip(queries, grad_scores)]
    grad_q = [
        [dot(key[:, a:b], part, (1, 1)) for part, (_, a, b) in zip(parts, BACKWARD_BLOCKS)]
        for key, parts in zip(keys, grad_scores)
    ]
    fill = lambda part: jnp.concatenate([jnp.zeros((32, ROWS - part.shape[1]), f32), part], 1) if part.shape[1] < ROWS else part
    blank = jnp.zeros((HEAD, WIDE - ROWS), f32)
    whole_q = [jnp.concatenate([sum(fill(part) for part in parts)[:HEAD] * (1.0 / math.sqrt(HEAD)), blank], 1) for parts in grad_q]
    whole_k = [part[:HEAD] * math.log(2.0) for part in grad_k]
    whole_v = [part[:HEAD] for part in grad_v]
    for k in range(0, BACKWARD_BATCH, 2):
        at = (base + k) * HEAD
        for offset, parts in ((0, whole_q), (WIDTH, whole_k), (2 * WIDTH, whole_v)):
            turned_ref[slot, offset + at : offset + at + 2 * HEAD, :] = jnp.concatenate(parts[k : k + 2], 0).astype(bf16)


def attention_backward(core_ref, query_far, key_far, value_far, mixed_far, grad_mixed_far, low_far, middle_far, high_far, first_far, weight_far,
                       column_far, turned_far, mine_ref, theirs_ref,
                       bias_ref, packed_ref, turned_ref,
                       query_ref, key_ref, value_ref, mixed_ref, grad_mixed_ref, low_ref, middle_ref, high_ref, first_ref, weight_ref, column_ref, semaphores):
    slots = mixed_ref.shape[0]
    copies = Copies(semaphores)
    loads = {"grad": [], "probs": [], "query": []}
    probs_refs = (low_ref, middle_ref, high_ref)
    for slot in range(slots):
        load = lambda pairs: [copies.start(away.at[slot], near.at[slot]) for away, near in pairs]
        loads["grad"].append(load(((value_far, value_ref), (grad_mixed_far, grad_mixed_ref), (mixed_far, mixed_ref))))
        loads["probs"].append([])
        for base in range(0, HEADS, LOAD_BATCH):
            if slot * HEADS + base < KEPT_HEADS:
                part = pl.ds(base, LOAD_BATCH)
                pairs = zip((low_far, middle_far, high_far), probs_refs)
                loads["probs"][slot].append([copies.start(away.at[slot, part], near.at[slot, part]) for away, near in pairs])
            if base == 0:
                loads["query"].append(load(((query_far, query_ref), (key_far, key_ref))))
    weights = [copies.start(first_far, first_ref.at[:, pl.ds(0, WIDTH)]), copies.start(weight_far, weight_ref), copies.start(column_far, column_ref)]
    core = core_ref[0]
    units = [(slot, base) for slot in range(slots) for base in range(0, HEADS, BACKWARD_BATCH)]
    ready = backward_slopes(units[0], copies, loads, value_ref, mixed_ref, grad_mixed_ref)
    for k, unit in enumerate(units):
        slot = unit[0]
        now, ready = ready, None
        if k + 1 < len(units):
            ready = backward_slopes(units[k + 1], copies, loads, value_ref, mixed_ref, grad_mixed_ref)
        backward_products(unit, *now, copies, loads, query_ref, key_ref, probs_refs, turned_ref)
        if unit[1] + BACKWARD_BATCH == HEADS:
            copies.start(turned_ref.at[slot], turned_far.at[slot])
    copies.wait(*weights)
    order = arrival_order()
    turned = jnp.concatenate([turned_ref[slot] for slot in range(slots)], 1)
    first_ref[:, WIDTH:] = jnp.ones((slots * WIDE, 128), bf16)
    grad_more = dot(first_ref[:, : WIDTH + 16], turned, (0, 1))
    grad_weight, sums = grad_more[:WIDTH], grad_more[WIDTH : WIDTH + 1]
    packed_ref[:, : 3 * WIDTH] = dot(order, grad_weight.astype(bf16), (0, 0)).astype(bf16)
    weight = weight_ref[...].astype(f32)
    grad_offset = jnp.sum(weight * sums, axis=1, keepdims=True)
    along = jnp.sum(grad_weight * weight, axis=1, keepdims=True)
    grad_gain = (along - column_ref[:, 1:2] * grad_offset) / column_ref[:, 0:1]
    bias_ref[0:WIDTH] = jnp.broadcast_to(sums[:, :WIDTH], (128, WIDTH)).T
    bias_ref[WIDTH : 2 * WIDTH] = jnp.broadcast_to(sums[:, 2 * WIDTH :], (128, WIDTH)).T
    lane = lax.broadcasted_iota(jnp.int32, (WIDTH, 128), 1)
    columns = jnp.zeros((WIDTH, 128), f32)
    for k, values in enumerate((grad_gain, grad_offset, bias_ref[pl.ds(0, WIDTH, stride=2), :], bias_ref[pl.ds(1, WIDTH, stride=2), :])):
        high, low = two_parts(values)
        columns = jnp.where(lane == k, high, jnp.where(lane == 4 + k, low, columns))
    packed_ref[:, 3 * WIDTH :] = dot(order, columns.astype(bf16), (0, 0)).astype(bf16)
    blank = jnp.zeros((CHIPS, 128), bf16)
    for side, ref in ((core, mine_ref), (1 - core, theirs_ref)):
        blocks = []
        for r in range(3):
            at = pl.multiple_of(side * 192 + 64 * r, 64)
            for j in range(10):
                blocks.append(packed_ref[pl.ds(at, 64), 128 * j : 128 * j + 128])
        ref[...] = jnp.swapaxes(jnp.stack(blocks + [blank, blank]), 0, 1)
    copies.wait_all()


def run_backward(core, query, key, value, mixed, grad_mixed, low, middle, high, first, weight, column):
    slots = mixed.shape[0]
    arrays = pl.BlockSpec(memory_space=pltpu.VMEM)
    away = pl.BlockSpec(memory_space=pl.ANY)
    return pl.pallas_call(
        attention_backward,
        in_specs=[pl.BlockSpec(memory_space=pltpu.SMEM)] + [away] * 11,
        out_specs=[away, arrays, arrays],
        out_shape=[
            pltpu.HBM((slots, 3 * WIDTH, WIDE), bf16),
            pltpu.VMEM((CHIPS, FIRST_ROWS, 128), bf16),
            pltpu.VMEM((CHIPS, FIRST_ROWS, 128), bf16),
        ],
        scratch_shapes=[
            pltpu.VMEM((2 * WIDTH + 8, 128), f32),
            pltpu.VMEM((WIDTH, 3 * WIDTH + 128), bf16),
            pltpu.VMEM((slots, 3 * WIDTH, WIDE), bf16),
        ]
        + [pltpu.VMEM((slots, rows, WIDE), bf16) for rows in (512, 512, 512, WIDTH, WIDTH)]
        + [pltpu.VMEM((slots, HEADS, *shape), bf16) for shape in probs_shapes()]
        + [pltpu.VMEM((slots * WIDE, WIDTH + 128), bf16), pltpu.VMEM((WIDTH, 3 * WIDTH), bf16), pltpu.VMEM((WIDTH, 128), f32), pltpu.SemaphoreType.DMA((70,))],
        compiler_params=params(56),
        cost_estimate=cost(22),
        name="attention_backward",
    )(core, *far(query, key, value, mixed, grad_mixed, low, middle, high, first, weight, column))


def input_backward(merged_far, turned_far, grad_resid_far, weight_far, column_far, out_far,
                   tokens_ref, turned_ref, grad_resid_ref, weight_ref, grad_first_ref, out_ref, column_ref, semaphores):
    slots = turned_ref.shape[0]
    copies = Copies(semaphores)
    first = [copies.start(weight_far, weight_ref), copies.start(turned_far.at[0], turned_ref.at[0])]
    turns = [copies.start(turned_far.at[slot], turned_ref.at[slot]) for slot in range(1, slots)]
    rest = [copies.start(column_far, column_ref), copies.start(merged_far, tokens_ref), copies.start(grad_resid_far, grad_resid_ref)]
    copies.wait(*first)
    for slot in range(slots):
        if slot:
            copies.wait(turns[slot - 1])
        grad_first_ref[slot * ROWS : slot * ROWS + ROWS, :] = dot(turned_ref[slot, :, :ROWS], weight_ref[...], (0, 1))
    copies.wait(*rest)
    gain = column_ref[...].T[0:1]
    half = ROWS // 2
    for low, high in ((0, half), (half, SPAN)):
        for slot in range(slots):
            at = slice(slot * ROWS + low, slot * ROWS + low + half)
            normed, inverse = norm_parts(tokens_ref[at, :].astype(f32))
            scaled = grad_first_ref[at, :] * gain
            mean_one = jnp.mean(scaled, axis=-1, keepdims=True)
            mean_two = jnp.mean(scaled * normed, axis=-1, keepdims=True)
            grad = grad_resid_ref[at, :] + inverse * (scaled - mean_one - normed * mean_two)
            out_ref[low:high, slot, :] = grad[: high - low]
        copies.start(out_ref.at[pl.ds(low, high - low)], out_far.at[pl.ds(low, high - low)])
    copies.wait_all()


def run_input_backward(merged, turned, grad_resid, weight, column):
    slots = turned.shape[0]
    arrays = pl.BlockSpec(memory_space=pltpu.VMEM)
    away = pl.BlockSpec(memory_space=pl.ANY)
    return pl.pallas_call(
        input_backward,
        in_specs=[away] * 5,
        out_specs=away,
        out_shape=pltpu.HBM((SPAN, slots, WIDTH), f32),
        scratch_shapes=[
            pltpu.VMEM((slots * ROWS, WIDTH), bf16),
            pltpu.VMEM((slots, 3 * WIDTH, WIDE), bf16),
            pltpu.VMEM((slots * ROWS, WIDTH), f32),
            pltpu.VMEM((WIDTH, 3 * WIDTH), bf16),
            pltpu.VMEM((slots * ROWS, WIDTH), f32),
            pltpu.VMEM((SPAN, slots, WIDTH), f32),
            pltpu.VMEM((WIDTH, 128), f32),
            pltpu.SemaphoreType.DMA((8,)),
        ],
        compiler_params=params(32),
        cost_estimate=cost(6),
        name="input_backward",
    )(*far(merged, turned, grad_resid, weight, column))


def to_chips(message):
    return lax.all_to_all(message, CHIP_AXES, 0, 0, tiled=True)


def to_column(message):
    return lax.all_to_all(message, COLUMN_AXES, 0, 0, tiled=True)


def along_line(message, shift):
    return lax.ppermute(message, LINE_AXIS, [(k, (k + shift) % LINE) for k in range(LINE)])


def across(message):
    return lax.ppermute(message, CORE_AXIS, [(0, 1), (1, 0)])


def shards(tokens, item_frames, ln1_gain, ln1_bias, qkv_weight, qv_bias, out_weight, out_bias, ln2_gain, ln2_bias,
           up_weight, up_bias, down_weight, down_bias, cotangent):
    together = lax.optimization_barrier
    core = lax.axis_index(CORE_AXIS).astype(jnp.int32).reshape(1)
    line = lax.axis_index(LINE_AXIS).astype(jnp.int32).reshape(1)
    first = run_pack_first(qkv_weight, ln1_gain, ln1_bias, qv_bias, out_weight, out_bias, ln2_gain, ln2_bias, down_bias, up_bias)
    first, up_weight = together((first, up_weight))
    first = to_chips(first)
    up_sent = up_weight.reshape(3, 16, 2, 4, 12).transpose(0, 2, 4, 1, 3).reshape(3, HIDDEN)
    second = run_pack_second(out_weight, up_sent, down_weight)
    tokens, cotangent = tokens.transpose(1, 0, 2), cotangent.transpose(1, 0, 2)
    first, second = together((first, second))
    first_other = across(first)
    second = to_chips(second)
    mixed, query, key, value, weight, normed, merged, low, middle, high, column, extra = run_forward(core, item_frames, tokens, first, first_other)
    second, mixed = together((second, mixed))
    other = across(second)
    arrived, own_down, up_b, turned_cotangent, near, near_mixed, slopes, extra = run_feed_forward_early(cotangent, merged, mixed, second, extra)
    activated, resid, other_down, row, grad_resid, grad_mixed, mine, theirs = run_feed_forward(
        core, near, near_mixed, turned_cotangent, arrived, own_down, up_b, slopes, other, extra)
    theirs = across(theirs)
    output = run_feed_forward_output(activated, resid, own_down, other_down, row)
    output, mine = together((output, mine))
    output = output.transpose(1, 0, 2)
    rest = run_add_halves(mine, theirs)
    rest, grad_mixed = together((rest, grad_mixed))
    rest = to_column(rest.reshape(CHIPS // LINE, LINE * REST_ROWS, 128))
    turned, mine, theirs = run_backward(core, query, key, value, mixed, grad_mixed, low, middle, high, normed, weight, column)
    theirs = across(theirs)
    own = run_add_halves(mine, theirs)
    own, rest = together((own, rest))
    own, turned = together((own, turned))
    own = to_chips(own)
    keep, *sent = run_sum_column(line, rest)
    sent = [along_line(part, shift + 1) for shift, part in enumerate(sent)]
    grad_out, grad_up, *others = run_unpack_rest(keep, *sent)
    grad_down, grad_out_b, grad_gain_two, grad_offset_two, grad_down_b, grad_up_b = others
    input_grad = run_input_backward(merged, turned, grad_resid, weight, column).transpose(1, 0, 2)
    grad_qkv, grad_gain, grad_offset, grad_qv = run_unpack_first(own)
    return (output, input_grad, grad_gain, grad_offset, grad_qkv, grad_qv, grad_out, grad_out_b, grad_gain_two, grad_offset_two,
            grad_up, grad_up_b, grad_down, grad_down_b)


def solution(mesh):
    split = Mesh(mesh.devices.reshape(4, 4, 2, mesh.shape["narrow"]), ALL)
    by_rank = lambda n: P(ALL, *([None] * (n - 1)))
    return jax.shard_map(
        shards,
        mesh=split,
        in_specs=tuple(by_rank(n) for n in (3, 2, 1, 1, 2, 1, 2, 1, 1, 1, 2, 1, 2, 1, 3)),
        out_specs=tuple(by_rank(n) for n in (3, 3, 1, 1, 2, 1, 2, 1, 1, 1, 2, 1, 2, 1)),
        check_vma=False,
    )
```

```python
import math

import jax
import jax.numpy as jnp
from jax import lax
from jax.experimental import pallas as pl
from jax.experimental.pallas import tpu as pltpu
from jax.sharding import Mesh
from jax.sharding import PartitionSpec as P

HEADS = 16
HEAD = 24
FRAME = 196
WIDTH = 384
HIDDEN = 1536
WIDE = 640
SPAN = 588
ROWS = 592
CHIPS = 64
FIRST_ROWS = 32
PACKED = 8
REST_ROWS = 88
SECOND_ROWS = 80
EPSILON = 1e-05
NEGATIVE = -1e30
bf16 = jnp.bfloat16
f32 = jnp.float32
FORWARD_BLOCKS = ((0, 128, 208), (128, 384, 400), (384, 640, 592))
FORWARD_BATCH = 8
LOAD_BATCH = 8
KEPT_HEADS = 24
BACKWARD_BATCH = 4
BACKWARD_BLOCKS = ((0, 0, 256), (192, 256, 512), (384, 512, 640))
ALL = ("wide_0", "wide_1", "wide_2", "narrow")
CHIP_AXES = ("wide_0", "wide_1", "narrow")
COLUMN_AXES = ("wide_0", "wide_1")
LINE_AXIS = "narrow"
LINE = 4
CORE_AXIS = "wide_2"


def dot(left, right, over):
    return lax.dot_general(left, right, (((over[0],), (over[1],)), ((), ())), preferred_element_type=f32)


def norm_parts(values):
    centred = values - jnp.mean(values, axis=-1, keepdims=True)
    inverse = lax.rsqrt(jnp.mean(centred * centred, axis=-1, keepdims=True) + EPSILON)
    return centred * inverse, inverse


def two_parts(values):
    high = values.astype(bf16).astype(f32)
    return high, values - high


def three_parts(values):
    high, rest = two_parts(values)
    middle, low = two_parts(rest)
    return high, middle, low


def rows_of(rows, width, count=8):
    index = lax.broadcasted_iota(jnp.int32, (count, width), 0)
    out = jnp.zeros((count, width), f32)
    for k, row in enumerate(rows):
        out = jnp.where(index == k, row, out)
    return out


def arrival_order():
    place = lax.broadcasted_iota(jnp.int32, (WIDTH, WIDTH), 1)
    feature = lax.broadcasted_iota(jnp.int32, (WIDTH, WIDTH), 0)
    core = (place >= WIDTH // 2).astype(jnp.int32)
    rest = place - core * (WIDTH // 2)
    row = rest >> 6
    chip = rest & 63
    return (feature == 3 * (8 * (chip >> 2) + 4 * core + (chip & 3)) + row).astype(f32).astype(bf16)


def mask_rows(counts_ref, slot):
    lane = lax.broadcasted_iota(jnp.int32, (1, WIDE), 1)
    first_end = counts_ref[slot, 0]
    second_end = first_end + counts_ref[slot, 1]
    third_end = second_end + counts_ref[slot, 2]
    group = [
        (f >= first_end).astype(jnp.int32) + (f >= second_end).astype(jnp.int32) + (f >= third_end).astype(jnp.int32)
        for f in range(3)
    ]
    hidden = []
    for f in range(3):
        row = jnp.full((1, WIDE), NEGATIVE, f32)
        for k in range(f + 1):
            seen = jnp.where(group[f] == group[k], 0.0, NEGATIVE).astype(f32)
            row = jnp.where((lane >= FRAME * k) & (lane < FRAME * (k + 1)), seen, row)
        hidden.append(row)
    frame = [((lane >= FRAME * f) & ((lane < FRAME * (f + 1)) | (f == 2))).astype(f32) for f in range(3)]
    return hidden, frame


def params(mebibytes):
    return pltpu.CompilerParams(vmem_limit_bytes=mebibytes * 2**20)


def cost(microseconds):
    return pl.CostEstimate(flops=int(microseconds * 1.1e9), bytes_accessed=2**20, transcendentals=0)


def shape_of(shape, dtype):
    return jax.ShapeDtypeStruct(shape, dtype)


def held(*arrays):
    return [pltpu.with_memory_space_constraint(a, pltpu.VMEM) for a in arrays]


def far(*arrays):
    return [pltpu.with_memory_space_constraint(a, pltpu.HBM) for a in arrays]


class Copies:
    def __init__(self, semaphores):
        self.semaphores, self.count, self.open = semaphores, 0, []

    def start(self, source, target):
        copy = pltpu.make_async_copy(source, target, self.semaphores.at[self.count])
        self.count += 1
        copy.start()
        self.open.append(copy)
        return copy

    def wait(self, *copies):
        for copy in copies:
            if any(copy is other for other in self.open):
                self.open = [other for other in self.open if other is not copy]
                copy.wait()

    def wait_all(self):
        self.wait(*self.open)


def pack_first(qkv_ref, gain_ref, offset_ref, qv_ref, out_w_ref, out_b_ref, gain_two_ref, offset_two_ref, down_b_ref, up_b_ref, out_far, rows_ref, block_ref, semaphores):
    rows_ref[...] = jnp.zeros_like(rows_ref)
    weight = qkv_ref[...].astype(f32)
    line = lambda ref, count: ref[...].astype(f32).reshape(1, count)
    gain, offset, qv = line(gain_ref, 3), line(offset_ref, 3), line(qv_ref, 6)
    for r in range(3):
        for j in range(9):
            rows_ref[10 * r + j : 10 * r + j + 1, :] = weight[r : r + 1, 128 * j : 128 * j + 128]
        rows_ref[10 * r + 9 : 10 * r + 10, 0:1] = gain[:, r : r + 1]
        rows_ref[10 * r + 9 : 10 * r + 10, 1:2] = offset[:, r : r + 1]
        rows_ref[10 * r + 9 : 10 * r + 10, 2:4] = qv[:, 2 * r : 2 * r + 2]
    for k, ref in enumerate((out_b_ref, gain_two_ref, offset_two_ref, down_b_ref)):
        values = line(ref, 3)
        for r in range(3):
            rows_ref[30:31, 4 * r + k : 4 * r + k + 1] = values[:, r : r + 1]
    rows_ref[30:31, 12:24] = line(up_b_ref, 12)
    rows_ref[31:32, :] = out_w_ref[...].astype(f32)[2:3, 256:384]
    block_ref[...] = jnp.broadcast_to(rows_ref[...].astype(bf16)[None], block_ref.shape)
    copies = Copies(semaphores)
    for at in range(0, CHIPS, PACKED):
        copies.start(block_ref, out_far.at[pl.ds(at, PACKED)])
    copies.wait_all()


def pack_second(out_w_ref, up_ref, down_ref, out_ref, rows_ref):
    out_w = out_w_ref[...].astype(f32)
    up = up_ref[...].astype(f32)
    down = down_ref[...].astype(f32)
    for k in range(8):
        rows_ref[k : k + 1, :] = out_w[k // 3 : k // 3 + 1, 128 * (k % 3) : 128 * (k % 3) + 128]
    for k in range(36):
        rows_ref[8 + k : 9 + k, :] = up[k // 12 : k // 12 + 1, 128 * (k % 12) : 128 * (k % 12) + 128]
        rows_ref[44 + k : 45 + k, :] = down[k // 3 : k // 3 + 1, 128 * (k % 3) : 128 * (k % 3) + 128]
    out_ref[...] = jnp.broadcast_to(rows_ref[...].astype(bf16)[None], out_ref.shape)


def merge_slots(raw_ref, merged_ref):
    both = jnp.swapaxes(raw_ref[...], 0, 1)
    for slot in range(both.shape[0]):
        at = slot * ROWS
        merged_ref[at + ROWS - 16 : at + ROWS, :] = jnp.zeros((16, WIDTH), bf16)
        merged_ref[at : at + SPAN, :] = both[slot]


def run_pack_first(*args):
    return pl.pallas_call(
        pack_first,
        out_shape=pltpu.HBM((CHIPS, FIRST_ROWS, 128), bf16),
        out_specs=pl.BlockSpec(memory_space=pl.ANY),
        scratch_shapes=[
            pltpu.VMEM((FIRST_ROWS, 128), f32),
            pltpu.VMEM((PACKED, FIRST_ROWS, 128), bf16),
            pltpu.SemaphoreType.DMA((CHIPS // PACKED,)),
        ],
        compiler_params=params(8),
        cost_estimate=cost(2),
        name="pack_first",
    )(*far(*args))


def run_pack_second(*args):
    return pl.pallas_call(
        pack_second,
        out_shape=pltpu.HBM((CHIPS, SECOND_ROWS, 128), bf16),
        scratch_shapes=[pltpu.VMEM((SECOND_ROWS, 128), f32)],
        compiler_params=params(8),
        cost_estimate=cost(2),
        name="pack_second",
    )(*far(*args))


def total(arrived_ref):
    return jnp.sum(arrived_ref[...].astype(f32), axis=0)


def spread_lanes(rows, lane, width):
    index = lax.broadcasted_iota(jnp.int32, (1, width), 1)
    out = jnp.zeros((1, width), f32)
    for k, row in enumerate(rows):
        out = jnp.where(index == k, row[:, lane : lane + 1], out)
    return out.reshape(width)


def unpack_first(arrived_ref, qkv_ref, gain_ref, offset_ref, qv_ref):
    sums = total(arrived_ref)
    more = []
    for r in range(3):
        for j in range(9):
            qkv_ref[r : r + 1, 128 * j : 128 * j + 128] = sums[10 * r + j : 10 * r + j + 1, :]
        row = sums[10 * r + 9 : 10 * r + 10, :]
        more.append(row[:, 0:4] + row[:, 4:8])
    gain_ref[...] = spread_lanes(more, 0, 3)
    offset_ref[...] = spread_lanes(more, 1, 3)
    index = lax.broadcasted_iota(jnp.int32, (1, 6), 1)
    out = jnp.zeros((1, 6), f32)
    for k in range(6):
        out = jnp.where(index == k, more[k // 2][:, 2 + k % 2 : 3 + k % 2], out)
    qv_ref[...] = out.reshape(6)


def run_unpack_first(arrived):
    return pl.pallas_call(
        unpack_first,
        out_shape=[shape_of((3, 3 * WIDTH), f32), shape_of((3,), f32), shape_of((3,), f32), shape_of((6,), f32)],
        compiler_params=params(8),
        cost_estimate=cost(2),
        name="unpack_first",
    )(arrived)


def sum_column(line_ref, arrived_ref, keep_ref, one_ref, two_ref, three_ref, sums_ref):
    sums_ref[...] = total(arrived_ref)
    block = lambda shift: sums_ref[pl.ds(pl.multiple_of(lax.rem(line_ref[0] + shift, LINE) * REST_ROWS, 8), REST_ROWS), :]
    keep_ref[...] = block(0)
    for shift, ref in enumerate((one_ref, two_ref, three_ref)):
        ref[...] = block(shift + 1).astype(bf16)


def run_sum_column(line, arrived):
    arrays = pl.BlockSpec(memory_space=pltpu.VMEM)
    part = shape_of((REST_ROWS, 128), bf16)
    return pl.pallas_call(
        sum_column,
        in_specs=[pl.BlockSpec(memory_space=pltpu.SMEM), arrays],
        out_shape=[shape_of((REST_ROWS, 128), f32), part, part, part],
        scratch_shapes=[pltpu.VMEM((LINE * REST_ROWS, 128), f32)],
        compiler_params=params(12),
        cost_estimate=cost(2),
        name="sum_column",
    )(line, arrived)


def unpack_rest(keep_ref, one_ref, two_ref, three_ref, out_ref, up_ref, down_ref, out_b_ref, gain_ref, offset_ref, down_b_ref, up_b_ref, pairs_ref, turned_ref):
    sums = keep_ref[...] + sum(ref[...].astype(f32) for ref in (one_ref, two_ref, three_ref))
    more = []
    for r in range(3):
        for j in range(3):
            out_ref[r : r + 1, 128 * j : 128 * j + 128] = sums[3 * r + j : 3 * r + j + 1, :]
        line = sums[9 + 12 * r : 21 + 12 * r, :]
        pairs_ref[pl.ds(24 * r, 12, stride=2), 0:64] = line[:, 0:64]
        pairs_ref[pl.ds(24 * r + 1, 12, stride=2), 0:64] = line[:, 64:128]
        row = sums[81 + r : 82 + r, :]
        more.append(row[:, 0:4] + row[:, 4:8])
    turned_ref[...] = pairs_ref[...].T
    by_line = [turned_ref[pl.ds(y, 16, stride=4), :] for y in range(LINE)]
    for r in range(3):
        pieces = [by_line[y][:, 24 * r + 12 * c : 24 * r + 12 * c + 12] for c in range(2) for y in range(LINE)]
        lines = jnp.concatenate(pieces, 1)
        for column in range(16):
            up_ref[r : r + 1, 96 * column : 96 * column + 96] = lines[column : column + 1]
    for r in range(12):
        for j in range(3):
            down_ref[r : r + 1, 128 * j : 128 * j + 128] = sums[45 + 3 * r + j : 46 + 3 * r + j, :]
    for k, ref in enumerate((out_b_ref, gain_ref, offset_ref, down_b_ref)):
        ref[...] = spread_lanes(more, k, 3)
    up_b_ref[...] = (sums[84:85, 0:12] + sums[84:85, 12:24]).reshape(12)


def run_unpack_rest(*parts):
    return pl.pallas_call(
        unpack_rest,
        out_shape=[shape_of((3, WIDTH), f32), shape_of((3, HIDDEN), f32), shape_of((12, WIDTH), f32)]
        + [shape_of((3,), f32)] * 4
        + [shape_of((12,), f32)],
        scratch_shapes=[pltpu.VMEM((128, 128), f32), pltpu.VMEM((128, 128), f32)],
        compiler_params=params(12),
        cost_estimate=cost(2),
        name="unpack_rest",
    )(*parts)


def add_halves(mine_ref, theirs_ref, out_far, out_ref, semaphores):
    copies = Copies(semaphores)
    count = CHIPS // 4
    for at in range(0, CHIPS, count):
        out_ref[at : at + count] = mine_ref[at : at + count] + theirs_ref[at : at + count]
        part = pl.ds(at, count)
        copies.start(out_ref.at[part], out_far.at[part])
    copies.wait_all()


def run_add_halves(mine, theirs):
    arrays = pl.BlockSpec(memory_space=pltpu.VMEM)
    return pl.pallas_call(
        add_halves,
        in_specs=[arrays, arrays],
        out_specs=pl.BlockSpec(memory_space=pl.ANY),
        out_shape=pltpu.HBM(mine.shape, bf16),
        scratch_shapes=[pltpu.VMEM(mine.shape, bf16), pltpu.SemaphoreType.DMA((4,))],
        compiler_params=params(12),
        cost_estimate=cost(1),
        name="add_halves",
    )(*held(mine, theirs))


def forward_scores(unit, projected_ref, bias_ref, key_ref, value_ref, more):
    slot, base = unit
    scale = math.log2(math.e) / math.sqrt(HEAD)
    lanes = slice(slot * WIDE, slot * WIDE + WIDE)
    query_more, key_more, value_more = more[slot]
    wide = lambda start: jnp.concatenate([bias_ref[start : start + HEAD, :]] * (WIDE // 128), 1)
    queries, scores = [], []
    for h in range(base, base + FORWARD_BATCH):
        at = h * HEAD
        query = (projected_ref[at : at + HEAD, lanes] + wide(at)) * scale
        key = projected_ref[at + WIDTH : at + WIDTH + HEAD, lanes]
        value = projected_ref[at + 2 * WIDTH : at + 2 * WIDTH + HEAD, lanes] + wide(at + WIDTH)
        query = jnp.concatenate([query, query_more], 0)
        key = jnp.concatenate([key, key_more], 0).astype(bf16)
        key_ref[slot, 32 * h : 32 * h + 32, :] = key
        value_ref[slot, 32 * h : 32 * h + 32, :] = jnp.concatenate([value, value_more], 0).astype(bf16)
        low = query.astype(bf16)
        queries.append(query)
        scores.append([dot(key[:, :count], low[:, a:b], (0, 0)) for a, b, count in FORWARD_BLOCKS])
    return queries, scores


def forward_mixed(unit, queries, scores, mixed_scratch, query_ref, value_ref):
    slot, base = unit
    heads = range(base, base + FORWARD_BATCH)
    peaks = [[jnp.max(part, axis=0, keepdims=True) for part in parts] for parts in scores]
    weights = [[jnp.exp2(part - top).astype(bf16) for part, top in zip(*pair)] for pair in zip(scores, peaks)]
    values = [value_ref[slot, 32 * h : 32 * h + 32, :] for h in heads]
    got = [
        [dot(value[:, :count], part, (1, 0)) for part, (_, _, count) in zip(parts, FORWARD_BLOCKS)]
        for value, parts in zip(values, weights)
    ]
    zero = jnp.zeros((1, WIDE), f32)
    for h, query, tops, parts in zip(heads, queries, peaks, got):
        both = jnp.concatenate(parts, 1)
        row_total = both[HEAD : HEAD + 1]
        mixed_scratch[h * HEAD : h * HEAD + HEAD, :] = both[:HEAD] * (1.0 / row_total)
        logs = jnp.concatenate(tops, 1) + jnp.log2(row_total)
        log_rows = rows_of([zero, zero, zero, *three_parts(-logs)], WIDE)
        query_ref[slot, 32 * h : 32 * h + 32, :] = (query + jnp.concatenate([jnp.zeros((HEAD, WIDE), f32), log_rows], 0)).astype(bf16)


def forward_probs(unit, query_ref, key_ref, refs):
    slot, base = unit
    for h in range(base, base + FORWARD_BATCH):
        query, key = query_ref[slot, 32 * h : 32 * h + 32, :], key_ref[slot, 32 * h : 32 * h + 32, :]
        for ref, (start, a, b) in zip(refs, BACKWARD_BLOCKS):
            ref[h] = jnp.exp2(dot(query[:, start:ROWS], key[:, a:b], (0, 0))).astype(bf16)


def attention_forward(core_ref, counts_ref, tokens_far, own_ref, other_ref,
                      mixed_far, query_far, key_far, value_far, weight_far, first_far, merged_far, low_far, middle_far, high_far, column_far, extra_far,
                      first_ref, projected_ref, mixed_scratch, arrived_ref, bias_ref,
                      raw_ref, tokens_ref, mixed_ref, query_ref, key_ref, value_ref, weight_ref, low_ref, middle_ref, high_ref, column_ref, extra_ref, semaphores):
    slots = mixed_ref.shape[0]
    copies = Copies(semaphores)
    copies.start(tokens_far, raw_ref)
    core = core_ref[0]
    for k, (side, ref) in enumerate(((core, own_ref), (1 - core, other_ref))):
        blocks = jnp.swapaxes(ref[...], 0, 1)
        for r in range(3):
            at = pl.multiple_of(side * 192 + 64 * r, 64)
            for j in range(10):
                arrived_ref[pl.ds(at, 64), 128 * j : 128 * j + 128] = blocks[10 * r + j]
        extra_ref[2 * k] = blocks[30]
        extra_ref[2 * k + 1] = blocks[31]
    order = arrival_order()
    ordered = dot(order, arrived_ref[...], (1, 0))
    weight_ref[...] = ordered[:, : 3 * WIDTH].astype(bf16)
    column_ref[...] = ordered[:, 3 * WIDTH :]
    rows = dot(arrived_ref[:, 3 * WIDTH :], order, (0, 1))
    gain, offset = rows[0:1], rows[1:2]
    for s in range(2):
        column = ordered[:, 3 * WIDTH + 2 + s : 3 * WIDTH + 3 + s]
        bias_ref[pl.ds(s, WIDTH, stride=2), :] = jnp.broadcast_to(column, (WIDTH, 128))
    first_ref[...] = jnp.zeros_like(first_ref)
    copies.wait_all()
    merge_slots(raw_ref, tokens_ref)
    copies.start(tokens_ref, merged_far)
    copies.start(weight_ref, weight_far)
    copies.start(column_ref, column_far)
    copies.start(extra_ref, extra_far)
    for slot in range(slots):
        normed, _ = norm_parts(tokens_ref[slot * ROWS : slot * ROWS + ROWS, :].astype(f32))
        first_ref[slot * WIDE : slot * WIDE + ROWS, :] = (normed * gain + offset).astype(bf16)
    copies.start(first_ref, first_far)
    projected_ref[...] = dot(weight_ref[...], first_ref[...], (0, 1))
    one = jnp.ones((1, WIDE), f32)
    more = []
    for slot in range(slots):
        hidden, frame = mask_rows(counts_ref, slot)
        more.append((rows_of(frame, WIDE), rows_of(hidden + [one, one, one], WIDE), rows_of([one, one, one], WIDE)))
    units = [(slot, base) for slot in range(slots) for base in range(0, HEADS, FORWARD_BATCH)]
    refs = (low_ref, middle_ref, high_ref)
    kept = {}

    def probs(unit):
        slot, base = unit
        if slot * HEADS + base >= KEPT_HEADS:
            return
        copies.wait(*kept.get((slot - 1, base // LOAD_BATCH), ()))
        forward_probs(unit, query_ref, key_ref, refs)
        if (base + FORWARD_BATCH) % LOAD_BATCH == 0:
            part = pl.ds(base // LOAD_BATCH * LOAD_BATCH, LOAD_BATCH)
            pairs = zip(refs, (low_far, middle_far, high_far))
            kept[slot, base // LOAD_BATCH] = [copies.start(near.at[part], away.at[slot, part]) for near, away in pairs]

    def scores(unit):
        slot, base = unit
        got = forward_scores(unit, projected_ref, bias_ref, key_ref, value_ref, more)
        if base + FORWARD_BATCH == HEADS:
            for near, away in ((key_ref, key_far), (value_ref, value_far)):
                copies.start(near.at[slot], away.at[slot])
        return got

    ready = scores(units[0])
    for k, unit in enumerate(units):
        slot = unit[0]
        now, ready = ready, None
        if k + 1 < len(units):
            ready = scores(units[k + 1])
        if k >= 1:
            probs(units[k - 1])
        forward_mixed(unit, *now, mixed_scratch, query_ref, value_ref)
        if unit[1] + FORWARD_BATCH == HEADS:
            mixed_ref[slot] = mixed_scratch[...].astype(bf16)
            for near, away in ((query_ref, query_far), (mixed_ref, mixed_far)):
                copies.start(near.at[slot], away.at[slot])
    probs(units[-1])
    copies.wait_all()


def probs_shapes():
    return [(ROWS - start, b - a) for start, a, b in BACKWARD_BLOCKS]


def run_forward(core, counts, tokens, own, other):
    slots = tokens.shape[1]
    scalars = pl.BlockSpec(memory_space=pltpu.SMEM)
    arrays = pl.BlockSpec(memory_space=pltpu.VMEM)
    away = pl.BlockSpec(memory_space=pl.ANY)
    return pl.pallas_call(
        attention_forward,
        in_specs=[scalars, scalars, away, arrays, arrays],
        out_specs=[away] * 12,
        out_shape=[pltpu.HBM((slots, rows, WIDE), bf16) for rows in (WIDTH, 512, 512, 512)]
        + [pltpu.HBM((WIDTH, 3 * WIDTH), bf16), pltpu.HBM((slots * WIDE, WIDTH), bf16), pltpu.HBM((slots * ROWS, WIDTH), bf16)]
        + [pltpu.HBM((slots, HEADS, *shape), bf16) for shape in probs_shapes()]
        + [pltpu.HBM((WIDTH, 128), f32), pltpu.HBM((4, 64, 128), bf16)],
        scratch_shapes=[
            pltpu.VMEM((slots * WIDE, WIDTH), bf16),
            pltpu.VMEM((3 * WIDTH, slots * WIDE), f32),
            pltpu.VMEM((WIDTH, WIDE), f32),
            pltpu.VMEM((WIDTH, 3 * WIDTH + 128), bf16),
            pltpu.VMEM((2 * WIDTH + 8, 128), f32),
            pltpu.VMEM((SPAN, slots, WIDTH), bf16),
            pltpu.VMEM((slots * ROWS, WIDTH), bf16),
        ]
        + [pltpu.VMEM((slots, rows, WIDE), bf16) for rows in (WIDTH, 512, 512, 512)]
        + [pltpu.VMEM((WIDTH, 3 * WIDTH), bf16)]
        + [pltpu.VMEM((HEADS, *shape), bf16) for shape in probs_shapes()]
        + [pltpu.VMEM((WIDTH, 128), f32), pltpu.VMEM((4, 64, 128), bf16), pltpu.SemaphoreType.DMA((40,))],
        compiler_params=params(48),
        cost_estimate=cost(20),
        name="attention_forward",
    )(core, counts, *far(tokens), *held(own, other))


def feed_forward_early(cotangent_far, merged_far, mixed_far, extra_far, own_ref,
                       arrived_ref, down_ref, up_b_ref, cotangent_ref, tokens_ref, mixed_ref, slopes_ref, extra_ref, raw_ref, semaphores):
    copies = Copies(semaphores)
    extra = copies.start(extra_far, extra_ref)
    raw = copies.start(cotangent_far, raw_ref)
    copies.start(mixed_far, mixed_ref)
    copies.start(merged_far, tokens_ref)
    unpack_side(own_ref, lambda: (copies.wait(extra), extra_ref[0], extra_ref[1])[1:], arrived_ref, down_ref, up_b_ref)
    copies.wait(raw)
    merge_slots(raw_ref, cotangent_ref)
    slopes_ref[...] = dot(cotangent_ref[...], down_ref[...], (1, 1))
    copies.wait_all()


def unpack_side(message_ref, extra, arrived_ref, down_ref, up_b_ref):
    blocks = jnp.swapaxes(message_ref[...], 0, 1)
    for r in range(12):
        for j in range(3):
            down_ref[64 * r : 64 * r + 64, 128 * j : 128 * j + 128] = blocks[44 + 3 * r + j]
    for r in range(3):
        for j in range(12):
            arrived_ref[64 * r : 64 * r + 64, 384 + 128 * j : 512 + 128 * j] = blocks[8 + 12 * r + j]
    vectors, tile = extra()
    vectors = vectors.astype(f32)
    for r in range(3):
        rows = slice(64 * r, 64 * r + 64)
        for j in range(3):
            arrived_ref[rows, 128 * j : 128 * j + 128] = tile if 3 * r + j == 8 else blocks[3 * r + j]
        arrived_ref[rows, 1920:2048] = (pltpu.roll(vectors, 128 - 4 * r, 1) if r else vectors).astype(bf16)
    turned = vectors.T
    up_b_ref[0:1, :] = jnp.concatenate([turned[12 + r : 13 + r] for r in range(12)], 1)


def run_feed_forward_early(cotangent, merged, mixed, own, extra):
    _, slots, _ = cotangent.shape
    arrays = pl.BlockSpec(memory_space=pltpu.VMEM)
    away = pl.BlockSpec(memory_space=pl.ANY)
    return pl.pallas_call(
        feed_forward_early,
        in_specs=[away, away, away, away, arrays],
        out_shape=[
            pltpu.VMEM((WIDTH // 2, 2048), bf16),
            pltpu.VMEM((HIDDEN // 2, WIDTH), bf16),
            pltpu.VMEM((8, HIDDEN // 2), f32),
            pltpu.VMEM((slots * ROWS, WIDTH), bf16),
            pltpu.VMEM((slots * ROWS, WIDTH), bf16),
            pltpu.VMEM((slots, WIDTH, WIDE), bf16),
            pltpu.VMEM((slots * ROWS, HIDDEN // 2), f32),
            pltpu.VMEM((4, 64, 128), bf16),
        ],
        scratch_shapes=[pltpu.VMEM((SPAN, slots, WIDTH), bf16), pltpu.SemaphoreType.DMA((4,))],
        compiler_params=params(16),
        cost_estimate=cost(3),
        name="feed_forward_early",
    )(*far(cotangent, merged, mixed, extra), *held(own))


def feed_forward(core_ref, tokens_ref, mixed_ref, cotangent_ref, own_arrived_ref, own_down_ref, own_up_b_ref, slopes_ref, other_ref, extra_ref,
                 activated_ref, resid_ref, other_down_ref, row_ref, grad_resid_far, grad_mixed_far, mine_ref, theirs_ref,
                 arrived_ref, ordered_ref, up_b_ref, packed_ref, grad_down_ref, grad_resid_ref, grad_mixed_ref, second_ref, grad_up_ref,
                 semaphores):
    slots = mixed_ref.shape[0]
    block = 768
    root = math.sqrt(2.0 / math.pi)
    copies = Copies(semaphores)
    core = core_ref[0]
    sides = (core, 1 - core)
    places = [pl.multiple_of(side * (WIDTH // 2), 64) for side in sides]
    unpack_side(other_ref, lambda: (extra_ref[2], extra_ref[3]), arrived_ref, other_down_ref, up_b_ref)
    downs = (own_down_ref, other_down_ref)
    up_bs = (own_up_b_ref, up_b_ref)
    order = arrival_order()
    packed_ref[pl.ds(places[0], WIDTH // 2), :] = own_arrived_ref[...]
    packed_ref[pl.ds(places[1], WIDTH // 2), :] = arrived_ref[...]
    row_ref[...] = dot(packed_ref[:, 1920:], order, (0, 1))[0:8]
    ordered_ref[...] = dot(order, packed_ref[:, :1920], (1, 0)).astype(bf16)
    out_w = ordered_ref[:, :WIDTH]
    up_w = lambda half, at: ordered_ref[:, pl.ds(pl.multiple_of(WIDTH + sides[half] * (HIDDEN // 2) + at, 128), block)]
    out_b, gain, offset = (row_ref[k : k + 1] for k in range(3))
    spans = [slice(slot * ROWS, slot * ROWS + ROWS) for slot in range(slots)]
    norms = {}

    def enter(slot):
        resid = tokens_ref[spans[slot], :].astype(f32) + dot(mixed_ref[slot, :, :ROWS], out_w, (0, 0)) + out_b
        resid_ref[spans[slot], :] = resid
        norms[slot] = norm_parts(resid)
        second_ref[spans[slot], :] = (norms[slot][0] * gain + offset).astype(bf16)

    def products(work):
        slot, half, at = work
        rows = spans[slot]
        up = dot(second_ref[rows, :], up_w(half, at), (1, 0))
        if half == 0:
            return up, slopes_ref[rows, at : at + block]
        return up, dot(cotangent_ref[rows, :], other_down_ref[at : at + block, :], (1, 1))

    lines = {}

    def activate(work, up, grad_activated):
        slot, half, at = work
        rows, cols = spans[slot], slice(half * (HIDDEN // 2) + at, half * (HIDDEN // 2) + at + block)
        up = up + up_bs[half][0:1, at : at + block]
        square = up * up
        tanh = jnp.tanh(up * (root + (root * 0.044715) * square))
        half_tanh = 0.5 + 0.5 * tanh
        activated_ref[rows, cols] = (up * half_tanh).astype(bf16)
        slope = half_tanh + (up * (2.0 * half_tanh * (1.0 - half_tanh))) * (root + (3 * root * 0.044715) * square)
        grad_up = grad_activated * slope
        grad_up_ref[rows, cols] = grad_up.astype(bf16)
        line = jnp.sum(grad_up, axis=0, keepdims=True)
        lines[half, at] = lines[half, at] + line if (half, at) in lines else line

    works = [(slot, half, at) for slot in range(slots) for half in range(2) for at in range(0, HIDDEN // 2, block)]
    enter(0)
    ready = products(works[0])
    for slot in range(1, slots):
        enter(slot)
    for k, work in enumerate(works):
        now = ready
        if k + 1 < len(works):
            ready = products(works[k + 1])
        activate(work, *now)

    grad_branch = cotangent_ref[...]
    halves = [slice(0, HIDDEN // 2), slice(HIDDEN // 2, HIDDEN)]
    side_w = [ordered_ref[:, pl.ds(pl.multiple_of(WIDTH + side * (HIDDEN // 2), 128), HIDDEN // 2)] for side in sides]
    grad_seconds = [sum(dot(grad_up_ref[rows, cols], weight, (1, 1)) for cols, weight in zip(halves, side_w)) for rows in spans]
    attended, sums = [], []

    def leave(slot):
        normed, inverse = norms[slot]
        grad_second = grad_seconds[slot]
        scaled = grad_second * gain
        mean_one = jnp.mean(scaled, axis=-1, keepdims=True)
        mean_two = jnp.mean(scaled * normed, axis=-1, keepdims=True)
        grad_full = cotangent_ref[spans[slot], :].astype(f32)
        grad_resid = grad_full + inverse * (scaled - mean_one - normed * mean_two)
        grad_resid_ref[spans[slot], :] = grad_resid
        low = grad_resid.astype(bf16)
        attended.append(low)
        parts = [low.astype(f32), grad_second * normed, grad_second, grad_full]
        sums.append(jnp.concatenate([jnp.sum(part, axis=0, keepdims=True) for part in parts], 0))

    for slot in range(slots):
        leave(slot)
        cols = halves[slot % 2]
        grad_down_ref[cols, :] = dot(activated_ref[:, cols], grad_branch, (0, 0)).astype(bf16)
    copies.start(grad_resid_ref, grad_resid_far)
    for slot in range(slots):
        grad_mixed_ref[slot, :, 512:WIDE] = jnp.zeros((WIDTH, WIDE - 512), bf16)
        grad_mixed_ref[slot, :, :ROWS] = dot(out_w, attended[slot], (1, 1)).astype(bf16)
    copies.start(grad_mixed_ref, grad_mixed_far)
    grad_out = sum(dot(mixed_ref[slot, :, :ROWS], attended[slot], (1, 0)) for slot in range(slots))
    for side, cols in zip(sides, halves):
        at = pl.multiple_of(WIDTH + side * (HIDDEN // 2), 128)
        ordered_ref[:, pl.ds(at, HIDDEN // 2)] = dot(second_ref[...], grad_up_ref[:, cols], (0, 0)).astype(bf16)
    ordered_ref[:, :WIDTH] = grad_out.astype(bf16)
    packed_ref[:, :1920] = dot(order, ordered_ref[...], (0, 0)).astype(bf16)
    high, low = two_parts(sum(sums))
    rows = jnp.concatenate([high, low, jnp.zeros((120, WIDTH), f32)], 0).astype(bf16)
    packed_ref[:, 1920:] = dot(order, rows, (0, 1)).astype(bf16)
    blank = jnp.zeros((CHIPS, 128), bf16)
    for half, (place, ref) in enumerate(zip(places, (mine_ref, theirs_ref))):
        blocks = [blank] * REST_ROWS
        for r in range(3):
            at = pl.multiple_of(place + 64 * r, 64)
            for j in range(15):
                blocks[3 * r + j if j < 3 else 6 + 12 * r + j] = packed_ref[pl.ds(at, 64), 128 * j : 128 * j + 128]
            blocks[81 + r] = packed_ref[pl.ds(at, 64), 1920:2048]
        for r in range(12):
            at = half * (HIDDEN // 2) + 64 * r
            for j in range(3):
                blocks[45 + 3 * r + j] = grad_down_ref[at : at + 64, 128 * j : 128 * j + 128]
        high, low = two_parts(jnp.concatenate([lines[half, at] for at in range(0, HIDDEN // 2, block)], 1))
        rows = [part[:, 64 * r : 64 * r + 64] for part in (high, low) for r in range(12)]
        blocks[84] = rows_of(rows, 64, 128).T.astype(bf16)
        ref[...] = jnp.swapaxes(jnp.stack(blocks), 0, 1)
    copies.wait_all()


def run_feed_forward(core, tokens, mixed, cotangent, arrived, down, up_b, slopes, other, extra):
    slots = mixed.shape[0]
    arrays = pl.BlockSpec(memory_space=pltpu.VMEM)
    away = pl.BlockSpec(memory_space=pl.ANY)
    return pl.pallas_call(
        feed_forward,
        in_specs=[pl.BlockSpec(memory_space=pltpu.SMEM)] + [arrays] * 9,
        out_specs=[arrays, arrays, arrays, arrays, away, away, arrays, arrays],
        out_shape=[
            pltpu.VMEM((slots * ROWS, HIDDEN), bf16),
            pltpu.VMEM((slots * ROWS, WIDTH), f32),
            pltpu.VMEM((HIDDEN // 2, WIDTH), bf16),
            pltpu.VMEM((8, WIDTH), f32),
            pltpu.HBM((slots * ROWS, WIDTH), f32),
            pltpu.HBM((slots, WIDTH, WIDE), bf16),
            pltpu.VMEM((CHIPS, REST_ROWS, 128), bf16),
            pltpu.VMEM((CHIPS, REST_ROWS, 128), bf16),
        ],
        scratch_shapes=[
            pltpu.VMEM((WIDTH // 2, 2048), bf16),
            pltpu.VMEM((WIDTH, 1920), bf16),
            pltpu.VMEM((8, HIDDEN // 2), f32),
            pltpu.VMEM((WIDTH, 2048), bf16),
            pltpu.VMEM((HIDDEN, WIDTH), bf16),
            pltpu.VMEM((slots * ROWS, WIDTH), f32),
            pltpu.VMEM((slots, WIDTH, WIDE), bf16),
            pltpu.VMEM((slots * ROWS, WIDTH), bf16),
            pltpu.VMEM((slots * ROWS, HIDDEN), bf16),
            pltpu.SemaphoreType.DMA((2,)),
        ],
        compiler_params=params(34),
        cost_estimate=cost(17),
        name="feed_forward",
    )(core, *held(tokens, mixed, cotangent, arrived, down, up_b, slopes, other, extra))


def feed_forward_output(activated_ref, resid_ref, own_down_ref, other_down_ref, row_ref, out_far, out_ref, semaphores):
    slots = out_ref.shape[1]
    copies = Copies(semaphores)
    half, middle = HIDDEN // 2, ROWS // 2
    for low, high in ((0, middle), (middle, SPAN)):
        both = []
        for slot in range(slots):
            at = slice(slot * ROWS + low, slot * ROWS + low + middle)
            result = resid_ref[at, :] + row_ref[3:4]
            result += dot(activated_ref[at, :half], own_down_ref[...], (1, 0)) + dot(activated_ref[at, half:], other_down_ref[...], (1, 0))
            both.append(result[: high - low])
        out_ref[low:high] = jnp.swapaxes(jnp.stack(both), 0, 1).astype(bf16)
        part = pl.ds(low, high - low)
        copies.start(out_ref.at[part], out_far.at[part])
    copies.wait_all()


def run_feed_forward_output(*args):
    slots = args[1].shape[0] // ROWS
    return pl.pallas_call(
        feed_forward_output,
        out_specs=pl.BlockSpec(memory_space=pl.ANY),
        out_shape=pltpu.HBM((SPAN, slots, WIDTH), bf16),
        scratch_shapes=[pltpu.VMEM((SPAN, slots, WIDTH), bf16), pltpu.SemaphoreType.DMA((2,))],
        compiler_params=params(20),
        cost_estimate=cost(3),
        name="feed_forward_output",
    )(*held(*args))


def backward_slopes(unit, copies, loads, value_ref, mixed_ref, grad_mixed_ref):
    slot, base = unit
    copies.wait(*loads["grad"][slot])
    grads, slopes = [], []
    for h in range(base, base + BACKWARD_BATCH):
        both = slice(48 * (h // 2), 48 * (h // 2) + 48)
        part = slice(HEAD * (h % 2), HEAD * (h % 2) + HEAD)
        grad = grad_mixed_ref[slot, both, :].astype(f32)[part]
        mixed = mixed_ref[slot, both, :].astype(f32)[part]
        shift = jnp.sum(grad * mixed, axis=0, keepdims=True)
        grad = jnp.concatenate([grad, rows_of(three_parts(-shift), WIDE)], 0).astype(bf16)
        value = value_ref[slot, 32 * h : 32 * h + 32, :]
        grads.append(grad)
        slopes.append([dot(grad[:, start:ROWS], value[:, a:b], (0, 0)) for start, a, b in BACKWARD_BLOCKS])
    return grads, slopes


def backward_products(unit, grads, slopes, copies, loads, query_ref, key_ref, probs_refs, turned_ref):
    slot, base = unit
    heads = range(base, base + BACKWARD_BATCH)
    copies.wait(*loads["query"][slot])
    queries = [query_ref[slot, 32 * h : 32 * h + 32, :] for h in heads]
    keys = [key_ref[slot, 32 * h : 32 * h + 32, :] for h in heads]
    if slot * HEADS + base < KEPT_HEADS:
        copies.wait(*loads["probs"][slot][base // LOAD_BATCH])
        probs = [[ref[slot, h].astype(f32) for ref in probs_refs] for h in heads]
    else:
        probs = [
            [jnp.exp2(dot(query[:, start:ROWS], key[:, a:b], (0, 0))) for start, a, b in BACKWARD_BLOCKS]
            for query, key in zip(queries, keys)
        ]
    grad_scores = [[(part * slope).astype(bf16) for part, slope in zip(*pair)] for pair in zip(probs, slopes)]
    probs = [[part.astype(bf16) for part in parts] for parts in probs]
    over = lambda left, parts: jnp.concatenate(
        [dot(left[:, start:ROWS], part, (1, 0)) for part, (start, _, _) in zip(parts, BACKWARD_BLOCKS)], 1)
    grad_v = [over(grad, parts) for grad, parts in zip(grads, probs)]
    grad_k = [over(query, parts) for query, parts in zip(queries, grad_scores)]
    grad_q = [
        [dot(key[:, a:b], part, (1, 1)) for part, (_, a, b) in zip(parts, BACKWARD_BLOCKS)]
        for key, parts in zip(keys, grad_scores)
    ]
    fill = lambda part: jnp.concatenate([jnp.zeros((32, ROWS - part.shape[1]), f32), part], 1) if part.shape[1] < ROWS else part
    blank = jnp.zeros((HEAD, WIDE - ROWS), f32)
    whole_q = [jnp.concatenate([sum(fill(part) for part in parts)[:HEAD] * (1.0 / math.sqrt(HEAD)), blank], 1) for parts in grad_q]
    whole_k = [part[:HEAD] * math.log(2.0) for part in grad_k]
    whole_v = [part[:HEAD] for part in grad_v]
    for k in range(0, BACKWARD_BATCH, 2):
        at = (base + k) * HEAD
        for offset, parts in ((0, whole_q), (WIDTH, whole_k), (2 * WIDTH, whole_v)):
            turned_ref[slot, offset + at : offset + at + 2 * HEAD, :] = jnp.concatenate(parts[k : k + 2], 0).astype(bf16)


def attention_backward(core_ref, query_far, key_far, value_far, mixed_far, grad_mixed_far, low_far, middle_far, high_far, first_far, weight_far,
                       column_far, turned_far, mine_ref, theirs_ref,
                       bias_ref, packed_ref, turned_ref,
                       query_ref, key_ref, value_ref, mixed_ref, grad_mixed_ref, low_ref, middle_ref, high_ref, first_ref, weight_ref, column_ref, semaphores):
    slots = mixed_ref.shape[0]
    copies = Copies(semaphores)
    loads = {"grad": [], "probs": [], "query": []}
    probs_refs = (low_ref, middle_ref, high_ref)
    for slot in range(slots):
        load = lambda pairs: [copies.start(away.at[slot], near.at[slot]) for away, near in pairs]
        loads["grad"].append(load(((value_far, value_ref), (grad_mixed_far, grad_mixed_ref), (mixed_far, mixed_ref))))
        loads["probs"].append([])
        for base in range(0, HEADS, LOAD_BATCH):
            if slot * HEADS + base < KEPT_HEADS:
                part = pl.ds(base, LOAD_BATCH)
                pairs = zip((low_far, middle_far, high_far), probs_refs)
                loads["probs"][slot].append([copies.start(away.at[slot, part], near.at[slot, part]) for away, near in pairs])
            if base == 0:
                loads["query"].append(load(((query_far, query_ref), (key_far, key_ref))))
    weights = [copies.start(first_far, first_ref.at[:, pl.ds(0, WIDTH)]), copies.start(weight_far, weight_ref), copies.start(column_far, column_ref)]
    core = core_ref[0]
    units = [(slot, base) for slot in range(slots) for base in range(0, HEADS, BACKWARD_BATCH)]
    ready = backward_slopes(units[0], copies, loads, value_ref, mixed_ref, grad_mixed_ref)
    for k, unit in enumerate(units):
        slot = unit[0]
        now, ready = ready, None
        if k + 1 < len(units):
            ready = backward_slopes(units[k + 1], copies, loads, value_ref, mixed_ref, grad_mixed_ref)
        backward_products(unit, *now, copies, loads, query_ref, key_ref, probs_refs, turned_ref)
        if unit[1] + BACKWARD_BATCH == HEADS:
            copies.start(turned_ref.at[slot], turned_far.at[slot])
    copies.wait(*weights)
    order = arrival_order()
    turned = jnp.concatenate([turned_ref[slot] for slot in range(slots)], 1)
    first_ref[:, WIDTH:] = jnp.ones((slots * WIDE, 128), bf16)
    grad_more = dot(first_ref[:, : WIDTH + 16], turned, (0, 1))
    grad_weight, sums = grad_more[:WIDTH], grad_more[WIDTH : WIDTH + 1]
    packed_ref[:, : 3 * WIDTH] = dot(order, grad_weight.astype(bf16), (0, 0)).astype(bf16)
    weight = weight_ref[...].astype(f32)
    grad_offset = jnp.sum(weight * sums, axis=1, keepdims=True)
    along = jnp.sum(grad_weight * weight, axis=1, keepdims=True)
    grad_gain = (along - column_ref[:, 1:2] * grad_offset) / column_ref[:, 0:1]
    bias_ref[0:WIDTH] = jnp.broadcast_to(sums[:, :WIDTH], (128, WIDTH)).T
    bias_ref[WIDTH : 2 * WIDTH] = jnp.broadcast_to(sums[:, 2 * WIDTH :], (128, WIDTH)).T
    lane = lax.broadcasted_iota(jnp.int32, (WIDTH, 128), 1)
    columns = jnp.zeros((WIDTH, 128), f32)
    for k, values in enumerate((grad_gain, grad_offset, bias_ref[pl.ds(0, WIDTH, stride=2), :], bias_ref[pl.ds(1, WIDTH, stride=2), :])):
        high, low = two_parts(values)
        columns = jnp.where(lane == k, high, jnp.where(lane == 4 + k, low, columns))
    packed_ref[:, 3 * WIDTH :] = dot(order, columns.astype(bf16), (0, 0)).astype(bf16)
    blank = jnp.zeros((CHIPS, 128), bf16)
    for side, ref in ((core, mine_ref), (1 - core, theirs_ref)):
        blocks = []
        for r in range(3):
            at = pl.multiple_of(side * 192 + 64 * r, 64)
            for j in range(10):
                blocks.append(packed_ref[pl.ds(at, 64), 128 * j : 128 * j + 128])
        ref[...] = jnp.swapaxes(jnp.stack(blocks + [blank, blank]), 0, 1)
    copies.wait_all()


def run_backward(core, query, key, value, mixed, grad_mixed, low, middle, high, first, weight, column):
    slots = mixed.shape[0]
    arrays = pl.BlockSpec(memory_space=pltpu.VMEM)
    away = pl.BlockSpec(memory_space=pl.ANY)
    return pl.pallas_call(
        attention_backward,
        in_specs=[pl.BlockSpec(memory_space=pltpu.SMEM)] + [away] * 11,
        out_specs=[away, arrays, arrays],
        out_shape=[
            pltpu.HBM((slots, 3 * WIDTH, WIDE), bf16),
            pltpu.VMEM((CHIPS, FIRST_ROWS, 128), bf16),
            pltpu.VMEM((CHIPS, FIRST_ROWS, 128), bf16),
        ],
        scratch_shapes=[
            pltpu.VMEM((2 * WIDTH + 8, 128), f32),
            pltpu.VMEM((WIDTH, 3 * WIDTH + 128), bf16),
            pltpu.VMEM((slots, 3 * WIDTH, WIDE), bf16),
        ]
        + [pltpu.VMEM((slots, rows, WIDE), bf16) for rows in (512, 512, 512, WIDTH, WIDTH)]
        + [pltpu.VMEM((slots, HEADS, *shape), bf16) for shape in probs_shapes()]
        + [pltpu.VMEM((slots * WIDE, WIDTH + 128), bf16), pltpu.VMEM((WIDTH, 3 * WIDTH), bf16), pltpu.VMEM((WIDTH, 128), f32), pltpu.SemaphoreType.DMA((70,))],
        compiler_params=params(56),
        cost_estimate=cost(22),
        name="attention_backward",
    )(core, *far(query, key, value, mixed, grad_mixed, low, middle, high, first, weight, column))


def input_backward(merged_far, turned_far, grad_resid_far, weight_far, column_far, out_far,
                   tokens_ref, turned_ref, grad_resid_ref, weight_ref, grad_first_ref, out_ref, column_ref, semaphores):
    slots = turned_ref.shape[0]
    copies = Copies(semaphores)
    first = [copies.start(weight_far, weight_ref), copies.start(turned_far.at[0], turned_ref.at[0])]
    turns = [copies.start(turned_far.at[slot], turned_ref.at[slot]) for slot in range(1, slots)]
    rest = [copies.start(column_far, column_ref), copies.start(merged_far, tokens_ref), copies.start(grad_resid_far, grad_resid_ref)]
    copies.wait(*first)
    for slot in range(slots):
        if slot:
            copies.wait(turns[slot - 1])
        grad_first_ref[slot * ROWS : slot * ROWS + ROWS, :] = dot(turned_ref[slot, :, :ROWS], weight_ref[...], (0, 1))
    copies.wait(*rest)
    gain = column_ref[...].T[0:1]
    half = ROWS // 2
    for low, high in ((0, half), (half, SPAN)):
        for slot in range(slots):
            at = slice(slot * ROWS + low, slot * ROWS + low + half)
            normed, inverse = norm_parts(tokens_ref[at, :].astype(f32))
            scaled = grad_first_ref[at, :] * gain
            mean_one = jnp.mean(scaled, axis=-1, keepdims=True)
            mean_two = jnp.mean(scaled * normed, axis=-1, keepdims=True)
            grad = grad_resid_ref[at, :] + inverse * (scaled - mean_one - normed * mean_two)
            out_ref[low:high, slot, :] = grad[: high - low]
        copies.start(out_ref.at[pl.ds(low, high - low)], out_far.at[pl.ds(low, high - low)])
    copies.wait_all()


def run_input_backward(merged, turned, grad_resid, weight, column):
    slots = turned.shape[0]
    arrays = pl.BlockSpec(memory_space=pltpu.VMEM)
    away = pl.BlockSpec(memory_space=pl.ANY)
    return pl.pallas_call(
        input_backward,
        in_specs=[away] * 5,
        out_specs=away,
        out_shape=pltpu.HBM((SPAN, slots, WIDTH), f32),
        scratch_shapes=[
            pltpu.VMEM((slots * ROWS, WIDTH), bf16),
            pltpu.VMEM((slots, 3 * WIDTH, WIDE), bf16),
            pltpu.VMEM((slots * ROWS, WIDTH), f32),
            pltpu.VMEM((WIDTH, 3 * WIDTH), bf16),
            pltpu.VMEM((slots * ROWS, WIDTH), f32),
            pltpu.VMEM((SPAN, slots, WIDTH), f32),
            pltpu.VMEM((WIDTH, 128), f32),
            pltpu.SemaphoreType.DMA((8,)),
        ],
        compiler_params=params(32),
        cost_estimate=cost(6),
        name="input_backward",
    )(*far(merged, turned, grad_resid, weight, column))


def to_chips(message):
    return lax.all_to_all(message, CHIP_AXES, 0, 0, tiled=True)


def to_column(message):
    return lax.all_to_all(message, COLUMN_AXES, 0, 0, tiled=True)


def along_line(message, shift):
    return lax.ppermute(message, LINE_AXIS, [(k, (k + shift) % LINE) for k in range(LINE)])


def across(message):
    return lax.ppermute(message, CORE_AXIS, [(0, 1), (1, 0)])


def shards(tokens, item_frames, ln1_gain, ln1_bias, qkv_weight, qv_bias, out_weight, out_bias, ln2_gain, ln2_bias,
           up_weight, up_bias, down_weight, down_bias, cotangent):
    together = lax.optimization_barrier
    core = lax.axis_index(CORE_AXIS).astype(jnp.int32).reshape(1)
    line = lax.axis_index(LINE_AXIS).astype(jnp.int32).reshape(1)
    first = run_pack_first(qkv_weight, ln1_gain, ln1_bias, qv_bias, out_weight, out_bias, ln2_gain, ln2_bias, down_bias, up_bias)
    first, up_weight = together((first, up_weight))
    first = to_chips(first)
    up_sent = up_weight.reshape(3, 16, 2, 4, 12).transpose(0, 2, 4, 1, 3).reshape(3, HIDDEN)
    second = run_pack_second(out_weight, up_sent, down_weight)
    tokens, cotangent = tokens.transpose(1, 0, 2), cotangent.transpose(1, 0, 2)
    first, second = together((first, second))
    first_other = across(first)
    second = to_chips(second)
    mixed, query, key, value, weight, normed, merged, low, middle, high, column, extra = run_forward(core, item_frames, tokens, first, first_other)
    second, mixed = together((second, mixed))
    other = across(second)
    arrived, own_down, up_b, turned_cotangent, near, near_mixed, slopes, extra = run_feed_forward_early(cotangent, merged, mixed, second, extra)
    activated, resid, other_down, row, grad_resid, grad_mixed, mine, theirs = run_feed_forward(
        core, near, near_mixed, turned_cotangent, arrived, own_down, up_b, slopes, other, extra)
    theirs = across(theirs)
    output = run_feed_forward_output(activated, resid, own_down, other_down, row)
    output, mine = together((output, mine))
    output = output.transpose(1, 0, 2)
    rest = run_add_halves(mine, theirs)
    rest, grad_mixed = together((rest, grad_mixed))
    rest = to_column(rest.reshape(CHIPS // LINE, LINE * REST_ROWS, 128))
    turned, mine, theirs = run_backward(core, query, key, value, mixed, grad_mixed, low, middle, high, normed, weight, column)
    theirs = across(theirs)
    own = run_add_halves(mine, theirs)
    own, rest = together((own, rest))
    own, turned = together((own, turned))
    own = to_chips(own)
    keep, *sent = run_sum_column(line, rest)
    sent = [along_line(part, shift + 1) for shift, part in enumerate(sent)]
    grad_out, grad_up, *others = run_unpack_rest(keep, *sent)
    grad_down, grad_out_b, grad_gain_two, grad_offset_two, grad_down_b, grad_up_b = others
    input_grad = run_input_backward(merged, turned, grad_resid, weight, column).transpose(1, 0, 2)
    grad_qkv, grad_gain, grad_offset, grad_qv = run_unpack_first(own)
    return (output, input_grad, grad_gain, grad_offset, grad_qkv, grad_qv, grad_out, grad_out_b, grad_gain_two, grad_offset_two,
            grad_up, grad_up_b, grad_down, grad_down_b)


def solution(mesh):
    split = Mesh(mesh.devices.reshape(4, 4, 2, mesh.shape["narrow"]), ALL)
    by_rank = lambda n: P(ALL, *([None] * (n - 1)))
    return jax.shard_map(
        shards,
        mesh=split,
        in_specs=tuple(by_rank(n) for n in (3, 2, 1, 1, 2, 1, 2, 1, 1, 1, 2, 1, 2, 1, 3)),
        out_specs=tuple(by_rank(n) for n in (3, 3, 1, 1, 2, 1, 2, 1, 1, 1, 2, 1, 2, 1)),
        check_vma=False,
    )
```
